32 devices in a mesh: group: 8 (over z, core), tensor: 4 (over y, x).
Axes of the slice: x: 2, y: 2, z: 4, core: 2. Of those that a mesh axis runs over, the one named last changes fastest.
Arguments:
- hidden_x: bfloat16 [16, 8, 8192], P('group', None, 'tensor'), may hold values from -6 to 6
- base_weight: bfloat16 [2048, 8192], P(None, 'tensor'), may hold values from -0.0625 to 0.0625
- delta_codes: bfloat16 [2048, 8192], P('group', 'tensor'), may hold values from -4 to 4
- delta_scales: bfloat16 [2048, 64], P('group', 'tensor'), may hold values from 0.0019989014 to 0.019897461
- owner_map: int32 [8], replicated, may hold values from 0 to 7, each once
- kv_cache: bfloat16 [16, 1024, 2048], P('group', 'tensor'), may hold values from -6 to 6
- queries: bfloat16 [16, 8, 8192], P('group'), may hold values from -180 to 180
- lengths: int32 [16], P('group'), may hold values from 256 to 1024, as said below
Outputs:
- new_kv: bfloat16 [16, 8, 2048], P('group', None, 'tensor')
- attended: bfloat16 [16, 8, 8192], P('group', None, 'tensor')
The draws below stay inside these ranges and needn't reach their ends.
Inputs may be any that keep to these rules, and one draw needn't show every extreme that they name: `owner_map`: a permutation of the shard indices. Row r's entries are its first lengths[r] cache positions; some row is full.
All inputs are finite; a program needn't handle non-finite values.
Results may differ from the reference program's by a relative error of at most 0.009.
Values may be sent and summed in bfloat16 or wider, within the bound.
No kernel may reach another device: no remote copies, remote signals or barrier semaphores. Data moves between devices by JAX's collectives and lax.ppermute only.
A program may use at most 64 MiB of HBM per device.

```python
import math
import jax
import jax.numpy as jnp
from jax import lax

D = 8192
H = 64
KVH = 8
HD = 128
BLK = 128
STEPS = 8
CACHE_DEV = 256
CACHE = 1024
ROWS_ALL = 16
OUT = 2048
N_GROUP = 8
N_TENSOR = 4


def anchor_keys(key):
    anchor = jnp.clip(jax.random.normal(jax.random.fold_in(key, 77), (ROWS_ALL, KVH * HD), jnp.float32), -6.0, 6.0)
    anchor = anchor.at[:, 0].set(6.0)
    return anchor.at[:, 1].set(-6.0)


def draw_kv_cache(key, part):
    anchor = anchor_keys(key)
    key = jax.random.fold_in(key, 11)
    base = jnp.clip(jax.random.normal(key, (ROWS_ALL, CACHE, 2 * KVH * HD), jnp.float32), -6.0, 6.0)
    base = base.at[:, 0, :KVH * HD].set(anchor)
    return base.astype(jnp.bfloat16)


def draw_queries(key, part):
    key = jax.random.fold_in(key, 23)
    fresh = jnp.clip(jax.random.normal(key, (ROWS_ALL, STEPS, H * HD), jnp.float32), -6.0, 6.0)
    return fresh.astype(jnp.bfloat16)


def draw_lengths(key, part):
    key = jax.random.fold_in(key, 5)
    values = jax.random.randint(key, (ROWS_ALL,), CACHE // 4, CACHE + 1)
    full_row = jax.random.randint(jax.random.fold_in(key, 6), (), 0, ROWS_ALL)
    values = jnp.where(jnp.arange(ROWS_ALL) == full_row, CACHE, values)
    return values.astype(jnp.int32)


def shard_levels(rng, dims, pieces, smallest, largest):
    def one(axis_at, shards_of):
        draws = jax.random.uniform(jax.random.fold_in(jax.random.fold_in(rng, 6), axis_at), (shards_of,), jnp.float32, smallest / len(pieces), largest / len(pieces))
        return jnp.repeat(jnp.exp(draws), dims[axis_at] // shards_of).reshape((-1,) + (1,) * (len(dims) - axis_at - 1))

    level = one(*pieces[0])
    for cut in pieces[1:]:
        level = level * one(*cut)
    return level


def gaussian(key, shape, spread, reach, shards=(), kind=jnp.bfloat16):
    entries = jax.random.normal(key, shape, jnp.float32) * spread
    if len(shards) > 0:
        entries = shard_levels(key, shape, shards, -0.22, 0.18) * entries
    return jnp.clip(entries, min=-reach, max=reach).astype(kind)


def setup_inputs(seed: int = 0) -> dict:
    keys = jax.random.split(jax.random.key(seed), 9)
    return {
        "hidden_x": gaussian(keys[0], (ROWS_ALL, STEPS, D), 1.0, 6.0, ((0, 8), (2, 4))),
        "base_weight": gaussian(keys[1], (OUT, D), D ** -0.5, 0.0625, ((1, 4),)),
        "delta_codes": gaussian(keys[2], (OUT, D), 1.0, 4.0, ((0, 8), (1, 4))),
        "delta_scales": jnp.clip(jnp.exp(math.log(0.019897461) - 2.2979944 * jax.random.uniform(keys[3], (OUT, D // BLK), jnp.float32) ** shard_levels(keys[3], (OUT, D // BLK), ((0, 8), (1, 4)), -0.2, 0.2)), 0.0019989014, 0.019897461).astype(jnp.bfloat16),
        "owner_map": jax.random.permutation(keys[4], N_GROUP).astype(jnp.int32),
        "kv_cache": draw_kv_cache(jax.random.fold_in(keys[8], 71), 0),
        "queries": draw_queries(jax.random.fold_in(keys[8], 71), 0),
        "lengths": draw_lengths(jax.random.fold_in(keys[8], 71), 0),
    }


NEGATIVE = -1e30


def attend_row(query_row, cache_row, length_row, new_row):
    score_scale = HD ** -0.5
    kv_width = KVH * HD
    per_group = H // KVH
    grouped_query = query_row.astype(jnp.float32).reshape(STEPS, KVH, per_group, HD)
    cache_keys = cache_row[:, :kv_width].astype(jnp.float32).reshape(N_TENSOR, CACHE_DEV, KVH, HD)
    cache_values = cache_row[:, kv_width:].astype(jnp.float32).reshape(N_TENSOR, CACHE_DEV, KVH, HD)
    scores = jnp.einsum("skgd,nckd->skgnc", grouped_query, cache_keys) * score_scale
    positions = jnp.arange(CACHE, dtype=jnp.int32).reshape(N_TENSOR, CACHE_DEV)
    usable = (positions < length_row)[None, None, None, :, :]
    block_peak = jnp.max(jnp.where(usable, scores, NEGATIVE), axis=-1)
    weights = jnp.where(usable, jnp.exp(scores - block_peak[..., None]), 0.0)
    weight_total = jnp.sum(weights, axis=-1)
    rounded = lax.optimization_barrier(weights.astype(jnp.bfloat16)).astype(jnp.float32)
    weighted = jnp.einsum("skgnc,nckd->skgnd", rounded, cache_values)
    cache_peak = jnp.max(block_peak, axis=-1)
    rescale = jnp.exp(block_peak - cache_peak[..., None])
    cache_total = jnp.sum(weight_total * rescale, axis=-1)
    cache_sum = jnp.sum(weighted * rescale[..., None], axis=-2)
    stored_new = lax.optimization_barrier(new_row).astype(jnp.float32)
    new_keys = stored_new[:, :kv_width].reshape(STEPS, KVH, HD)
    new_values = stored_new[:, kv_width:].reshape(STEPS, KVH, HD)
    near_scores = jnp.einsum("skgd,tkd->skgt", grouped_query, new_keys) * score_scale
    causal = (jnp.arange(STEPS)[:, None] >= jnp.arange(STEPS)[None, :])[:, None, None, :]
    near_peak = jnp.max(jnp.where(causal, near_scores, NEGATIVE), axis=-1)
    near_weights = jnp.where(causal, jnp.exp(near_scores - near_peak[..., None]), 0.0)
    near_total = jnp.sum(near_weights, axis=-1)
    near_rounded = lax.optimization_barrier(near_weights.astype(jnp.bfloat16)).astype(jnp.float32)
    near_sum = jnp.einsum("skgt,tkd->skgd", near_rounded, new_values)
    joined_peak = jnp.maximum(cache_peak, near_peak)
    cache_scale = jnp.exp(cache_peak - joined_peak)
    near_scale = jnp.exp(near_peak - joined_peak)
    numerator = cache_sum * cache_scale[..., None] + near_sum * near_scale[..., None]
    denominator = cache_total * cache_scale + near_total * near_scale
    return (numerator / denominator[..., None]).astype(jnp.bfloat16).reshape(STEPS, H * HD)


def reference(hidden_x, base_weight, delta_codes, delta_scales, owner_map, kv_cache, queries, lengths):
    kv_width = KVH * HD
    out_width = 2 * kv_width
    owner_block = out_width // N_GROUP
    code_values = delta_codes.astype(jnp.float32).reshape(out_width, D // BLK, BLK)
    dequantized = (code_values * delta_scales.astype(jnp.float32)[:, :, None]).reshape(out_width, D).astype(jnp.bfloat16)
    stored = dequantized.reshape(N_GROUP, owner_block, D)
    ordered = jnp.zeros_like(stored).at[owner_map].set(stored).reshape(out_width, D)
    token_rows = hidden_x.reshape(ROWS_ALL * STEPS, D)
    projected = jnp.dot(token_rows, base_weight.T, preferred_element_type=jnp.float32) + jnp.dot(token_rows, ordered.T, preferred_element_type=jnp.float32)
    new_kv = projected.astype(jnp.bfloat16).reshape(ROWS_ALL, STEPS, out_width)

    def one_row(items):
        return attend_row(items[0], items[1], items[2], items[3])

    attended = lax.map(one_row, (queries, kv_cache, lengths, new_kv))
    return new_kv, attended
```

```python
import jax
import jax.numpy as jnp
from jax import lax
from jax.sharding import PartitionSpec as P

H = 64
KVH = 8
HD = 128


NEGATIVE = -1e30


def dequantize(code_values, block_scales):
    blocks = block_scales.shape[1]
    widened = code_values.astype(jnp.float32).reshape(code_values.shape[0], blocks, -1)
    return (
        (widened * block_scales.astype(jnp.float32)[:, :, None])
        .reshape(code_values.shape[0], -1)
        .astype(jnp.bfloat16)
    )


def combine(left_part, right_part):
    left_peak, left_total, left_sum = left_part
    right_peak, right_total, right_sum = right_part
    joined = jnp.maximum(left_peak, right_peak)
    left_scale = jnp.exp(left_peak - joined)
    right_scale = jnp.exp(right_peak - joined)
    return (
        joined,
        left_total * left_scale + right_total * right_scale,
        left_sum * left_scale[..., None] + right_sum * right_scale[..., None],
    )


def swap(x, axis, distance):
    if distance == 0:
        return x
    size = lax.axis_size(axis)
    return lax.ppermute(x, axis, [(k, k ^ distance) for k in range(size)])


def on_device(
    hidden_x, base_weight, delta_codes, delta_scales, owner_map, kv_cache, queries, lengths
):
    score_scale = HD ** (-0.5)
    kv_width = KVH * HD
    per_group = H // KVH
    group_count = lax.axis_size("group")
    tensor_count = lax.axis_size("tensor")
    group_place = lax.axis_index("group")
    tensor_place = lax.axis_index("tensor")
    row_count, step_count, local_width = hidden_x.shape
    tokens = row_count * step_count
    owner_block = delta_codes.shape[0]
    out_width = base_weight.shape[0]
    token_rows = hidden_x.reshape(tokens, local_width)

    pairs = group_count // 2
    gathered = jnp.concatenate([swap(token_rows, "group", 2 * d) for d in range(pairs)], axis=0)
    mate_codes = swap(delta_codes, "group", 1)
    mate_scales = swap(delta_scales, "group", 1)

    grouped_query = queries.reshape(row_count, step_count, KVH, per_group, HD)
    cache_keys = kv_cache[:, :, :kv_width].reshape(row_count, -1, KVH, HD)
    cache_values = kv_cache[:, :, kv_width:].reshape(row_count, -1, KVH, HD)
    cache_len = cache_keys.shape[1]
    scores = (
        jnp.einsum(
            "rskgd,rckd->rskgc", grouped_query, cache_keys, preferred_element_type=jnp.float32
        )
        * score_scale
    )
    positions = tensor_place * cache_len + jnp.arange(cache_len, dtype=jnp.int32)
    usable = (positions[None, :] < lengths[:, None])[:, None, None, None, :]
    block_peak = jnp.max(jnp.where(usable, scores, NEGATIVE), axis=-1)
    weights = jnp.where(usable, jnp.exp(scores - block_peak[..., None]), 0.0)
    weight_total = jnp.sum(weights, axis=-1)
    weighted = jnp.einsum(
        "rskgc,rckd->rskgd",
        weights.astype(jnp.bfloat16),
        cache_values,
        preferred_element_type=jnp.float32,
    )
    heads_own = H // tensor_count
    stats = jnp.stack([block_peak, weight_total], axis=0).reshape(2, row_count, step_count, H)
    sums = weighted.reshape(row_count, step_count, H, HD)
    parts = None
    for dt in range(tensor_count):
        head_to = (tensor_place ^ dt) * heads_own
        stats_part = swap(lax.dynamic_slice_in_dim(stats, head_to, heads_own, 3), "tensor", dt)
        sums_part = swap(lax.dynamic_slice_in_dim(sums, head_to, heads_own, 2), "tensor", dt)
        part = (stats_part[0], stats_part[1], sums_part)
        parts = part if parts is None else combine(parts, part)
    peak_own, total_own, sum_own = parts

    own = lax.dot_general(
        gathered,
        dequantize(delta_codes, delta_scales),
        (((1,), (1,)), ((), ())),
        preferred_element_type=jnp.float32,
    )
    mate = lax.dot_general(
        gathered,
        dequantize(mate_codes, mate_scales),
        (((1,), (1,)), ((), ())),
        preferred_element_type=jnp.float32,
    )
    both = []
    for k, part in enumerate((own, mate)):
        block = owner_map[group_place ^ k]
        base_rows = lax.dynamic_slice_in_dim(base_weight, block * owner_block, owner_block, 0)
        both.append(
            part
            + lax.dot_general(
                gathered,
                base_rows,
                (((1,), (1,)), ((), ())),
                preferred_element_type=jnp.float32,
            )
        )
    partial = jnp.stack(both, axis=1).reshape(pairs, tokens, 2, owner_block)
    arrived = jnp.stack([swap(partial[d], "group", 2 * d) for d in range(pairs)], axis=0)
    blocks = arrived.transpose(0, 2, 1, 3).reshape(group_count, tokens, owner_block)
    shard_of = jnp.zeros((group_count,), jnp.int32).at[owner_map].set(
        jnp.arange(group_count, dtype=jnp.int32)
    )
    ordered = (
        jnp.take(blocks, shard_of ^ group_place, axis=0)
        .transpose(1, 0, 2)
        .reshape(tokens, out_width)
    )

    slice_width = out_width // tensor_count
    near_heads = max(1, heads_own // per_group)
    near_width = near_heads * HD
    summed = None
    for dt in range(tensor_count):
        to = tensor_place ^ dt
        near_start = (to * heads_own // per_group) * HD
        piece = jnp.concatenate(
            [
                lax.dynamic_slice_in_dim(ordered, near_start, near_width, 1),
                lax.dynamic_slice_in_dim(ordered, kv_width + near_start, near_width, 1),
                lax.dynamic_slice_in_dim(ordered, to * slice_width, slice_width, 1),
            ],
            axis=1,
        )
        piece = swap(piece, "tensor", dt)
        summed = piece if summed is None else summed + piece
    stored = summed.astype(jnp.bfloat16).reshape(row_count, step_count, -1)
    new_out = stored[:, :, 2 * near_width :]
    new_keys = stored[:, :, :near_width].reshape(row_count, step_count, near_heads, HD)
    new_values = stored[:, :, near_width : 2 * near_width].reshape(
        row_count, step_count, near_heads, HD
    )
    own_query = lax.dynamic_slice_in_dim(
        queries.reshape(row_count, step_count, H, HD), tensor_place * heads_own, heads_own, 2
    ).reshape(row_count, step_count, near_heads, -1, HD)
    near_scores = (
        jnp.einsum("rskgd,rtkd->rskgt", own_query, new_keys, preferred_element_type=jnp.float32)
        * score_scale
    )
    causal = (jnp.arange(step_count)[:, None] >= jnp.arange(step_count)[None, :])[
        None, :, None, None, :
    ]
    near_peak = jnp.max(jnp.where(causal, near_scores, NEGATIVE), axis=-1)
    near_weights = jnp.where(causal, jnp.exp(near_scores - near_peak[..., None]), 0.0)
    near_total = jnp.sum(near_weights, axis=-1)
    near_sum = jnp.einsum(
        "rskgt,rtkd->rskgd",
        near_weights.astype(jnp.bfloat16),
        new_values,
        preferred_element_type=jnp.float32,
    )
    shape = (row_count, step_count, heads_own)
    _, denominator, numerator = combine(
        (peak_own, total_own, sum_own),
        (near_peak.reshape(shape), near_total.reshape(shape), near_sum.reshape(shape + (HD,))),
    )
    attended = (
        (numerator / denominator[..., None])
        .astype(jnp.bfloat16)
        .reshape(row_count, step_count, heads_own * HD)
    )
    return (new_out, attended)


def solution(mesh):
    in_specs = (
        P("group", None, "tensor"),
        P(None, "tensor"),
        P("group", "tensor"),
        P("group", "tensor"),
        P(),
        P("group", "tensor", None),
        P("group", None, None),
        P("group"),
    )
    out_specs = (P("group", None, "tensor"), P("group", None, "tensor"))
    return jax.shard_map(
        on_device, mesh=mesh, in_specs=in_specs, out_specs=out_specs, check_vma=False
    )
```

```python
import jax
import jax.numpy as jnp
from jax import lax
from jax.sharding import PartitionSpec as P

H = 64
KVH = 8
HD = 128


NEGATIVE = -1e30


def dequantize(code_values, block_scales):
    blocks = block_scales.shape[1]
    widened = code_values.astype(jnp.float32).reshape(code_values.shape[0], blocks, -1)
    return (
        (widened * block_scales.astype(jnp.float32)[:, :, None])
        .reshape(code_values.shape[0], -1)
        .astype(jnp.bfloat16)
    )


def combine(left_part, right_part):
    left_peak, left_total, left_sum = left_part
    right_peak, right_total, right_sum = right_part
    joined = jnp.maximum(left_peak, right_peak)
    left_scale = jnp.exp(left_peak - joined)
    right_scale = jnp.exp(right_peak - joined)
    return (
        joined,
        left_total * left_scale + right_total * right_scale,
        left_sum * left_scale[..., None] + right_sum * right_scale[..., None],
    )


def swap(x, axis, distance):
    if distance == 0:
        return x
    size = lax.axis_size(axis)
    return lax.ppermute(x, axis, [(k, k ^ distance) for k in range(size)])


def trade(x, axis, stride):
    size = lax.axis_size(axis)
    if stride == 1:
        return lax.all_to_all(x, axis, 0, 0)
    groups = [list(range(k, size, stride)) for k in range(stride)]
    return lax.all_to_all(x, axis, 0, 0, axis_index_groups=groups)


def on_device(
    hidden_x, base_weight, delta_codes, delta_scales, owner_map, kv_cache, queries, lengths
):
    score_scale = HD ** (-0.5)
    kv_width = KVH * HD
    per_group = H // KVH
    group_count = lax.axis_size("group")
    tensor_count = lax.axis_size("tensor")
    group_place = lax.axis_index("group")
    tensor_place = lax.axis_index("tensor")
    row_count, step_count, local_width = hidden_x.shape
    tokens = row_count * step_count
    owner_block = delta_codes.shape[0]
    out_width = base_weight.shape[0]
    token_rows = hidden_x.reshape(tokens, local_width)

    pairs = group_count // 2
    copies = jnp.broadcast_to(token_rows[None], (pairs, tokens, local_width))
    gathered = trade(copies, "group", 2).reshape(pairs * tokens, local_width)
    mate_codes = swap(delta_codes, "group", 1)
    mate_scales = swap(delta_scales, "group", 1)

    grouped_query = queries.reshape(row_count, step_count, KVH, per_group, HD)
    cache_keys = kv_cache[:, :, :kv_width].reshape(row_count, -1, KVH, HD)
    cache_values = kv_cache[:, :, kv_width:].reshape(row_count, -1, KVH, HD)
    cache_len = cache_keys.shape[1]
    scores = (
        jnp.einsum(
            "rskgd,rckd->rskgc", grouped_query, cache_keys, preferred_element_type=jnp.float32
        )
        * score_scale
    )
    positions = tensor_place * cache_len + jnp.arange(cache_len, dtype=jnp.int32)
    usable = (positions[None, :] < lengths[:, None])[:, None, None, None, :]
    block_peak = jnp.max(jnp.where(usable, scores, NEGATIVE), axis=-1)
    weights = jnp.where(usable, jnp.exp(scores - block_peak[..., None]), 0.0)
    weight_total = jnp.sum(weights, axis=-1)
    weighted = jnp.einsum(
        "rskgc,rckd->rskgd",
        weights.astype(jnp.bfloat16),
        cache_values,
        preferred_element_type=jnp.float32,
    )
    heads_own = H // tensor_count
    stats = jnp.stack([block_peak, weight_total], axis=0).reshape(2, row_count, step_count, H)
    sums = weighted.reshape(row_count, step_count, H, HD)
    stats = trade(stats.reshape(-1, tensor_count, heads_own).transpose(1, 0, 2), "tensor", 1)
    sums = trade(
        sums.reshape(row_count, step_count, tensor_count, heads_own, HD).transpose(2, 0, 1, 3, 4),
        "tensor",
        1,
    )
    stats = stats.reshape(tensor_count, 2, row_count, step_count, heads_own)
    parts = None
    for k in range(tensor_count):
        part = (stats[k, 0], stats[k, 1], sums[k])
        parts = part if parts is None else combine(parts, part)
    peak_own, total_own, sum_own = parts

    own = lax.dot_general(
        gathered,
        dequantize(delta_codes, delta_scales),
        (((1,), (1,)), ((), ())),
        preferred_element_type=jnp.float32,
    )
    mate = lax.dot_general(
        gathered,
        dequantize(mate_codes, mate_scales),
        (((1,), (1,)), ((), ())),
        preferred_element_type=jnp.float32,
    )
    both = []
    for k, part in enumerate((own, mate)):
        block = owner_map[group_place ^ k]
        base_rows = lax.dynamic_slice_in_dim(base_weight, block * owner_block, owner_block, 0)
        both.append(
            part
            + lax.dot_general(
                gathered,
                base_rows,
                (((1,), (1,)), ((), ())),
                preferred_element_type=jnp.float32,
            )
        )
    partial = jnp.stack(both, axis=1).reshape(pairs, tokens, 2, owner_block)
    arrived = trade(partial, "group", 2)
    blocks = arrived.transpose(0, 2, 1, 3).reshape(group_count, tokens, owner_block)
    shard_of = jnp.zeros((group_count,), jnp.int32).at[owner_map].set(
        jnp.arange(group_count, dtype=jnp.int32)
    )
    ordered = (
        jnp.take(blocks, shard_of ^ (group_place & 1), axis=0)
        .transpose(1, 0, 2)
        .reshape(tokens, out_width)
    )

    slice_width = out_width // tensor_count
    near_heads = max(1, heads_own // per_group)
    near_width = near_heads * HD
    pieces = []
    for to in range(tensor_count):
        near_start = (to * heads_own // per_group) * HD
        pieces.append(
            jnp.concatenate(
                [
                    ordered[:, near_start : near_start + near_width],
                    ordered[:, kv_width + near_start : kv_width + near_start + near_width],
                    ordered[:, to * slice_width : (to + 1) * slice_width],
                ],
                axis=1,
            )
        )
    summed = jnp.sum(trade(jnp.stack(pieces, axis=0), "tensor", 1), axis=0)
    stored = summed.astype(jnp.bfloat16).reshape(row_count, step_count, -1)
    new_out = stored[:, :, 2 * near_width :]
    new_keys = stored[:, :, :near_width].reshape(row_count, step_count, near_heads, HD)
    new_values = stored[:, :, near_width : 2 * near_width].reshape(
        row_count, step_count, near_heads, HD
    )
    own_query = lax.dynamic_slice_in_dim(
        queries.reshape(row_count, step_count, H, HD), tensor_place * heads_own, heads_own, 2
    ).reshape(row_count, step_count, near_heads, -1, HD)
    near_scores = (
        jnp.einsum("rskgd,rtkd->rskgt", own_query, new_keys, preferred_element_type=jnp.float32)
        * score_scale
    )
    causal = (jnp.arange(step_count)[:, None] >= jnp.arange(step_count)[None, :])[
        None, :, None, None, :
    ]
    near_peak = jnp.max(jnp.where(causal, near_scores, NEGATIVE), axis=-1)
    near_weights = jnp.where(causal, jnp.exp(near_scores - near_peak[..., None]), 0.0)
    near_total = jnp.sum(near_weights, axis=-1)
    near_sum = jnp.einsum(
        "rskgt,rtkd->rskgd",
        near_weights.astype(jnp.bfloat16),
        new_values,
        preferred_element_type=jnp.float32,
    )
    shape = (row_count, step_count, heads_own)
    _, denominator, numerator = combine(
        (peak_own, total_own, sum_own),
        (near_peak.reshape(shape), near_total.reshape(shape), near_sum.reshape(shape + (HD,))),
    )
    attended = (
        (numerator / denominator[..., None])
        .astype(jnp.bfloat16)
        .reshape(row_count, step_count, heads_own * HD)
    )
    return (new_out, attended)


def solution(mesh):
    in_specs = (
        P("group", None, "tensor"),
        P(None, "tensor"),
        P("group", "tensor"),
        P("group", "tensor"),
        P(),
        P("group", "tensor", None),
        P("group", None, None),
        P("group"),
    )
    out_specs = (P("group", None, "tensor"), P("group", None, "tensor"))
    return jax.shard_map(
        on_device, mesh=mesh, in_specs=in_specs, out_specs=out_specs, check_vma=False
    )
```

```python
import functools
import jax
import jax.numpy as jnp
from jax import lax
from jax.experimental import pallas as pl
from jax.experimental.pallas import tpu as pltpu
from jax.sharding import PartitionSpec as P

H = 64
KVH = 8
HD = 128
LANES = 128
SUBLANES = 8


NEGATIVE = -1e30
SCORE_SCALE = HD ** (-0.5)
NT = (((1,), (1,)), ((), ()))
TN = (((0,), (0,)), ((), ()))
VMEM = pl.BlockSpec(memory_space=pltpu.VMEM)
SMEM = pl.BlockSpec(memory_space=pltpu.SMEM)
ANY = pl.BlockSpec(memory_space=pl.ANY)


def dot(left, right, dims):
    return lax.dot_general(left, right, dims, preferred_element_type=jnp.float32)


def dequantize(code_values, block_scales):
    blocks = block_scales.shape[1]
    widened = code_values.astype(jnp.float32).reshape(code_values.shape[0], blocks, -1)
    return (
        (widened * block_scales.astype(jnp.float32)[:, :, None])
        .reshape(code_values.shape[0], -1)
        .astype(jnp.bfloat16)
    )


def swap(x, axis, distance):
    size = lax.axis_size(axis)
    return lax.ppermute(x, axis, [(k, k ^ distance) for k in range(size)])


def params(megabytes):
    return pltpu.CompilerParams(vmem_limit_bytes=megabytes << 20)


def head_rows(block, row, steps, heads):
    mine = block[row * steps : (row + 1) * steps]
    return jnp.concatenate([mine[:, h * HD : (h + 1) * HD] for h in range(heads)], axis=0)


def cache_kernel(rows, steps, own, chunk, lengths_ref, query_ref, cache_ref, own_query_ref, *parts):
    place = lax.axis_index("tensor")
    cache_len = cache_ref.shape[0] // rows
    per_group = H // KVH
    chunks = own // chunk
    height = chunk * steps
    position = lax.broadcasted_iota(jnp.int32, (height, cache_len), 1)
    lane = lax.broadcasted_iota(jnp.int32, (chunks * height, LANES), 1)
    for d, part in enumerate(parts):
        totals = [[None] * chunks for _ in range(rows)]
        for j in range(chunks):
            head = (place ^ d) * own + j * chunk
            kv_lane = pl.multiple_of((head // per_group) * HD, HD)
            block = query_ref[:, pl.ds(pl.multiple_of(head * HD, HD), chunk * HD)]
            block = block.astype(jnp.float32)
            for r in range(rows):
                query = head_rows(block, r, steps, chunk).astype(jnp.bfloat16)
                at = (r * chunks + j) * height
                if d == 0:
                    own_query_ref[at : at + height] = query
                here = pl.ds(r * cache_len, cache_len)
                keys = cache_ref[here, pl.ds(kv_lane, HD)]
                values = cache_ref[here, pl.ds(kv_lane + KVH * HD, HD)]
                usable = position < lengths_ref[r] - place * cache_len
                scores = jnp.where(usable, dot(query, keys, NT) * SCORE_SCALE, NEGATIVE)
                peak = jnp.max(scores, axis=1, keepdims=True)
                weights = jnp.where(usable, jnp.exp(scores - peak), 0.0)
                total = jnp.sum(weights, axis=1, keepdims=True)
                part[at : at + height] = jnp.dot(
                    weights.astype(jnp.bfloat16), values, preferred_element_type=jnp.float32
                )
                totals[r][j] = (peak, total)
        stats = []
        for r in range(rows):
            peak = jnp.concatenate([pair[0] for pair in totals[r]], axis=0)
            total = jnp.concatenate([pair[1] for pair in totals[r]], axis=0)
            flat = jnp.where(lane == 0, peak, total)
            if chunks * height < LANES:
                pad = jnp.zeros((LANES - chunks * height, LANES), jnp.float32)
                flat = jnp.concatenate([flat, pad], axis=0)
            stats.append(flat.T[:2])
        stats.append(jnp.zeros((SUBLANES - 2 * rows, LANES), jnp.float32))
        end = rows * chunks * height
        part[end : end + SUBLANES] = jnp.concatenate(stats, axis=0)


def cache_partials(queries, cache, lengths, rows, steps, own, ways):
    chunk = min(own, H // KVH)
    height = rows * own * steps
    part = jax.ShapeDtypeStruct((height + SUBLANES, LANES), jnp.float32)
    out = pl.pallas_call(
        functools.partial(cache_kernel, rows, steps, own, chunk),
        out_shape=[jax.ShapeDtypeStruct((height, HD), jnp.bfloat16)] + [part] * ways,
        in_specs=[SMEM, VMEM, VMEM],
        out_specs=[VMEM] * (1 + ways),
        compiler_params=params(32),
        cost_estimate=pl.CostEstimate(
            flops=4 * height * ways * HD * cache.shape[0] // rows,
            bytes_accessed=2 * cache.size + 2 * queries.size,
            transcendentals=height * ways * cache.shape[0] // rows,
        ),
        name="cache_partials",
    )(lengths, queries, cache)
    return out[0], out[1:]


def project_kernel(pairs, owner_ref, own_ref, mate_ref, base_ref, *refs):
    tokens, outs = refs[:pairs], refs[pairs : 2 * pairs]
    base_blocks, arrived = refs[2 * pairs :]
    place = lax.axis_index("group")
    block = own_ref.shape[0]
    copies = []
    for k in range(2):
        start = pl.multiple_of(owner_ref[place ^ k] * block, block)
        copy = pltpu.make_async_copy(
            base_ref.at[pl.ds(start, block)], base_blocks.at[k], arrived.at[k]
        )
        copy.start()
        copies.append(copy)
    stacked = jnp.concatenate([ref[...] for ref in tokens], axis=0)
    count = tokens[0].shape[0]
    deltas = [dot(ref[...], stacked, NT) for ref in (own_ref, mate_ref)]
    for k in range(2):
        copies[k].wait()
        whole = (dot(base_blocks[k], stacked, NT) + deltas[k]).T
        for d in range(pairs):
            outs[d][:, k * block : (k + 1) * block] = whole[d * count : (d + 1) * count]


def project(owner_map, own, mate, base_weight, tokens):
    pairs = len(tokens)
    block = own.shape[0]
    count, width = tokens[0].shape
    return pl.pallas_call(
        functools.partial(project_kernel, pairs),
        out_shape=[jax.ShapeDtypeStruct((count, 2 * block), jnp.float32)] * pairs,
        in_specs=[SMEM, VMEM, VMEM, ANY] + [VMEM] * pairs,
        out_specs=[VMEM] * pairs,
        scratch_shapes=[
            pltpu.VMEM((2, block, width), jnp.bfloat16),
            pltpu.SemaphoreType.DMA((2,)),
        ],
        compiler_params=params(32),
        cost_estimate=pl.CostEstimate(
            flops=8 * block * width * count * pairs,
            bytes_accessed=8 * block * width,
            transcendentals=0,
        ),
        name="project",
    )(owner_map, own, mate, base_weight, *tokens)


def pack_kernel(pairs, ways, near, wide, owner_ref, *refs):
    arrived, outs, ordered = refs[:pairs], refs[pairs : pairs + ways], refs[-1]
    place = lax.axis_index("group")
    to_place = lax.axis_index("tensor")
    shards, _, block = ordered.shape
    for d in range(pairs):
        for k in range(2):
            ordered[owner_ref[place ^ (2 * d + k)]] = arrived[d][:, k * block : (k + 1) * block]
    for d, out in enumerate(outs):
        to = to_place ^ d
        for n in range(near):
            out[:, n * block : (n + 1) * block] = ordered[to * near + n]
            at = (near + n) * block
            out[:, at : at + block] = ordered[shards // 2 + to * near + n]
        for n in range(wide):
            at = (2 * near + n) * block
            out[:, at : at + block] = ordered[to * wide + n]


def pack_pieces(owner_map, arrived, block, ways, near_width, slice_width):
    pairs = len(arrived)
    count = arrived[0].shape[0]
    shards = 2 * pairs
    kv_width = KVH * HD
    if block % LANES == 0 and near_width % block == 0 and slice_width % block == 0:
        piece = jax.ShapeDtypeStruct((count, 2 * near_width + slice_width), jnp.float32)
        kernel = functools.partial(
            pack_kernel, pairs, ways, near_width // block, slice_width // block
        )
        return pl.pallas_call(
            kernel,
            out_shape=[piece] * ways,
            in_specs=[SMEM] + [VMEM] * pairs,
            out_specs=[VMEM] * ways,
            scratch_shapes=[pltpu.VMEM((shards, count, block), jnp.float32)],
            name="pack_pieces",
        )(owner_map, *arrived)
    blocks = jnp.stack(arrived, axis=0).reshape(pairs, count, 2, block).transpose(0, 2, 1, 3)
    shard_of = jnp.zeros((shards,), jnp.int32).at[owner_map].set(
        jnp.arange(shards, dtype=jnp.int32)
    )
    taken = jnp.take(
        blocks.reshape(shards, count, block), shard_of ^ lax.axis_index("group"), axis=0
    )
    ordered = taken.transpose(1, 0, 2).reshape(count, shards * block)
    per_device = H // ways
    pieces = []
    for d in range(ways):
        to = lax.axis_index("tensor") ^ d
        near = (to * per_device // (H // KVH)) * HD
        parts = [(near, near_width), (kv_width + near, near_width), (to * slice_width, slice_width)]
        cuts = [lax.dynamic_slice_in_dim(ordered, start, width, 1) for start, width in parts]
        pieces.append(jnp.concatenate(cuts, axis=1))
    return pieces


def finish_kernel(rows, steps, own, chunk, near_width, ways, query_ref, *refs):
    pieces, parts = refs[:ways], refs[ways : 2 * ways]
    new_ref, attended_ref = refs[2 * ways :]
    chunks = own // chunk
    height = chunk * steps
    end = rows * chunks * height
    summed = pieces[0][...]
    for piece in pieces[1:]:
        summed = summed + piece[...]
    stored = summed.astype(jnp.bfloat16)
    new_ref[...] = stored[:, 2 * near_width :]
    near = stored[:, : 2 * near_width].astype(jnp.float32)
    key_step = lax.broadcasted_iota(jnp.int32, (steps, height), 0)
    query_step = lax.broadcasted_iota(jnp.int32, (steps, height), 1) % steps
    causal = key_step <= query_step
    stats = [part[end : end + SUBLANES] for part in parts]
    factors, near_sums = [], []
    for r in range(rows):
        peaks, totals = [], []
        for j in range(chunks):
            at = (r * chunks + j) * height
            query = query_ref[at : at + height]
            step_rows = slice(r * steps, (r + 1) * steps)
            keys = near[step_rows, j * HD : (j + 1) * HD].astype(jnp.bfloat16)
            values = near[step_rows, near_width + j * HD : near_width + (j + 1) * HD]
            scores = jnp.where(causal, dot(keys, query, NT) * SCORE_SCALE, NEGATIVE)
            peak = jnp.max(scores, axis=0, keepdims=True)
            weights = jnp.where(causal, jnp.exp(scores - peak), 0.0)
            peaks.append(peak)
            totals.append(jnp.sum(weights, axis=0, keepdims=True))
            near_sums.append(dot(weights.astype(jnp.bfloat16), values.astype(jnp.bfloat16), TN))
        lanes = chunks * height
        pad = [jnp.zeros((1, LANES - lanes), jnp.float32)] if lanes < LANES else []
        peaks = [s[2 * r : 2 * r + 1] for s in stats] + [jnp.concatenate(peaks + pad, axis=1)]
        totals = [s[2 * r + 1 : 2 * r + 2] for s in stats] + [jnp.concatenate(totals + pad, axis=1)]
        top = functools.reduce(jnp.maximum, peaks)
        scales = [jnp.exp(peak - top) for peak in peaks]
        total = sum(scale * one for scale, one in zip(scales, totals))
        if pad:
            total = jnp.where(total == 0.0, 1.0, total)
        factors += [scale / total for scale in scales]
    lines = -(-len(factors) // SUBLANES) * SUBLANES
    if lines > len(factors):
        factors.append(jnp.zeros((lines - len(factors), LANES), jnp.float32))
    columns = jnp.concatenate(factors, axis=0).T
    for j in range(chunks):
        merged = []
        for r in range(rows):
            at = (r * chunks + j) * height
            here = slice(j * height, (j + 1) * height)
            first = r * (ways + 1)
            out = near_sums[r * chunks + j] * columns[here, first + ways : first + ways + 1]
            for d, part in enumerate(parts):
                out = out + part[at : at + height] * columns[here, first + d : first + d + 1]
            merged.append(out)
        for h in range(chunk):
            both = [out[h * steps : (h + 1) * steps] for out in merged]
            lane = (j * chunk + h) * HD
            attended_ref[:, lane : lane + HD] = jnp.concatenate(both, axis=0).astype(jnp.bfloat16)


def finish(own_query, pieces, parts, rows, steps, own, near_width):
    ways = len(pieces)
    count, width = pieces[0].shape
    return pl.pallas_call(
        functools.partial(
            finish_kernel, rows, steps, own, min(own, H // KVH), near_width, ways
        ),
        out_shape=[
            jax.ShapeDtypeStruct((count, width - 2 * near_width), jnp.bfloat16),
            jax.ShapeDtypeStruct((count, own * HD), jnp.bfloat16),
        ],
        in_specs=[VMEM] * (1 + 2 * ways),
        out_specs=[VMEM] * 2,
        name="finish",
    )(own_query, *pieces, *parts)


def on_device(
    hidden_x, base_weight, delta_codes, delta_scales, owner_map, kv_cache, queries, lengths
):
    group_count = lax.axis_size("group")
    tensor_count = lax.axis_size("tensor")
    rows, steps, local_width = hidden_x.shape
    tokens = rows * steps
    owner_block = delta_codes.shape[0]
    heads_own = H // tensor_count
    slice_width = base_weight.shape[0] // tensor_count
    near_width = max(1, heads_own // (H // KVH)) * HD
    pairs = group_count // 2

    mine = hidden_x.reshape(tokens, local_width)
    token_rows = [mine] + [swap(mine, "group", 2 * d) for d in range(1, pairs)]
    own_delta = dequantize(delta_codes, delta_scales)
    mate_delta = swap(own_delta, "group", 1)

    own_query, partials = cache_partials(
        queries.reshape(tokens, H * HD),
        kv_cache.reshape(-1, 2 * KVH * HD),
        lengths,
        rows,
        steps,
        heads_own,
        tensor_count,
    )
    partials = [partials[0]] + [swap(partials[d], "tensor", d) for d in range(1, tensor_count)]

    projected = project(owner_map, own_delta, mate_delta, base_weight, token_rows)
    arrived = [projected[0]] + [swap(projected[d], "group", 2 * d) for d in range(1, pairs)]
    pieces = pack_pieces(owner_map, arrived, owner_block, tensor_count, near_width, slice_width)
    pieces = [pieces[0]] + [swap(pieces[d], "tensor", d) for d in range(1, tensor_count)]
    new_out, attended = finish(own_query, pieces, partials, rows, steps, heads_own, near_width)
    return (new_out.reshape(rows, steps, -1), attended.reshape(rows, steps, -1))


def solution(mesh):
    in_specs = (
        P("group", None, "tensor"),
        P(None, "tensor"),
        P("group", "tensor"),
        P("group", "tensor"),
        P(),
        P("group", "tensor", None),
        P("group", None, None),
        P("group"),
    )
    out_specs = (P("group", None, "tensor"), P("group", None, "tensor"))
    return jax.shard_map(
        on_device, mesh=mesh, in_specs=in_specs, out_specs=out_specs, check_vma=False
    )
```

```python
import functools
import jax
import jax.numpy as jnp
from jax import lax
from jax.experimental import pallas as pl
from jax.experimental.pallas import tpu as pltpu
from jax.sharding import PartitionSpec as P

H = 64
KVH = 8
HD = 128
BLK = 128
LANES = 128
SUBLANES = 8


NEGATIVE = -1e30
SCORE_SCALE = HD ** (-0.5)
CACHE_KIB = 53 << 10
WEIGHTS_KIB = 46 << 10
PROJECT_KIB = 16 << 10
NT = (((1,), (1,)), ((), ()))
TN = (((0,), (0,)), ((), ()))
VMEM = pl.BlockSpec(memory_space=pltpu.VMEM)
SMEM = pl.BlockSpec(memory_space=pltpu.SMEM)
HBM = pl.BlockSpec(memory_space=pltpu.HBM)


def dot(left, right, dims):
    return lax.dot_general(left, right, dims, preferred_element_type=jnp.float32)


def swap(x, axis, distance):
    size = lax.axis_size(axis)
    return lax.ppermute(x, axis, [(k, k ^ distance) for k in range(size)])


def params(kibibytes):
    return pltpu.CompilerParams(vmem_limit_bytes=kibibytes << 10)


def head_rows(block, row, steps, heads):
    mine = block[row * steps : (row + 1) * steps]
    return jnp.concatenate([mine[:, h * HD : (h + 1) * HD] for h in range(heads)], axis=0)


def weights_kernel(owner_ref, own_codes, mate_codes, own_scales, mate_scales, base_hbm, *refs):
    deltas, base_ref, arrived = refs[:2], refs[2], refs[3]
    place = lax.axis_index("group")
    block = own_codes.shape[0]
    copies = []
    for k in range(2):
        start = pl.multiple_of(owner_ref[place ^ k] * block, block)
        copy = pltpu.make_async_copy(
            base_hbm.at[pl.ds(start, block)], base_ref.at[k], arrived.at[k]
        )
        copy.start()
        copies.append(copy)
    for codes_ref, scales_ref, out_ref in zip(
        (own_codes, mate_codes), (own_scales, mate_scales), deltas
    ):
        scales = scales_ref[...].astype(jnp.float32).T
        for n in range(scales.shape[1]):
            lanes = slice(n * BLK, (n + 1) * BLK)
            values = codes_ref[:, lanes].astype(jnp.float32) * scales[:, n : n + 1]
            out_ref[:, lanes] = values.astype(jnp.bfloat16)
    for copy in copies:
        copy.wait()


def weights(owner_map, codes, scales, base_weight):
    delta = jax.ShapeDtypeStruct(codes[0].shape, jnp.bfloat16)
    return pl.pallas_call(
        weights_kernel,
        out_shape=[delta, delta, jax.ShapeDtypeStruct((2,) + delta.shape, jnp.bfloat16)],
        in_specs=[SMEM] + [VMEM] * 4 + [HBM],
        out_specs=[VMEM] * 3,
        scratch_shapes=[pltpu.SemaphoreType.DMA((2,))],
        compiler_params=params(WEIGHTS_KIB),
        cost_estimate=pl.CostEstimate(
            flops=2 * delta.size, bytes_accessed=16 * delta.size, transcendentals=0
        ),
        name="weights",
    )(owner_map, *codes, *[one.T for one in scales], base_weight)


def cache_kernel(rows, steps, own, chunk, lengths_ref, tokens_hbm, query_hbm, cache_hbm, *refs):
    tokens_ref, own_query_ref, parts = refs[0], refs[1], refs[2:-3]
    query_ref, cache_ref, arrived = refs[-3:]
    cache_len = cache_ref.shape[0] // rows
    copies = [pltpu.make_async_copy(query_hbm, query_ref, arrived.at[0])]
    for r in range(rows):
        here = pl.ds(r * cache_len, cache_len)
        copies.append(
            pltpu.make_async_copy(cache_hbm.at[here], cache_ref.at[here], arrived.at[1 + r])
        )
    copies.append(pltpu.make_async_copy(tokens_hbm, tokens_ref, arrived.at[1 + rows]))
    for copy in copies:
        copy.start()
    for copy in copies:
        copy.wait()

    place = lax.axis_index("tensor")
    chunks = own // chunk
    height = chunk * steps
    width = chunks * HD
    position = lax.broadcasted_iota(jnp.int32, (cache_len, chunks * height), 0)
    usable = [position < lengths_ref[r] - place * cache_len for r in range(rows)]
    for d, part in enumerate(parts):
        head = (place ^ d) * own
        kv_lane = pl.multiple_of((head // (H // KVH)) * HD, HD)
        block = query_ref[:, pl.ds(pl.multiple_of(head * HD, HD), own * HD)].astype(jnp.float32)
        stats = []
        for r in range(rows):
            at = r * chunks * height
            query = head_rows(block, r, steps, own)
            if d == 0:
                own_query_ref[at : at + chunks * height] = query.astype(jnp.bfloat16)
            spread = []
            for j in range(chunks):
                line = [jnp.zeros((height, HD), jnp.float32)] * chunks
                line[j] = query[j * height : (j + 1) * height]
                spread.append(jnp.concatenate(line, axis=1))
            spread = jnp.concatenate(spread, axis=0).astype(jnp.bfloat16)
            here = pl.ds(r * cache_len, cache_len)
            keys = cache_ref[here, pl.ds(kv_lane, width)]
            values = cache_ref[here, pl.ds(kv_lane + KVH * HD, width)]
            scores = jnp.where(usable[r], dot(keys, spread, NT) * SCORE_SCALE, 2.0 * NEGATIVE)
            peak = jnp.maximum(jnp.max(scores, axis=0, keepdims=True), NEGATIVE)
            weights = jnp.exp(scores - peak)
            stats += [peak, jnp.sum(weights, axis=0, keepdims=True)]
            sums = dot(weights.astype(jnp.bfloat16), values, TN)
            for j in range(chunks):
                here = slice(j * height, (j + 1) * height)
                part[at + j * height : at + (j + 1) * height] = sums[here, j * HD : (j + 1) * HD]
        stats.append(jnp.zeros((SUBLANES - 2 * rows, chunks * height), jnp.float32))
        stats = jnp.concatenate(stats, axis=0)
        if chunks * height < LANES:
            pad = jnp.zeros((SUBLANES, LANES - chunks * height), jnp.float32)
            stats = jnp.concatenate([stats, pad], axis=1)
        end = rows * chunks * height
        part[end : end + SUBLANES] = stats


def cache_partials(tokens, queries, cache, lengths, rows, steps, own, ways):
    chunk = min(own, H // KVH)
    height = rows * own * steps
    part = jax.ShapeDtypeStruct((height + SUBLANES, LANES), jnp.float32)
    out = pl.pallas_call(
        functools.partial(cache_kernel, rows, steps, own, chunk),
        out_shape=[
            jax.ShapeDtypeStruct(tokens.shape, tokens.dtype),
            jax.ShapeDtypeStruct((height, HD), jnp.bfloat16),
        ]
        + [part] * ways,
        in_specs=[SMEM, HBM, HBM, HBM],
        out_specs=[VMEM] * (2 + ways),
        scratch_shapes=[
            pltpu.VMEM(queries.shape, queries.dtype),
            pltpu.VMEM(cache.shape, cache.dtype),
            pltpu.SemaphoreType.DMA((2 + rows,)),
        ],
        compiler_params=params(CACHE_KIB),
        cost_estimate=pl.CostEstimate(
            flops=4 * height * ways * HD * cache.shape[0] // rows,
            bytes_accessed=2 * cache.size + 2 * queries.size,
            transcendentals=height * ways * cache.shape[0] // rows,
        ),
        name="cache_partials",
    )(lengths, tokens, queries, cache)
    return out[0], out[1], out[2:]


def project_kernel(pairs, own_ref, mate_ref, base_ref, *refs):
    tokens, outs = refs[:pairs], refs[pairs:]
    block = own_ref.shape[0]
    stacked = jnp.concatenate([ref[...] for ref in tokens], axis=0)
    count = tokens[0].shape[0]
    for k, delta_ref in enumerate((own_ref, mate_ref)):
        whole = (dot(base_ref[k], stacked, NT) + dot(delta_ref[...], stacked, NT)).T
        for d in range(pairs):
            outs[d][:, k * block : (k + 1) * block] = whole[d * count : (d + 1) * count]


def project(own, mate, base, tokens):
    pairs = len(tokens)
    block = own.shape[0]
    count, width = tokens[0].shape
    return pl.pallas_call(
        functools.partial(project_kernel, pairs),
        out_shape=[jax.ShapeDtypeStruct((count, 2 * block), jnp.float32)] * pairs,
        in_specs=[VMEM] * (3 + pairs),
        out_specs=[VMEM] * pairs,
        compiler_params=params(PROJECT_KIB),
        cost_estimate=pl.CostEstimate(
            flops=8 * block * width * count * pairs,
            bytes_accessed=8 * block * width,
            transcendentals=0,
        ),
        name="project",
    )(own, mate, base, *tokens)


def pack_kernel(pairs, ways, near, wide, owner_ref, *refs):
    arrived, outs, ordered = refs[:pairs], refs[pairs : pairs + ways], refs[-1]
    place = lax.axis_index("group")
    to_place = lax.axis_index("tensor")
    shards, _, block = ordered.shape
    for d in range(pairs):
        for k in range(2):
            ordered[owner_ref[place ^ (2 * d + k)]] = arrived[d][:, k * block : (k + 1) * block]
    for d, out in enumerate(outs):
        to = to_place ^ d
        for n in range(near):
            out[:, n * block : (n + 1) * block] = ordered[to * near + n]
            at = (near + n) * block
            out[:, at : at + block] = ordered[shards // 2 + to * near + n]
        for n in range(wide):
            at = (2 * near + n) * block
            out[:, at : at + block] = ordered[to * wide + n]


def pack_pieces(owner_map, arrived, block, ways, near_width, slice_width):
    pairs = len(arrived)
    count = arrived[0].shape[0]
    shards = 2 * pairs
    kv_width = KVH * HD
    if block % LANES == 0 and near_width % block == 0 and slice_width % block == 0:
        piece = jax.ShapeDtypeStruct((count, 2 * near_width + slice_width), jnp.float32)
        kernel = functools.partial(
            pack_kernel, pairs, ways, near_width // block, slice_width // block
        )
        return pl.pallas_call(
            kernel,
            out_shape=[piece] * ways,
            in_specs=[SMEM] + [VMEM] * pairs,
            out_specs=[VMEM] * ways,
            scratch_shapes=[pltpu.VMEM((shards, count, block), jnp.float32)],
            compiler_params=params(8192),
            name="pack_pieces",
        )(owner_map, *arrived)
    blocks = jnp.stack(arrived, axis=0).reshape(pairs, count, 2, block).transpose(0, 2, 1, 3)
    shard_of = jnp.zeros((shards,), jnp.int32).at[owner_map].set(
        jnp.arange(shards, dtype=jnp.int32)
    )
    taken = jnp.take(
        blocks.reshape(shards, count, block), shard_of ^ lax.axis_index("group"), axis=0
    )
    ordered = taken.transpose(1, 0, 2).reshape(count, shards * block)
    per_device = H // ways
    pieces = []
    for d in range(ways):
        to = lax.axis_index("tensor") ^ d
        near = (to * per_device // (H // KVH)) * HD
        parts = [(near, near_width), (kv_width + near, near_width), (to * slice_width, slice_width)]
        cuts = [lax.dynamic_slice_in_dim(ordered, start, width, 1) for start, width in parts]
        pieces.append(jnp.concatenate(cuts, axis=1))
    return pieces


def finish_kernel(rows, steps, own, chunk, near_width, ways, query_ref, *refs):
    pieces, parts = refs[:ways], refs[ways : 2 * ways]
    new_ref, attended_ref = refs[2 * ways :]
    chunks = own // chunk
    height = chunk * steps
    end = rows * chunks * height
    summed = pieces[0][...]
    for piece in pieces[1:]:
        summed = summed + piece[...]
    stored = summed.astype(jnp.bfloat16)
    new_ref[...] = stored[:, 2 * near_width :]
    near = stored[:, : 2 * near_width].astype(jnp.float32)
    key_step = lax.broadcasted_iota(jnp.int32, (steps, height), 0)
    query_step = lax.broadcasted_iota(jnp.int32, (steps, height), 1) % steps
    causal = key_step <= query_step
    stats = [part[end : end + SUBLANES] for part in parts]
    factors, near_sums = [], []
    for r in range(rows):
        peaks, totals = [], []
        for j in range(chunks):
            at = (r * chunks + j) * height
            query = query_ref[at : at + height]
            step_rows = slice(r * steps, (r + 1) * steps)
            keys = near[step_rows, j * HD : (j + 1) * HD].astype(jnp.bfloat16)
            values = near[step_rows, near_width + j * HD : near_width + (j + 1) * HD]
            scores = jnp.where(causal, dot(keys, query, NT) * SCORE_SCALE, NEGATIVE)
            peak = jnp.max(scores, axis=0, keepdims=True)
            weights = jnp.where(causal, jnp.exp(scores - peak), 0.0)
            peaks.append(peak)
            totals.append(jnp.sum(weights, axis=0, keepdims=True))
            near_sums.append(dot(weights.astype(jnp.bfloat16), values.astype(jnp.bfloat16), TN))
        lanes = chunks * height
        pad = [jnp.zeros((1, LANES - lanes), jnp.float32)] if lanes < LANES else []
        peaks = [s[2 * r : 2 * r + 1] for s in stats] + [jnp.concatenate(peaks + pad, axis=1)]
        totals = [s[2 * r + 1 : 2 * r + 2] for s in stats] + [jnp.concatenate(totals + pad, axis=1)]
        top = functools.reduce(jnp.maximum, peaks)
        scales = [jnp.exp(peak - top) for peak in peaks]
        total = sum(scale * one for scale, one in zip(scales, totals))
        if pad:
            total = jnp.where(total == 0.0, 1.0, total)
        factors += [scale / total for scale in scales]
    lines = -(-len(factors) // SUBLANES) * SUBLANES
    if lines > len(factors):
        factors.append(jnp.zeros((lines - len(factors), LANES), jnp.float32))
    columns = jnp.concatenate(factors, axis=0).T
    for j in range(chunks):
        merged = []
        for r in range(rows):
            at = (r * chunks + j) * height
            here = slice(j * height, (j + 1) * height)
            first = r * (ways + 1)
            out = near_sums[r * chunks + j] * columns[here, first + ways : first + ways + 1]
            for d, part in enumerate(parts):
                out = out + part[at : at + height] * columns[here, first + d : first + d + 1]
            merged.append(out)
        for h in range(chunk):
            both = [out[h * steps : (h + 1) * steps] for out in merged]
            lane = (j * chunk + h) * HD
            attended_ref[:, lane : lane + HD] = jnp.concatenate(both, axis=0).astype(jnp.bfloat16)


def finish(own_query, pieces, parts, rows, steps, own, near_width):
    ways = len(pieces)
    count, width = pieces[0].shape
    return pl.pallas_call(
        functools.partial(
            finish_kernel, rows, steps, own, min(own, H // KVH), near_width, ways
        ),
        out_shape=[
            jax.ShapeDtypeStruct((count, width - 2 * near_width), jnp.bfloat16),
            jax.ShapeDtypeStruct((count, own * HD), jnp.bfloat16),
        ],
        in_specs=[VMEM] * (1 + 2 * ways),
        out_specs=[VMEM] * 2,
        compiler_params=params(8192),
        name="finish",
    )(own_query, *pieces, *parts)


def on_device(
    hidden_x, base_weight, delta_codes, delta_scales, owner_map, kv_cache, queries, lengths
):
    group_count = lax.axis_size("group")
    tensor_count = lax.axis_size("tensor")
    rows, steps, local_width = hidden_x.shape
    tokens = rows * steps
    owner_block = delta_codes.shape[0]
    heads_own = H // tensor_count
    slice_width = base_weight.shape[0] // tensor_count
    near_width = max(1, heads_own // (H // KVH)) * HD
    pairs = group_count // 2

    mine = hidden_x.reshape(tokens, local_width)
    token_rows = [mine] + [swap(mine, "group", 2 * d) for d in range(1, pairs)]
    codes = [delta_codes, swap(delta_codes, "group", 1)]
    scales = [delta_scales, swap(delta_scales, "group", 1)]

    own_tokens, own_query, partials = cache_partials(
        mine,
        queries.reshape(tokens, H * HD),
        kv_cache.reshape(-1, 2 * KVH * HD),
        lengths,
        rows,
        steps,
        heads_own,
        tensor_count,
    )
    partials = [partials[0]] + [swap(partials[d], "tensor", d) for d in range(1, tensor_count)]

    own_delta, mate_delta, base_blocks = weights(owner_map, codes, scales, base_weight)
    projected = project(own_delta, mate_delta, base_blocks, [own_tokens] + token_rows[1:])
    arrived = [projected[0]] + [swap(projected[d], "group", 2 * d) for d in range(1, pairs)]
    pieces = pack_pieces(owner_map, arrived, owner_block, tensor_count, near_width, slice_width)
    pieces = [pieces[0]] + [swap(pieces[d], "tensor", d) for d in range(1, tensor_count)]
    new_out, attended = finish(own_query, pieces, partials, rows, steps, heads_own, near_width)
    return (new_out.reshape(rows, steps, -1), attended.reshape(rows, steps, -1))


def solution(mesh):
    in_specs = (
        P("group", None, "tensor"),
        P(None, "tensor"),
        P("group", "tensor"),
        P("group", "tensor"),
        P(),
        P("group", "tensor", None),
        P("group", None, None),
        P("group"),
    )
    out_specs = (P("group", None, "tensor"), P("group", None, "tensor"))
    return jax.shard_map(
        on_device, mesh=mesh, in_specs=in_specs, out_specs=out_specs, check_vma=False
    )
```

```python
import functools
import jax
import jax.numpy as jnp
from jax import lax
from jax.experimental import pallas as pl
from jax.experimental.pallas import tpu as pltpu
from jax.sharding import PartitionSpec as P

H = 64
KVH = 8
HD = 128
BLK = 128
LANES = 128
SUBLANES = 8


NEGATIVE = -1e30
SCORE_SCALE = HD ** (-0.5)
WEIGHTS_KIB = 47 << 10
CACHE_KIB = 24 << 10
PROJECT_KIB = 16 << 10
NT = (((1,), (1,)), ((), ()))
TN = (((0,), (0,)), ((), ()))
VMEM = pl.BlockSpec(memory_space=pltpu.VMEM)
SMEM = pl.BlockSpec(memory_space=pltpu.SMEM)
HBM = pl.BlockSpec(memory_space=pltpu.HBM)


def dot(left, right, dims):
    return lax.dot_general(left, right, dims, preferred_element_type=jnp.float32)


def swap(x, axis, distance):
    size = lax.axis_size(axis)
    return lax.ppermute(x, axis, [(k, k ^ distance) for k in range(size)])


def params(kibibytes):
    return pltpu.CompilerParams(vmem_limit_bytes=kibibytes << 10)


def head_rows(block, row, steps, heads):
    mine = block[row * steps : (row + 1) * steps]
    return jnp.concatenate([mine[:, h * HD : (h + 1) * HD] for h in range(heads)], axis=0)


def weights_kernel(starts_ref, scales_ref, codes_ref, base_hbm, delta_ref, base_ref, arrived):
    block = codes_ref.shape[0]
    loads = []
    for k in range(2):
        start = starts_ref[lax.axis_index("group") ^ k]
        here = pl.ds(pl.multiple_of(start, block), block)
        loads.append(pltpu.make_async_copy(base_hbm.at[here], base_ref.at[k], arrived.at[k]))
        loads[k].start()
    scales = scales_ref[...].T
    for n in range(scales.shape[1]):
        lanes = slice(n * BLK, (n + 1) * BLK)
        values = codes_ref[:, lanes].astype(jnp.float32) * scales[:, n : n + 1]
        delta_ref[:, lanes] = values.astype(jnp.bfloat16)
    for load in loads:
        load.wait()


def weights(starts, scales, codes, base):
    return pl.pallas_call(
        weights_kernel,
        out_shape=[
            jax.ShapeDtypeStruct(codes.shape, jnp.bfloat16),
            jax.ShapeDtypeStruct((2,) + codes.shape, jnp.bfloat16),
        ],
        in_specs=[SMEM, VMEM, VMEM, HBM],
        out_specs=[VMEM] * 2,
        scratch_shapes=[pltpu.SemaphoreType.DMA((2,))],
        compiler_params=params(WEIGHTS_KIB),
        cost_estimate=pl.CostEstimate(
            flops=codes.size, bytes_accessed=12 * codes.size, transcendentals=0
        ),
        name="weights",
    )(starts, scales.astype(jnp.float32).T, codes, base)


def cache_kernel(rows, steps, own, chunk, limits_ref, query_ref, cache_ref, own_query_ref, *parts):
    place = lax.axis_index("tensor")
    cache_len = cache_ref.shape[0] // rows
    chunks = own // chunk
    height = chunk * steps
    width = chunks * HD
    position = lax.broadcasted_iota(jnp.int32, (cache_len, chunks * height), 0)

    def kv_lane(d):
        return pl.multiple_of(((place ^ d) * own // (H // KVH)) * HD, HD)

    def score(r, d):
        head = (place ^ d) * own
        queries = query_ref[:, pl.ds(pl.multiple_of(head * HD, HD), own * HD)]
        query = head_rows(queries.astype(jnp.float32), r, steps, own)
        if d == 0:
            at = r * chunks * height
            own_query_ref[at : at + chunks * height] = query.astype(jnp.bfloat16)
        spread = []
        for j in range(chunks):
            line = [jnp.zeros((height, HD), jnp.float32)] * chunks
            line[j] = query[j * height : (j + 1) * height]
            spread.append(jnp.concatenate(line, axis=1))
        spread = jnp.concatenate(spread, axis=0).astype(jnp.bfloat16)
        keys = cache_ref[pl.ds(r * cache_len, cache_len), pl.ds(kv_lane(d), width)]
        return dot(keys, spread, NT)

    units = [(r, d) for r in range(rows) for d in range(len(parts))]
    ahead = []
    for n in range(len(units) + 1):
        if n < len(units):
            ahead.append(score(*units[n]))
        if n == 0:
            continue
        r, d = units[n - 1]
        at = r * chunks * height
        usable = position < limits_ref[r]
        scores = jnp.where(usable, ahead.pop(0) * SCORE_SCALE, 2.0 * NEGATIVE)
        peak = jnp.maximum(jnp.max(scores, axis=0, keepdims=True), NEGATIVE)
        weights = jnp.exp(scores - peak)
        total = jnp.sum(weights, axis=0, keepdims=True)
        lane = pl.ds(kv_lane(d) + KVH * HD, width)
        values = cache_ref[pl.ds(r * cache_len, cache_len), lane]
        sums = dot(weights.astype(jnp.bfloat16), values, TN)
        for j in range(chunks):
            here = slice(j * height, (j + 1) * height)
            parts[d][at + j * height : at + (j + 1) * height] = sums[here, j * HD : (j + 1) * HD]
        end = rows * chunks * height + 2 * r
        parts[d][end : end + 1, : chunks * height] = peak
        parts[d][end + 1 : end + 2, : chunks * height] = total


def cache_partials(limits, queries, cache, rows, steps, own, ways):
    height = rows * own * steps
    part = jax.ShapeDtypeStruct((height + SUBLANES, LANES), jnp.float32)
    out = pl.pallas_call(
        functools.partial(cache_kernel, rows, steps, own, min(own, H // KVH)),
        out_shape=[jax.ShapeDtypeStruct((height, HD), jnp.bfloat16)] + [part] * ways,
        in_specs=[SMEM, VMEM, VMEM],
        out_specs=[VMEM] * (1 + ways),
        compiler_params=params(CACHE_KIB),
        cost_estimate=pl.CostEstimate(
            flops=4 * height * ways * HD * cache.shape[0] // rows,
            bytes_accessed=2 * cache.size + 2 * queries.size,
            transcendentals=height * ways * cache.shape[0] // rows,
        ),
        name="cache_partials",
    )(limits, queries, cache)
    return out[0], out[1:]


def project_kernel(pairs, own_ref, mate_ref, base_ref, *refs):
    tokens, outs = refs[:pairs], refs[pairs:]
    block = own_ref.shape[0]
    stacked = jnp.concatenate([ref[...] for ref in tokens], axis=0)
    count = tokens[0].shape[0]
    for k, delta_ref in enumerate((own_ref, mate_ref)):
        whole = (dot(base_ref[k], stacked, NT) + dot(delta_ref[...], stacked, NT)).T
        for d in range(pairs):
            outs[d][:, k * block : (k + 1) * block] = whole[d * count : (d + 1) * count]


def project(own, mate, base, tokens):
    pairs = len(tokens)
    block = own.shape[0]
    count, width = tokens[0].shape
    return pl.pallas_call(
        functools.partial(project_kernel, pairs),
        out_shape=[jax.ShapeDtypeStruct((count, 2 * block), jnp.float32)] * pairs,
        in_specs=[VMEM] * (3 + pairs),
        out_specs=[VMEM] * pairs,
        compiler_params=params(PROJECT_KIB),
        cost_estimate=pl.CostEstimate(
            flops=8 * block * width * count * pairs,
            bytes_accessed=8 * block * width,
            transcendentals=0,
        ),
        name="project",
    )(own, mate, base, *tokens)


def pack_kernel(pairs, ways, near, wide, owner_ref, *refs):
    arrived, outs, ordered = refs[:pairs], refs[pairs : pairs + ways], refs[-1]
    place = lax.axis_index("group")
    to_place = lax.axis_index("tensor")
    shards, _, block = ordered.shape
    for d in range(pairs):
        for k in range(2):
            ordered[owner_ref[place ^ (2 * d + k)]] = arrived[d][:, k * block : (k + 1) * block]
    for d, out in enumerate(outs):
        to = to_place ^ d
        for n in range(near):
            out[:, n * block : (n + 1) * block] = ordered[to * near + n]
            at = (near + n) * block
            out[:, at : at + block] = ordered[shards // 2 + to * near + n]
        for n in range(wide):
            at = (2 * near + n) * block
            out[:, at : at + block] = ordered[to * wide + n]


def pack_pieces(owner_map, arrived, block, ways, near_width, slice_width):
    pairs = len(arrived)
    count = arrived[0].shape[0]
    shards = 2 * pairs
    kv_width = KVH * HD
    if block % LANES == 0 and near_width % block == 0 and slice_width % block == 0:
        piece = jax.ShapeDtypeStruct((count, 2 * near_width + slice_width), jnp.float32)
        kernel = functools.partial(
            pack_kernel, pairs, ways, near_width // block, slice_width // block
        )
        return pl.pallas_call(
            kernel,
            out_shape=[piece] * ways,
            in_specs=[SMEM] + [VMEM] * pairs,
            out_specs=[VMEM] * ways,
            scratch_shapes=[pltpu.VMEM((shards, count, block), jnp.float32)],
            compiler_params=params(8192),
            name="pack_pieces",
        )(owner_map, *arrived)
    blocks = jnp.stack(arrived, axis=0).reshape(pairs, count, 2, block).transpose(0, 2, 1, 3)
    shard_of = jnp.zeros((shards,), jnp.int32).at[owner_map].set(
        jnp.arange(shards, dtype=jnp.int32)
    )
    taken = jnp.take(
        blocks.reshape(shards, count, block), shard_of ^ lax.axis_index("group"), axis=0
    )
    ordered = taken.transpose(1, 0, 2).reshape(count, shards * block)
    per_device = H // ways
    pieces = []
    for d in range(ways):
        to = lax.axis_index("tensor") ^ d
        near = (to * per_device // (H // KVH)) * HD
        parts = [(near, near_width), (kv_width + near, near_width), (to * slice_width, slice_width)]
        cuts = [lax.dynamic_slice_in_dim(ordered, start, width, 1) for start, width in parts]
        pieces.append(jnp.concatenate(cuts, axis=1))
    return pieces


def finish_kernel(rows, steps, own, chunk, near_width, ways, query_ref, *refs):
    pieces, parts = refs[:ways], refs[ways : 2 * ways]
    new_ref, attended_ref = refs[2 * ways :]
    chunks = own // chunk
    height = chunk * steps
    end = rows * chunks * height
    summed = pieces[0][...]
    for piece in pieces[1:]:
        summed = summed + piece[...]
    stored = summed.astype(jnp.bfloat16)
    new_ref[...] = stored[:, 2 * near_width :]
    near = stored[:, : 2 * near_width].astype(jnp.float32)
    key_step = lax.broadcasted_iota(jnp.int32, (steps, height), 0)
    query_step = lax.broadcasted_iota(jnp.int32, (steps, height), 1) % steps
    causal = key_step <= query_step
    stats = [part[end : end + SUBLANES] for part in parts]
    factors, near_sums = [], []
    for r in range(rows):
        peaks, totals = [], []
        for j in range(chunks):
            at = (r * chunks + j) * height
            query = query_ref[at : at + height]
            step_rows = slice(r * steps, (r + 1) * steps)
            keys = near[step_rows, j * HD : (j + 1) * HD].astype(jnp.bfloat16)
            values = near[step_rows, near_width + j * HD : near_width + (j + 1) * HD]
            scores = jnp.where(causal, dot(keys, query, NT) * SCORE_SCALE, NEGATIVE)
            peak = jnp.max(scores, axis=0, keepdims=True)
            weights = jnp.where(causal, jnp.exp(scores - peak), 0.0)
            peaks.append(peak)
            totals.append(jnp.sum(weights, axis=0, keepdims=True))
            near_sums.append(dot(weights.astype(jnp.bfloat16), values.astype(jnp.bfloat16), TN))
        lanes = chunks * height
        pad = [jnp.zeros((1, LANES - lanes), jnp.float32)] if lanes < LANES else []
        peaks = [s[2 * r : 2 * r + 1] for s in stats] + [jnp.concatenate(peaks + pad, axis=1)]
        totals = [s[2 * r + 1 : 2 * r + 2] for s in stats] + [jnp.concatenate(totals + pad, axis=1)]
        top = functools.reduce(jnp.maximum, peaks)
        scales = [jnp.exp(peak - top) for peak in peaks]
        total = sum(scale * one for scale, one in zip(scales, totals))
        if pad:
            total = jnp.where(total == 0.0, 1.0, total)
        factors += [scale / total for scale in scales]
    lines = -(-len(factors) // SUBLANES) * SUBLANES
    if lines > len(factors):
        factors.append(jnp.zeros((lines - len(factors), LANES), jnp.float32))
    columns = jnp.concatenate(factors, axis=0).T
    for j in range(chunks):
        merged = []
        for r in range(rows):
            at = (r * chunks + j) * height
            here = slice(j * height, (j + 1) * height)
            first = r * (ways + 1)
            out = near_sums[r * chunks + j] * columns[here, first + ways : first + ways + 1]
            for d, part in enumerate(parts):
                out = out + part[at : at + height] * columns[here, first + d : first + d + 1]
            merged.append(out)
        for h in range(chunk):
            both = [out[h * steps : (h + 1) * steps] for out in merged]
            lane = (j * chunk + h) * HD
            attended_ref[:, lane : lane + HD] = jnp.concatenate(both, axis=0).astype(jnp.bfloat16)


def finish(own_query, pieces, parts, rows, steps, own, near_width):
    ways = len(pieces)
    count, width = pieces[0].shape
    return pl.pallas_call(
        functools.partial(
            finish_kernel, rows, steps, own, min(own, H // KVH), near_width, ways
        ),
        out_shape=[
            jax.ShapeDtypeStruct((count, width - 2 * near_width), jnp.bfloat16),
            jax.ShapeDtypeStruct((count, own * HD), jnp.bfloat16),
        ],
        in_specs=[VMEM] * (1 + 2 * ways),
        out_specs=[VMEM] * 2,
        compiler_params=params(8192),
        name="finish",
    )(own_query, *pieces, *parts)


def on_device(
    hidden_x, base_weight, delta_codes, delta_scales, owner_map, kv_cache, queries, lengths
):
    group_count = lax.axis_size("group")
    tensor_count = lax.axis_size("tensor")
    rows, steps, local_width = hidden_x.shape
    tokens = rows * steps
    owner_block = delta_codes.shape[0]
    heads_own = H // tensor_count
    slice_width = base_weight.shape[0] // tensor_count
    near_width = max(1, heads_own // (H // KVH)) * HD
    pairs = group_count // 2

    mine = hidden_x.reshape(tokens, local_width)
    token_rows = [mine] + [swap(mine, "group", 2 * d) for d in range(1, pairs)]
    own_delta, base_blocks = weights(
        owner_map * owner_block, delta_scales, delta_codes, base_weight
    )
    mate_delta = swap(own_delta, "group", 1)
    cache_len = kv_cache.shape[1]
    own_query, partials = cache_partials(
        lengths - lax.axis_index("tensor") * cache_len,
        queries.reshape(tokens, H * HD),
        kv_cache.reshape(rows * cache_len, 2 * KVH * HD),
        rows,
        steps,
        heads_own,
        tensor_count,
    )
    partials = [partials[0]] + [swap(partials[d], "tensor", d) for d in range(1, tensor_count)]

    projected = project(own_delta, mate_delta, base_blocks, token_rows)
    arrived = [projected[0]] + [swap(projected[d], "group", 2 * d) for d in range(1, pairs)]
    pieces = pack_pieces(owner_map, arrived, owner_block, tensor_count, near_width, slice_width)
    pieces = [pieces[0]] + [swap(pieces[d], "tensor", d) for d in range(1, tensor_count)]
    new_out, attended = finish(own_query, pieces, partials, rows, steps, heads_own, near_width)
    return (new_out.reshape(rows, steps, -1), attended.reshape(rows, steps, -1))


def solution(mesh):
    in_specs = (
        P("group", None, "tensor"),
        P(None, "tensor"),
        P("group", "tensor"),
        P("group", "tensor"),
        P(),
        P("group", "tensor", None),
        P("group", None, None),
        P("group"),
    )
    out_specs = (P("group", None, "tensor"), P("group", None, "tensor"))
    return jax.shard_map(
        on_device, mesh=mesh, in_specs=in_specs, out_specs=out_specs, check_vma=False
    )
```

```python
import functools
import jax
import jax.numpy as jnp
from jax import lax
from jax.experimental import pallas as pl
from jax.experimental.pallas import tpu as pltpu
from jax.sharding import PartitionSpec as P

H = 64
KVH = 8
HD = 128
BLK = 128
LANES = 128
SUBLANES = 8


NEGATIVE = -1e30
SCORE_SCALE = HD ** (-0.5)
CACHE_KIB = 50 << 10
WEIGHTS_KIB = 16 << 10
PROJECT_KIB = 16 << 10
NT = (((1,), (1,)), ((), ()))
TN = (((0,), (0,)), ((), ()))
VMEM = pl.BlockSpec(memory_space=pltpu.VMEM)
SMEM = pl.BlockSpec(memory_space=pltpu.SMEM)
HBM = pl.BlockSpec(memory_space=pltpu.HBM)


def dot(left, right, dims):
    return lax.dot_general(left, right, dims, preferred_element_type=jnp.float32)


def swap(x, axis, distance):
    size = lax.axis_size(axis)
    return lax.ppermute(x, axis, [(k, k ^ distance) for k in range(size)])


def distances(size):
    return [0] + list(range(size - 1, 0, -1))


def params(kibibytes):
    return pltpu.CompilerParams(vmem_limit_bytes=kibibytes << 10)


def head_rows(block, row, steps, heads):
    mine = block[row * steps : (row + 1) * steps]
    return jnp.concatenate([mine[:, h * HD : (h + 1) * HD] for h in range(heads)], axis=0)


def weights_kernel(own_codes, mate_codes, own_scales, mate_scales, own_ref, mate_ref):
    for codes_ref, scales_ref, out_ref in (
        (own_codes, own_scales, own_ref),
        (mate_codes, mate_scales, mate_ref),
    ):
        scales = scales_ref[...].astype(jnp.float32).T
        for n in range(scales.shape[1]):
            lanes = slice(n * BLK, (n + 1) * BLK)
            values = codes_ref[:, lanes].astype(jnp.float32) * scales[:, n : n + 1]
            out_ref[:, lanes] = values.astype(jnp.bfloat16)


def weights(codes, scales):
    return pl.pallas_call(
        weights_kernel,
        out_shape=[jax.ShapeDtypeStruct(one.shape, jnp.bfloat16) for one in codes],
        in_specs=[VMEM] * 4,
        out_specs=[VMEM] * 2,
        compiler_params=params(WEIGHTS_KIB),
        cost_estimate=pl.CostEstimate(
            flops=2 * codes[0].size, bytes_accessed=8 * codes[0].size, transcendentals=0
        ),
        name="weights",
    )(*codes, *[one.T for one in scales])


def cache_kernel(rows, steps, own, chunk, scalars_ref, query_hbm, cache_hbm, base_hbm, *refs):
    base_ref, own_query_ref, parts = refs[0], refs[1], refs[2:-3]
    query_ref, cache_ref, arrived = refs[-3:]
    place = lax.axis_index("tensor")
    cache_len = cache_ref.shape[0] // rows
    block = base_ref.shape[1]
    shards = lax.axis_size("group")
    query_load = pltpu.make_async_copy(query_hbm, query_ref, arrived.at[0])
    cache_loads, base_loads = [], []
    for r in range(rows):
        here = pl.ds(r * cache_len, cache_len)
        cache_loads.append(
            pltpu.make_async_copy(cache_hbm.at[here], cache_ref.at[here], arrived.at[1 + r])
        )
    for k in range(2):
        start = scalars_ref[lax.axis_index("group") ^ k] * block
        here = pl.ds(pl.multiple_of(start, block), block)
        base_loads.append(
            pltpu.make_async_copy(base_hbm.at[here], base_ref.at[k], arrived.at[1 + rows + k])
        )
    for load in [query_load] + cache_loads + base_loads:
        load.start()
    query_load.wait()

    chunks = own // chunk
    height = chunk * steps
    width = chunks * HD
    position = lax.broadcasted_iota(jnp.int32, (cache_len, chunks * height), 0)

    def kv_lane(d):
        return pl.multiple_of(((place ^ order[d]) * own // (H // KVH)) * HD, HD)

    def score(r, d):
        head = (place ^ order[d]) * own
        queries = query_ref[:, pl.ds(pl.multiple_of(head * HD, HD), own * HD)]
        query = head_rows(queries.astype(jnp.float32), r, steps, own)
        if d == 0:
            at = r * chunks * height
            own_query_ref[at : at + chunks * height] = query.astype(jnp.bfloat16)
        spread = []
        for j in range(chunks):
            line = [jnp.zeros((height, HD), jnp.float32)] * chunks
            line[j] = query[j * height : (j + 1) * height]
            spread.append(jnp.concatenate(line, axis=1))
        spread = jnp.concatenate(spread, axis=0).astype(jnp.bfloat16)
        keys = cache_ref[pl.ds(r * cache_len, cache_len), pl.ds(kv_lane(d), width)]
        return dot(keys, spread, NT)

    order = distances(len(parts))
    units = [(r, d) for r in range(rows) for d in range(len(parts))]
    ahead = []
    for n in range(len(units) + 1):
        if n < len(units):
            if n % len(parts) == 0:
                cache_loads[n // len(parts)].wait()
            ahead.append(score(*units[n]))
        if n == 0:
            continue
        r, d = units[n - 1]
        at = r * chunks * height
        usable = position < scalars_ref[shards + r] - place * cache_len
        scores = jnp.where(usable, ahead.pop(0) * SCORE_SCALE, 2.0 * NEGATIVE)
        peak = jnp.maximum(jnp.max(scores, axis=0, keepdims=True), NEGATIVE)
        weights = jnp.exp(scores - peak)
        total = jnp.sum(weights, axis=0, keepdims=True)
        lane = pl.ds(kv_lane(d) + KVH * HD, width)
        values = cache_ref[pl.ds(r * cache_len, cache_len), lane]
        sums = dot(weights.astype(jnp.bfloat16), values, TN)
        for j in range(chunks):
            here = slice(j * height, (j + 1) * height)
            parts[d][at + j * height : at + (j + 1) * height] = sums[here, j * HD : (j + 1) * HD]
        end = rows * chunks * height + 2 * r
        parts[d][end : end + 1, : chunks * height] = peak
        parts[d][end + 1 : end + 2, : chunks * height] = total
    for load in base_loads:
        load.wait()


def cache_partials(scalars, queries, cache, base, block, rows, steps, own, ways):
    height = rows * own * steps
    part = jax.ShapeDtypeStruct((height + SUBLANES, LANES), jnp.float32)
    out = pl.pallas_call(
        functools.partial(cache_kernel, rows, steps, own, min(own, H // KVH)),
        out_shape=[
            jax.ShapeDtypeStruct((2, block, base.shape[1]), jnp.bfloat16),
            jax.ShapeDtypeStruct((height, HD), jnp.bfloat16),
        ]
        + [part] * ways,
        in_specs=[SMEM, HBM, HBM, HBM],
        out_specs=[VMEM] * (2 + ways),
        scratch_shapes=[
            pltpu.VMEM(queries.shape, queries.dtype),
            pltpu.VMEM(cache.shape, cache.dtype),
            pltpu.SemaphoreType.DMA((3 + rows,)),
        ],
        compiler_params=params(CACHE_KIB),
        cost_estimate=pl.CostEstimate(
            flops=4 * height * ways * HD * cache.shape[0] // rows,
            bytes_accessed=2 * cache.size + 2 * queries.size + 4 * block * base.shape[1],
            transcendentals=height * ways * cache.shape[0] // rows,
        ),
        name="cache_partials",
    )(scalars, queries, cache, base)
    return out[0], out[1], out[2:]


def project_kernel(pairs, own_ref, mate_ref, base_ref, *refs):
    tokens, outs = refs[:pairs], refs[pairs:]
    block = own_ref.shape[0]
    stacked = jnp.concatenate([ref[...] for ref in tokens], axis=0)
    count = tokens[0].shape[0]
    for k, delta_ref in enumerate((own_ref, mate_ref)):
        whole = (dot(base_ref[k], stacked, NT) + dot(delta_ref[...], stacked, NT)).T
        for n in range(pairs):
            outs[n][:, k * block : (k + 1) * block] = whole[n * count : (n + 1) * count]


def project(own, mate, base, tokens):
    pairs = len(tokens)
    block = own.shape[0]
    count, width = tokens[0].shape
    return pl.pallas_call(
        functools.partial(project_kernel, pairs),
        out_shape=[jax.ShapeDtypeStruct((count, 2 * block), jnp.float32)] * pairs,
        in_specs=[VMEM] * (3 + pairs),
        out_specs=[VMEM] * pairs,
        compiler_params=params(PROJECT_KIB),
        cost_estimate=pl.CostEstimate(
            flops=8 * block * width * count * pairs,
            bytes_accessed=8 * block * width,
            transcendentals=0,
        ),
        name="project",
    )(own, mate, base, *tokens)


def pack_kernel(pairs, ways, near, wide, owner_ref, *refs):
    arrived, outs, ordered = refs[:pairs], refs[pairs : pairs + ways], refs[-1]
    place = lax.axis_index("group")
    to_place = lax.axis_index("tensor")
    shards, _, block = ordered.shape
    for piece, d in zip(arrived, distances(pairs)):
        for k in range(2):
            ordered[owner_ref[place ^ (2 * d + k)]] = piece[:, k * block : (k + 1) * block]
    for out, d in zip(outs, distances(ways)):
        to = to_place ^ d
        for n in range(near):
            out[:, n * block : (n + 1) * block] = ordered[to * near + n]
            at = (near + n) * block
            out[:, at : at + block] = ordered[shards // 2 + to * near + n]
        for n in range(wide):
            at = (2 * near + n) * block
            out[:, at : at + block] = ordered[to * wide + n]


def pack_pieces(owner_map, arrived, block, ways, near_width, slice_width):
    pairs = len(arrived)
    count = arrived[0].shape[0]
    shards = 2 * pairs
    kv_width = KVH * HD
    if block % LANES == 0 and near_width % block == 0 and slice_width % block == 0:
        piece = jax.ShapeDtypeStruct((count, 2 * near_width + slice_width), jnp.float32)
        kernel = functools.partial(
            pack_kernel, pairs, ways, near_width // block, slice_width // block
        )
        return pl.pallas_call(
            kernel,
            out_shape=[piece] * ways,
            in_specs=[SMEM] + [VMEM] * pairs,
            out_specs=[VMEM] * ways,
            scratch_shapes=[pltpu.VMEM((shards, count, block), jnp.float32)],
            compiler_params=params(8192),
            name="pack_pieces",
        )(owner_map, *arrived)
    nearest = [arrived[distances(pairs).index(d)] for d in range(pairs)]
    blocks = jnp.stack(nearest, axis=0).reshape(pairs, count, 2, block).transpose(0, 2, 1, 3)
    shard_of = jnp.zeros((shards,), jnp.int32).at[owner_map].set(
        jnp.arange(shards, dtype=jnp.int32)
    )
    taken = jnp.take(
        blocks.reshape(shards, count, block), shard_of ^ lax.axis_index("group"), axis=0
    )
    ordered = taken.transpose(1, 0, 2).reshape(count, shards * block)
    per_device = H // ways
    pieces = []
    for d in distances(ways):
        to = lax.axis_index("tensor") ^ d
        near = (to * per_device // (H // KVH)) * HD
        parts = [(near, near_width), (kv_width + near, near_width), (to * slice_width, slice_width)]
        cuts = [lax.dynamic_slice_in_dim(ordered, start, width, 1) for start, width in parts]
        pieces.append(jnp.concatenate(cuts, axis=1))
    return pieces


def finish_kernel(rows, steps, own, chunk, near_width, ways, query_ref, *refs):
    pieces, parts = refs[:ways], refs[ways : 2 * ways]
    new_ref, attended_ref = refs[2 * ways :]
    chunks = own // chunk
    height = chunk * steps
    end = rows * chunks * height
    summed = pieces[0][...]
    for piece in pieces[1:]:
        summed = summed + piece[...]
    stored = summed.astype(jnp.bfloat16)
    new_ref[...] = stored[:, 2 * near_width :]
    near = stored[:, : 2 * near_width].astype(jnp.float32)
    key_step = lax.broadcasted_iota(jnp.int32, (steps, height), 0)
    query_step = lax.broadcasted_iota(jnp.int32, (steps, height), 1) % steps
    causal = key_step <= query_step
    stats = [part[end : end + SUBLANES] for part in parts]
    factors, near_sums = [], []
    for r in range(rows):
        peaks, totals = [], []
        for j in range(chunks):
            at = (r * chunks + j) * height
            query = query_ref[at : at + height]
            step_rows = slice(r * steps, (r + 1) * steps)
            keys = near[step_rows, j * HD : (j + 1) * HD].astype(jnp.bfloat16)
            values = near[step_rows, near_width + j * HD : near_width + (j + 1) * HD]
            scores = jnp.where(causal, dot(keys, query, NT) * SCORE_SCALE, NEGATIVE)
            peak = jnp.max(scores, axis=0, keepdims=True)
            weights = jnp.where(causal, jnp.exp(scores - peak), 0.0)
            peaks.append(peak)
            totals.append(jnp.sum(weights, axis=0, keepdims=True))
            near_sums.append(dot(weights.astype(jnp.bfloat16), values.astype(jnp.bfloat16), TN))
        lanes = chunks * height
        pad = [jnp.zeros((1, LANES - lanes), jnp.float32)] if lanes < LANES else []
        peaks = [s[2 * r : 2 * r + 1] for s in stats] + [jnp.concatenate(peaks + pad, axis=1)]
        totals = [s[2 * r + 1 : 2 * r + 2] for s in stats] + [jnp.concatenate(totals + pad, axis=1)]
        top = functools.reduce(jnp.maximum, peaks)
        scales = [jnp.exp(peak - top) for peak in peaks]
        total = sum(scale * one for scale, one in zip(scales, totals))
        if pad:
            total = jnp.where(total == 0.0, 1.0, total)
        factors += [scale / total for scale in scales]
    lines = -(-len(factors) // SUBLANES) * SUBLANES
    if lines > len(factors):
        factors.append(jnp.zeros((lines - len(factors), LANES), jnp.float32))
    columns = jnp.concatenate(factors, axis=0).T
    for j in range(chunks):
        merged = []
        for r in range(rows):
            at = (r * chunks + j) * height
            here = slice(j * height, (j + 1) * height)
            first = r * (ways + 1)
            out = near_sums[r * chunks + j] * columns[here, first + ways : first + ways + 1]
            for d, part in enumerate(parts):
                out = out + part[at : at + height] * columns[here, first + d : first + d + 1]
            merged.append(out)
        for h in range(chunk):
            both = [out[h * steps : (h + 1) * steps] for out in merged]
            lane = (j * chunk + h) * HD
            attended_ref[:, lane : lane + HD] = jnp.concatenate(both, axis=0).astype(jnp.bfloat16)


def finish(own_query, pieces, parts, rows, steps, own, near_width):
    ways = len(pieces)
    count, width = pieces[0].shape
    return pl.pallas_call(
        functools.partial(
            finish_kernel, rows, steps, own, min(own, H // KVH), near_width, ways
        ),
        out_shape=[
            jax.ShapeDtypeStruct((count, width - 2 * near_width), jnp.bfloat16),
            jax.ShapeDtypeStruct((count, own * HD), jnp.bfloat16),
        ],
        in_specs=[VMEM] * (1 + 2 * ways),
        out_specs=[VMEM] * 2,
        compiler_params=params(8192),
        name="finish",
    )(own_query, *pieces, *parts)


def on_device(
    hidden_x, base_weight, delta_codes, delta_scales, owner_map, kv_cache, queries, lengths
):
    group_count = lax.axis_size("group")
    tensor_count = lax.axis_size("tensor")
    rows, steps, local_width = hidden_x.shape
    tokens = rows * steps
    owner_block = delta_codes.shape[0]
    heads_own = H // tensor_count
    slice_width = base_weight.shape[0] // tensor_count
    near_width = max(1, heads_own // (H // KVH)) * HD
    pairs = group_count // 2

    def exchange(arrays, axis, stride):
        places = distances(len(arrays))[1:]
        return [arrays[0]] + [swap(x, axis, stride * d) for x, d in zip(arrays[1:], places)]

    mine = hidden_x.reshape(tokens, local_width)
    token_rows = exchange([mine] * pairs, "group", 2)
    codes = [delta_codes, swap(delta_codes, "group", 1)]
    scales = [delta_scales, swap(delta_scales, "group", 1)]

    cache_len = kv_cache.shape[1]
    base_blocks, own_query, partials = cache_partials(
        jnp.concatenate([owner_map, lengths]),
        queries.reshape(tokens, H * HD),
        kv_cache.reshape(rows * cache_len, 2 * KVH * HD),
        base_weight,
        owner_block,
        rows,
        steps,
        heads_own,
        tensor_count,
    )
    own_delta, mate_delta = weights(codes, scales)
    projected = project(own_delta, mate_delta, base_blocks, token_rows)

    arrived = exchange(projected, "group", 2)
    held = lax.optimization_barrier((arrived[-1], partials[2:]))
    arrived, partials = arrived[:-1] + [held[0]], partials[:2] + held[1]
    partials = exchange(partials, "tensor", 1)
    pieces = pack_pieces(owner_map, arrived, owner_block, tensor_count, near_width, slice_width)
    pieces = exchange(pieces, "tensor", 1)
    new_out, attended = finish(own_query, pieces, partials, rows, steps, heads_own, near_width)
    return (new_out.reshape(rows, steps, -1), attended.reshape(rows, steps, -1))


def solution(mesh):
    in_specs = (
        P("group", None, "tensor"),
        P(None, "tensor"),
        P("group", "tensor"),
        P("group", "tensor"),
        P(),
        P("group", "tensor", None),
        P("group", None, None),
        P("group"),
    )
    out_specs = (P("group", None, "tensor"), P("group", None, "tensor"))
    return jax.shard_map(
        on_device, mesh=mesh, in_specs=in_specs, out_specs=out_specs, check_vma=False
    )
```

```python
import functools
import jax
import jax.numpy as jnp
from jax import lax
from jax.experimental import pallas as pl
from jax.experimental.pallas import tpu as pltpu
from jax.sharding import PartitionSpec as P

H = 64
KVH = 8
HD = 128
BLK = 128
LANES = 128
SUBLANES = 8


NEGATIVE = -1e30
SCORE_SCALE = HD ** (-0.5)
CACHE_HINT = 120_000_000
WEIGHTS_HINT = 100_000
PROJECT_HINT = 60_000_000
PACK_HINT = 60_000_000
CACHE_KIB = 24 << 10
WEIGHTS_KIB = 16 << 10
PROJECT_KIB = 16 << 10
NT = (((1,), (1,)), ((), ()))
TN = (((0,), (0,)), ((), ()))
VMEM = pl.BlockSpec(memory_space=pltpu.VMEM)
SMEM = pl.BlockSpec(memory_space=pltpu.SMEM)
HBM = pl.BlockSpec(memory_space=pltpu.HBM)


def hint(size):
    return pl.CostEstimate(flops=0, bytes_accessed=size, transcendentals=0)


def dot(left, right, dims):
    return lax.dot_general(left, right, dims, preferred_element_type=jnp.float32)


def swap(x, axis, distance):
    size = lax.axis_size(axis)
    return lax.ppermute(x, axis, [(k, k ^ distance) for k in range(size)])


def distances(size):
    return [0] + list(range(size - 1, 0, -1))


def params(kibibytes):
    return pltpu.CompilerParams(vmem_limit_bytes=kibibytes << 10)


def head_rows(block, row, steps, heads):
    mine = block[row * steps : (row + 1) * steps]
    return jnp.concatenate([mine[:, h * HD : (h + 1) * HD] for h in range(heads)], axis=0)


def weights_kernel(
    own_codes_hbm, own_scales_hbm, mate_codes, mate_scales, own_ref, mate_ref, codes, scales, arrived
):
    loads = [
        pltpu.make_async_copy(own_scales_hbm, scales, arrived.at[0]),
        pltpu.make_async_copy(own_codes_hbm, codes, arrived.at[1]),
    ]
    for load in loads:
        load.start()

    def dequantize(codes_ref, scales_ref, out_ref):
        columns = scales_ref[...].astype(jnp.float32).T
        for n in range(columns.shape[1]):
            lanes = slice(n * BLK, (n + 1) * BLK)
            values = codes_ref[:, lanes].astype(jnp.float32) * columns[:, n : n + 1]
            out_ref[:, lanes] = values.astype(jnp.bfloat16)

    dequantize(mate_codes, mate_scales, mate_ref)
    for load in loads:
        load.wait()
    dequantize(codes, scales, own_ref)


def weights(codes, scales):
    own = [pltpu.with_memory_space_constraint(x, pltpu.HBM) for x in (codes[0], scales[0].T)]
    return pl.pallas_call(
        weights_kernel,
        out_shape=[jax.ShapeDtypeStruct(one.shape, jnp.bfloat16) for one in codes],
        in_specs=[HBM, HBM, VMEM, VMEM],
        out_specs=[VMEM] * 2,
        scratch_shapes=[
            pltpu.VMEM(codes[0].shape, codes[0].dtype),
            pltpu.VMEM(scales[0].shape[::-1], scales[0].dtype),
            pltpu.SemaphoreType.DMA((2,)),
        ],
        compiler_params=params(WEIGHTS_KIB),
        cost_estimate=hint(WEIGHTS_HINT),
        name="weights",
    )(*own, codes[1], scales[1].T)


def cache_kernel(
    rows, steps, own, chunk, owner_ref, lengths_ref, query_ref, cache_ref, base_hbm, *refs
):
    base_ref, own_query_ref, parts, arrived = refs[0], refs[1], refs[2:-1], refs[-1]
    place = lax.axis_index("tensor")
    cache_len = cache_ref.shape[0] // rows
    block = base_ref.shape[1]
    base_loads = []
    for k in range(2):
        start = owner_ref[lax.axis_index("group") ^ k] * block
        here = pl.ds(pl.multiple_of(start, block), block)
        base_loads.append(pltpu.make_async_copy(base_hbm.at[here], base_ref.at[k], arrived.at[k]))
        base_loads[k].start()

    chunks = own // chunk
    height = chunk * steps
    width = chunks * HD
    position = lax.broadcasted_iota(jnp.int32, (cache_len, chunks * height), 0)

    def kv_lane(d):
        return pl.multiple_of(((place ^ order[d]) * own // (H // KVH)) * HD, HD)

    def score(r, d):
        head = (place ^ order[d]) * own
        queries = query_ref[:, pl.ds(pl.multiple_of(head * HD, HD), own * HD)]
        query = head_rows(queries.astype(jnp.float32), r, steps, own)
        if d == 0:
            at = r * chunks * height
            own_query_ref[at : at + chunks * height] = query.astype(jnp.bfloat16)
        spread = []
        for j in range(chunks):
            line = [jnp.zeros((height, HD), jnp.float32)] * chunks
            line[j] = query[j * height : (j + 1) * height]
            spread.append(jnp.concatenate(line, axis=1))
        spread = jnp.concatenate(spread, axis=0).astype(jnp.bfloat16)
        keys = cache_ref[pl.ds(r * cache_len, cache_len), pl.ds(kv_lane(d), width)]
        return dot(keys, spread, NT)

    order = distances(len(parts))
    units = [(r, d) for r in range(rows) for d in range(len(parts))]
    ahead = []
    for n in range(len(units) + 1):
        if n < len(units):
            ahead.append(score(*units[n]))
        if n == 0:
            continue
        r, d = units[n - 1]
        at = r * chunks * height
        usable = position < lengths_ref[r] - place * cache_len
        scores = jnp.where(usable, ahead.pop(0) * SCORE_SCALE, 2.0 * NEGATIVE)
        peak = jnp.maximum(jnp.max(scores, axis=0, keepdims=True), NEGATIVE)
        weights = jnp.exp(scores - peak)
        total = jnp.sum(weights, axis=0, keepdims=True)
        lane = pl.ds(kv_lane(d) + KVH * HD, width)
        values = cache_ref[pl.ds(r * cache_len, cache_len), lane]
        sums = dot(weights.astype(jnp.bfloat16), values, TN)
        for j in range(chunks):
            here = slice(j * height, (j + 1) * height)
            parts[d][at + j * height : at + (j + 1) * height] = sums[here, j * HD : (j + 1) * HD]
        end = rows * chunks * height + 2 * r
        parts[d][end : end + 1, : chunks * height] = peak
        parts[d][end + 1 : end + 2, : chunks * height] = total
    for load in base_loads:
        load.wait()


def cache_partials(owner_map, lengths, queries, cache, base, block, rows, steps, own, ways):
    height = rows * own * steps
    part = jax.ShapeDtypeStruct((height + SUBLANES, LANES), jnp.float32)
    out = pl.pallas_call(
        functools.partial(cache_kernel, rows, steps, own, min(own, H // KVH)),
        out_shape=[
            jax.ShapeDtypeStruct((2, block, base.shape[1]), jnp.bfloat16),
            jax.ShapeDtypeStruct((height, HD), jnp.bfloat16),
        ]
        + [part] * ways,
        in_specs=[SMEM, SMEM, VMEM, VMEM, HBM],
        out_specs=[VMEM] * (2 + ways),
        scratch_shapes=[
            pltpu.SemaphoreType.DMA((2,)),
        ],
        compiler_params=params(CACHE_KIB),
        cost_estimate=hint(CACHE_HINT),
        name="cache_partials",
    )(owner_map, lengths, queries, cache, pltpu.with_memory_space_constraint(base, pltpu.HBM))
    return out[0], out[1], out[2:]


def project_kernel(pairs, own_ref, mate_ref, base_ref, *refs):
    tokens, outs = refs[:pairs], refs[pairs:]
    block = own_ref.shape[0]
    stacked = jnp.concatenate([ref[...] for ref in tokens], axis=0)
    count = tokens[0].shape[0]
    for k, delta_ref in enumerate((own_ref, mate_ref)):
        whole = (dot(base_ref[k], stacked, NT) + dot(delta_ref[...], stacked, NT)).T
        for n in range(pairs):
            outs[n][:, k * block : (k + 1) * block] = whole[n * count : (n + 1) * count]


def project(own, mate, base, tokens):
    pairs = len(tokens)
    block = own.shape[0]
    count, width = tokens[0].shape
    return pl.pallas_call(
        functools.partial(project_kernel, pairs),
        out_shape=[jax.ShapeDtypeStruct((count, 2 * block), jnp.float32)] * pairs,
        in_specs=[VMEM] * (3 + pairs),
        out_specs=[VMEM] * pairs,
        compiler_params=params(PROJECT_KIB),
        cost_estimate=hint(PROJECT_HINT),
        name="project",
    )(own, mate, base, *tokens)


def pack_kernel(pairs, ways, near, wide, owner_ref, *refs):
    arrived, outs, ordered = refs[:pairs], refs[pairs : pairs + ways], refs[-1]
    place = lax.axis_index("group")
    to_place = lax.axis_index("tensor")
    shards, _, block = ordered.shape
    for piece, d in zip(arrived, distances(pairs)):
        for k in range(2):
            ordered[owner_ref[place ^ (2 * d + k)]] = piece[:, k * block : (k + 1) * block]
    for out, d in zip(outs, distances(ways)):
        to = to_place ^ d
        for n in range(near):
            out[:, n * block : (n + 1) * block] = ordered[to * near + n]
            at = (near + n) * block
            out[:, at : at + block] = ordered[shards // 2 + to * near + n]
        for n in range(wide):
            at = (2 * near + n) * block
            out[:, at : at + block] = ordered[to * wide + n]


def pack_pieces(owner_map, arrived, block, ways, near_width, slice_width):
    pairs = len(arrived)
    count = arrived[0].shape[0]
    shards = 2 * pairs
    kv_width = KVH * HD
    if block % LANES == 0 and near_width % block == 0 and slice_width % block == 0:
        piece = jax.ShapeDtypeStruct((count, 2 * near_width + slice_width), jnp.float32)
        kernel = functools.partial(
            pack_kernel, pairs, ways, near_width // block, slice_width // block
        )
        return pl.pallas_call(
            kernel,
            out_shape=[piece] * ways,
            in_specs=[SMEM] + [VMEM] * pairs,
            out_specs=[VMEM] * ways,
            scratch_shapes=[pltpu.VMEM((shards, count, block), jnp.float32)],
            compiler_params=params(8192),
            cost_estimate=hint(PACK_HINT),
            name="pack_pieces",
        )(owner_map, *arrived)
    nearest = [arrived[distances(pairs).index(d)] for d in range(pairs)]
    blocks = jnp.stack(nearest, axis=0).reshape(pairs, count, 2, block).transpose(0, 2, 1, 3)
    shard_of = jnp.zeros((shards,), jnp.int32).at[owner_map].set(
        jnp.arange(shards, dtype=jnp.int32)
    )
    taken = jnp.take(
        blocks.reshape(shards, count, block), shard_of ^ lax.axis_index("group"), axis=0
    )
    ordered = taken.transpose(1, 0, 2).reshape(count, shards * block)
    per_device = H // ways
    pieces = []
    for d in distances(ways):
        to = lax.axis_index("tensor") ^ d
        near = (to * per_device // (H // KVH)) * HD
        parts = [(near, near_width), (kv_width + near, near_width), (to * slice_width, slice_width)]
        cuts = [lax.dynamic_slice_in_dim(ordered, start, width, 1) for start, width in parts]
        pieces.append(jnp.concatenate(cuts, axis=1))
    return pieces


def finish_kernel(rows, steps, own, chunk, near_width, ways, query_ref, *refs):
    pieces, parts = refs[:ways], refs[ways : 2 * ways]
    new_ref, attended_ref = refs[2 * ways :]
    chunks = own // chunk
    height = chunk * steps
    end = rows * chunks * height
    summed = pieces[0][...]
    for piece in pieces[1:]:
        summed = summed + piece[...]
    stored = summed.astype(jnp.bfloat16)
    new_ref[...] = stored[:, 2 * near_width :]
    near = stored[:, : 2 * near_width].astype(jnp.float32)
    key_step = lax.broadcasted_iota(jnp.int32, (steps, height), 0)
    query_step = lax.broadcasted_iota(jnp.int32, (steps, height), 1) % steps
    causal = key_step <= query_step
    stats = [part[end : end + SUBLANES] for part in parts]
    factors, near_sums = [], []
    for r in range(rows):
        peaks, totals = [], []
        for j in range(chunks):
            at = (r * chunks + j) * height
            query = query_ref[at : at + height]
            step_rows = slice(r * steps, (r + 1) * steps)
            keys = near[step_rows, j * HD : (j + 1) * HD].astype(jnp.bfloat16)
            values = near[step_rows, near_width + j * HD : near_width + (j + 1) * HD]
            scores = jnp.where(causal, dot(keys, query, NT) * SCORE_SCALE, NEGATIVE)
            peak = jnp.max(scores, axis=0, keepdims=True)
            weights = jnp.where(causal, jnp.exp(scores - peak), 0.0)
            peaks.append(peak)
            totals.append(jnp.sum(weights, axis=0, keepdims=True))
            near_sums.append(dot(weights.astype(jnp.bfloat16), values.astype(jnp.bfloat16), TN))
        lanes = chunks * height
        pad = [jnp.zeros((1, LANES - lanes), jnp.float32)] if lanes < LANES else []
        peaks = [s[2 * r : 2 * r + 1] for s in stats] + [jnp.concatenate(peaks + pad, axis=1)]
        totals = [s[2 * r + 1 : 2 * r + 2] for s in stats] + [jnp.concatenate(totals + pad, axis=1)]
        top = functools.reduce(jnp.maximum, peaks)
        scales = [jnp.exp(peak - top) for peak in peaks]
        total = sum(scale * one for scale, one in zip(scales, totals))
        if pad:
            total = jnp.where(total == 0.0, 1.0, total)
        factors += [scale / total for scale in scales]
    lines = -(-len(factors) // SUBLANES) * SUBLANES
    if lines > len(factors):
        factors.append(jnp.zeros((lines - len(factors), LANES), jnp.float32))
    columns = jnp.concatenate(factors, axis=0).T
    for j in range(chunks):
        merged = []
        for r in range(rows):
            at = (r * chunks + j) * height
            here = slice(j * height, (j + 1) * height)
            first = r * (ways + 1)
            out = near_sums[r * chunks + j] * columns[here, first + ways : first + ways + 1]
            for d, part in enumerate(parts):
                out = out + part[at : at + height] * columns[here, first + d : first + d + 1]
            merged.append(out)
        for h in range(chunk):
            both = [out[h * steps : (h + 1) * steps] for out in merged]
            lane = (j * chunk + h) * HD
            attended_ref[:, lane : lane + HD] = jnp.concatenate(both, axis=0).astype(jnp.bfloat16)


def finish(own_query, pieces, parts, rows, steps, own, near_width):
    ways = len(pieces)
    count, width = pieces[0].shape
    return pl.pallas_call(
        functools.partial(
            finish_kernel, rows, steps, own, min(own, H // KVH), near_width, ways
        ),
        out_shape=[
            jax.ShapeDtypeStruct((count, width - 2 * near_width), jnp.bfloat16),
            jax.ShapeDtypeStruct((count, own * HD), jnp.bfloat16),
        ],
        in_specs=[VMEM] * (1 + 2 * ways),
        out_specs=[VMEM] * 2,
        compiler_params=params(8192),
        name="finish",
    )(own_query, *pieces, *parts)


def on_device(
    hidden_x, base_weight, delta_codes, delta_scales, owner_map, kv_cache, queries, lengths
):
    group_count = lax.axis_size("group")
    tensor_count = lax.axis_size("tensor")
    rows, steps, local_width = hidden_x.shape
    tokens = rows * steps
    owner_block = delta_codes.shape[0]
    heads_own = H // tensor_count
    slice_width = base_weight.shape[0] // tensor_count
    near_width = max(1, heads_own // (H // KVH)) * HD
    pairs = group_count // 2

    def exchange(arrays, axis, stride):
        places = distances(len(arrays))[1:]
        return [arrays[0]] + [swap(x, axis, stride * d) for x, d in zip(arrays[1:], places)]

    token_rows = exchange([hidden_x.reshape(tokens, local_width)] * pairs, "group", 2)
    codes = [delta_codes, swap(delta_codes, "group", 1)]
    scales = [delta_scales, swap(delta_scales, "group", 1)]

    own_delta, mate_delta = weights(codes, scales)
    behind, own_delta = lax.optimization_barrier((owner_map, own_delta))
    base_blocks, own_query, partials = cache_partials(
        behind,
        lengths,
        queries.reshape(tokens, H * HD),
        kv_cache.reshape(-1, 2 * KVH * HD),
        base_weight,
        owner_block,
        rows,
        steps,
        heads_own,
        tensor_count,
    )
    partials = exchange(partials, "tensor", 1)
    projected = project(own_delta, mate_delta, base_blocks, token_rows)
    arrived = exchange(projected, "group", 2)
    pieces = pack_pieces(owner_map, arrived, owner_block, tensor_count, near_width, slice_width)
    pieces = exchange(pieces, "tensor", 1)
    new_out, attended = finish(own_query, pieces, partials, rows, steps, heads_own, near_width)
    return (new_out.reshape(rows, steps, -1), attended.reshape(rows, steps, -1))


def solution(mesh):
    in_specs = (
        P("group", None, "tensor"),
        P(None, "tensor"),
        P("group", "tensor"),
        P("group", "tensor"),
        P(),
        P("group", "tensor", None),
        P("group", None, None),
        P("group"),
    )
    out_specs = (P("group", None, "tensor"), P("group", None, "tensor"))
    return jax.shard_map(
        on_device, mesh=mesh, in_specs=in_specs, out_specs=out_specs, check_vma=False
    )
```

```python
import functools
import jax
import jax.numpy as jnp
from jax import lax
from jax.experimental import pallas as pl
from jax.experimental.pallas import tpu as pltpu
from jax.sharding import PartitionSpec as P

H = 64
KVH = 8
HD = 128
BLK = 128
LANES = 128
SUBLANES = 8


NEGATIVE = -1e30
SCORE_SCALE = HD ** (-0.5)
CACHE_HINT = 120_000_000
WEIGHTS_HINT = 6_000_000
PROJECT_HINT = 60_000_000
PACK_HINT = 60_000_000
CACHE_KIB = 24 << 10
WEIGHTS_KIB = 16 << 10
PROJECT_KIB = 16 << 10
NT = (((1,), (1,)), ((), ()))
TN = (((0,), (0,)), ((), ()))
VMEM = pl.BlockSpec(memory_space=pltpu.VMEM)
SMEM = pl.BlockSpec(memory_space=pltpu.SMEM)
HBM = pl.BlockSpec(memory_space=pltpu.HBM)


def hint(size):
    return pl.CostEstimate(flops=0, bytes_accessed=size, transcendentals=0)


def dot(left, right, dims):
    return lax.dot_general(left, right, dims, preferred_element_type=jnp.float32)


def swap(x, axis, distance):
    size = lax.axis_size(axis)
    return lax.ppermute(x, axis, [(k, k ^ distance) for k in range(size)])


def distances(size):
    return [0] + list(range(size - 1, 0, -1))


def params(kibibytes):
    return pltpu.CompilerParams(vmem_limit_bytes=kibibytes << 10)


def head_rows(block, row, steps, heads):
    mine = block[row * steps : (row + 1) * steps]
    return jnp.concatenate([mine[:, h * HD : (h + 1) * HD] for h in range(heads)], axis=0)


def dequantize(codes_ref, scales_ref, out_ref):
    columns = scales_ref[...].astype(jnp.float32).T
    for n in range(columns.shape[1]):
        lanes = slice(n * BLK, (n + 1) * BLK)
        values = codes_ref[:, lanes].astype(jnp.float32) * columns[:, n : n + 1]
        out_ref[:, lanes] = values.astype(jnp.bfloat16)


def own_weights_kernel(
    owner_hbm, scales_hbm, codes_hbm, base_hbm, out_ref, base_ref, owner_ref, scales_ref, codes_ref,
    arrived,
):
    place = lax.axis_index("group")
    block = codes_ref.shape[0]
    owner_load = pltpu.make_async_copy(owner_hbm, owner_ref, arrived.at[0])
    loads = [
        pltpu.make_async_copy(scales_hbm, scales_ref, arrived.at[1]),
        pltpu.make_async_copy(codes_hbm, codes_ref, arrived.at[2]),
    ]
    for load in [owner_load] + loads:
        load.start()
    owner_load.wait()
    base_loads = []
    for k in range(2):
        here = pl.ds(pl.multiple_of(owner_ref[place ^ k] * block, block), block)
        base_loads.append(
            pltpu.make_async_copy(base_hbm.at[here], base_ref.at[k], arrived.at[3 + k])
        )
        base_loads[k].start()
    for load in loads:
        load.wait()
    dequantize(codes_ref, scales_ref, out_ref)
    for load in base_loads:
        load.wait()


def own_weights(owner_map, scales, codes, base):
    operands = [
        pltpu.with_memory_space_constraint(x, pltpu.HBM) for x in (owner_map, scales.T, codes, base)
    ]
    return pl.pallas_call(
        own_weights_kernel,
        out_shape=[
            jax.ShapeDtypeStruct(codes.shape, jnp.bfloat16),
            jax.ShapeDtypeStruct((2,) + codes.shape, jnp.bfloat16),
        ],
        in_specs=[HBM] * 4,
        out_specs=[VMEM] * 2,
        scratch_shapes=[
            pltpu.SMEM(owner_map.shape, owner_map.dtype),
            pltpu.VMEM(scales.shape[::-1], scales.dtype),
            pltpu.VMEM(codes.shape, codes.dtype),
            pltpu.SemaphoreType.DMA((5,)),
        ],
        compiler_params=params(WEIGHTS_KIB),
        cost_estimate=hint(WEIGHTS_HINT),
        name="own_weights",
    )(*operands)


def mate_weights(codes, scales):
    return pl.pallas_call(
        dequantize,
        out_shape=jax.ShapeDtypeStruct(codes.shape, jnp.bfloat16),
        in_specs=[VMEM, VMEM],
        out_specs=VMEM,
        compiler_params=params(WEIGHTS_KIB),
        cost_estimate=hint(8 * codes.size),
        name="mate_weights",
    )(codes, scales.T)


def cache_kernel(rows, steps, own, chunk, lengths_ref, query_ref, cache_ref, own_query_ref, *parts):
    place = lax.axis_index("tensor")
    cache_len = cache_ref.shape[0] // rows
    chunks = own // chunk
    height = chunk * steps
    width = chunks * HD
    position = lax.broadcasted_iota(jnp.int32, (cache_len, chunks * height), 0)

    def kv_lane(d):
        return pl.multiple_of(((place ^ order[d]) * own // (H // KVH)) * HD, HD)

    def score(r, d):
        head = (place ^ order[d]) * own
        queries = query_ref[:, pl.ds(pl.multiple_of(head * HD, HD), own * HD)]
        query = head_rows(queries.astype(jnp.float32), r, steps, own)
        if d == 0:
            at = r * chunks * height
            own_query_ref[at : at + chunks * height] = query.astype(jnp.bfloat16)
        spread = []
        for j in range(chunks):
            line = [jnp.zeros((height, HD), jnp.float32)] * chunks
            line[j] = query[j * height : (j + 1) * height]
            spread.append(jnp.concatenate(line, axis=1))
        spread = jnp.concatenate(spread, axis=0).astype(jnp.bfloat16)
        keys = cache_ref[pl.ds(r * cache_len, cache_len), pl.ds(kv_lane(d), width)]
        return dot(keys, spread, NT)

    order = distances(len(parts))
    units = [(r, d) for r in range(rows) for d in range(len(parts))]
    ahead = []
    for n in range(len(units) + 1):
        if n < len(units):
            ahead.append(score(*units[n]))
        if n == 0:
            continue
        r, d = units[n - 1]
        at = r * chunks * height
        usable = position < lengths_ref[r] - place * cache_len
        scores = jnp.where(usable, ahead.pop(0) * SCORE_SCALE, 2.0 * NEGATIVE)
        peak = jnp.maximum(jnp.max(scores, axis=0, keepdims=True), NEGATIVE)
        weights = jnp.exp(scores - peak)
        total = jnp.sum(weights, axis=0, keepdims=True)
        lane = pl.ds(kv_lane(d) + KVH * HD, width)
        values = cache_ref[pl.ds(r * cache_len, cache_len), lane]
        sums = dot(weights.astype(jnp.bfloat16), values, TN)
        for j in range(chunks):
            here = slice(j * height, (j + 1) * height)
            parts[d][at + j * height : at + (j + 1) * height] = sums[here, j * HD : (j + 1) * HD]
        end = rows * chunks * height + 2 * r
        parts[d][end : end + 1, : chunks * height] = peak
        parts[d][end + 1 : end + 2, : chunks * height] = total


def cache_partials(lengths, queries, cache, rows, steps, own, ways):
    height = rows * own * steps
    part = jax.ShapeDtypeStruct((height + SUBLANES, LANES), jnp.float32)
    out = pl.pallas_call(
        functools.partial(cache_kernel, rows, steps, own, min(own, H // KVH)),
        out_shape=[jax.ShapeDtypeStruct((height, HD), jnp.bfloat16)] + [part] * ways,
        in_specs=[SMEM, VMEM, VMEM],
        out_specs=[VMEM] * (1 + ways),
        compiler_params=params(CACHE_KIB),
        cost_estimate=hint(CACHE_HINT),
        name="cache_partials",
    )(lengths, queries, cache)
    return out[0], out[1:]


def project_kernel(pairs, own_ref, mate_ref, base_ref, *refs):
    tokens, outs = refs[:pairs], refs[pairs:]
    block = own_ref.shape[0]
    stacked = jnp.concatenate([ref[...] for ref in tokens], axis=0)
    count = tokens[0].shape[0]
    for k, delta_ref in enumerate((own_ref, mate_ref)):
        whole = (dot(base_ref[k], stacked, NT) + dot(delta_ref[...], stacked, NT)).T
        for n in range(pairs):
            outs[n][:, k * block : (k + 1) * block] = whole[n * count : (n + 1) * count]


def project(own, mate, base, tokens):
    pairs = len(tokens)
    block = own.shape[0]
    count, width = tokens[0].shape
    return pl.pallas_call(
        functools.partial(project_kernel, pairs),
        out_shape=[jax.ShapeDtypeStruct((count, 2 * block), jnp.float32)] * pairs,
        in_specs=[VMEM] * (3 + pairs),
        out_specs=[VMEM] * pairs,
        compiler_params=params(PROJECT_KIB),
        cost_estimate=hint(PROJECT_HINT),
        name="project",
    )(own, mate, base, *tokens)


def pack_kernel(pairs, ways, near, wide, owner_ref, *refs):
    arrived, outs, ordered = refs[:pairs], refs[pairs : pairs + ways], refs[-1]
    place = lax.axis_index("group")
    to_place = lax.axis_index("tensor")
    shards, _, block = ordered.shape
    for piece, d in zip(arrived, distances(pairs)):
        for k in range(2):
            ordered[owner_ref[place ^ (2 * d + k)]] = piece[:, k * block : (k + 1) * block]
    for out, d in zip(outs, distances(ways)):
        to = to_place ^ d
        for n in range(near):
            out[:, n * block : (n + 1) * block] = ordered[to * near + n]
            at = (near + n) * block
            out[:, at : at + block] = ordered[shards // 2 + to * near + n]
        for n in range(wide):
            at = (2 * near + n) * block
            out[:, at : at + block] = ordered[to * wide + n]


def pack_pieces(owner_map, arrived, block, ways, near_width, slice_width):
    pairs = len(arrived)
    count = arrived[0].shape[0]
    shards = 2 * pairs
    kv_width = KVH * HD
    if block % LANES == 0 and near_width % block == 0 and slice_width % block == 0:
        piece = jax.ShapeDtypeStruct((count, 2 * near_width + slice_width), jnp.float32)
        kernel = functools.partial(
            pack_kernel, pairs, ways, near_width // block, slice_width // block
        )
        return pl.pallas_call(
            kernel,
            out_shape=[piece] * ways,
            in_specs=[SMEM] + [VMEM] * pairs,
            out_specs=[VMEM] * ways,
            scratch_shapes=[pltpu.VMEM((shards, count, block), jnp.float32)],
            compiler_params=params(8192),
            cost_estimate=hint(PACK_HINT),
            name="pack_pieces",
        )(owner_map, *arrived)
    nearest = [arrived[distances(pairs).index(d)] for d in range(pairs)]
    blocks = jnp.stack(nearest, axis=0).reshape(pairs, count, 2, block).transpose(0, 2, 1, 3)
    shard_of = jnp.zeros((shards,), jnp.int32).at[owner_map].set(
        jnp.arange(shards, dtype=jnp.int32)
    )
    taken = jnp.take(
        blocks.reshape(shards, count, block), shard_of ^ lax.axis_index("group"), axis=0
    )
    ordered = taken.transpose(1, 0, 2).reshape(count, shards * block)
    per_device = H // ways
    pieces = []
    for d in distances(ways):
        to = lax.axis_index("tensor") ^ d
        near = (to * per_device // (H // KVH)) * HD
        parts = [(near, near_width), (kv_width + near, near_width), (to * slice_width, slice_width)]
        cuts = [lax.dynamic_slice_in_dim(ordered, start, width, 1) for start, width in parts]
        pieces.append(jnp.concatenate(cuts, axis=1))
    return pieces


def finish_kernel(rows, steps, own, chunk, near_width, ways, query_ref, *refs):
    pieces, parts = refs[:ways], refs[ways : 2 * ways]
    new_ref, attended_ref = refs[2 * ways :]
    chunks = own // chunk
    height = chunk * steps
    end = rows * chunks * height
    summed = pieces[0][...]
    for piece in pieces[1:]:
        summed = summed + piece[...]
    stored = summed.astype(jnp.bfloat16)
    new_ref[...] = stored[:, 2 * near_width :]
    near = stored[:, : 2 * near_width].astype(jnp.float32)
    key_step = lax.broadcasted_iota(jnp.int32, (steps, height), 0)
    query_step = lax.broadcasted_iota(jnp.int32, (steps, height), 1) % steps
    causal = key_step <= query_step
    stats = [part[end : end + SUBLANES] for part in parts]
    factors, near_sums = [], []
    for r in range(rows):
        peaks, totals = [], []
        for j in range(chunks):
            at = (r * chunks + j) * height
            query = query_ref[at : at + height]
            step_rows = slice(r * steps, (r + 1) * steps)
            keys = near[step_rows, j * HD : (j + 1) * HD].astype(jnp.bfloat16)
            values = near[step_rows, near_width + j * HD : near_width + (j + 1) * HD]
            scores = jnp.where(causal, dot(keys, query, NT) * SCORE_SCALE, NEGATIVE)
            peak = jnp.max(scores, axis=0, keepdims=True)
            weights = jnp.where(causal, jnp.exp(scores - peak), 0.0)
            peaks.append(peak)
            totals.append(jnp.sum(weights, axis=0, keepdims=True))
            near_sums.append(dot(weights.astype(jnp.bfloat16), values.astype(jnp.bfloat16), TN))
        lanes = chunks * height
        pad = [jnp.zeros((1, LANES - lanes), jnp.float32)] if lanes < LANES else []
        peaks = [s[2 * r : 2 * r + 1] for s in stats] + [jnp.concatenate(peaks + pad, axis=1)]
        totals = [s[2 * r + 1 : 2 * r + 2] for s in stats] + [jnp.concatenate(totals + pad, axis=1)]
        top = functools.reduce(jnp.maximum, peaks)
        scales = [jnp.exp(peak - top) for peak in peaks]
        total = sum(scale * one for scale, one in zip(scales, totals))
        if pad:
            total = jnp.where(total == 0.0, 1.0, total)
        factors += [scale / total for scale in scales]
    lines = -(-len(factors) // SUBLANES) * SUBLANES
    if lines > len(factors):
        factors.append(jnp.zeros((lines - len(factors), LANES), jnp.float32))
    columns = jnp.concatenate(factors, axis=0).T
    for j in range(chunks):
        merged = []
        for r in range(rows):
            at = (r * chunks + j) * height
            here = slice(j * height, (j + 1) * height)
            first = r * (ways + 1)
            out = near_sums[r * chunks + j] * columns[here, first + ways : first + ways + 1]
            for d, part in enumerate(parts):
                out = out + part[at : at + height] * columns[here, first + d : first + d + 1]
            merged.append(out)
        for h in range(chunk):
            both = [out[h * steps : (h + 1) * steps] for out in merged]
            lane = (j * chunk + h) * HD
            attended_ref[:, lane : lane + HD] = jnp.concatenate(both, axis=0).astype(jnp.bfloat16)


def finish(own_query, pieces, parts, rows, steps, own, near_width):
    ways = len(pieces)
    count, width = pieces[0].shape
    return pl.pallas_call(
        functools.partial(
            finish_kernel, rows, steps, own, min(own, H // KVH), near_width, ways
        ),
        out_shape=[
            jax.ShapeDtypeStruct((count, width - 2 * near_width), jnp.bfloat16),
            jax.ShapeDtypeStruct((count, own * HD), jnp.bfloat16),
        ],
        in_specs=[VMEM] * (1 + 2 * ways),
        out_specs=[VMEM] * 2,
        compiler_params=params(8192),
        name="finish",
    )(own_query, *pieces, *parts)


def on_device(
    hidden_x, base_weight, delta_codes, delta_scales, owner_map, kv_cache, queries, lengths
):
    group_count = lax.axis_size("group")
    tensor_count = lax.axis_size("tensor")
    rows, steps, local_width = hidden_x.shape
    tokens = rows * steps
    owner_block = delta_codes.shape[0]
    heads_own = H // tensor_count
    slice_width = base_weight.shape[0] // tensor_count
    near_width = max(1, heads_own // (H // KVH)) * HD
    pairs = group_count // 2

    def exchange(arrays, axis, stride):
        places = distances(len(arrays))[1:]
        return [arrays[0]] + [swap(x, axis, stride * d) for x, d in zip(arrays[1:], places)]

    token_rows = exchange([hidden_x.reshape(tokens, local_width)] * pairs, "group", 2)
    mate_codes = swap(delta_codes, "group", 1)
    mate_scales = swap(delta_scales, "group", 1)

    own_delta, base_blocks = own_weights(owner_map, delta_scales, delta_codes, base_weight)
    mate_delta = mate_weights(mate_codes, mate_scales)
    behind, mate_delta = lax.optimization_barrier((lengths, mate_delta))
    own_query, partials = cache_partials(
        behind,
        queries.reshape(tokens, H * HD),
        kv_cache.reshape(-1, 2 * KVH * HD),
        rows,
        steps,
        heads_own,
        tensor_count,
    )
    partials = exchange(partials, "tensor", 1)
    own_query, base_blocks = lax.optimization_barrier((own_query, base_blocks))
    projected = project(own_delta, mate_delta, base_blocks, token_rows)
    arrived = exchange(projected, "group", 2)
    pieces = pack_pieces(owner_map, arrived, owner_block, tensor_count, near_width, slice_width)
    pieces = exchange(pieces, "tensor", 1)
    new_out, attended = finish(own_query, pieces, partials, rows, steps, heads_own, near_width)
    return (new_out.reshape(rows, steps, -1), attended.reshape(rows, steps, -1))


def solution(mesh):
    in_specs = (
        P("group", None, "tensor"),
        P(None, "tensor"),
        P("group", "tensor"),
        P("group", "tensor"),
        P(),
        P("group", "tensor", None),
        P("group", None, None),
        P("group"),
    )
    out_specs = (P("group", None, "tensor"), P("group", None, "tensor"))
    return jax.shard_map(
        on_device, mesh=mesh, in_specs=in_specs, out_specs=out_specs, check_vma=False
    )
```

```python
import functools
import jax
import jax.numpy as jnp
from jax import lax
from jax.experimental import pallas as pl
from jax.experimental.pallas import tpu as pltpu
from jax.sharding import PartitionSpec as P

H = 64
KVH = 8
HD = 128
BLK = 128
LANES = 128
SUBLANES = 8


NEGATIVE = -1e30
SCORE_SCALE = HD ** (-0.5)
CACHE_HINT = 120_000_000
WEIGHTS_HINT = 6_000_000
PROJECT_HINT = 60_000_000
PACK_HINT = 60_000_000
CACHE_KIB = 24 << 10
WEIGHTS_KIB = 16 << 10
PROJECT_KIB = 16 << 10
NT = (((1,), (1,)), ((), ()))
TN = (((0,), (0,)), ((), ()))
VMEM = pl.BlockSpec(memory_space=pltpu.VMEM)
SMEM = pl.BlockSpec(memory_space=pltpu.SMEM)
HBM = pl.BlockSpec(memory_space=pltpu.HBM)


def split(x):
    high = x.astype(jnp.bfloat16).astype(jnp.float32)
    middle = (x - high).astype(jnp.bfloat16).astype(jnp.float32)
    return [high, middle, x - high - middle]


def stats_rows(dtype):
    return SUBLANES if dtype == jnp.float32 else 2 * SUBLANES


def put_stats(ref, index, stats):
    dtype = ref.dtype
    lines = [x for one in stats for x in ([one] if dtype == jnp.float32 else split(one))]
    lanes = lines[0].shape[1]
    count = stats_rows(dtype)
    lines.append(jnp.zeros((count - len(lines), lanes), jnp.float32))
    tile = jnp.concatenate(lines, axis=0)
    if lanes < LANES:
        tile = jnp.concatenate([tile, jnp.zeros((count, LANES - lanes), jnp.float32)], axis=1)
    ref[index, ref.shape[1] - count :] = tile.astype(dtype)


def get_stats(ref, index, rows):
    dtype = ref.dtype
    tile = ref[index, ref.shape[1] - stats_rows(dtype) :].astype(jnp.float32)
    lines = [tile[n : n + 1] for n in range(2 * rows * (1 if dtype == jnp.float32 else 3))]
    if dtype != jnp.float32:
        lines = [a + b + c for a, b, c in zip(lines[::3], lines[1::3], lines[2::3])]
    return [(lines[2 * r], lines[2 * r + 1]) for r in range(rows)]


def hint(size):
    return pl.CostEstimate(flops=0, bytes_accessed=size, transcendentals=0)


def dot(left, right, dims):
    return lax.dot_general(left, right, dims, preferred_element_type=jnp.float32)


def swap(x, axis, distance):
    size = lax.axis_size(axis)
    return lax.ppermute(x, axis, [(k, k ^ distance) for k in range(size)])


def distances(size):
    return [0] + list(range(size - 1, 0, -1))


def params(kibibytes):
    return pltpu.CompilerParams(vmem_limit_bytes=kibibytes << 10)


def head_rows(block, row, steps, heads):
    mine = block[row * steps : (row + 1) * steps]
    return jnp.concatenate([mine[:, h * HD : (h + 1) * HD] for h in range(heads)], axis=0)


def dequantize(codes_ref, scales_ref, out_ref):
    columns = scales_ref[...].astype(jnp.float32).T
    for n in range(columns.shape[1]):
        lanes = slice(n * BLK, (n + 1) * BLK)
        values = codes_ref[:, lanes].astype(jnp.float32) * columns[:, n : n + 1]
        out_ref[:, lanes] = values.astype(jnp.bfloat16)


def own_weights_kernel(
    owner_hbm, scales_hbm, codes_hbm, base_hbm, out_ref, base_ref, owner_ref, scales_ref, codes_ref,
    arrived,
):
    place = lax.axis_index("group")
    block = codes_ref.shape[0]
    owner_load = pltpu.make_async_copy(owner_hbm, owner_ref, arrived.at[0])
    loads = [
        pltpu.make_async_copy(scales_hbm, scales_ref, arrived.at[1]),
        pltpu.make_async_copy(codes_hbm, codes_ref, arrived.at[2]),
    ]
    for load in [owner_load] + loads:
        load.start()
    owner_load.wait()
    base_loads = []
    for k in range(2):
        here = pl.ds(pl.multiple_of(owner_ref[place ^ k] * block, block), block)
        base_loads.append(
            pltpu.make_async_copy(base_hbm.at[here], base_ref.at[k], arrived.at[3 + k])
        )
        base_loads[k].start()
    for load in loads:
        load.wait()
    dequantize(codes_ref, scales_ref, out_ref)
    for load in base_loads:
        load.wait()


def own_weights(owner_map, scales, codes, base):
    operands = [
        pltpu.with_memory_space_constraint(x, pltpu.HBM) for x in (owner_map, scales.T, codes, base)
    ]
    return pl.pallas_call(
        own_weights_kernel,
        out_shape=[
            jax.ShapeDtypeStruct(codes.shape, jnp.bfloat16),
            jax.ShapeDtypeStruct((2,) + codes.shape, jnp.bfloat16),
        ],
        in_specs=[HBM] * 4,
        out_specs=[VMEM] * 2,
        scratch_shapes=[
            pltpu.SMEM(owner_map.shape, owner_map.dtype),
            pltpu.VMEM(scales.shape[::-1], scales.dtype),
            pltpu.VMEM(codes.shape, codes.dtype),
            pltpu.SemaphoreType.DMA((5,)),
        ],
        compiler_params=params(WEIGHTS_KIB),
        cost_estimate=hint(WEIGHTS_HINT),
        name="own_weights",
    )(*operands)


def mate_weights(codes, scales):
    return pl.pallas_call(
        dequantize,
        out_shape=jax.ShapeDtypeStruct(codes.shape, jnp.bfloat16),
        in_specs=[VMEM, VMEM],
        out_specs=VMEM,
        compiler_params=params(WEIGHTS_KIB),
        cost_estimate=hint(1000),
        name="mate_weights",
    )(codes, scales.T)


def cache_kernel(
    rows, steps, own, chunk, lengths_ref, query_ref, cache_ref, own_query_ref, kept_ref, sent_ref
):
    place = lax.axis_index("tensor")
    cache_len = cache_ref.shape[0] // rows
    chunks = own // chunk
    height = chunk * steps
    width = chunks * HD
    position = lax.broadcasted_iota(jnp.int32, (cache_len, chunks * height), 0)

    def kv_lane(d):
        return pl.multiple_of(((place ^ d) * own // (H // KVH)) * HD, HD)

    def score(r, d):
        head = (place ^ d) * own
        queries = query_ref[:, pl.ds(pl.multiple_of(head * HD, HD), own * HD)]
        query = head_rows(queries.astype(jnp.float32), r, steps, own)
        if d == 0:
            at = r * chunks * height
            own_query_ref[at : at + chunks * height] = query.astype(jnp.bfloat16)
        spread = []
        for j in range(chunks):
            line = [jnp.zeros((height, HD), jnp.float32)] * chunks
            line[j] = query[j * height : (j + 1) * height]
            spread.append(jnp.concatenate(line, axis=1))
        spread = jnp.concatenate(spread, axis=0).astype(jnp.bfloat16)
        keys = cache_ref[pl.ds(r * cache_len, cache_len), pl.ds(kv_lane(d), width)]
        return dot(keys, spread, NT)

    units = [(r, d) for d in range(2 * kept_ref.shape[0]) for r in range(rows)]
    ahead = []
    for n in range(len(units) + 1):
        if n < len(units):
            ahead.append(score(*units[n]))
        if n == 0:
            continue
        r, d = units[n - 1]
        at = r * chunks * height
        usable = position < lengths_ref[r] - place * cache_len
        scores = jnp.where(usable, ahead.pop(0) * SCORE_SCALE, 2.0 * NEGATIVE)
        peak = jnp.maximum(jnp.max(scores, axis=0, keepdims=True), NEGATIVE)
        weights = jnp.exp(scores - peak)
        total = jnp.sum(weights, axis=0, keepdims=True)
        lane = pl.ds(kv_lane(d) + KVH * HD, width)
        values = cache_ref[pl.ds(r * cache_len, cache_len), lane]
        sums = dot(weights.astype(jnp.bfloat16), values, TN)
        ref, index = (sent_ref if d % 2 else kept_ref), d // 2
        for j in range(chunks):
            here = slice(j * height, (j + 1) * height)
            mine = sums[here, j * HD : (j + 1) * HD].astype(ref.dtype)
            ref[index, at + j * height : at + (j + 1) * height] = mine
        stats = (stats if r > 0 else []) + [peak, total]
        if r == rows - 1:
            put_stats(ref, index, stats)


def part_shape(count, height, dtype):
    return jax.ShapeDtypeStruct((count, height + stats_rows(dtype), LANES), dtype)


def cache_partials(lengths, queries, cache, rows, steps, own, ways):
    height = rows * own * steps
    return pl.pallas_call(
        functools.partial(cache_kernel, rows, steps, own, min(own, H // KVH)),
        out_shape=[
            jax.ShapeDtypeStruct((height, HD), jnp.bfloat16),
            part_shape(ways // 2, height, jnp.float32),
            part_shape(ways // 2, height, jnp.bfloat16),
        ],
        in_specs=[SMEM, VMEM, VMEM],
        out_specs=[VMEM] * 3,
        compiler_params=params(CACHE_KIB),
        cost_estimate=hint(CACHE_HINT),
        name="cache_partials",
    )(lengths, queries, cache)


def merge_kernel(rows, span, kept_ref, came_ref, next_ref, sent_ref):
    for n in range(kept_ref.shape[0]):
        ref, index = (sent_ref if n % 2 else next_ref), n // 2
        stats, factors = [], []
        for one, two in zip(get_stats(kept_ref, n, rows), get_stats(came_ref, n, rows)):
            peak = jnp.maximum(one[0], two[0])
            scales = [jnp.exp(one[0] - peak), jnp.exp(two[0] - peak)]
            stats += [peak, one[1] * scales[0] + two[1] * scales[1]]
            factors += scales
        factors.append(jnp.zeros((SUBLANES - len(factors), LANES), jnp.float32))
        columns = jnp.concatenate(factors, axis=0).T[:span]
        for r in range(rows):
            here = slice(r * span, (r + 1) * span)
            left = kept_ref[n, here] * columns[:, 2 * r : 2 * r + 1]
            right = came_ref[n, here].astype(jnp.float32) * columns[:, 2 * r + 1 : 2 * r + 2]
            ref[index, here] = (left + right).astype(ref.dtype)
        put_stats(ref, index, stats)


def merge(kept, came, rows):
    count = kept.shape[0]
    height = kept.shape[1] - stats_rows(kept.dtype)
    return pl.pallas_call(
        functools.partial(merge_kernel, rows, height // rows),
        out_shape=[
            part_shape(count // 2, height, jnp.float32),
            part_shape(count // 2, height, jnp.bfloat16),
        ],
        in_specs=[VMEM] * 2,
        out_specs=[VMEM] * 2,
        compiler_params=params(8192),
        cost_estimate=hint(4 * kept.size),
        name="merge_partials",
    )(kept, came)


def project_kernel(pairs, own_ref, mate_ref, base_ref, *refs):
    tokens, outs = refs[:pairs], refs[pairs:]
    block = own_ref.shape[0]
    stacked = jnp.concatenate([ref[...] for ref in tokens], axis=0)
    count = tokens[0].shape[0]
    for k, delta_ref in enumerate((own_ref, mate_ref)):
        whole = (dot(base_ref[k], stacked, NT) + dot(delta_ref[...], stacked, NT)).T
        for n in range(pairs):
            outs[n][:, k * block : (k + 1) * block] = whole[n * count : (n + 1) * count]


def project(own, mate, base, tokens):
    pairs = len(tokens)
    block = own.shape[0]
    count, width = tokens[0].shape
    return pl.pallas_call(
        functools.partial(project_kernel, pairs),
        out_shape=[jax.ShapeDtypeStruct((count, 2 * block), jnp.float32)] * pairs,
        in_specs=[VMEM] * (3 + pairs),
        out_specs=[VMEM] * pairs,
        compiler_params=params(PROJECT_KIB),
        cost_estimate=hint(PROJECT_HINT),
        name="project",
    )(own, mate, base, *tokens)


def pack_kernel(pairs, ways, near, wide, owner_ref, *refs):
    arrived, outs, ordered = refs[:pairs], refs[pairs : pairs + ways], refs[-1]
    place = lax.axis_index("group")
    to_place = lax.axis_index("tensor")
    shards, _, block = ordered.shape
    for piece, d in zip(arrived, distances(pairs)):
        for k in range(2):
            ordered[owner_ref[place ^ (2 * d + k)]] = piece[:, k * block : (k + 1) * block]
    for out, d in zip(outs, distances(ways)):
        to = to_place ^ d
        for n in range(near):
            out[:, n * block : (n + 1) * block] = ordered[to * near + n]
            at = (near + n) * block
            out[:, at : at + block] = ordered[shards // 2 + to * near + n]
        for n in range(wide):
            at = (2 * near + n) * block
            out[:, at : at + block] = ordered[to * wide + n]


def pack_pieces(owner_map, arrived, block, ways, near_width, slice_width):
    pairs = len(arrived)
    count = arrived[0].shape[0]
    shards = 2 * pairs
    kv_width = KVH * HD
    if block % LANES == 0 and near_width % block == 0 and slice_width % block == 0:
        piece = jax.ShapeDtypeStruct((count, 2 * near_width + slice_width), jnp.float32)
        kernel = functools.partial(
            pack_kernel, pairs, ways, near_width // block, slice_width // block
        )
        return pl.pallas_call(
            kernel,
            out_shape=[piece] * ways,
            in_specs=[SMEM] + [VMEM] * pairs,
            out_specs=[VMEM] * ways,
            scratch_shapes=[pltpu.VMEM((shards, count, block), jnp.float32)],
            compiler_params=params(8192),
            cost_estimate=hint(PACK_HINT),
            name="pack_pieces",
        )(owner_map, *arrived)
    nearest = [arrived[distances(pairs).index(d)] for d in range(pairs)]
    blocks = jnp.stack(nearest, axis=0).reshape(pairs, count, 2, block).transpose(0, 2, 1, 3)
    shard_of = jnp.zeros((shards,), jnp.int32).at[owner_map].set(
        jnp.arange(shards, dtype=jnp.int32)
    )
    taken = jnp.take(
        blocks.reshape(shards, count, block), shard_of ^ lax.axis_index("group"), axis=0
    )
    ordered = taken.transpose(1, 0, 2).reshape(count, shards * block)
    per_device = H // ways
    pieces = []
    for d in distances(ways):
        to = lax.axis_index("tensor") ^ d
        near = (to * per_device // (H // KVH)) * HD
        parts = [(near, near_width), (kv_width + near, near_width), (to * slice_width, slice_width)]
        cuts = [lax.dynamic_slice_in_dim(ordered, start, width, 1) for start, width in parts]
        pieces.append(jnp.concatenate(cuts, axis=1))
    return pieces


def finish_kernel(rows, steps, own, chunk, near_width, ways, query_ref, *refs):
    pieces, parts = refs[:ways], refs[ways : ways + 2]
    new_ref, attended_ref = refs[ways + 2 :]
    chunks = own // chunk
    height = chunk * steps
    summed = pieces[0][...]
    for piece in pieces[1:]:
        summed = summed + piece[...]
    stored = summed.astype(jnp.bfloat16)
    new_ref[...] = stored[:, 2 * near_width :]
    near = stored[:, : 2 * near_width].astype(jnp.float32)
    key_step = lax.broadcasted_iota(jnp.int32, (steps, height), 0)
    query_step = lax.broadcasted_iota(jnp.int32, (steps, height), 1) % steps
    causal = key_step <= query_step
    stats = [get_stats(part, 0, rows) for part in parts]
    factors, near_sums = [], []
    for r in range(rows):
        peaks, totals = [], []
        for j in range(chunks):
            at = (r * chunks + j) * height
            query = query_ref[at : at + height]
            step_rows = slice(r * steps, (r + 1) * steps)
            keys = near[step_rows, j * HD : (j + 1) * HD].astype(jnp.bfloat16)
            values = near[step_rows, near_width + j * HD : near_width + (j + 1) * HD]
            scores = jnp.where(causal, dot(keys, query, NT) * SCORE_SCALE, NEGATIVE)
            peak = jnp.max(scores, axis=0, keepdims=True)
            weights = jnp.where(causal, jnp.exp(scores - peak), 0.0)
            peaks.append(peak)
            totals.append(jnp.sum(weights, axis=0, keepdims=True))
            near_sums.append(dot(weights.astype(jnp.bfloat16), values.astype(jnp.bfloat16), TN))
        lanes = chunks * height
        pad = [jnp.zeros((1, LANES - lanes), jnp.float32)] if lanes < LANES else []
        peaks = [one[r][0] for one in stats] + [jnp.concatenate(peaks + pad, axis=1)]
        totals = [one[r][1] for one in stats] + [jnp.concatenate(totals + pad, axis=1)]
        top = functools.reduce(jnp.maximum, peaks)
        scales = [jnp.exp(peak - top) for peak in peaks]
        total = sum(scale * one for scale, one in zip(scales, totals))
        if pad:
            total = jnp.where(total == 0.0, 1.0, total)
        factors += [scale / total for scale in scales]
    lines = -(-len(factors) // SUBLANES) * SUBLANES
    if lines > len(factors):
        factors.append(jnp.zeros((lines - len(factors), LANES), jnp.float32))
    columns = jnp.concatenate(factors, axis=0).T
    for j in range(chunks):
        merged = []
        for r in range(rows):
            at = (r * chunks + j) * height
            here = slice(j * height, (j + 1) * height)
            first = r * (len(parts) + 1)
            last = first + len(parts)
            out = near_sums[r * chunks + j] * columns[here, last : last + 1]
            for n, part in enumerate(parts):
                mine = part[0, at : at + height].astype(jnp.float32)
                out = out + mine * columns[here, first + n : first + n + 1]
            merged.append(out)
        for h in range(chunk):
            both = [out[h * steps : (h + 1) * steps] for out in merged]
            lane = (j * chunk + h) * HD
            attended_ref[:, lane : lane + HD] = jnp.concatenate(both, axis=0).astype(jnp.bfloat16)


def finish(own_query, pieces, parts, rows, steps, own, near_width):
    ways = len(pieces)
    count, width = pieces[0].shape
    return pl.pallas_call(
        functools.partial(
            finish_kernel, rows, steps, own, min(own, H // KVH), near_width, ways
        ),
        out_shape=[
            jax.ShapeDtypeStruct((count, width - 2 * near_width), jnp.bfloat16),
            jax.ShapeDtypeStruct((count, own * HD), jnp.bfloat16),
        ],
        in_specs=[VMEM] * (3 + ways),
        out_specs=[VMEM] * 2,
        compiler_params=params(8192),
        name="finish",
    )(own_query, *pieces, *parts)


def on_device(
    hidden_x, base_weight, delta_codes, delta_scales, owner_map, kv_cache, queries, lengths
):
    group_count = lax.axis_size("group")
    tensor_count = lax.axis_size("tensor")
    rows, steps, local_width = hidden_x.shape
    tokens = rows * steps
    owner_block = delta_codes.shape[0]
    heads_own = H // tensor_count
    slice_width = base_weight.shape[0] // tensor_count
    near_width = max(1, heads_own // (H // KVH)) * HD
    pairs = group_count // 2

    def exchange(arrays, axis, stride):
        places = distances(len(arrays))[1:]
        return [arrays[0]] + [swap(x, axis, stride * d) for x, d in zip(arrays[1:], places)]

    def near_first(arrays):
        return arrays[:1] + arrays[:0:-1]

    token_rows = exchange([hidden_x.reshape(tokens, local_width)] * pairs, "group", 2)
    mate_codes = swap(delta_codes, "group", 1)
    mate_scales = swap(delta_scales, "group", 1)

    own_delta, base_blocks = own_weights(owner_map, delta_scales, delta_codes, base_weight)
    mate_delta = mate_weights(mate_codes, mate_scales)
    behind, mate_delta = lax.optimization_barrier((lengths, mate_delta))
    own_query, kept, sent = cache_partials(
        behind,
        queries.reshape(tokens, H * HD),
        kv_cache.reshape(-1, 2 * KVH * HD),
        rows,
        steps,
        heads_own,
        tensor_count,
    )
    own_query, base_blocks = lax.optimization_barrier((own_query, base_blocks))
    projected = project(own_delta, mate_delta, base_blocks, near_first(token_rows))
    projected, sent = lax.optimization_barrier((projected, sent))
    step = 1
    while step < tensor_count:
        came = swap(sent, "tensor", step)
        step *= 2
        if step < tensor_count:
            kept, sent = merge(kept, came, rows)
    arrived = exchange(near_first(projected), "group", 2)
    pieces = pack_pieces(owner_map, arrived, owner_block, tensor_count, near_width, slice_width)
    pieces = exchange(pieces, "tensor", 1)
    new_out, attended = finish(
        own_query, pieces, [kept, came], rows, steps, heads_own, near_width
    )
    return (new_out.reshape(rows, steps, -1), attended.reshape(rows, steps, -1))


def solution(mesh):
    in_specs = (
        P("group", None, "tensor"),
        P(None, "tensor"),
        P("group", "tensor"),
        P("group", "tensor"),
        P(),
        P("group", "tensor", None),
        P("group", None, None),
        P("group"),
    )
    out_specs = (P("group", None, "tensor"), P("group", None, "tensor"))
    return jax.shard_map(
        on_device, mesh=mesh, in_specs=in_specs, out_specs=out_specs, check_vma=False
    )
```

```python
import functools
import jax
import jax.numpy as jnp
from jax import lax
from jax.experimental import pallas as pl
from jax.experimental.pallas import tpu as pltpu
from jax.sharding import PartitionSpec as P

H = 64
KVH = 8
HD = 128
BLK = 128
LANES = 128
SUBLANES = 8


NEGATIVE = -1e30
SCORE_SCALE = HD ** (-0.5)
CACHE_HINT = 120_000_000
WEIGHTS_HINT = 6_000_000
PROJECT_HINT = 60_000_000
PACK_HINT = 60_000_000
CACHE_KIB = 24 << 10
WEIGHTS_KIB = 16 << 10
PROJECT_KIB = 16 << 10
NT = (((1,), (1,)), ((), ()))
TN = (((0,), (0,)), ((), ()))
VMEM = pl.BlockSpec(memory_space=pltpu.VMEM)
SMEM = pl.BlockSpec(memory_space=pltpu.SMEM)
HBM = pl.BlockSpec(memory_space=pltpu.HBM)


def split(x):
    high = x.astype(jnp.bfloat16).astype(jnp.float32)
    middle = (x - high).astype(jnp.bfloat16).astype(jnp.float32)
    return [high, middle, x - high - middle]


def stats_rows(dtype):
    return SUBLANES if dtype == jnp.float32 else 2 * SUBLANES


def put_stats(ref, index, stats):
    dtype = ref.dtype
    lines = [x for one in stats for x in ([one] if dtype == jnp.float32 else split(one))]
    lanes = lines[0].shape[1]
    count = stats_rows(dtype)
    lines.append(jnp.zeros((count - len(lines), lanes), jnp.float32))
    tile = jnp.concatenate(lines, axis=0)
    if lanes < LANES:
        tile = jnp.concatenate([tile, jnp.zeros((count, LANES - lanes), jnp.float32)], axis=1)
    ref[index, ref.shape[1] - count :] = tile.astype(dtype)


def get_stats(ref, index, rows):
    dtype = ref.dtype
    tile = ref[index, ref.shape[1] - stats_rows(dtype) :].astype(jnp.float32)
    lines = [tile[n : n + 1] for n in range(2 * rows * (1 if dtype == jnp.float32 else 3))]
    if dtype != jnp.float32:
        lines = [a + b + c for a, b, c in zip(lines[::3], lines[1::3], lines[2::3])]
    return [(lines[2 * r], lines[2 * r + 1]) for r in range(rows)]


def hint(size):
    return pl.CostEstimate(flops=0, bytes_accessed=size, transcendentals=0)


def dot(left, right, dims):
    return lax.dot_general(left, right, dims, preferred_element_type=jnp.float32)


def swap(x, axis, distance):
    size = lax.axis_size(axis)
    return lax.ppermute(x, axis, [(k, k ^ distance) for k in range(size)])


def distances(size):
    return [0] + list(range(size - 1, 0, -1))


def params(kibibytes):
    return pltpu.CompilerParams(vmem_limit_bytes=kibibytes << 10)


def head_rows(block, row, steps, heads):
    mine = block[row * steps : (row + 1) * steps]
    return jnp.concatenate([mine[:, h * HD : (h + 1) * HD] for h in range(heads)], axis=0)


def dequantize(codes_ref, scales_ref, out_ref):
    columns = scales_ref[...].astype(jnp.float32).T
    for n in range(columns.shape[1]):
        lanes = slice(n * BLK, (n + 1) * BLK)
        values = codes_ref[:, lanes].astype(jnp.float32) * columns[:, n : n + 1]
        out_ref[:, lanes] = values.astype(jnp.bfloat16)


def load_kernel(
    owner_hbm, scales_hbm, codes_hbm, query_hbm, cache_hbm, base_hbm,
    out_ref, base_ref, query_ref, cache_ref, owner_ref, scales_ref, codes_ref, arrived,
):
    place = lax.axis_index("group")
    block = codes_ref.shape[0]
    owner_load = pltpu.make_async_copy(owner_hbm, owner_ref, arrived.at[0])
    loads = [
        pltpu.make_async_copy(scales_hbm, scales_ref, arrived.at[1]),
        pltpu.make_async_copy(codes_hbm, codes_ref, arrived.at[2]),
    ]
    later = [
        pltpu.make_async_copy(query_hbm, query_ref, arrived.at[3]),
        pltpu.make_async_copy(cache_hbm, cache_ref, arrived.at[4]),
    ]
    for load in [owner_load] + loads + later:
        load.start()
    owner_load.wait()
    for k in range(2):
        here = pl.ds(pl.multiple_of(owner_ref[place ^ k] * block, block), block)
        load = pltpu.make_async_copy(base_hbm.at[here], base_ref.at[k], arrived.at[5 + k])
        load.start()
        later.append(load)
    for load in loads:
        load.wait()
    dequantize(codes_ref, scales_ref, out_ref)
    for load in later:
        load.wait()


def load_operands(owner_map, scales, codes, queries, cache, base):
    operands = [
        pltpu.with_memory_space_constraint(x, pltpu.HBM)
        for x in (owner_map, scales.T, codes, queries, cache, base)
    ]
    return pl.pallas_call(
        load_kernel,
        out_shape=[
            jax.ShapeDtypeStruct(codes.shape, jnp.bfloat16),
            jax.ShapeDtypeStruct((2,) + codes.shape, jnp.bfloat16),
            jax.ShapeDtypeStruct(queries.shape, jnp.bfloat16),
            jax.ShapeDtypeStruct(cache.shape, jnp.bfloat16),
        ],
        in_specs=[HBM] * 6,
        out_specs=[VMEM] * 4,
        scratch_shapes=[
            pltpu.SMEM(owner_map.shape, owner_map.dtype),
            pltpu.VMEM(scales.shape[::-1], scales.dtype),
            pltpu.VMEM(codes.shape, codes.dtype),
            pltpu.SemaphoreType.DMA((7,)),
        ],
        compiler_params=params(WEIGHTS_KIB),
        cost_estimate=hint(WEIGHTS_HINT),
        name="load_operands",
    )(*operands)


def mate_weights(codes, scales):
    return pl.pallas_call(
        dequantize,
        out_shape=jax.ShapeDtypeStruct(codes.shape, jnp.bfloat16),
        in_specs=[VMEM, VMEM],
        out_specs=VMEM,
        compiler_params=params(WEIGHTS_KIB),
        cost_estimate=hint(1000),
        name="mate_weights",
    )(codes, scales.T)


def cache_kernel(
    rows, steps, own, chunk, lengths_ref, query_ref, cache_ref, own_query_ref, kept_ref, sent_ref
):
    place = lax.axis_index("tensor")
    cache_len = cache_ref.shape[0] // rows
    chunks = own // chunk
    height = chunk * steps
    width = chunks * HD
    position = lax.broadcasted_iota(jnp.int32, (cache_len, chunks * height), 0)

    def kv_lane(d):
        return pl.multiple_of(((place ^ d) * own // (H // KVH)) * HD, HD)

    def score(r, d):
        head = (place ^ d) * own
        queries = query_ref[:, pl.ds(pl.multiple_of(head * HD, HD), own * HD)]
        query = head_rows(queries.astype(jnp.float32), r, steps, own)
        if d == 0:
            at = r * chunks * height
            own_query_ref[at : at + chunks * height] = query.astype(jnp.bfloat16)
        spread = []
        for j in range(chunks):
            line = [jnp.zeros((height, HD), jnp.float32)] * chunks
            line[j] = query[j * height : (j + 1) * height]
            spread.append(jnp.concatenate(line, axis=1))
        spread = jnp.concatenate(spread, axis=0).astype(jnp.bfloat16)
        keys = cache_ref[pl.ds(r * cache_len, cache_len), pl.ds(kv_lane(d), width)]
        return dot(keys, spread, NT)

    units = [(r, d) for d in range(2 * kept_ref.shape[0]) for r in range(rows)]
    ahead = []
    for n in range(len(units) + 1):
        if n < len(units):
            ahead.append(score(*units[n]))
        if n == 0:
            continue
        r, d = units[n - 1]
        at = r * chunks * height
        usable = position < lengths_ref[r] - place * cache_len
        scores = jnp.where(usable, ahead.pop(0) * SCORE_SCALE, 2.0 * NEGATIVE)
        peak = jnp.maximum(jnp.max(scores, axis=0, keepdims=True), NEGATIVE)
        weights = jnp.exp(scores - peak)
        total = jnp.sum(weights, axis=0, keepdims=True)
        lane = pl.ds(kv_lane(d) + KVH * HD, width)
        values = cache_ref[pl.ds(r * cache_len, cache_len), lane]
        sums = dot(weights.astype(jnp.bfloat16), values, TN)
        ref, index = (sent_ref if d % 2 else kept_ref), d // 2
        for j in range(chunks):
            here = slice(j * height, (j + 1) * height)
            mine = sums[here, j * HD : (j + 1) * HD].astype(ref.dtype)
            ref[index, at + j * height : at + (j + 1) * height] = mine
        stats = (stats if r > 0 else []) + [peak, total]
        if r == rows - 1:
            put_stats(ref, index, stats)


def part_shape(count, height, dtype):
    return jax.ShapeDtypeStruct((count, height + stats_rows(dtype), LANES), dtype)


def cache_partials(lengths, queries, cache, rows, steps, own, ways):
    height = rows * own * steps
    return pl.pallas_call(
        functools.partial(cache_kernel, rows, steps, own, min(own, H // KVH)),
        out_shape=[
            jax.ShapeDtypeStruct((height, HD), jnp.bfloat16),
            part_shape(ways // 2, height, jnp.float32),
            part_shape(ways // 2, height, jnp.bfloat16),
        ],
        in_specs=[SMEM, VMEM, VMEM],
        out_specs=[VMEM] * 3,
        compiler_params=params(CACHE_KIB),
        cost_estimate=hint(CACHE_HINT),
        name="cache_partials",
    )(lengths, queries, cache)


def merge_kernel(rows, span, kept_ref, came_ref, next_ref, sent_ref):
    for n in range(kept_ref.shape[0]):
        ref, index = (sent_ref if n % 2 else next_ref), n // 2
        stats, factors = [], []
        for one, two in zip(get_stats(kept_ref, n, rows), get_stats(came_ref, n, rows)):
            peak = jnp.maximum(one[0], two[0])
            scales = [jnp.exp(one[0] - peak), jnp.exp(two[0] - peak)]
            stats += [peak, one[1] * scales[0] + two[1] * scales[1]]
            factors += scales
        factors.append(jnp.zeros((SUBLANES - len(factors), LANES), jnp.float32))
        columns = jnp.concatenate(factors, axis=0).T[:span]
        for r in range(rows):
            here = slice(r * span, (r + 1) * span)
            left = kept_ref[n, here] * columns[:, 2 * r : 2 * r + 1]
            right = came_ref[n, here].astype(jnp.float32) * columns[:, 2 * r + 1 : 2 * r + 2]
            ref[index, here] = (left + right).astype(ref.dtype)
        put_stats(ref, index, stats)


def merge(kept, came, rows):
    count = kept.shape[0]
    height = kept.shape[1] - stats_rows(kept.dtype)
    return pl.pallas_call(
        functools.partial(merge_kernel, rows, height // rows),
        out_shape=[
            part_shape(count // 2, height, jnp.float32),
            part_shape(count // 2, height, jnp.bfloat16),
        ],
        in_specs=[VMEM] * 2,
        out_specs=[VMEM] * 2,
        compiler_params=params(8192),
        cost_estimate=hint(4 * kept.size),
        name="merge_partials",
    )(kept, came)


def project_kernel(pairs, own_ref, mate_ref, base_ref, *refs):
    tokens, outs = refs[:pairs], refs[pairs:]
    block = own_ref.shape[0]
    stacked = jnp.concatenate([ref[...] for ref in tokens], axis=0)
    count = tokens[0].shape[0]
    for k, delta_ref in enumerate((own_ref, mate_ref)):
        whole = (dot(base_ref[k], stacked, NT) + dot(delta_ref[...], stacked, NT)).T
        for n in range(pairs):
            outs[n][:, k * block : (k + 1) * block] = whole[n * count : (n + 1) * count]


def project(own, mate, base, tokens):
    pairs = len(tokens)
    block = own.shape[0]
    count, width = tokens[0].shape
    return pl.pallas_call(
        functools.partial(project_kernel, pairs),
        out_shape=[jax.ShapeDtypeStruct((count, 2 * block), jnp.float32)] * pairs,
        in_specs=[VMEM] * (3 + pairs),
        out_specs=[VMEM] * pairs,
        compiler_params=params(PROJECT_KIB),
        cost_estimate=hint(PROJECT_HINT),
        name="project",
    )(own, mate, base, *tokens)


def pack_kernel(pairs, ways, near, wide, owner_ref, *refs):
    arrived, outs, ordered = refs[:pairs], refs[pairs : pairs + ways], refs[-1]
    place = lax.axis_index("group")
    to_place = lax.axis_index("tensor")
    shards, _, block = ordered.shape
    for piece, d in zip(arrived, distances(pairs)):
        for k in range(2):
            ordered[owner_ref[place ^ (2 * d + k)]] = piece[:, k * block : (k + 1) * block]
    for out, d in zip(outs, distances(ways)):
        to = to_place ^ d
        for n in range(near):
            out[:, n * block : (n + 1) * block] = ordered[to * near + n]
            at = (near + n) * block
            out[:, at : at + block] = ordered[shards // 2 + to * near + n]
        for n in range(wide):
            at = (2 * near + n) * block
            out[:, at : at + block] = ordered[to * wide + n]


def pack_pieces(owner_map, arrived, block, ways, near_width, slice_width):
    pairs = len(arrived)
    count = arrived[0].shape[0]
    shards = 2 * pairs
    kv_width = KVH * HD
    if block % LANES == 0 and near_width % block == 0 and slice_width % block == 0:
        piece = jax.ShapeDtypeStruct((count, 2 * near_width + slice_width), jnp.float32)
        kernel = functools.partial(
            pack_kernel, pairs, ways, near_width // block, slice_width // block
        )
        return pl.pallas_call(
            kernel,
            out_shape=[piece] * ways,
            in_specs=[SMEM] + [VMEM] * pairs,
            out_specs=[VMEM] * ways,
            scratch_shapes=[pltpu.VMEM((shards, count, block), jnp.float32)],
            compiler_params=params(8192),
            cost_estimate=hint(PACK_HINT),
            name="pack_pieces",
        )(owner_map, *arrived)
    nearest = [arrived[distances(pairs).index(d)] for d in range(pairs)]
    blocks = jnp.stack(nearest, axis=0).reshape(pairs, count, 2, block).transpose(0, 2, 1, 3)
    shard_of = jnp.zeros((shards,), jnp.int32).at[owner_map].set(
        jnp.arange(shards, dtype=jnp.int32)
    )
    taken = jnp.take(
        blocks.reshape(shards, count, block), shard_of ^ lax.axis_index("group"), axis=0
    )
    ordered = taken.transpose(1, 0, 2).reshape(count, shards * block)
    per_device = H // ways
    pieces = []
    for d in distances(ways):
        to = lax.axis_index("tensor") ^ d
        near = (to * per_device // (H // KVH)) * HD
        parts = [(near, near_width), (kv_width + near, near_width), (to * slice_width, slice_width)]
        cuts = [lax.dynamic_slice_in_dim(ordered, start, width, 1) for start, width in parts]
        pieces.append(jnp.concatenate(cuts, axis=1))
    return pieces


def finish_kernel(rows, steps, own, chunk, near_width, ways, query_ref, *refs):
    pieces, parts = refs[:ways], refs[ways : ways + 2]
    new_ref, attended_ref = refs[ways + 2 :]
    chunks = own // chunk
    height = chunk * steps
    summed = pieces[0][...]
    for piece in pieces[1:]:
        summed = summed + piece[...]
    stored = summed.astype(jnp.bfloat16)
    new_ref[...] = stored[:, 2 * near_width :]
    near = stored[:, : 2 * near_width].astype(jnp.float32)
    key_step = lax.broadcasted_iota(jnp.int32, (steps, height), 0)
    query_step = lax.broadcasted_iota(jnp.int32, (steps, height), 1) % steps
    causal = key_step <= query_step
    stats = [get_stats(part, 0, rows) for part in parts]
    factors, near_sums = [], []
    for r in range(rows):
        peaks, totals = [], []
        for j in range(chunks):
            at = (r * chunks + j) * height
            query = query_ref[at : at + height]
            step_rows = slice(r * steps, (r + 1) * steps)
            keys = near[step_rows, j * HD : (j + 1) * HD].astype(jnp.bfloat16)
            values = near[step_rows, near_width + j * HD : near_width + (j + 1) * HD]
            scores = jnp.where(causal, dot(keys, query, NT) * SCORE_SCALE, NEGATIVE)
            peak = jnp.max(scores, axis=0, keepdims=True)
            weights = jnp.where(causal, jnp.exp(scores - peak), 0.0)
            peaks.append(peak)
            totals.append(jnp.sum(weights, axis=0, keepdims=True))
            near_sums.append(dot(weights.astype(jnp.bfloat16), values.astype(jnp.bfloat16), TN))
        lanes = chunks * height
        pad = [jnp.zeros((1, LANES - lanes), jnp.float32)] if lanes < LANES else []
        peaks = [one[r][0] for one in stats] + [jnp.concatenate(peaks + pad, axis=1)]
        totals = [one[r][1] for one in stats] + [jnp.concatenate(totals + pad, axis=1)]
        top = functools.reduce(jnp.maximum, peaks)
        scales = [jnp.exp(peak - top) for peak in peaks]
        total = sum(scale * one for scale, one in zip(scales, totals))
        if pad:
            total = jnp.where(total == 0.0, 1.0, total)
        factors += [scale / total for scale in scales]
    lines = -(-len(factors) // SUBLANES) * SUBLANES
    if lines > len(factors):
        factors.append(jnp.zeros((lines - len(factors), LANES), jnp.float32))
    columns = jnp.concatenate(factors, axis=0).T
    for j in range(chunks):
        merged = []
        for r in range(rows):
            at = (r * chunks + j) * height
            here = slice(j * height, (j + 1) * height)
            first = r * (len(parts) + 1)
            last = first + len(parts)
            out = near_sums[r * chunks + j] * columns[here, last : last + 1]
            for n, part in enumerate(parts):
                mine = part[0, at : at + height].astype(jnp.float32)
                out = out + mine * columns[here, first + n : first + n + 1]
            merged.append(out)
        for h in range(chunk):
            both = [out[h * steps : (h + 1) * steps] for out in merged]
            lane = (j * chunk + h) * HD
            attended_ref[:, lane : lane + HD] = jnp.concatenate(both, axis=0).astype(jnp.bfloat16)


def finish(own_query, pieces, parts, rows, steps, own, near_width):
    ways = len(pieces)
    count, width = pieces[0].shape
    return pl.pallas_call(
        functools.partial(
            finish_kernel, rows, steps, own, min(own, H // KVH), near_width, ways
        ),
        out_shape=[
            jax.ShapeDtypeStruct((count, width - 2 * near_width), jnp.bfloat16),
            jax.ShapeDtypeStruct((count, own * HD), jnp.bfloat16),
        ],
        in_specs=[VMEM] * (3 + ways),
        out_specs=[VMEM] * 2,
        compiler_params=params(8192),
        name="finish",
    )(own_query, *pieces, *parts)


def on_device(
    hidden_x, base_weight, delta_codes, delta_scales, owner_map, kv_cache, queries, lengths
):
    group_count = lax.axis_size("group")
    tensor_count = lax.axis_size("tensor")
    rows, steps, local_width = hidden_x.shape
    tokens = rows * steps
    owner_block = delta_codes.shape[0]
    heads_own = H // tensor_count
    slice_width = base_weight.shape[0] // tensor_count
    near_width = max(1, heads_own // (H // KVH)) * HD
    pairs = group_count // 2

    def exchange(arrays, axis, stride):
        places = distances(len(arrays))[1:]
        return [arrays[0]] + [swap(x, axis, stride * d) for x, d in zip(arrays[1:], places)]

    def near_first(arrays):
        return arrays[:1] + arrays[:0:-1]

    token_rows = exchange([hidden_x.reshape(tokens, local_width)] * pairs, "group", 2)
    mate_codes = swap(delta_codes, "group", 1)
    mate_scales = swap(delta_scales, "group", 1)

    own_delta, base_blocks, all_queries, cache = load_operands(
        owner_map,
        delta_scales,
        delta_codes,
        queries.reshape(tokens, H * HD),
        kv_cache.reshape(-1, 2 * KVH * HD),
        base_weight,
    )
    mate_delta = mate_weights(mate_codes, mate_scales)
    behind, mate_delta = lax.optimization_barrier((lengths, mate_delta))
    own_query, kept, sent = cache_partials(
        behind,
        all_queries,
        cache,
        rows,
        steps,
        heads_own,
        tensor_count,
    )
    own_query, base_blocks = lax.optimization_barrier((own_query, base_blocks))
    token_rows, sent = lax.optimization_barrier((token_rows, sent))
    projected = project(own_delta, mate_delta, base_blocks, near_first(token_rows))
    step = 1
    while step < tensor_count:
        came = swap(sent, "tensor", step)
        step *= 2
        if step < tensor_count:
            kept, sent = merge(kept, came, rows)
    arrived = exchange(near_first(projected), "group", 2)
    pieces = pack_pieces(owner_map, arrived, owner_block, tensor_count, near_width, slice_width)
    pieces = exchange(pieces, "tensor", 1)
    new_out, attended = finish(
        own_query, pieces, [kept, came], rows, steps, heads_own, near_width
    )
    return (new_out.reshape(rows, steps, -1), attended.reshape(rows, steps, -1))


def solution(mesh):
    in_specs = (
        P("group", None, "tensor"),
        P(None, "tensor"),
        P("group", "tensor"),
        P("group", "tensor"),
        P(),
        P("group", "tensor", None),
        P("group", None, None),
        P("group"),
    )
    out_specs = (P("group", None, "tensor"), P("group", None, "tensor"))
    return jax.shard_map(
        on_device, mesh=mesh, in_specs=in_specs, out_specs=out_specs, check_vma=False
    )
```

```python
import functools
import jax
import jax.numpy as jnp
from jax import lax
from jax.experimental import pallas as pl
from jax.experimental.pallas import tpu as pltpu
from jax.sharding import PartitionSpec as P

H = 64
KVH = 8
HD = 128
BLK = 128
LANES = 128
SUBLANES = 8


NEGATIVE = -1e30
SCORE_SCALE = HD ** (-0.5)
CACHE_HINT = 120_000_000
PROJECT_HINT = 60_000_000
PACK_HINT = 60_000_000
CACHE_KIB = 24 << 10
WEIGHTS_KIB = 16 << 10
PROJECT_KIB = 16 << 10
NT = (((1,), (1,)), ((), ()))
TN = (((0,), (0,)), ((), ()))
VMEM = pl.BlockSpec(memory_space=pltpu.VMEM)
SMEM = pl.BlockSpec(memory_space=pltpu.SMEM)
HBM = pl.BlockSpec(memory_space=pltpu.HBM)


def split(x):
    high = x.astype(jnp.bfloat16).astype(jnp.float32)
    middle = (x - high).astype(jnp.bfloat16).astype(jnp.float32)
    return [high, middle, x - high - middle]


def stats_rows(dtype):
    return SUBLANES if dtype == jnp.float32 else 2 * SUBLANES


def put_stats(ref, index, stats):
    dtype = ref.dtype
    lines = [x for one in stats for x in ([one] if dtype == jnp.float32 else split(one))]
    lanes = lines[0].shape[1]
    count = stats_rows(dtype)
    lines.append(jnp.zeros((count - len(lines), lanes), jnp.float32))
    tile = jnp.concatenate(lines, axis=0)
    if lanes < LANES:
        tile = jnp.concatenate([tile, jnp.zeros((count, LANES - lanes), jnp.float32)], axis=1)
    ref[index, ref.shape[1] - count :] = tile.astype(dtype)


def get_stats(ref, index, rows):
    dtype = ref.dtype
    tile = ref[index, ref.shape[1] - stats_rows(dtype) :].astype(jnp.float32)
    lines = [tile[n : n + 1] for n in range(2 * rows * (1 if dtype == jnp.float32 else 3))]
    if dtype != jnp.float32:
        lines = [a + b + c for a, b, c in zip(lines[::3], lines[1::3], lines[2::3])]
    return [(lines[2 * r], lines[2 * r + 1]) for r in range(rows)]


def hint(size):
    return pl.CostEstimate(flops=0, bytes_accessed=size, transcendentals=0)


def dot(left, right, dims):
    return lax.dot_general(left, right, dims, preferred_element_type=jnp.float32)


def swap(x, axis, distance):
    size = lax.axis_size(axis)
    return lax.ppermute(x, axis, [(k, k ^ distance) for k in range(size)])


def distances(size):
    return [0] + list(range(size - 1, 0, -1))


def params(kibibytes):
    return pltpu.CompilerParams(vmem_limit_bytes=kibibytes << 10)


def head_rows(block, row, steps, heads):
    mine = block[row * steps : (row + 1) * steps]
    return jnp.concatenate([mine[:, h * HD : (h + 1) * HD] for h in range(heads)], axis=0)


def dequantize(codes_ref, scales_ref, out_ref):
    columns = scales_ref[...].astype(jnp.float32).T
    for n in range(columns.shape[1]):
        lanes = slice(n * BLK, (n + 1) * BLK)
        values = codes_ref[:, lanes].astype(jnp.float32) * columns[:, n : n + 1]
        out_ref[:, lanes] = values.astype(jnp.bfloat16)


def mate_weights(codes, scales):
    return pl.pallas_call(
        dequantize,
        out_shape=jax.ShapeDtypeStruct(codes.shape, jnp.bfloat16),
        in_specs=[VMEM, VMEM],
        out_specs=VMEM,
        compiler_params=params(WEIGHTS_KIB),
        cost_estimate=hint(1000),
        name="mate_weights",
    )(codes, scales.T)


def prepare_kernel(
    rows, steps, own, chunk,
    owner_hbm, lengths_hbm, scales_hbm, codes_hbm, query_hbm, cache_hbm, base_hbm,
    delta_ref, base_ref, own_query_ref, kept_ref, sent_ref,
    owner_ref, lengths_ref, scales_ref, codes_ref, query_ref, cache_ref, arrived,
):
    place = lax.axis_index("tensor")
    block = codes_ref.shape[0]
    cache_len = cache_ref.shape[0] // rows
    owner_load = pltpu.make_async_copy(owner_hbm, owner_ref, arrived.at[0])
    first_loads = [
        pltpu.make_async_copy(lengths_hbm, lengths_ref, arrived.at[1]),
        pltpu.make_async_copy(scales_hbm, scales_ref, arrived.at[2]),
        pltpu.make_async_copy(codes_hbm, codes_ref, arrived.at[3]),
        pltpu.make_async_copy(query_hbm, query_ref, arrived.at[4]),
    ]
    cache_loads = []
    for r in range(rows):
        here = pl.ds(r * cache_len, cache_len)
        cache_loads.append(
            pltpu.make_async_copy(cache_hbm.at[here], cache_ref.at[here], arrived.at[5 + r])
        )
    for load in [owner_load] + first_loads + cache_loads:
        load.start()
    owner_load.wait()
    base_loads = []
    for k in range(2):
        start = owner_ref[lax.axis_index("group") ^ k] * block
        here = pl.ds(pl.multiple_of(start, block), block)
        base_loads.append(
            pltpu.make_async_copy(base_hbm.at[here], base_ref.at[k], arrived.at[5 + rows + k])
        )
        base_loads[k].start()
    for load in first_loads:
        load.wait()
    dequantize(codes_ref, scales_ref, delta_ref)

    chunks = own // chunk
    height = chunk * steps
    width = chunks * HD
    position = lax.broadcasted_iota(jnp.int32, (cache_len, chunks * height), 0)

    def kv_lane(d):
        return pl.multiple_of(((place ^ d) * own // (H // KVH)) * HD, HD)

    def score(r, d):
        head = (place ^ d) * own
        queries = query_ref[:, pl.ds(pl.multiple_of(head * HD, HD), own * HD)]
        query = head_rows(queries.astype(jnp.float32), r, steps, own)
        if d == 0:
            at = r * chunks * height
            own_query_ref[at : at + chunks * height] = query.astype(jnp.bfloat16)
        spread = []
        for j in range(chunks):
            line = [jnp.zeros((height, HD), jnp.float32)] * chunks
            line[j] = query[j * height : (j + 1) * height]
            spread.append(jnp.concatenate(line, axis=1))
        spread = jnp.concatenate(spread, axis=0).astype(jnp.bfloat16)
        keys = cache_ref[pl.ds(r * cache_len, cache_len), pl.ds(kv_lane(d), width)]
        return dot(keys, spread, NT)

    units = [(r, d) for r in range(rows) for d in range(2 * kept_ref.shape[0])]
    stats = [[] for _ in range(2 * kept_ref.shape[0])]
    ahead = []
    for n in range(len(units) + 1):
        if n < len(units):
            if units[n][1] == 0:
                cache_loads[units[n][0]].wait()
            ahead.append(score(*units[n]))
        if n == 0:
            continue
        r, d = units[n - 1]
        at = r * chunks * height
        usable = position < lengths_ref[r] - place * cache_len
        scores = jnp.where(usable, ahead.pop(0) * SCORE_SCALE, 2.0 * NEGATIVE)
        peak = jnp.maximum(jnp.max(scores, axis=0, keepdims=True), NEGATIVE)
        weights = jnp.exp(scores - peak)
        total = jnp.sum(weights, axis=0, keepdims=True)
        lane = pl.ds(kv_lane(d) + KVH * HD, width)
        values = cache_ref[pl.ds(r * cache_len, cache_len), lane]
        sums = dot(weights.astype(jnp.bfloat16), values, TN)
        ref, index = (sent_ref if d % 2 else kept_ref), d // 2
        for j in range(chunks):
            here = slice(j * height, (j + 1) * height)
            mine = sums[here, j * HD : (j + 1) * HD].astype(ref.dtype)
            ref[index, at + j * height : at + (j + 1) * height] = mine
        stats[d] += [peak, total]
        if r == rows - 1:
            put_stats(ref, index, stats[d])
    for load in base_loads:
        load.wait()


def part_shape(count, height, dtype):
    return jax.ShapeDtypeStruct((count, height + stats_rows(dtype), LANES), dtype)


def prepare(owner_map, lengths, scales, codes, queries, cache, base, rows, steps, own, ways):
    height = rows * own * steps
    operands = [
        pltpu.with_memory_space_constraint(x, pltpu.HBM)
        for x in (owner_map, lengths, scales.T, codes, queries, cache, base)
    ]
    return pl.pallas_call(
        functools.partial(prepare_kernel, rows, steps, own, min(own, H // KVH)),
        out_shape=[
            jax.ShapeDtypeStruct(codes.shape, jnp.bfloat16),
            jax.ShapeDtypeStruct((2,) + codes.shape, jnp.bfloat16),
            jax.ShapeDtypeStruct((height, HD), jnp.bfloat16),
            part_shape(ways // 2, height, jnp.float32),
            part_shape(ways // 2, height, jnp.bfloat16),
        ],
        in_specs=[HBM] * len(operands),
        out_specs=[VMEM] * 5,
        scratch_shapes=[
            pltpu.SMEM(owner_map.shape, owner_map.dtype),
            pltpu.SMEM(lengths.shape, lengths.dtype),
            pltpu.VMEM(scales.shape[::-1], scales.dtype),
            pltpu.VMEM(codes.shape, codes.dtype),
            pltpu.VMEM(queries.shape, queries.dtype),
            pltpu.VMEM(cache.shape, cache.dtype),
            pltpu.SemaphoreType.DMA((7 + rows,)),
        ],
        compiler_params=params(CACHE_KIB),
        cost_estimate=hint(CACHE_HINT),
        name="prepare",
    )(*operands)


def merge_kernel(rows, span, kept_ref, came_ref, next_ref, sent_ref=None):
    for n in range(kept_ref.shape[0]):
        ref, index = (sent_ref if n % 2 else next_ref), n // 2
        stats, factors = [], []
        for one, two in zip(get_stats(kept_ref, n, rows), get_stats(came_ref, n, rows)):
            peak = jnp.maximum(one[0], two[0])
            scales = [jnp.exp(one[0] - peak), jnp.exp(two[0] - peak)]
            stats += [peak, one[1] * scales[0] + two[1] * scales[1]]
            factors += scales
        factors.append(jnp.zeros((SUBLANES - len(factors), LANES), jnp.float32))
        columns = jnp.concatenate(factors, axis=0).T[:span]
        for r in range(rows):
            here = slice(r * span, (r + 1) * span)
            left = kept_ref[n, here] * columns[:, 2 * r : 2 * r + 1]
            right = came_ref[n, here].astype(jnp.float32) * columns[:, 2 * r + 1 : 2 * r + 2]
            ref[index, here] = (left + right).astype(ref.dtype)
        put_stats(ref, index, stats)


def merge(kept, came, rows):
    count = kept.shape[0]
    height = kept.shape[1] - stats_rows(kept.dtype)
    shapes = [part_shape((count + 1) // 2, height, jnp.float32)]
    if count > 1:
        shapes.append(part_shape(count // 2, height, jnp.bfloat16))
    return pl.pallas_call(
        functools.partial(merge_kernel, rows, height // rows),
        out_shape=shapes,
        in_specs=[VMEM] * 2,
        out_specs=[VMEM] * len(shapes),
        compiler_params=params(8192),
        cost_estimate=hint(4 * kept.size),
        name="merge_partials",
    )(kept, came)


def project_kernel(pairs, own_ref, mate_ref, base_ref, *refs):
    tokens, outs = refs[:pairs], refs[pairs:]
    block = own_ref.shape[0]
    stacked = jnp.concatenate([ref[...] for ref in tokens], axis=0)
    count = tokens[0].shape[0]
    for k, delta_ref in enumerate((own_ref, mate_ref)):
        whole = (dot(base_ref[k], stacked, NT) + dot(delta_ref[...], stacked, NT)).T
        for n in range(pairs):
            outs[n][:, k * block : (k + 1) * block] = whole[n * count : (n + 1) * count]


def project(own, mate, base, tokens):
    pairs = len(tokens)
    block = own.shape[0]
    count, width = tokens[0].shape
    return pl.pallas_call(
        functools.partial(project_kernel, pairs),
        out_shape=[jax.ShapeDtypeStruct((count, 2 * block), jnp.float32)] * pairs,
        in_specs=[VMEM] * (3 + pairs),
        out_specs=[VMEM] * pairs,
        compiler_params=params(PROJECT_KIB),
        cost_estimate=hint(PROJECT_HINT),
        name="project",
    )(own, mate, base, *tokens)


def pack_kernel(pairs, ways, near, wide, owner_ref, *refs):
    arrived, outs, ordered = refs[:pairs], refs[pairs : pairs + ways], refs[-1]
    place = lax.axis_index("group")
    to_place = lax.axis_index("tensor")
    shards, _, block = ordered.shape
    for piece, d in zip(arrived, distances(pairs)):
        for k in range(2):
            ordered[owner_ref[place ^ (2 * d + k)]] = piece[:, k * block : (k + 1) * block]
    for out, d in zip(outs, distances(ways)):
        to = to_place ^ d
        for n in range(near):
            out[:, n * block : (n + 1) * block] = ordered[to * near + n]
            at = (near + n) * block
            out[:, at : at + block] = ordered[shards // 2 + to * near + n]
        for n in range(wide):
            at = (2 * near + n) * block
            out[:, at : at + block] = ordered[to * wide + n]


def pack_pieces(owner_map, arrived, block, ways, near_width, slice_width):
    pairs = len(arrived)
    count = arrived[0].shape[0]
    shards = 2 * pairs
    kv_width = KVH * HD
    if block % LANES == 0 and near_width % block == 0 and slice_width % block == 0:
        piece = jax.ShapeDtypeStruct((count, 2 * near_width + slice_width), jnp.float32)
        kernel = functools.partial(
            pack_kernel, pairs, ways, near_width // block, slice_width // block
        )
        return pl.pallas_call(
            kernel,
            out_shape=[piece] * ways,
            in_specs=[SMEM] + [VMEM] * pairs,
            out_specs=[VMEM] * ways,
            scratch_shapes=[pltpu.VMEM((shards, count, block), jnp.float32)],
            compiler_params=params(8192),
            cost_estimate=hint(PACK_HINT),
            name="pack_pieces",
        )(owner_map, *arrived)
    nearest = [arrived[distances(pairs).index(d)] for d in range(pairs)]
    blocks = jnp.stack(nearest, axis=0).reshape(pairs, count, 2, block).transpose(0, 2, 1, 3)
    shard_of = jnp.zeros((shards,), jnp.int32).at[owner_map].set(
        jnp.arange(shards, dtype=jnp.int32)
    )
    taken = jnp.take(
        blocks.reshape(shards, count, block), shard_of ^ lax.axis_index("group"), axis=0
    )
    ordered = taken.transpose(1, 0, 2).reshape(count, shards * block)
    per_device = H // ways
    pieces = []
    for d in distances(ways):
        to = lax.axis_index("tensor") ^ d
        near = (to * per_device // (H // KVH)) * HD
        parts = [(near, near_width), (kv_width + near, near_width), (to * slice_width, slice_width)]
        cuts = [lax.dynamic_slice_in_dim(ordered, start, width, 1) for start, width in parts]
        pieces.append(jnp.concatenate(cuts, axis=1))
    return pieces


def finish_kernel(rows, steps, own, chunk, near_width, ways, query_ref, *refs):
    pieces, part = refs[:ways], refs[ways]
    new_ref, attended_ref = refs[ways + 1 :]
    chunks = own // chunk
    height = chunk * steps
    span = chunks * height
    summed = pieces[0][...]
    for piece in pieces[1:]:
        summed = summed + piece[...]
    stored = summed.astype(jnp.bfloat16)
    new_ref[...] = stored[:, 2 * near_width :]
    near = stored[:, : 2 * near_width].astype(jnp.float32)
    key_step = lax.broadcasted_iota(jnp.int32, (steps, span), 0)
    query_step = lax.broadcasted_iota(jnp.int32, (steps, span), 1) % steps
    causal = key_step <= query_step
    scores = []
    for r in range(rows):
        spread = []
        for j in range(chunks):
            line = [jnp.zeros((height, HD), jnp.bfloat16)] * chunks
            line[j] = query_ref[r * span + j * height : r * span + (j + 1) * height]
            spread.append(jnp.concatenate(line, axis=1))
        keys = near[r * steps : (r + 1) * steps, :near_width].astype(jnp.bfloat16)
        scores.append(dot(keys, jnp.concatenate(spread, axis=0), NT) * SCORE_SCALE)
    factors, near_sums = [], []
    for r, (cache_peak, cache_total) in enumerate(get_stats(part, 0, rows)):
        masked = jnp.where(causal, scores[r], NEGATIVE)
        peak = jnp.max(masked, axis=0, keepdims=True)
        weights = jnp.where(causal, jnp.exp(masked - peak), 0.0)
        total = jnp.sum(weights, axis=0, keepdims=True)
        values = near[r * steps : (r + 1) * steps, near_width:].astype(jnp.bfloat16)
        near_sums.append(dot(weights.astype(jnp.bfloat16), values, TN))
        cache_peak, cache_total = cache_peak[:, :span], cache_total[:, :span]
        top = jnp.maximum(peak, cache_peak)
        scales = [jnp.exp(cache_peak - top), jnp.exp(peak - top)]
        whole = cache_total * scales[0] + total * scales[1]
        factors += [scale / whole for scale in scales]
    factors.append(jnp.zeros((SUBLANES - len(factors), span), jnp.float32))
    columns = jnp.concatenate(factors, axis=0)
    if span < LANES:
        pad = jnp.zeros((SUBLANES, LANES - span), jnp.float32)
        columns = jnp.concatenate([columns, pad], axis=1)
    columns = columns.T
    for j in range(chunks):
        here = slice(j * height, (j + 1) * height)
        merged = []
        for r in range(rows):
            cached = part[0, r * span + j * height : r * span + (j + 1) * height]
            fresh = near_sums[r][here, j * HD : (j + 1) * HD]
            merged.append(
                cached * columns[here, 2 * r : 2 * r + 1]
                + fresh * columns[here, 2 * r + 1 : 2 * r + 2]
            )
        for h in range(chunk):
            both = [out[h * steps : (h + 1) * steps] for out in merged]
            lane = (j * chunk + h) * HD
            attended_ref[:, lane : lane + HD] = jnp.concatenate(both, axis=0).astype(jnp.bfloat16)


def finish(own_query, pieces, part, rows, steps, own, near_width):
    ways = len(pieces)
    count, width = pieces[0].shape
    return pl.pallas_call(
        functools.partial(
            finish_kernel, rows, steps, own, min(own, H // KVH), near_width, ways
        ),
        out_shape=[
            jax.ShapeDtypeStruct((count, width - 2 * near_width), jnp.bfloat16),
            jax.ShapeDtypeStruct((count, own * HD), jnp.bfloat16),
        ],
        in_specs=[VMEM] * (2 + ways),
        out_specs=[VMEM] * 2,
        compiler_params=params(8192),
        name="finish",
    )(own_query, *pieces, part)


def on_device(
    hidden_x, base_weight, delta_codes, delta_scales, owner_map, kv_cache, queries, lengths
):
    group_count = lax.axis_size("group")
    tensor_count = lax.axis_size("tensor")
    rows, steps, local_width = hidden_x.shape
    tokens = rows * steps
    owner_block = delta_codes.shape[0]
    heads_own = H // tensor_count
    slice_width = base_weight.shape[0] // tensor_count
    near_width = max(1, heads_own // (H // KVH)) * HD
    pairs = group_count // 2

    def exchange(arrays, axis, stride):
        places = distances(len(arrays))[1:]
        return [arrays[0]] + [swap(x, axis, stride * d) for x, d in zip(arrays[1:], places)]

    def near_first(arrays):
        return arrays[:1] + arrays[:0:-1]

    token_rows = exchange([hidden_x.reshape(tokens, local_width)] * pairs, "group", 2)
    mate_codes = swap(delta_codes, "group", 1)
    mate_scales = swap(delta_scales, "group", 1)

    own_delta, base_blocks, own_query, kept, sent = prepare(
        owner_map,
        lengths,
        delta_scales,
        delta_codes,
        queries.reshape(tokens, H * HD),
        kv_cache.reshape(-1, 2 * KVH * HD),
        base_weight,
        rows,
        steps,
        heads_own,
        tensor_count,
    )
    mate_delta = mate_weights(mate_codes, mate_scales)
    behind = lax.optimization_barrier((*near_first(token_rows), mate_delta, sent))
    token_rows, mate_delta, sent = near_first(list(behind[:pairs])), behind[-2], behind[-1]
    projected = project(own_delta, mate_delta, base_blocks, near_first(token_rows))
    step = 1
    while step < tensor_count:
        came = swap(sent, "tensor", step)
        kept, *sent = merge(kept, came, rows)
        sent = sent[0] if sent else None
        step *= 2
    arrived = exchange(near_first(projected), "group", 2)
    pieces = pack_pieces(owner_map, arrived, owner_block, tensor_count, near_width, slice_width)
    pieces = exchange(pieces, "tensor", 1)
    new_out, attended = finish(own_query, pieces, kept, rows, steps, heads_own, near_width)
    return (new_out.reshape(rows, steps, -1), attended.reshape(rows, steps, -1))


def solution(mesh):
    in_specs = (
        P("group", None, "tensor"),
        P(None, "tensor"),
        P("group", "tensor"),
        P("group", "tensor"),
        P(),
        P("group", "tensor", None),
        P("group", None, None),
        P("group"),
    )
    out_specs = (P("group", None, "tensor"), P("group", None, "tensor"))
    return jax.shard_map(
        on_device, mesh=mesh, in_specs=in_specs, out_specs=out_specs, check_vma=False
    )
```

```python
import functools
import jax
import jax.numpy as jnp
from jax import lax
from jax.experimental import pallas as pl
from jax.experimental.pallas import tpu as pltpu
from jax.sharding import PartitionSpec as P

H = 64
KVH = 8
HD = 128
BLK = 128
LANES = 128
SUBLANES = 8


NEGATIVE = -1e30
SCORE_SCALE = HD ** (-0.5)
CACHE_HINT = 120_000_000
PROJECT_HINT = 60_000_000
PACK_HINT = 60_000_000
CACHE_KIB = 24 << 10
WEIGHTS_KIB = 16 << 10
PROJECT_KIB = 16 << 10
NT = (((1,), (1,)), ((), ()))
TN = (((0,), (0,)), ((), ()))
VMEM = pl.BlockSpec(memory_space=pltpu.VMEM)
SMEM = pl.BlockSpec(memory_space=pltpu.SMEM)
HBM = pl.BlockSpec(memory_space=pltpu.HBM)


def split(x):
    high = x.astype(jnp.bfloat16).astype(jnp.float32)
    middle = (x - high).astype(jnp.bfloat16).astype(jnp.float32)
    return [high, middle, x - high - middle]


def stats_rows(dtype):
    return SUBLANES if dtype == jnp.float32 else 2 * SUBLANES


def put_stats(ref, stats):
    dtype = ref.dtype
    lines = [x for one in stats for x in ([one] if dtype == jnp.float32 else split(one))]
    lanes = lines[0].shape[1]
    count = stats_rows(dtype)
    lines.append(jnp.zeros((count - len(lines), lanes), jnp.float32))
    tile = jnp.concatenate(lines, axis=0)
    if lanes < LANES:
        tile = jnp.concatenate([tile, jnp.zeros((count, LANES - lanes), jnp.float32)], axis=1)
    ref[ref.shape[0] - count :] = tile.astype(dtype)


def get_stats(ref, rows):
    dtype = ref.dtype
    tile = ref[ref.shape[0] - stats_rows(dtype) :].astype(jnp.float32)
    lines = [tile[n : n + 1] for n in range(2 * rows * (1 if dtype == jnp.float32 else 3))]
    if dtype != jnp.float32:
        lines = [a + b + c for a, b, c in zip(lines[::3], lines[1::3], lines[2::3])]
    return [(lines[2 * r], lines[2 * r + 1]) for r in range(rows)]


def hint(size):
    return pl.CostEstimate(flops=0, bytes_accessed=size, transcendentals=0)


def dot(left, right, dims):
    return lax.dot_general(left, right, dims, preferred_element_type=jnp.float32)


def swap(x, axis, distance):
    size = lax.axis_size(axis)
    return lax.ppermute(x, axis, [(k, k ^ distance) for k in range(size)])


def distances(size):
    return [0] + list(range(size - 1, 0, -1))


def params(kibibytes):
    return pltpu.CompilerParams(vmem_limit_bytes=kibibytes << 10)


def head_rows(block, row, steps, heads):
    mine = block[row * steps : (row + 1) * steps]
    return jnp.concatenate([mine[:, h * HD : (h + 1) * HD] for h in range(heads)], axis=0)


def dequantize(codes_ref, scales_ref, out_ref):
    columns = scales_ref[...].astype(jnp.float32).T
    for n in range(columns.shape[1]):
        lanes = slice(n * BLK, (n + 1) * BLK)
        values = codes_ref[:, lanes].astype(jnp.float32) * columns[:, n : n + 1]
        out_ref[:, lanes] = values.astype(jnp.bfloat16)


def mate_weights(codes, scales):
    return pl.pallas_call(
        dequantize,
        out_shape=jax.ShapeDtypeStruct(codes.shape, jnp.bfloat16),
        in_specs=[VMEM, VMEM],
        out_specs=VMEM,
        compiler_params=params(WEIGHTS_KIB),
        cost_estimate=hint(1000),
        name="mate_weights",
    )(codes, scales.T)


def prepare_kernel(
    rows, steps, own, chunk,
    owner_hbm, lengths_hbm, scales_hbm, codes_hbm, query_hbm, cache_hbm, base_hbm,
    *refs,
):
    delta_ref, base_ref, own_query_ref, parts = refs[0], refs[1], refs[2], refs[3:-7]
    owner_ref, lengths_ref, scales_ref, codes_ref, query_ref, cache_ref, arrived = refs[-7:]
    order = distances(len(parts))
    place = lax.axis_index("tensor")
    block = codes_ref.shape[0]
    cache_len = cache_ref.shape[0] // rows
    owner_load = pltpu.make_async_copy(owner_hbm, owner_ref, arrived.at[0])
    first_loads = [
        pltpu.make_async_copy(lengths_hbm, lengths_ref, arrived.at[1]),
        pltpu.make_async_copy(scales_hbm, scales_ref, arrived.at[2]),
        pltpu.make_async_copy(codes_hbm, codes_ref, arrived.at[3]),
        pltpu.make_async_copy(query_hbm, query_ref, arrived.at[4]),
    ]
    cache_loads = []
    for r in range(rows):
        here = pl.ds(r * cache_len, cache_len)
        cache_loads.append(
            pltpu.make_async_copy(cache_hbm.at[here], cache_ref.at[here], arrived.at[5 + r])
        )
    for load in [owner_load] + first_loads + cache_loads:
        load.start()
    owner_load.wait()
    base_loads = []
    for k in range(2):
        start = owner_ref[lax.axis_index("group") ^ k] * block
        here = pl.ds(pl.multiple_of(start, block), block)
        base_loads.append(
            pltpu.make_async_copy(base_hbm.at[here], base_ref.at[k], arrived.at[5 + rows + k])
        )
        base_loads[k].start()
    for load in first_loads:
        load.wait()
    dequantize(codes_ref, scales_ref, delta_ref)

    chunks = own // chunk
    height = chunk * steps
    width = chunks * HD
    position = lax.broadcasted_iota(jnp.int32, (cache_len, chunks * height), 0)

    def kv_lane(d):
        return pl.multiple_of(((place ^ d) * own // (H // KVH)) * HD, HD)

    def score(r, d):
        head = (place ^ d) * own
        queries = query_ref[:, pl.ds(pl.multiple_of(head * HD, HD), own * HD)]
        query = head_rows(queries.astype(jnp.float32), r, steps, own)
        if d == 0:
            at = r * chunks * height
            own_query_ref[at : at + chunks * height] = query.astype(jnp.bfloat16)
        spread = []
        for j in range(chunks):
            line = [jnp.zeros((height, HD), jnp.float32)] * chunks
            line[j] = query[j * height : (j + 1) * height]
            spread.append(jnp.concatenate(line, axis=1))
        spread = jnp.concatenate(spread, axis=0).astype(jnp.bfloat16)
        keys = cache_ref[pl.ds(r * cache_len, cache_len), pl.ds(kv_lane(d), width)]
        return dot(keys, spread, NT)

    units = [(r, n) for r in range(rows) for n in range(len(parts))]
    stats = [[] for _ in parts]
    ahead = []
    for at in range(len(units) + 1):
        if at < len(units):
            r, n = units[at]
            if n == 0:
                cache_loads[r].wait()
            ahead.append(score(r, order[n]))
        if at == 0:
            continue
        r, n = units[at - 1]
        usable = position < lengths_ref[r] - place * cache_len
        scores = jnp.where(usable, ahead.pop(0) * SCORE_SCALE, 2.0 * NEGATIVE)
        peak = jnp.maximum(jnp.max(scores, axis=0, keepdims=True), NEGATIVE)
        weights = jnp.exp(scores - peak)
        total = jnp.sum(weights, axis=0, keepdims=True)
        lane = pl.ds(kv_lane(order[n]) + KVH * HD, width)
        values = cache_ref[pl.ds(r * cache_len, cache_len), lane]
        sums = dot(weights.astype(jnp.bfloat16), values, TN)
        for j in range(chunks):
            here = slice(j * height, (j + 1) * height)
            first = (r * chunks + j) * height
            mine = sums[here, j * HD : (j + 1) * HD].astype(parts[n].dtype)
            parts[n][first : first + height] = mine
        stats[n] += [peak, total]
        if r == rows - 1:
            put_stats(parts[n], stats[n])
    for load in base_loads:
        load.wait()


def part_shape(height, dtype):
    return jax.ShapeDtypeStruct((height + stats_rows(dtype), LANES), dtype)


def prepare(owner_map, lengths, scales, codes, queries, cache, base, rows, steps, own, ways):
    height = rows * own * steps
    operands = [
        pltpu.with_memory_space_constraint(x, pltpu.HBM)
        for x in (owner_map, lengths, scales.T, codes, queries, cache, base)
    ]
    out = pl.pallas_call(
        functools.partial(prepare_kernel, rows, steps, own, min(own, H // KVH)),
        out_shape=[
            jax.ShapeDtypeStruct(codes.shape, jnp.bfloat16),
            jax.ShapeDtypeStruct((2,) + codes.shape, jnp.bfloat16),
            jax.ShapeDtypeStruct((height, HD), jnp.bfloat16),
            part_shape(height, jnp.float32),
        ]
        + [part_shape(height, jnp.bfloat16)] * (ways - 1),
        in_specs=[HBM] * len(operands),
        out_specs=[VMEM] * (3 + ways),
        scratch_shapes=[
            pltpu.SMEM(owner_map.shape, owner_map.dtype),
            pltpu.SMEM(lengths.shape, lengths.dtype),
            pltpu.VMEM(scales.shape[::-1], scales.dtype),
            pltpu.VMEM(codes.shape, codes.dtype),
            pltpu.VMEM(queries.shape, queries.dtype),
            pltpu.VMEM(cache.shape, cache.dtype),
            pltpu.SemaphoreType.DMA((7 + rows,)),
        ],
        compiler_params=params(CACHE_KIB),
        cost_estimate=hint(CACHE_HINT),
        name="prepare",
    )(*operands)
    return out[0], out[1], out[2], out[3:]


def merge_kernel(rows, span, *refs):
    parts, out_ref = refs[:-1], refs[-1]
    everything = [get_stats(part, rows) for part in parts]
    stats, factors = [], []
    for r in range(rows):
        peak = functools.reduce(jnp.maximum, [one[r][0] for one in everything])
        scales = [jnp.exp(one[r][0] - peak) for one in everything]
        stats += [peak, sum(one[r][1] * scale for one, scale in zip(everything, scales))]
        factors += scales
    lines = -(-len(factors) // SUBLANES) * SUBLANES
    if lines > len(factors):
        factors.append(jnp.zeros((lines - len(factors), LANES), jnp.float32))
    columns = jnp.concatenate(factors, axis=0).T[:span]
    for r in range(rows):
        here = slice(r * span, (r + 1) * span)
        terms = []
        for n, part in enumerate(parts):
            at = r * len(parts) + n
            terms.append(part[here].astype(jnp.float32) * columns[:, at : at + 1])
        out_ref[here] = sum(terms[1:], terms[0])
    put_stats(out_ref, stats)


def merge(parts, rows):
    height = parts[0].shape[0] - stats_rows(parts[0].dtype)
    return pl.pallas_call(
        functools.partial(merge_kernel, rows, height // rows),
        out_shape=part_shape(height, jnp.float32),
        in_specs=[VMEM] * len(parts),
        out_specs=VMEM,
        compiler_params=params(8192),
        cost_estimate=hint(1000),
        name="merge_partials",
    )(*parts)


def project_kernel(pairs, own_ref, mate_ref, base_ref, *refs):
    tokens, outs = refs[:pairs], refs[pairs:]
    block = own_ref.shape[0]
    stacked = jnp.concatenate([ref[...] for ref in tokens], axis=0)
    count = tokens[0].shape[0]
    for k, delta_ref in enumerate((own_ref, mate_ref)):
        whole = (dot(base_ref[k], stacked, NT) + dot(delta_ref[...], stacked, NT)).T
        for n in range(pairs):
            outs[n][:, k * block : (k + 1) * block] = whole[n * count : (n + 1) * count]


def project(own, mate, base, tokens):
    pairs = len(tokens)
    block = own.shape[0]
    count, width = tokens[0].shape
    return pl.pallas_call(
        functools.partial(project_kernel, pairs),
        out_shape=[jax.ShapeDtypeStruct((count, 2 * block), jnp.float32)] * pairs,
        in_specs=[VMEM] * (3 + pairs),
        out_specs=[VMEM] * pairs,
        compiler_params=params(PROJECT_KIB),
        cost_estimate=hint(PROJECT_HINT),
        name="project",
    )(own, mate, base, *tokens)


def pack_kernel(pairs, ways, near, wide, owner_ref, *refs):
    arrived, outs, ordered = refs[:pairs], refs[pairs : pairs + ways], refs[-1]
    place = lax.axis_index("group")
    to_place = lax.axis_index("tensor")
    shards, _, block = ordered.shape
    for piece, d in zip(arrived, distances(pairs)):
        for k in range(2):
            ordered[owner_ref[place ^ (2 * d + k)]] = piece[:, k * block : (k + 1) * block]
    for out, d in zip(outs, distances(ways)):
        to = to_place ^ d
        for n in range(near):
            out[:, n * block : (n + 1) * block] = ordered[to * near + n]
            at = (near + n) * block
            out[:, at : at + block] = ordered[shards // 2 + to * near + n]
        for n in range(wide):
            at = (2 * near + n) * block
            out[:, at : at + block] = ordered[to * wide + n]


def pack_pieces(owner_map, arrived, block, ways, near_width, slice_width):
    pairs = len(arrived)
    count = arrived[0].shape[0]
    shards = 2 * pairs
    kv_width = KVH * HD
    if block % LANES == 0 and near_width % block == 0 and slice_width % block == 0:
        piece = jax.ShapeDtypeStruct((count, 2 * near_width + slice_width), jnp.float32)
        kernel = functools.partial(
            pack_kernel, pairs, ways, near_width // block, slice_width // block
        )
        return pl.pallas_call(
            kernel,
            out_shape=[piece] * ways,
            in_specs=[SMEM] + [VMEM] * pairs,
            out_specs=[VMEM] * ways,
            scratch_shapes=[pltpu.VMEM((shards, count, block), jnp.float32)],
            compiler_params=params(8192),
            cost_estimate=hint(PACK_HINT),
            name="pack_pieces",
        )(owner_map, *arrived)
    nearest = [arrived[distances(pairs).index(d)] for d in range(pairs)]
    blocks = jnp.stack(nearest, axis=0).reshape(pairs, count, 2, block).transpose(0, 2, 1, 3)
    shard_of = jnp.zeros((shards,), jnp.int32).at[owner_map].set(
        jnp.arange(shards, dtype=jnp.int32)
    )
    taken = jnp.take(
        blocks.reshape(shards, count, block), shard_of ^ lax.axis_index("group"), axis=0
    )
    ordered = taken.transpose(1, 0, 2).reshape(count, shards * block)
    per_device = H // ways
    pieces = []
    for d in distances(ways):
        to = lax.axis_index("tensor") ^ d
        near = (to * per_device // (H // KVH)) * HD
        parts = [(near, near_width), (kv_width + near, near_width), (to * slice_width, slice_width)]
        cuts = [lax.dynamic_slice_in_dim(ordered, start, width, 1) for start, width in parts]
        pieces.append(jnp.concatenate(cuts, axis=1))
    return pieces


def finish_kernel(rows, steps, own, chunk, near_width, ways, query_ref, *refs):
    pieces, part = refs[:ways], refs[ways]
    new_ref, attended_ref = refs[ways + 1 :]
    chunks = own // chunk
    height = chunk * steps
    span = chunks * height
    summed = pieces[0][...]
    for piece in pieces[1:]:
        summed = summed + piece[...]
    stored = summed.astype(jnp.bfloat16)
    new_ref[...] = stored[:, 2 * near_width :]
    near = stored[:, : 2 * near_width].astype(jnp.float32)
    key_step = lax.broadcasted_iota(jnp.int32, (steps, span), 0)
    query_step = lax.broadcasted_iota(jnp.int32, (steps, span), 1) % steps
    causal = key_step <= query_step
    scores = []
    for r in range(rows):
        spread = []
        for j in range(chunks):
            line = [jnp.zeros((height, HD), jnp.bfloat16)] * chunks
            line[j] = query_ref[r * span + j * height : r * span + (j + 1) * height]
            spread.append(jnp.concatenate(line, axis=1))
        keys = near[r * steps : (r + 1) * steps, :near_width].astype(jnp.bfloat16)
        scores.append(dot(keys, jnp.concatenate(spread, axis=0), NT) * SCORE_SCALE)
    factors, near_sums = [], []
    for r, (cache_peak, cache_total) in enumerate(get_stats(part, rows)):
        masked = jnp.where(causal, scores[r], NEGATIVE)
        peak = jnp.max(masked, axis=0, keepdims=True)
        weights = jnp.where(causal, jnp.exp(masked - peak), 0.0)
        total = jnp.sum(weights, axis=0, keepdims=True)
        values = near[r * steps : (r + 1) * steps, near_width:].astype(jnp.bfloat16)
        near_sums.append(dot(weights.astype(jnp.bfloat16), values, TN))
        cache_peak, cache_total = cache_peak[:, :span], cache_total[:, :span]
        top = jnp.maximum(peak, cache_peak)
        scales = [jnp.exp(cache_peak - top), jnp.exp(peak - top)]
        whole = cache_total * scales[0] + total * scales[1]
        factors += [scale / whole for scale in scales]
    factors.append(jnp.zeros((SUBLANES - len(factors), span), jnp.float32))
    columns = jnp.concatenate(factors, axis=0)
    if span < LANES:
        pad = jnp.zeros((SUBLANES, LANES - span), jnp.float32)
        columns = jnp.concatenate([columns, pad], axis=1)
    columns = columns.T
    for j in range(chunks):
        here = slice(j * height, (j + 1) * height)
        merged = []
        for r in range(rows):
            cached = part[r * span + j * height : r * span + (j + 1) * height]
            fresh = near_sums[r][here, j * HD : (j + 1) * HD]
            merged.append(
                cached * columns[here, 2 * r : 2 * r + 1]
                + fresh * columns[here, 2 * r + 1 : 2 * r + 2]
            )
        for h in range(chunk):
            both = [out[h * steps : (h + 1) * steps] for out in merged]
            lane = (j * chunk + h) * HD
            attended_ref[:, lane : lane + HD] = jnp.concatenate(both, axis=0).astype(jnp.bfloat16)


def finish(own_query, pieces, part, rows, steps, own, near_width):
    ways = len(pieces)
    count, width = pieces[0].shape
    return pl.pallas_call(
        functools.partial(
            finish_kernel, rows, steps, own, min(own, H // KVH), near_width, ways
        ),
        out_shape=[
            jax.ShapeDtypeStruct((count, width - 2 * near_width), jnp.bfloat16),
            jax.ShapeDtypeStruct((count, own * HD), jnp.bfloat16),
        ],
        in_specs=[VMEM] * (2 + ways),
        out_specs=[VMEM] * 2,
        compiler_params=params(8192),
        name="finish",
    )(own_query, *pieces, part)


def on_device(
    hidden_x, base_weight, delta_codes, delta_scales, owner_map, kv_cache, queries, lengths
):
    group_count = lax.axis_size("group")
    tensor_count = lax.axis_size("tensor")
    rows, steps, local_width = hidden_x.shape
    tokens = rows * steps
    owner_block = delta_codes.shape[0]
    heads_own = H // tensor_count
    slice_width = base_weight.shape[0] // tensor_count
    near_width = max(1, heads_own // (H // KVH)) * HD
    pairs = group_count // 2

    def exchange(arrays, axis, stride):
        places = distances(len(arrays))[1:]
        return [arrays[0]] + [swap(x, axis, stride * d) for x, d in zip(arrays[1:], places)]

    def near_first(arrays):
        return arrays[:1] + arrays[:0:-1]

    token_rows = exchange([hidden_x.reshape(tokens, local_width)] * pairs, "group", 2)
    mate_codes = swap(delta_codes, "group", 1)
    mate_scales = swap(delta_scales, "group", 1)

    own_delta, base_blocks, own_query, partials = prepare(
        owner_map,
        lengths,
        delta_scales,
        delta_codes,
        queries.reshape(tokens, H * HD),
        kv_cache.reshape(-1, 2 * KVH * HD),
        base_weight,
        rows,
        steps,
        heads_own,
        tensor_count,
    )
    mate_delta = mate_weights(mate_codes, mate_scales)
    behind = lax.optimization_barrier((*near_first(token_rows), mate_delta, own_query))
    token_rows, mate_delta, own_query = near_first(list(behind[:pairs])), behind[-2], behind[-1]
    projected = project(own_delta, mate_delta, base_blocks, near_first(token_rows))
    arrived = exchange(near_first(projected), "group", 2)
    partials = exchange(partials, "tensor", 1)
    pieces = pack_pieces(owner_map, arrived, owner_block, tensor_count, near_width, slice_width)
    pieces = exchange(pieces, "tensor", 1)
    partial = merge(partials, rows)
    new_out, attended = finish(own_query, pieces, partial, rows, steps, heads_own, near_width)
    return (new_out.reshape(rows, steps, -1), attended.reshape(rows, steps, -1))


def solution(mesh):
    in_specs = (
        P("group", None, "tensor"),
        P(None, "tensor"),
        P("group", "tensor"),
        P("group", "tensor"),
        P(),
        P("group", "tensor", None),
        P("group", None, None),
        P("group"),
    )
    out_specs = (P("group", None, "tensor"), P("group", None, "tensor"))
    return jax.shard_map(
        on_device, mesh=mesh, in_specs=in_specs, out_specs=out_specs, check_vma=False
    )
```

```python
import functools
import jax
import jax.numpy as jnp
from jax import lax
from jax.experimental import pallas as pl
from jax.experimental.pallas import tpu as pltpu
from jax.sharding import PartitionSpec as P

H = 64
KVH = 8
HD = 128
BLK = 128
LANES = 128
SUBLANES = 8


NEGATIVE = -1e30
SCORE_SCALE = HD ** (-0.5)
CACHE_HINT = 120_000_000
PROJECT_HINT = 60_000_000
PACK_HINT = 60_000_000
CACHE_KIB = 24 << 10
WEIGHTS_KIB = 16 << 10
PROJECT_KIB = 16 << 10
NT = (((1,), (1,)), ((), ()))
TN = (((0,), (0,)), ((), ()))
VMEM = pl.BlockSpec(memory_space=pltpu.VMEM)
SMEM = pl.BlockSpec(memory_space=pltpu.SMEM)
HBM = pl.BlockSpec(memory_space=pltpu.HBM)


def split(x):
    high = x.astype(jnp.bfloat16).astype(jnp.float32)
    middle = (x - high).astype(jnp.bfloat16).astype(jnp.float32)
    return [high, middle, x - high - middle]


def stats_rows(dtype):
    return SUBLANES if dtype == jnp.float32 else 2 * SUBLANES


def put_stats(ref, index, stats):
    dtype = ref.dtype
    lines = [x for one in stats for x in ([one] if dtype == jnp.float32 else split(one))]
    lanes = lines[0].shape[1]
    count = stats_rows(dtype)
    lines.append(jnp.zeros((count - len(lines), lanes), jnp.float32))
    tile = jnp.concatenate(lines, axis=0)
    if lanes < LANES:
        tile = jnp.concatenate([tile, jnp.zeros((count, LANES - lanes), jnp.float32)], axis=1)
    ref[index, ref.shape[1] - count :] = tile.astype(dtype)


def get_stats(ref, index, rows):
    dtype = ref.dtype
    tile = ref[index, ref.shape[1] - stats_rows(dtype) :].astype(jnp.float32)
    lines = [tile[n : n + 1] for n in range(2 * rows * (1 if dtype == jnp.float32 else 3))]
    if dtype != jnp.float32:
        lines = [a + b + c for a, b, c in zip(lines[::3], lines[1::3], lines[2::3])]
    return [(lines[2 * r], lines[2 * r + 1]) for r in range(rows)]


def hint(size):
    return pl.CostEstimate(flops=0, bytes_accessed=size, transcendentals=0)


def dot(left, right, dims):
    return lax.dot_general(left, right, dims, preferred_element_type=jnp.float32)


def swap(x, axis, distance):
    size = lax.axis_size(axis)
    return lax.ppermute(x, axis, [(k, k ^ distance) for k in range(size)])


def distances(size):
    return [0] + list(range(size - 1, 0, -1))


def params(kibibytes):
    return pltpu.CompilerParams(vmem_limit_bytes=kibibytes << 10)


def head_rows(block, row, steps, heads):
    mine = block[row * steps : (row + 1) * steps]
    return jnp.concatenate([mine[:, h * HD : (h + 1) * HD] for h in range(heads)], axis=0)


def dequantize(codes_ref, scales_ref, out_ref):
    columns = scales_ref[...].astype(jnp.float32).T
    for n in range(columns.shape[1]):
        lanes = slice(n * BLK, (n + 1) * BLK)
        values = codes_ref[:, lanes].astype(jnp.float32) * columns[:, n : n + 1]
        out_ref[:, lanes] = values.astype(jnp.bfloat16)


def mate_weights(codes, scales):
    return pl.pallas_call(
        dequantize,
        out_shape=jax.ShapeDtypeStruct(codes.shape, jnp.bfloat16),
        in_specs=[VMEM, VMEM],
        out_specs=VMEM,
        compiler_params=params(WEIGHTS_KIB),
        cost_estimate=hint(1000),
        name="mate_weights",
    )(codes, scales.T)


def prepare_kernel(
    rows, steps, own, chunk,
    owner_hbm, lengths_hbm, scales_hbm, codes_hbm, query_hbm, cache_hbm, base_hbm,
    delta_ref, base_ref, own_query_ref, kept_ref, sent_ref,
    owner_ref, lengths_ref, scales_ref, codes_ref, query_ref, cache_ref, arrived,
):
    place = lax.axis_index("tensor")
    block = codes_ref.shape[0]
    cache_len = cache_ref.shape[0] // rows
    owner_load = pltpu.make_async_copy(owner_hbm, owner_ref, arrived.at[0])
    first_loads = [
        pltpu.make_async_copy(lengths_hbm, lengths_ref, arrived.at[1]),
        pltpu.make_async_copy(scales_hbm, scales_ref, arrived.at[2]),
        pltpu.make_async_copy(codes_hbm, codes_ref, arrived.at[3]),
        pltpu.make_async_copy(query_hbm, query_ref, arrived.at[4]),
    ]
    cache_loads = []
    for r in range(rows):
        here = pl.ds(r * cache_len, cache_len)
        cache_loads.append(
            pltpu.make_async_copy(cache_hbm.at[here], cache_ref.at[here], arrived.at[5 + r])
        )
    for load in [owner_load] + first_loads + cache_loads:
        load.start()
    owner_load.wait()
    base_loads = []
    for k in range(2):
        start = owner_ref[lax.axis_index("group") ^ k] * block
        here = pl.ds(pl.multiple_of(start, block), block)
        base_loads.append(
            pltpu.make_async_copy(base_hbm.at[here], base_ref.at[k], arrived.at[5 + rows + k])
        )
        base_loads[k].start()
    for load in first_loads:
        load.wait()
    dequantize(codes_ref, scales_ref, delta_ref)

    chunks = own // chunk
    height = chunk * steps
    width = chunks * HD
    position = lax.broadcasted_iota(jnp.int32, (cache_len, chunks * height), 0)

    def kv_lane(d):
        return pl.multiple_of(((place ^ d) * own // (H // KVH)) * HD, HD)

    def score(r, d):
        head = (place ^ d) * own
        queries = query_ref[:, pl.ds(pl.multiple_of(head * HD, HD), own * HD)]
        query = head_rows(queries.astype(jnp.float32), r, steps, own)
        if d == 0:
            at = r * chunks * height
            own_query_ref[at : at + chunks * height] = query.astype(jnp.bfloat16)
        spread = []
        for j in range(chunks):
            line = [jnp.zeros((height, HD), jnp.float32)] * chunks
            line[j] = query[j * height : (j + 1) * height]
            spread.append(jnp.concatenate(line, axis=1))
        spread = jnp.concatenate(spread, axis=0).astype(jnp.bfloat16)
        keys = cache_ref[pl.ds(r * cache_len, cache_len), pl.ds(kv_lane(d), width)]
        return dot(keys, spread, NT)

    units = [(r, d) for r in range(rows) for d in range(2 * kept_ref.shape[0])]
    stats = [[] for _ in range(2 * kept_ref.shape[0])]
    ahead = []
    for n in range(len(units) + 1):
        if n < len(units):
            if units[n][1] == 0:
                cache_loads[units[n][0]].wait()
            ahead.append(score(*units[n]))
        if n == 0:
            continue
        r, d = units[n - 1]
        at = r * chunks * height
        usable = position < lengths_ref[r] - place * cache_len
        scores = jnp.where(usable, ahead.pop(0) * SCORE_SCALE, 2.0 * NEGATIVE)
        peak = jnp.maximum(jnp.max(scores, axis=0, keepdims=True), NEGATIVE)
        weights = jnp.exp(scores - peak)
        total = jnp.sum(weights, axis=0, keepdims=True)
        lane = pl.ds(kv_lane(d) + KVH * HD, width)
        values = cache_ref[pl.ds(r * cache_len, cache_len), lane]
        sums = dot(weights.astype(jnp.bfloat16), values, TN)
        ref, index = (sent_ref if d % 2 else kept_ref), d // 2
        for j in range(chunks):
            here = slice(j * height, (j + 1) * height)
            mine = sums[here, j * HD : (j + 1) * HD].astype(ref.dtype)
            ref[index, at + j * height : at + (j + 1) * height] = mine
        stats[d] += [peak, total]
        if r == rows - 1:
            put_stats(ref, index, stats[d])
    for load in base_loads:
        load.wait()


def part_shape(count, height, dtype):
    return jax.ShapeDtypeStruct((count, height + stats_rows(dtype), LANES), dtype)


def prepare(owner_map, lengths, scales, codes, queries, cache, base, rows, steps, own, ways):
    height = rows * own * steps
    operands = [
        pltpu.with_memory_space_constraint(x, pltpu.HBM)
        for x in (owner_map, lengths, scales.T, codes, queries, cache, base)
    ]
    return pl.pallas_call(
        functools.partial(prepare_kernel, rows, steps, own, min(own, H // KVH)),
        out_shape=[
            jax.ShapeDtypeStruct(codes.shape, jnp.bfloat16),
            jax.ShapeDtypeStruct((2,) + codes.shape, jnp.bfloat16),
            jax.ShapeDtypeStruct((height, HD), jnp.bfloat16),
            part_shape(ways // 2, height, jnp.float32),
            part_shape(ways // 2, height, jnp.bfloat16),
        ],
        in_specs=[HBM] * len(operands),
        out_specs=[VMEM] * 5,
        scratch_shapes=[
            pltpu.SMEM(owner_map.shape, owner_map.dtype),
            pltpu.SMEM(lengths.shape, lengths.dtype),
            pltpu.VMEM(scales.shape[::-1], scales.dtype),
            pltpu.VMEM(codes.shape, codes.dtype),
            pltpu.VMEM(queries.shape, queries.dtype),
            pltpu.VMEM(cache.shape, cache.dtype),
            pltpu.SemaphoreType.DMA((7 + rows,)),
        ],
        compiler_params=params(CACHE_KIB),
        cost_estimate=hint(CACHE_HINT),
        name="prepare",
    )(*operands)


def merge_kernel(rows, span, kept_ref, came_ref, next_ref, sent_ref=None):
    for n in range(kept_ref.shape[0]):
        ref, index = (sent_ref if n % 2 else next_ref), n // 2
        stats, factors = [], []
        for one, two in zip(get_stats(kept_ref, n, rows), get_stats(came_ref, n, rows)):
            peak = jnp.maximum(one[0], two[0])
            scales = [jnp.exp(one[0] - peak), jnp.exp(two[0] - peak)]
            stats += [peak, one[1] * scales[0] + two[1] * scales[1]]
            factors += scales
        factors.append(jnp.zeros((SUBLANES - len(factors), LANES), jnp.float32))
        columns = jnp.concatenate(factors, axis=0).T[:span]
        for r in range(rows):
            here = slice(r * span, (r + 1) * span)
            left = kept_ref[n, here] * columns[:, 2 * r : 2 * r + 1]
            right = came_ref[n, here].astype(jnp.float32) * columns[:, 2 * r + 1 : 2 * r + 2]
            ref[index, here] = (left + right).astype(ref.dtype)
        put_stats(ref, index, stats)


def merge(kept, came, rows):
    count = kept.shape[0]
    height = kept.shape[1] - stats_rows(kept.dtype)
    shapes = [part_shape((count + 1) // 2, height, jnp.float32)]
    if count > 1:
        shapes.append(part_shape(count // 2, height, jnp.bfloat16))
    return pl.pallas_call(
        functools.partial(merge_kernel, rows, height // rows),
        out_shape=shapes,
        in_specs=[VMEM] * 2,
        out_specs=[VMEM] * len(shapes),
        compiler_params=params(8192),
        cost_estimate=hint(4 * kept.size),
        name="merge_partials",
    )(kept, came)


def project_kernel(pairs, own_ref, mate_ref, base_ref, *refs):
    tokens, outs = refs[:pairs], refs[pairs:]
    block = own_ref.shape[0]
    stacked = jnp.concatenate([ref[...] for ref in tokens], axis=0)
    count = tokens[0].shape[0]
    for k, delta_ref in enumerate((own_ref, mate_ref)):
        whole = dot(stacked, base_ref[k], NT) + dot(stacked, delta_ref[...], NT)
        for n in range(pairs):
            outs[n][:, k * block : (k + 1) * block] = whole[n * count : (n + 1) * count]


def project(own, mate, base, tokens):
    pairs = len(tokens)
    block = own.shape[0]
    count, width = tokens[0].shape
    return pl.pallas_call(
        functools.partial(project_kernel, pairs),
        out_shape=[jax.ShapeDtypeStruct((count, 2 * block), jnp.float32)] * pairs,
        in_specs=[VMEM] * (3 + pairs),
        out_specs=[VMEM] * pairs,
        compiler_params=params(PROJECT_KIB),
        cost_estimate=hint(PROJECT_HINT),
        name="project",
    )(own, mate, base, *tokens)


def pack_kernel(pairs, ways, near, wide, owner_ref, *refs):
    arrived, outs, ordered = refs[:pairs], refs[pairs : pairs + ways], refs[-1]
    place = lax.axis_index("group")
    to_place = lax.axis_index("tensor")
    shards, _, block = ordered.shape
    for piece, d in zip(arrived, distances(pairs)):
        for k in range(2):
            ordered[owner_ref[place ^ (2 * d + k)]] = piece[:, k * block : (k + 1) * block]
    for out, d in zip(outs, distances(ways)):
        to = to_place ^ d
        for n in range(near):
            out[:, n * block : (n + 1) * block] = ordered[to * near + n]
            at = (near + n) * block
            out[:, at : at + block] = ordered[shards // 2 + to * near + n]
        for n in range(wide):
            at = (2 * near + n) * block
            out[:, at : at + block] = ordered[to * wide + n]


def pack_pieces(owner_map, arrived, block, ways, near_width, slice_width):
    pairs = len(arrived)
    count = arrived[0].shape[0]
    shards = 2 * pairs
    kv_width = KVH * HD
    if block % LANES == 0 and near_width % block == 0 and slice_width % block == 0:
        piece = jax.ShapeDtypeStruct((count, 2 * near_width + slice_width), jnp.float32)
        kernel = functools.partial(
            pack_kernel, pairs, ways, near_width // block, slice_width // block
        )
        return pl.pallas_call(
            kernel,
            out_shape=[piece] * ways,
            in_specs=[SMEM] + [VMEM] * pairs,
            out_specs=[VMEM] * ways,
            scratch_shapes=[pltpu.VMEM((shards, count, block), jnp.float32)],
            compiler_params=params(8192),
            cost_estimate=hint(PACK_HINT),
            name="pack_pieces",
        )(owner_map, *arrived)
    nearest = [arrived[distances(pairs).index(d)] for d in range(pairs)]
    blocks = jnp.stack(nearest, axis=0).reshape(pairs, count, 2, block).transpose(0, 2, 1, 3)
    shard_of = jnp.zeros((shards,), jnp.int32).at[owner_map].set(
        jnp.arange(shards, dtype=jnp.int32)
    )
    taken = jnp.take(
        blocks.reshape(shards, count, block), shard_of ^ lax.axis_index("group"), axis=0
    )
    ordered = taken.transpose(1, 0, 2).reshape(count, shards * block)
    per_device = H // ways
    pieces = []
    for d in distances(ways):
        to = lax.axis_index("tensor") ^ d
        near = (to * per_device // (H // KVH)) * HD
        parts = [(near, near_width), (kv_width + near, near_width), (to * slice_width, slice_width)]
        cuts = [lax.dynamic_slice_in_dim(ordered, start, width, 1) for start, width in parts]
        pieces.append(jnp.concatenate(cuts, axis=1))
    return pieces


def finish_kernel(rows, steps, own, chunk, near_width, ways, query_ref, *refs):
    pieces, part = refs[:ways], refs[ways]
    new_ref, attended_ref = refs[ways + 1 :]
    chunks = own // chunk
    height = chunk * steps
    span = chunks * height
    summed = pieces[0][...]
    for piece in pieces[1:]:
        summed = summed + piece[...]
    stored = summed.astype(jnp.bfloat16)
    new_ref[...] = stored[:, 2 * near_width :]
    near = stored[:, : 2 * near_width].astype(jnp.float32)
    key_step = lax.broadcasted_iota(jnp.int32, (steps, span), 0)
    query_step = lax.broadcasted_iota(jnp.int32, (steps, span), 1) % steps
    causal = key_step <= query_step
    scores = []
    for r in range(rows):
        spread = []
        for j in range(chunks):
            line = [jnp.zeros((height, HD), jnp.bfloat16)] * chunks
            line[j] = query_ref[r * span + j * height : r * span + (j + 1) * height]
            spread.append(jnp.concatenate(line, axis=1))
        keys = near[r * steps : (r + 1) * steps, :near_width].astype(jnp.bfloat16)
        scores.append(dot(keys, jnp.concatenate(spread, axis=0), NT) * SCORE_SCALE)
    factors, near_sums = [], []
    for r, (cache_peak, cache_total) in enumerate(get_stats(part, 0, rows)):
        masked = jnp.where(causal, scores[r], NEGATIVE)
        peak = jnp.max(masked, axis=0, keepdims=True)
        weights = jnp.where(causal, jnp.exp(masked - peak), 0.0)
        total = jnp.sum(weights, axis=0, keepdims=True)
        values = near[r * steps : (r + 1) * steps, near_width:].astype(jnp.bfloat16)
        near_sums.append(dot(weights.astype(jnp.bfloat16), values, TN))
        cache_peak, cache_total = cache_peak[:, :span], cache_total[:, :span]
        top = jnp.maximum(peak, cache_peak)
        scales = [jnp.exp(cache_peak - top), jnp.exp(peak - top)]
        whole = cache_total * scales[0] + total * scales[1]
        factors += [scale / whole for scale in scales]
    factors.append(jnp.zeros((SUBLANES - len(factors), span), jnp.float32))
    columns = jnp.concatenate(factors, axis=0)
    if span < LANES:
        pad = jnp.zeros((SUBLANES, LANES - span), jnp.float32)
        columns = jnp.concatenate([columns, pad], axis=1)
    columns = columns.T
    for j in range(chunks):
        here = slice(j * height, (j + 1) * height)
        merged = []
        for r in range(rows):
            cached = part[0, r * span + j * height : r * span + (j + 1) * height]
            fresh = near_sums[r][here, j * HD : (j + 1) * HD]
            merged.append(
                cached * columns[here, 2 * r : 2 * r + 1]
                + fresh * columns[here, 2 * r + 1 : 2 * r + 2]
            )
        for h in range(chunk):
            both = [out[h * steps : (h + 1) * steps] for out in merged]
            lane = (j * chunk + h) * HD
            attended_ref[:, lane : lane + HD] = jnp.concatenate(both, axis=0).astype(jnp.bfloat16)


def finish(own_query, pieces, part, rows, steps, own, near_width):
    ways = len(pieces)
    count, width = pieces[0].shape
    return pl.pallas_call(
        functools.partial(
            finish_kernel, rows, steps, own, min(own, H // KVH), near_width, ways
        ),
        out_shape=[
            jax.ShapeDtypeStruct((count, width - 2 * near_width), jnp.bfloat16),
            jax.ShapeDtypeStruct((count, own * HD), jnp.bfloat16),
        ],
        in_specs=[VMEM] * (2 + ways),
        out_specs=[VMEM] * 2,
        compiler_params=params(8192),
        name="finish",
    )(own_query, *pieces, part)


def on_device(
    hidden_x, base_weight, delta_codes, delta_scales, owner_map, kv_cache, queries, lengths
):
    group_count = lax.axis_size("group")
    tensor_count = lax.axis_size("tensor")
    rows, steps, local_width = hidden_x.shape
    tokens = rows * steps
    owner_block = delta_codes.shape[0]
    heads_own = H // tensor_count
    slice_width = base_weight.shape[0] // tensor_count
    near_width = max(1, heads_own // (H // KVH)) * HD
    pairs = group_count // 2

    def exchange(arrays, axis, stride):
        places = distances(len(arrays))[1:]
        return [arrays[0]] + [swap(x, axis, stride * d) for x, d in zip(arrays[1:], places)]

    def near_first(arrays):
        return arrays[:1] + arrays[:0:-1]

    token_rows = exchange([hidden_x.reshape(tokens, local_width)] * pairs, "group", 2)
    mate_codes = swap(delta_codes, "group", 1)
    mate_scales = swap(delta_scales, "group", 1)

    own_delta, base_blocks, own_query, kept, sent = prepare(
        owner_map,
        lengths,
        delta_scales,
        delta_codes,
        queries.reshape(tokens, H * HD),
        kv_cache.reshape(-1, 2 * KVH * HD),
        base_weight,
        rows,
        steps,
        heads_own,
        tensor_count,
    )
    mate_delta = mate_weights(mate_codes, mate_scales)
    behind = lax.optimization_barrier((*near_first(token_rows), mate_delta, sent))
    token_rows, mate_delta, sent = near_first(list(behind[:pairs])), behind[-2], behind[-1]
    projected = project(own_delta, mate_delta, base_blocks, near_first(token_rows))
    step = 1
    while step < tensor_count:
        came = swap(sent, "tensor", step)
        kept, *sent = merge(kept, came, rows)
        sent = sent[0] if sent else None
        step *= 2
    arrived = exchange(near_first(projected), "group", 2)
    pieces = pack_pieces(owner_map, arrived, owner_block, tensor_count, near_width, slice_width)
    pieces = exchange(pieces, "tensor", 1)
    new_out, attended = finish(own_query, pieces, kept, rows, steps, heads_own, near_width)
    return (new_out.reshape(rows, steps, -1), attended.reshape(rows, steps, -1))


def solution(mesh):
    in_specs = (
        P("group", None, "tensor"),
        P(None, "tensor"),
        P("group", "tensor"),
        P("group", "tensor"),
        P(),
        P("group", "tensor", None),
        P("group", None, None),
        P("group"),
    )
    out_specs = (P("group", None, "tensor"), P("group", None, "tensor"))
    return jax.shard_map(
        on_device, mesh=mesh, in_specs=in_specs, out_specs=out_specs, check_vma=False
    )
```

```python
import functools
import jax
import jax.numpy as jnp
from jax import lax
from jax.experimental import pallas as pl
from jax.experimental.pallas import tpu as pltpu
from jax.sharding import PartitionSpec as P

H = 64
KVH = 8
HD = 128
BLK = 128
LANES = 128
SUBLANES = 8


NEGATIVE = -1e30
SCORE_SCALE = HD ** (-0.5)
CACHE_HINT = 120_000_000
PROJECT_HINT = 60_000_000
PACK_HINT = 60_000_000
CACHE_KIB = 24 << 10
WEIGHTS_KIB = 16 << 10
PROJECT_KIB = 16 << 10
NT = (((1,), (1,)), ((), ()))
TN = (((0,), (0,)), ((), ()))
VMEM = pl.BlockSpec(memory_space=pltpu.VMEM)
SMEM = pl.BlockSpec(memory_space=pltpu.SMEM)
HBM = pl.BlockSpec(memory_space=pltpu.HBM)


def split(x):
    high = x.astype(jnp.bfloat16).astype(jnp.float32)
    middle = (x - high).astype(jnp.bfloat16).astype(jnp.float32)
    return [high, middle, x - high - middle]


def stats_rows(dtype):
    return SUBLANES if dtype == jnp.float32 else 2 * SUBLANES


def put_stats(ref, index, stats):
    dtype = ref.dtype
    lines = [x for one in stats for x in ([one] if dtype == jnp.float32 else split(one))]
    lanes = lines[0].shape[1]
    count = stats_rows(dtype)
    lines.append(jnp.zeros((count - len(lines), lanes), jnp.float32))
    tile = jnp.concatenate(lines, axis=0)
    if lanes < LANES:
        tile = jnp.concatenate([tile, jnp.zeros((count, LANES - lanes), jnp.float32)], axis=1)
    ref[index, ref.shape[1] - count :] = tile.astype(dtype)


def get_stats(ref, index, rows):
    dtype = ref.dtype
    tile = ref[index, ref.shape[1] - stats_rows(dtype) :].astype(jnp.float32)
    lines = [tile[n : n + 1] for n in range(2 * rows * (1 if dtype == jnp.float32 else 3))]
    if dtype != jnp.float32:
        lines = [a + b + c for a, b, c in zip(lines[::3], lines[1::3], lines[2::3])]
    return [(lines[2 * r], lines[2 * r + 1]) for r in range(rows)]


def hint(size):
    return pl.CostEstimate(flops=0, bytes_accessed=size, transcendentals=0)


def dot(left, right, dims):
    return lax.dot_general(left, right, dims, preferred_element_type=jnp.float32)


def swap(x, axis, distance):
    size = lax.axis_size(axis)
    return lax.ppermute(x, axis, [(k, k ^ distance) for k in range(size)])


def distances(size):
    return [0] + list(range(size - 1, 0, -1))


def params(kibibytes):
    return pltpu.CompilerParams(vmem_limit_bytes=kibibytes << 10)


def head_rows(block, row, steps, heads):
    mine = block[row * steps : (row + 1) * steps]
    return jnp.concatenate([mine[:, h * HD : (h + 1) * HD] for h in range(heads)], axis=0)


def dequantize(codes_ref, scales_ref, out_ref):
    columns = scales_ref[...].astype(jnp.float32).T
    for n in range(columns.shape[1]):
        lanes = slice(n * BLK, (n + 1) * BLK)
        values = codes_ref[:, lanes].astype(jnp.float32) * columns[:, n : n + 1]
        out_ref[:, lanes] = values.astype(jnp.bfloat16)


def mate_weights(codes, scales):
    return pl.pallas_call(
        dequantize,
        out_shape=jax.ShapeDtypeStruct(codes.shape, jnp.bfloat16),
        in_specs=[VMEM, VMEM],
        out_specs=VMEM,
        compiler_params=params(WEIGHTS_KIB),
        cost_estimate=hint(1000),
        name="mate_weights",
    )(codes, scales.T)


def prepare_kernel(
    rows, steps, own, chunk,
    owner_hbm, lengths_hbm, scales_hbm, codes_hbm, query_hbm, cache_hbm, base_hbm,
    delta_ref, base_ref, own_query_ref, kept_ref, sent_ref,
    owner_ref, lengths_ref, scales_ref, codes_ref, query_ref, cache_ref, arrived,
):
    place = lax.axis_index("tensor")
    block = codes_ref.shape[0]
    cache_len = cache_ref.shape[0] // rows
    owner_load = pltpu.make_async_copy(owner_hbm, owner_ref, arrived.at[0])
    first_loads = [
        pltpu.make_async_copy(lengths_hbm, lengths_ref, arrived.at[1]),
        pltpu.make_async_copy(scales_hbm, scales_ref, arrived.at[2]),
        pltpu.make_async_copy(codes_hbm, codes_ref, arrived.at[3]),
        pltpu.make_async_copy(query_hbm, query_ref, arrived.at[4]),
    ]
    cache_loads = []
    for r in range(rows):
        here = pl.ds(r * cache_len, cache_len)
        cache_loads.append(
            pltpu.make_async_copy(cache_hbm.at[here], cache_ref.at[here], arrived.at[5 + r])
        )
    for load in [owner_load] + first_loads + cache_loads:
        load.start()
    owner_load.wait()
    base_loads = []
    for k in range(2):
        start = owner_ref[lax.axis_index("group") ^ k] * block
        here = pl.ds(pl.multiple_of(start, block), block)
        base_loads.append(
            pltpu.make_async_copy(base_hbm.at[here], base_ref.at[k], arrived.at[5 + rows + k])
        )
        base_loads[k].start()
    for load in first_loads:
        load.wait()
    dequantize(codes_ref, scales_ref, delta_ref)

    chunks = own // chunk
    height = chunk * steps
    width = chunks * HD
    position = lax.broadcasted_iota(jnp.int32, (cache_len, chunks * height), 0)

    def kv_lane(d):
        return pl.multiple_of(((place ^ d) * own // (H // KVH)) * HD, HD)

    def score(r, d):
        head = (place ^ d) * own
        queries = query_ref[:, pl.ds(pl.multiple_of(head * HD, HD), own * HD)]
        query = head_rows(queries.astype(jnp.float32), r, steps, own)
        if d == 0:
            at = r * chunks * height
            own_query_ref[at : at + chunks * height] = query.astype(jnp.bfloat16)
        spread = []
        for j in range(chunks):
            line = [jnp.zeros((height, HD), jnp.float32)] * chunks
            line[j] = query[j * height : (j + 1) * height]
            spread.append(jnp.concatenate(line, axis=1))
        spread = jnp.concatenate(spread, axis=0).astype(jnp.bfloat16)
        keys = cache_ref[pl.ds(r * cache_len, cache_len), pl.ds(kv_lane(d), width)]
        return dot(keys, spread, NT)

    units = [(r, d) for r in range(rows) for d in range(2 * kept_ref.shape[0])]
    stats = [[] for _ in range(2 * kept_ref.shape[0])]
    ahead = []
    for n in range(len(units) + 1):
        if n < len(units):
            if units[n][1] == 0:
                cache_loads[units[n][0]].wait()
            ahead.append(score(*units[n]))
        if n == 0:
            continue
        r, d = units[n - 1]
        at = r * chunks * height
        usable = position < lengths_ref[r] - place * cache_len
        scores = jnp.where(usable, ahead.pop(0) * SCORE_SCALE, 2.0 * NEGATIVE)
        peak = jnp.maximum(jnp.max(scores, axis=0, keepdims=True), NEGATIVE)
        weights = jnp.exp(scores - peak)
        total = jnp.sum(weights, axis=0, keepdims=True)
        lane = pl.ds(kv_lane(d) + KVH * HD, width)
        values = cache_ref[pl.ds(r * cache_len, cache_len), lane]
        sums = dot(weights.astype(jnp.bfloat16), values, TN)
        ref, index = (sent_ref if d % 2 else kept_ref), d // 2
        for j in range(chunks):
            here = slice(j * height, (j + 1) * height)
            mine = sums[here, j * HD : (j + 1) * HD].astype(ref.dtype)
            ref[index, at + j * height : at + (j + 1) * height] = mine
        stats[d] += [peak, total]
        if r == rows - 1:
            put_stats(ref, index, stats[d])
    for load in base_loads:
        load.wait()


def part_shape(count, height, dtype):
    return jax.ShapeDtypeStruct((count, height + stats_rows(dtype), LANES), dtype)


def prepare(owner_map, lengths, scales, codes, queries, cache, base, rows, steps, own, ways):
    height = rows * own * steps
    operands = [
        pltpu.with_memory_space_constraint(x, pltpu.HBM)
        for x in (owner_map, lengths, scales.T, codes, queries, cache, base)
    ]
    return pl.pallas_call(
        functools.partial(prepare_kernel, rows, steps, own, min(own, H // KVH)),
        out_shape=[
            jax.ShapeDtypeStruct(codes.shape, jnp.bfloat16),
            jax.ShapeDtypeStruct((2,) + codes.shape, jnp.bfloat16),
            jax.ShapeDtypeStruct((height, HD), jnp.bfloat16),
            part_shape(ways // 2, height, jnp.float32),
            part_shape(ways // 2, height, jnp.bfloat16),
        ],
        in_specs=[HBM] * len(operands),
        out_specs=[VMEM] * 5,
        scratch_shapes=[
            pltpu.SMEM(owner_map.shape, owner_map.dtype),
            pltpu.SMEM(lengths.shape, lengths.dtype),
            pltpu.VMEM(scales.shape[::-1], scales.dtype),
            pltpu.VMEM(codes.shape, codes.dtype),
            pltpu.VMEM(queries.shape, queries.dtype),
            pltpu.VMEM(cache.shape, cache.dtype),
            pltpu.SemaphoreType.DMA((7 + rows,)),
        ],
        compiler_params=params(CACHE_KIB),
        cost_estimate=hint(CACHE_HINT),
        name="prepare",
    )(*operands)


def merge_kernel(rows, span, kept_ref, came_ref, next_ref, sent_ref=None):
    for n in range(kept_ref.shape[0]):
        ref, index = (sent_ref if n % 2 else next_ref), n // 2
        stats, factors = [], []
        for one, two in zip(get_stats(kept_ref, n, rows), get_stats(came_ref, n, rows)):
            peak = jnp.maximum(one[0], two[0])
            scales = [jnp.exp(one[0] - peak), jnp.exp(two[0] - peak)]
            stats += [peak, one[1] * scales[0] + two[1] * scales[1]]
            factors += scales
        factors.append(jnp.zeros((SUBLANES - len(factors), LANES), jnp.float32))
        columns = jnp.concatenate(factors, axis=0).T[:span]
        for r in range(rows):
            here = slice(r * span, (r + 1) * span)
            left = kept_ref[n, here] * columns[:, 2 * r : 2 * r + 1]
            right = came_ref[n, here].astype(jnp.float32) * columns[:, 2 * r + 1 : 2 * r + 2]
            ref[index, here] = (left + right).astype(ref.dtype)
        put_stats(ref, index, stats)


def merge(kept, came, rows):
    count = kept.shape[0]
    height = kept.shape[1] - stats_rows(kept.dtype)
    shapes = [part_shape((count + 1) // 2, height, jnp.float32)]
    if count > 1:
        shapes.append(part_shape(count // 2, height, jnp.bfloat16))
    return pl.pallas_call(
        functools.partial(merge_kernel, rows, height // rows),
        out_shape=shapes,
        in_specs=[VMEM] * 2,
        out_specs=[VMEM] * len(shapes),
        compiler_params=params(8192),
        cost_estimate=hint(4 * kept.size),
        name="merge_partials",
    )(kept, came)


def project_kernel(pairs, own_ref, mate_ref, base_ref, *refs):
    tokens, outs = refs[:pairs], refs[pairs:]
    block = own_ref.shape[0]
    stacked = jnp.concatenate([ref[...] for ref in tokens], axis=0)
    count = tokens[0].shape[0]
    for k, delta_ref in enumerate((own_ref, mate_ref)):
        whole = (dot(base_ref[k], stacked, NT) + dot(delta_ref[...], stacked, NT)).T
        for n in range(pairs):
            outs[n][:, k * block : (k + 1) * block] = whole[n * count : (n + 1) * count]


def project(own, mate, base, tokens):
    pairs = len(tokens)
    block = own.shape[0]
    count, width = tokens[0].shape
    return pl.pallas_call(
        functools.partial(project_kernel, pairs),
        out_shape=[jax.ShapeDtypeStruct((count, 2 * block), jnp.float32)] * pairs,
        in_specs=[VMEM] * (3 + pairs),
        out_specs=[VMEM] * pairs,
        compiler_params=params(PROJECT_KIB),
        cost_estimate=hint(PROJECT_HINT),
        name="project",
    )(own, mate, base, *tokens)


def pack_kernel(pairs, ways, near, wide, owner_ref, *refs):
    arrived, outs, ordered = refs[:pairs], refs[pairs : pairs + ways], refs[-1]
    place = lax.axis_index("group")
    to_place = lax.axis_index("tensor")
    shards, _, block = ordered.shape
    for piece, d in zip(arrived, distances(pairs)):
        for k in range(2):
            ordered[owner_ref[place ^ (2 * d + k)]] = piece[:, k * block : (k + 1) * block]
    def put(out, at, values):
        out[:, at : at + block] = values.astype(out.dtype)

    for out, d in zip(outs, distances(ways)):
        to = to_place ^ d
        for n in range(near):
            key = ordered[to * near + n]
            put(out, n * block, key)
            if d != 0:
                put(out, (near + n) * block, key - key.astype(out.dtype).astype(jnp.float32))
        start = out.shape[1] - (near + wide) * block
        for n in range(near):
            put(out, start + n * block, ordered[shards // 2 + to * near + n])
        for n in range(wide):
            put(out, start + (near + n) * block, ordered[to * wide + n])


def pack_pieces(owner_map, arrived, block, ways, near_width, slice_width):
    pairs = len(arrived)
    count = arrived[0].shape[0]
    shards = 2 * pairs
    kv_width = KVH * HD
    if block % LANES == 0 and near_width % block == 0 and slice_width % block == 0:
        piece = jax.ShapeDtypeStruct((count, 2 * near_width + slice_width), jnp.float32)
        sent = jax.ShapeDtypeStruct((count, 3 * near_width + slice_width), jnp.bfloat16)
        kernel = functools.partial(
            pack_kernel, pairs, ways, near_width // block, slice_width // block
        )
        return pl.pallas_call(
            kernel,
            out_shape=[piece] + [sent] * (ways - 1),
            in_specs=[SMEM] + [VMEM] * pairs,
            out_specs=[VMEM] * ways,
            scratch_shapes=[pltpu.VMEM((shards, count, block), jnp.float32)],
            compiler_params=params(8192),
            cost_estimate=hint(PACK_HINT),
            name="pack_pieces",
        )(owner_map, *arrived)
    nearest = [arrived[distances(pairs).index(d)] for d in range(pairs)]
    blocks = jnp.stack(nearest, axis=0).reshape(pairs, count, 2, block).transpose(0, 2, 1, 3)
    shard_of = jnp.zeros((shards,), jnp.int32).at[owner_map].set(
        jnp.arange(shards, dtype=jnp.int32)
    )
    taken = jnp.take(
        blocks.reshape(shards, count, block), shard_of ^ lax.axis_index("group"), axis=0
    )
    ordered = taken.transpose(1, 0, 2).reshape(count, shards * block)
    per_device = H // ways
    pieces = []
    for d in distances(ways):
        to = lax.axis_index("tensor") ^ d
        near = (to * per_device // (H // KVH)) * HD
        parts = [(near, near_width), (kv_width + near, near_width), (to * slice_width, slice_width)]
        cuts = [lax.dynamic_slice_in_dim(ordered, start, width, 1) for start, width in parts]
        if d != 0:
            rounded = [cut.astype(jnp.bfloat16) for cut in cuts]
            rest = (cuts[0] - rounded[0].astype(jnp.float32)).astype(jnp.bfloat16)
            cuts = [rounded[0], rest] + rounded[1:]
        pieces.append(jnp.concatenate(cuts, axis=1))
    return pieces


def finish_kernel(rows, steps, own, chunk, near_width, ways, query_ref, *refs):
    pieces, part = refs[:ways], refs[ways]
    new_ref, attended_ref = refs[ways + 1 :]
    chunks = own // chunk
    height = chunk * steps
    span = chunks * height
    summed = pieces[0][...]
    for piece in pieces[1:]:
        came = piece[...].astype(jnp.float32)
        keys = came[:, :near_width] + came[:, near_width : 2 * near_width]
        summed = summed + jnp.concatenate([keys, came[:, 2 * near_width :]], axis=1)
    stored = summed.astype(jnp.bfloat16)
    new_ref[...] = stored[:, 2 * near_width :]
    near = stored[:, : 2 * near_width].astype(jnp.float32)
    key_step = lax.broadcasted_iota(jnp.int32, (steps, span), 0)
    query_step = lax.broadcasted_iota(jnp.int32, (steps, span), 1) % steps
    causal = key_step <= query_step
    scores = []
    for r in range(rows):
        spread = []
        for j in range(chunks):
            line = [jnp.zeros((height, HD), jnp.bfloat16)] * chunks
            line[j] = query_ref[r * span + j * height : r * span + (j + 1) * height]
            spread.append(jnp.concatenate(line, axis=1))
        keys = near[r * steps : (r + 1) * steps, :near_width].astype(jnp.bfloat16)
        scores.append(dot(keys, jnp.concatenate(spread, axis=0), NT) * SCORE_SCALE)
    factors, near_sums = [], []
    for r, (cache_peak, cache_total) in enumerate(get_stats(part, 0, rows)):
        masked = jnp.where(causal, scores[r], NEGATIVE)
        peak = jnp.max(masked, axis=0, keepdims=True)
        weights = jnp.where(causal, jnp.exp(masked - peak), 0.0)
        total = jnp.sum(weights, axis=0, keepdims=True)
        values = near[r * steps : (r + 1) * steps, near_width:].astype(jnp.bfloat16)
        near_sums.append(dot(weights.astype(jnp.bfloat16), values, TN))
        cache_peak, cache_total = cache_peak[:, :span], cache_total[:, :span]
        top = jnp.maximum(peak, cache_peak)
        scales = [jnp.exp(cache_peak - top), jnp.exp(peak - top)]
        whole = cache_total * scales[0] + total * scales[1]
        factors += [scale / whole for scale in scales]
    factors.append(jnp.zeros((SUBLANES - len(factors), span), jnp.float32))
    columns = jnp.concatenate(factors, axis=0)
    if span < LANES:
        pad = jnp.zeros((SUBLANES, LANES - span), jnp.float32)
        columns = jnp.concatenate([columns, pad], axis=1)
    columns = columns.T
    for j in range(chunks):
        here = slice(j * height, (j + 1) * height)
        merged = []
        for r in range(rows):
            cached = part[0, r * span + j * height : r * span + (j + 1) * height]
            fresh = near_sums[r][here, j * HD : (j + 1) * HD]
            merged.append(
                cached * columns[here, 2 * r : 2 * r + 1]
                + fresh * columns[here, 2 * r + 1 : 2 * r + 2]
            )
        for h in range(chunk):
            both = [out[h * steps : (h + 1) * steps] for out in merged]
            lane = (j * chunk + h) * HD
            attended_ref[:, lane : lane + HD] = jnp.concatenate(both, axis=0).astype(jnp.bfloat16)


def finish(own_query, pieces, part, rows, steps, own, near_width):
    ways = len(pieces)
    count, width = pieces[0].shape
    return pl.pallas_call(
        functools.partial(
            finish_kernel, rows, steps, own, min(own, H // KVH), near_width, ways
        ),
        out_shape=[
            jax.ShapeDtypeStruct((count, width - 2 * near_width), jnp.bfloat16),
            jax.ShapeDtypeStruct((count, own * HD), jnp.bfloat16),
        ],
        in_specs=[VMEM] * (2 + ways),
        out_specs=[VMEM] * 2,
        compiler_params=params(8192),
        name="finish",
    )(own_query, *pieces, part)


def on_device(
    hidden_x, base_weight, delta_codes, delta_scales, owner_map, kv_cache, queries, lengths
):
    group_count = lax.axis_size("group")
    tensor_count = lax.axis_size("tensor")
    rows, steps, local_width = hidden_x.shape
    tokens = rows * steps
    owner_block = delta_codes.shape[0]
    heads_own = H // tensor_count
    slice_width = base_weight.shape[0] // tensor_count
    near_width = max(1, heads_own // (H // KVH)) * HD
    pairs = group_count // 2

    def exchange(arrays, axis, stride):
        places = distances(len(arrays))[1:]
        return [arrays[0]] + [swap(x, axis, stride * d) for x, d in zip(arrays[1:], places)]

    def near_first(arrays):
        return arrays[:1] + arrays[:0:-1]

    token_rows = exchange([hidden_x.reshape(tokens, local_width)] * pairs, "group", 2)
    mate_codes = swap(delta_codes, "group", 1)
    mate_scales = swap(delta_scales, "group", 1)

    own_delta, base_blocks, own_query, kept, sent = prepare(
        owner_map,
        lengths,
        delta_scales,
        delta_codes,
        queries.reshape(tokens, H * HD),
        kv_cache.reshape(-1, 2 * KVH * HD),
        base_weight,
        rows,
        steps,
        heads_own,
        tensor_count,
    )
    mate_delta = mate_weights(mate_codes, mate_scales)
    behind = lax.optimization_barrier((*near_first(token_rows), mate_delta, sent))
    token_rows, mate_delta, sent = near_first(list(behind[:pairs])), behind[-2], behind[-1]
    projected = project(own_delta, mate_delta, base_blocks, near_first(token_rows))
    step = 1
    while step < tensor_count:
        came = swap(sent, "tensor", step)
        kept, *sent = merge(kept, came, rows)
        sent = sent[0] if sent else None
        step *= 2
    arrived = exchange(near_first(projected), "group", 2)
    pieces = pack_pieces(owner_map, arrived, owner_block, tensor_count, near_width, slice_width)
    pieces = exchange(pieces, "tensor", 1)
    new_out, attended = finish(own_query, pieces, kept, rows, steps, heads_own, near_width)
    return (new_out.reshape(rows, steps, -1), attended.reshape(rows, steps, -1))


def solution(mesh):
    in_specs = (
        P("group", None, "tensor"),
        P(None, "tensor"),
        P("group", "tensor"),
        P("group", "tensor"),
        P(),
        P("group", "tensor", None),
        P("group", None, None),
        P("group"),
    )
    out_specs = (P("group", None, "tensor"), P("group", None, "tensor"))
    return jax.shard_map(
        on_device, mesh=mesh, in_specs=in_specs, out_specs=out_specs, check_vma=False
    )
```

```python
import functools
import jax
import jax.numpy as jnp
from jax import lax
from jax.experimental import pallas as pl
from jax.experimental.pallas import tpu as pltpu
from jax.sharding import PartitionSpec as P

H = 64
KVH = 8
HD = 128
BLK = 128
LANES = 128
SUBLANES = 8


NEGATIVE = -1e30
SCORE_SCALE = HD ** (-0.5)
CACHE_HINT = 120_000_000
PROJECT_HINT = 60_000_000
PACK_HINT = 60_000_000
CACHE_KIB = 24 << 10
WEIGHTS_KIB = 16 << 10
PROJECT_KIB = 16 << 10
NT = (((1,), (1,)), ((), ()))
TN = (((0,), (0,)), ((), ()))
VMEM = pl.BlockSpec(memory_space=pltpu.VMEM)
SMEM = pl.BlockSpec(memory_space=pltpu.SMEM)
HBM = pl.BlockSpec(memory_space=pltpu.HBM)


def split(x):
    high = x.astype(jnp.bfloat16).astype(jnp.float32)
    middle = (x - high).astype(jnp.bfloat16).astype(jnp.float32)
    return [high, middle, x - high - middle]


def stats_rows(dtype):
    return SUBLANES if dtype == jnp.float32 else 2 * SUBLANES


def put_stats(ref, stats):
    dtype = ref.dtype
    lines = [x for one in stats for x in ([one] if dtype == jnp.float32 else split(one))]
    lanes = lines[0].shape[1]
    count = stats_rows(dtype)
    lines.append(jnp.zeros((count - len(lines), lanes), jnp.float32))
    tile = jnp.concatenate(lines, axis=0)
    if lanes < LANES:
        tile = jnp.concatenate([tile, jnp.zeros((count, LANES - lanes), jnp.float32)], axis=1)
    ref[ref.shape[0] - count :] = tile.astype(dtype)


def get_stats(ref, rows):
    dtype = ref.dtype
    tile = ref[ref.shape[0] - stats_rows(dtype) :].astype(jnp.float32)
    lines = [tile[n : n + 1] for n in range(2 * rows * (1 if dtype == jnp.float32 else 3))]
    if dtype != jnp.float32:
        lines = [a + b + c for a, b, c in zip(lines[::3], lines[1::3], lines[2::3])]
    return [(lines[2 * r], lines[2 * r + 1]) for r in range(rows)]


def hint(size):
    return pl.CostEstimate(flops=0, bytes_accessed=size, transcendentals=0)


def dot(left, right, dims):
    return lax.dot_general(left, right, dims, preferred_element_type=jnp.float32)


def swap(x, axis, distance):
    size = lax.axis_size(axis)
    return lax.ppermute(x, axis, [(k, k ^ distance) for k in range(size)])


def distances(size):
    return [0] + list(range(size - 1, 0, -1))


def params(kibibytes):
    return pltpu.CompilerParams(vmem_limit_bytes=kibibytes << 10)


def head_rows(block, row, steps, heads):
    mine = block[row * steps : (row + 1) * steps]
    return jnp.concatenate([mine[:, h * HD : (h + 1) * HD] for h in range(heads)], axis=0)


def dequantize(codes_ref, scales_ref, out_ref):
    columns = scales_ref[...].astype(jnp.float32).T
    for n in range(columns.shape[1]):
        lanes = slice(n * BLK, (n + 1) * BLK)
        values = codes_ref[:, lanes].astype(jnp.float32) * columns[:, n : n + 1]
        out_ref[:, lanes] = values.astype(jnp.bfloat16)


def mate_weights(codes, scales):
    return pl.pallas_call(
        dequantize,
        out_shape=jax.ShapeDtypeStruct(codes.shape, jnp.bfloat16),
        in_specs=[VMEM, VMEM],
        out_specs=VMEM,
        compiler_params=params(WEIGHTS_KIB),
        cost_estimate=hint(1000),
        name="mate_weights",
    )(codes, scales.T)


def prepare_kernel(
    rows, steps, own, chunk,
    owner_hbm, lengths_hbm, scales_hbm, codes_hbm, query_hbm, cache_hbm, base_hbm,
    *refs,
):
    delta_ref, base_ref, own_query_ref, parts = refs[0], refs[1], refs[2], refs[3:-7]
    owner_ref, lengths_ref, scales_ref, codes_ref, query_ref, cache_ref, arrived = refs[-7:]
    order = distances(len(parts))
    place = lax.axis_index("tensor")
    block = codes_ref.shape[0]
    cache_len = cache_ref.shape[0] // rows
    owner_load = pltpu.make_async_copy(owner_hbm, owner_ref, arrived.at[0])
    first_loads = [
        pltpu.make_async_copy(lengths_hbm, lengths_ref, arrived.at[1]),
        pltpu.make_async_copy(scales_hbm, scales_ref, arrived.at[2]),
        pltpu.make_async_copy(codes_hbm, codes_ref, arrived.at[3]),
        pltpu.make_async_copy(query_hbm, query_ref, arrived.at[4]),
    ]
    cache_loads = []
    for r in range(rows):
        here = pl.ds(r * cache_len, cache_len)
        cache_loads.append(
            pltpu.make_async_copy(cache_hbm.at[here], cache_ref.at[here], arrived.at[5 + r])
        )
    for load in [owner_load] + first_loads + cache_loads:
        load.start()
    owner_load.wait()
    base_loads = []
    for k in range(2):
        start = owner_ref[lax.axis_index("group") ^ k] * block
        here = pl.ds(pl.multiple_of(start, block), block)
        base_loads.append(
            pltpu.make_async_copy(base_hbm.at[here], base_ref.at[k], arrived.at[5 + rows + k])
        )
        base_loads[k].start()
    for load in first_loads:
        load.wait()
    dequantize(codes_ref, scales_ref, delta_ref)

    chunks = own // chunk
    height = chunk * steps
    width = chunks * HD
    position = lax.broadcasted_iota(jnp.int32, (cache_len, chunks * height), 0)

    def kv_lane(d):
        return pl.multiple_of(((place ^ d) * own // (H // KVH)) * HD, HD)

    def score(r, d):
        head = (place ^ d) * own
        queries = query_ref[:, pl.ds(pl.multiple_of(head * HD, HD), own * HD)]
        query = head_rows(queries.astype(jnp.float32), r, steps, own)
        if d == 0:
            at = r * chunks * height
            own_query_ref[at : at + chunks * height] = query.astype(jnp.bfloat16)
        spread = []
        for j in range(chunks):
            line = [jnp.zeros((height, HD), jnp.float32)] * chunks
            line[j] = query[j * height : (j + 1) * height]
            spread.append(jnp.concatenate(line, axis=1))
        spread = jnp.concatenate(spread, axis=0).astype(jnp.bfloat16)
        keys = cache_ref[pl.ds(r * cache_len, cache_len), pl.ds(kv_lane(d), width)]
        return dot(keys, spread, NT)

    units = [(r, n) for r in range(rows) for n in range(len(parts))]
    stats = [[] for _ in parts]
    ahead = []
    for at in range(len(units) + 1):
        if at < len(units):
            r, n = units[at]
            if n == 0:
                cache_loads[r].wait()
            ahead.append(score(r, order[n]))
        if at == 0:
            continue
        r, n = units[at - 1]
        usable = position < lengths_ref[r] - place * cache_len
        scores = jnp.where(usable, ahead.pop(0) * SCORE_SCALE, 2.0 * NEGATIVE)
        peak = jnp.maximum(jnp.max(scores, axis=0, keepdims=True), NEGATIVE)
        weights = jnp.exp(scores - peak)
        total = jnp.sum(weights, axis=0, keepdims=True)
        lane = pl.ds(kv_lane(order[n]) + KVH * HD, width)
        values = cache_ref[pl.ds(r * cache_len, cache_len), lane]
        sums = dot(weights.astype(jnp.bfloat16), values, TN)
        for j in range(chunks):
            here = slice(j * height, (j + 1) * height)
            first = (r * chunks + j) * height
            mine = sums[here, j * HD : (j + 1) * HD].astype(parts[n].dtype)
            parts[n][first : first + height] = mine
        stats[n] += [peak, total]
        if r == rows - 1:
            put_stats(parts[n], stats[n])
    for load in base_loads:
        load.wait()


def part_shape(height, dtype):
    return jax.ShapeDtypeStruct((height + stats_rows(dtype), LANES), dtype)


def prepare(owner_map, lengths, scales, codes, queries, cache, base, rows, steps, own, ways):
    height = rows * own * steps
    operands = [
        pltpu.with_memory_space_constraint(x, pltpu.HBM)
        for x in (owner_map, lengths, scales.T, codes, queries, cache, base)
    ]
    out = pl.pallas_call(
        functools.partial(prepare_kernel, rows, steps, own, min(own, H // KVH)),
        out_shape=[
            jax.ShapeDtypeStruct(codes.shape, jnp.bfloat16),
            jax.ShapeDtypeStruct((2,) + codes.shape, jnp.bfloat16),
            jax.ShapeDtypeStruct((height, HD), jnp.bfloat16),
            part_shape(height, jnp.float32),
        ]
        + [part_shape(height, jnp.bfloat16)] * (ways - 1),
        in_specs=[HBM] * len(operands),
        out_specs=[VMEM] * (3 + ways),
        scratch_shapes=[
            pltpu.SMEM(owner_map.shape, owner_map.dtype),
            pltpu.SMEM(lengths.shape, lengths.dtype),
            pltpu.VMEM(scales.shape[::-1], scales.dtype),
            pltpu.VMEM(codes.shape, codes.dtype),
            pltpu.VMEM(queries.shape, queries.dtype),
            pltpu.VMEM(cache.shape, cache.dtype),
            pltpu.SemaphoreType.DMA((7 + rows,)),
        ],
        compiler_params=params(CACHE_KIB),
        cost_estimate=hint(CACHE_HINT),
        name="prepare",
    )(*operands)
    return out[0], out[1], out[2], out[3:]


def merge_kernel(rows, span, *refs):
    parts, out_ref = refs[:-1], refs[-1]
    everything = [get_stats(part, rows) for part in parts]
    stats, factors = [], []
    for r in range(rows):
        peak = functools.reduce(jnp.maximum, [one[r][0] for one in everything])
        scales = [jnp.exp(one[r][0] - peak) for one in everything]
        stats += [peak, sum(one[r][1] * scale for one, scale in zip(everything, scales))]
        factors += scales
    lines = -(-len(factors) // SUBLANES) * SUBLANES
    if lines > len(factors):
        factors.append(jnp.zeros((lines - len(factors), LANES), jnp.float32))
    columns = jnp.concatenate(factors, axis=0).T[:span]
    for r in range(rows):
        here = slice(r * span, (r + 1) * span)
        terms = []
        for n, part in enumerate(parts):
            at = r * len(parts) + n
            terms.append(part[here].astype(jnp.float32) * columns[:, at : at + 1])
        out_ref[here] = sum(terms[1:], terms[0])
    put_stats(out_ref, stats)


def merge(parts, rows):
    height = parts[0].shape[0] - stats_rows(parts[0].dtype)
    return pl.pallas_call(
        functools.partial(merge_kernel, rows, height // rows),
        out_shape=part_shape(height, jnp.float32),
        in_specs=[VMEM] * len(parts),
        out_specs=VMEM,
        compiler_params=params(8192),
        cost_estimate=hint(1000),
        name="merge_partials",
    )(*parts)


def project_kernel(pairs, own_ref, mate_ref, base_ref, *refs):
    tokens, outs = refs[:pairs], refs[pairs:]
    block = own_ref.shape[0]
    stacked = jnp.concatenate([ref[...] for ref in tokens], axis=0)
    count = tokens[0].shape[0]
    for k, delta_ref in enumerate((own_ref, mate_ref)):
        whole = (dot(base_ref[k], stacked, NT) + dot(delta_ref[...], stacked, NT)).T
        for n in range(pairs):
            outs[n][:, k * block : (k + 1) * block] = whole[n * count : (n + 1) * count]


def project(own, mate, base, tokens):
    pairs = len(tokens)
    block = own.shape[0]
    count, width = tokens[0].shape
    return pl.pallas_call(
        functools.partial(project_kernel, pairs),
        out_shape=[jax.ShapeDtypeStruct((count, 2 * block), jnp.float32)] * pairs,
        in_specs=[VMEM] * (3 + pairs),
        out_specs=[VMEM] * pairs,
        compiler_params=params(PROJECT_KIB),
        cost_estimate=hint(PROJECT_HINT),
        name="project",
    )(own, mate, base, *tokens)


def pack_kernel(pairs, ways, near, wide, owner_ref, *refs):
    arrived, outs, ordered = refs[:pairs], refs[pairs : pairs + ways], refs[-1]
    place = lax.axis_index("group")
    to_place = lax.axis_index("tensor")
    shards, _, block = ordered.shape
    for piece, d in zip(arrived, distances(pairs)):
        for k in range(2):
            ordered[owner_ref[place ^ (2 * d + k)]] = piece[:, k * block : (k + 1) * block]
    def put(out, at, values):
        out[:, at : at + block] = values.astype(out.dtype)

    for out, d in zip(outs, distances(ways)):
        to = to_place ^ d
        for n in range(near):
            key = ordered[to * near + n]
            put(out, n * block, key)
            if d != 0:
                put(out, (near + n) * block, key - key.astype(out.dtype).astype(jnp.float32))
        start = out.shape[1] - (near + wide) * block
        for n in range(near):
            put(out, start + n * block, ordered[shards // 2 + to * near + n])
        for n in range(wide):
            put(out, start + (near + n) * block, ordered[to * wide + n])


def pack_pieces(owner_map, arrived, block, ways, near_width, slice_width):
    pairs = len(arrived)
    count = arrived[0].shape[0]
    shards = 2 * pairs
    kv_width = KVH * HD
    if block % LANES == 0 and near_width % block == 0 and slice_width % block == 0:
        piece = jax.ShapeDtypeStruct((count, 2 * near_width + slice_width), jnp.float32)
        sent = jax.ShapeDtypeStruct((count, 3 * near_width + slice_width), jnp.bfloat16)
        kernel = functools.partial(
            pack_kernel, pairs, ways, near_width // block, slice_width // block
        )
        return pl.pallas_call(
            kernel,
            out_shape=[piece] + [sent] * (ways - 1),
            in_specs=[SMEM] + [VMEM] * pairs,
            out_specs=[VMEM] * ways,
            scratch_shapes=[pltpu.VMEM((shards, count, block), jnp.float32)],
            compiler_params=params(8192),
            cost_estimate=hint(PACK_HINT),
            name="pack_pieces",
        )(owner_map, *arrived)
    nearest = [arrived[distances(pairs).index(d)] for d in range(pairs)]
    blocks = jnp.stack(nearest, axis=0).reshape(pairs, count, 2, block).transpose(0, 2, 1, 3)
    shard_of = jnp.zeros((shards,), jnp.int32).at[owner_map].set(
        jnp.arange(shards, dtype=jnp.int32)
    )
    taken = jnp.take(
        blocks.reshape(shards, count, block), shard_of ^ lax.axis_index("group"), axis=0
    )
    ordered = taken.transpose(1, 0, 2).reshape(count, shards * block)
    per_device = H // ways
    pieces = []
    for d in distances(ways):
        to = lax.axis_index("tensor") ^ d
        near = (to * per_device // (H // KVH)) * HD
        parts = [(near, near_width), (kv_width + near, near_width), (to * slice_width, slice_width)]
        cuts = [lax.dynamic_slice_in_dim(ordered, start, width, 1) for start, width in parts]
        if d != 0:
            rounded = [cut.astype(jnp.bfloat16) for cut in cuts]
            rest = (cuts[0] - rounded[0].astype(jnp.float32)).astype(jnp.bfloat16)
            cuts = [rounded[0], rest] + rounded[1:]
        pieces.append(jnp.concatenate(cuts, axis=1))
    return pieces


def finish_kernel(rows, steps, own, chunk, near_width, ways, query_ref, *refs):
    pieces, part = refs[:ways], refs[ways]
    new_ref, attended_ref = refs[ways + 1 :]
    chunks = own // chunk
    height = chunk * steps
    span = chunks * height
    summed = pieces[0][...]
    for piece in pieces[1:]:
        came = piece[...].astype(jnp.float32)
        keys = came[:, :near_width] + came[:, near_width : 2 * near_width]
        summed = summed + jnp.concatenate([keys, came[:, 2 * near_width :]], axis=1)
    stored = summed.astype(jnp.bfloat16)
    new_ref[...] = stored[:, 2 * near_width :]
    near = stored[:, : 2 * near_width].astype(jnp.float32)
    key_step = lax.broadcasted_iota(jnp.int32, (steps, span), 0)
    query_step = lax.broadcasted_iota(jnp.int32, (steps, span), 1) % steps
    causal = key_step <= query_step
    scores = []
    for r in range(rows):
        spread = []
        for j in range(chunks):
            line = [jnp.zeros((height, HD), jnp.bfloat16)] * chunks
            line[j] = query_ref[r * span + j * height : r * span + (j + 1) * height]
            spread.append(jnp.concatenate(line, axis=1))
        keys = near[r * steps : (r + 1) * steps, :near_width].astype(jnp.bfloat16)
        scores.append(dot(keys, jnp.concatenate(spread, axis=0), NT) * SCORE_SCALE)
    factors, near_sums = [], []
    for r, (cache_peak, cache_total) in enumerate(get_stats(part, rows)):
        masked = jnp.where(causal, scores[r], NEGATIVE)
        peak = jnp.max(masked, axis=0, keepdims=True)
        weights = jnp.where(causal, jnp.exp(masked - peak), 0.0)
        total = jnp.sum(weights, axis=0, keepdims=True)
        values = near[r * steps : (r + 1) * steps, near_width:].astype(jnp.bfloat16)
        near_sums.append(dot(weights.astype(jnp.bfloat16), values, TN))
        cache_peak, cache_total = cache_peak[:, :span], cache_total[:, :span]
        top = jnp.maximum(peak, cache_peak)
        scales = [jnp.exp(cache_peak - top), jnp.exp(peak - top)]
        whole = cache_total * scales[0] + total * scales[1]
        factors += [scale / whole for scale in scales]
    factors.append(jnp.zeros((SUBLANES - len(factors), span), jnp.float32))
    columns = jnp.concatenate(factors, axis=0)
    if span < LANES:
        pad = jnp.zeros((SUBLANES, LANES - span), jnp.float32)
        columns = jnp.concatenate([columns, pad], axis=1)
    columns = columns.T
    for j in range(chunks):
        here = slice(j * height, (j + 1) * height)
        merged = []
        for r in range(rows):
            cached = part[r * span + j * height : r * span + (j + 1) * height]
            fresh = near_sums[r][here, j * HD : (j + 1) * HD]
            merged.append(
                cached * columns[here, 2 * r : 2 * r + 1]
                + fresh * columns[here, 2 * r + 1 : 2 * r + 2]
            )
        for h in range(chunk):
            both = [out[h * steps : (h + 1) * steps] for out in merged]
            lane = (j * chunk + h) * HD
            attended_ref[:, lane : lane + HD] = jnp.concatenate(both, axis=0).astype(jnp.bfloat16)


def finish(own_query, pieces, part, rows, steps, own, near_width):
    ways = len(pieces)
    count, width = pieces[0].shape
    return pl.pallas_call(
        functools.partial(
            finish_kernel, rows, steps, own, min(own, H // KVH), near_width, ways
        ),
        out_shape=[
            jax.ShapeDtypeStruct((count, width - 2 * near_width), jnp.bfloat16),
            jax.ShapeDtypeStruct((count, own * HD), jnp.bfloat16),
        ],
        in_specs=[VMEM] * (2 + ways),
        out_specs=[VMEM] * 2,
        compiler_params=params(8192),
        name="finish",
    )(own_query, *pieces, part)


def on_device(
    hidden_x, base_weight, delta_codes, delta_scales, owner_map, kv_cache, queries, lengths
):
    group_count = lax.axis_size("group")
    tensor_count = lax.axis_size("tensor")
    rows, steps, local_width = hidden_x.shape
    tokens = rows * steps
    owner_block = delta_codes.shape[0]
    heads_own = H // tensor_count
    slice_width = base_weight.shape[0] // tensor_count
    near_width = max(1, heads_own // (H // KVH)) * HD
    pairs = group_count // 2

    def exchange(arrays, axis, stride):
        places = distances(len(arrays))[1:]
        return [arrays[0]] + [swap(x, axis, stride * d) for x, d in zip(arrays[1:], places)]

    def near_first(arrays):
        return arrays[:1] + arrays[:0:-1]

    token_rows = exchange([hidden_x.reshape(tokens, local_width)] * pairs, "group", 2)
    mate_codes = swap(delta_codes, "group", 1)
    mate_scales = swap(delta_scales, "group", 1)

    own_delta, base_blocks, own_query, partials = prepare(
        owner_map,
        lengths,
        delta_scales,
        delta_codes,
        queries.reshape(tokens, H * HD),
        kv_cache.reshape(-1, 2 * KVH * HD),
        base_weight,
        rows,
        steps,
        heads_own,
        tensor_count,
    )
    mate_delta = mate_weights(mate_codes, mate_scales)
    behind = lax.optimization_barrier((*near_first(token_rows), mate_delta, own_query))
    token_rows, mate_delta, own_query = near_first(list(behind[:pairs])), behind[-2], behind[-1]
    projected = project(own_delta, mate_delta, base_blocks, near_first(token_rows))
    arrived = exchange(near_first(projected), "group", 2)
    partials = exchange(partials, "tensor", 1)
    pieces = pack_pieces(owner_map, arrived, owner_block, tensor_count, near_width, slice_width)
    pieces = exchange(pieces, "tensor", 1)
    partial = merge(near_first(partials), rows)
    new_out, attended = finish(own_query, pieces, partial, rows, steps, heads_own, near_width)
    return (new_out.reshape(rows, steps, -1), attended.reshape(rows, steps, -1))


def solution(mesh):
    in_specs = (
        P("group", None, "tensor"),
        P(None, "tensor"),
        P("group", "tensor"),
        P("group", "tensor"),
        P(),
        P("group", "tensor", None),
        P("group", None, None),
        P("group"),
    )
    out_specs = (P("group", None, "tensor"), P("group", None, "tensor"))
    return jax.shard_map(
        on_device, mesh=mesh, in_specs=in_specs, out_specs=out_specs, check_vma=False
    )
```

```python
import functools
import jax
import jax.numpy as jnp
from jax import lax
from jax.experimental import pallas as pl
from jax.experimental.pallas import tpu as pltpu
from jax.sharding import PartitionSpec as P

H = 64
KVH = 8
HD = 128
BLK = 128
LANES = 128
SUBLANES = 8


NEGATIVE = -1e30
SCORE_SCALE = HD ** (-0.5)
PART = 64
CACHE_HINT = 120_000_000
PROJECT_HINT = 60_000_000
PACK_HINT = 60_000_000
CACHE_KIB = 24 << 10
WEIGHTS_KIB = 16 << 10
PROJECT_KIB = 16 << 10
NT = (((1,), (1,)), ((), ()))
TN = (((0,), (0,)), ((), ()))
VMEM = pl.BlockSpec(memory_space=pltpu.VMEM)
SMEM = pl.BlockSpec(memory_space=pltpu.SMEM)
HBM = pl.BlockSpec(memory_space=pltpu.HBM)


def split(x):
    high = x.astype(jnp.bfloat16).astype(jnp.float32)
    middle = (x - high).astype(jnp.bfloat16).astype(jnp.float32)
    return [high, middle, x - high - middle]


def stats_rows(dtype):
    return SUBLANES if dtype == jnp.float32 else 2 * SUBLANES


def put_stats(ref, stats):
    dtype = ref.dtype
    lines = [x for one in stats for x in ([one] if dtype == jnp.float32 else split(one))]
    lanes = lines[0].shape[1]
    count = stats_rows(dtype)
    lines.append(jnp.zeros((count - len(lines), lanes), jnp.float32))
    tile = jnp.concatenate(lines, axis=0)
    if lanes < LANES:
        tile = jnp.concatenate([tile, jnp.zeros((count, LANES - lanes), jnp.float32)], axis=1)
    ref[ref.shape[0] - count :] = tile.astype(dtype)


def get_stats(ref, rows):
    dtype = ref.dtype
    tile = ref[ref.shape[0] - stats_rows(dtype) :].astype(jnp.float32)
    lines = [tile[n : n + 1] for n in range(2 * rows * (1 if dtype == jnp.float32 else 3))]
    if dtype != jnp.float32:
        lines = [a + b + c for a, b, c in zip(lines[::3], lines[1::3], lines[2::3])]
    return [(lines[2 * r], lines[2 * r + 1]) for r in range(rows)]


def hint(size):
    return pl.CostEstimate(flops=0, bytes_accessed=size, transcendentals=0)


def dot(left, right, dims):
    return lax.dot_general(left, right, dims, preferred_element_type=jnp.float32)


def swap(x, axis, distance):
    size = lax.axis_size(axis)
    return lax.ppermute(x, axis, [(k, k ^ distance) for k in range(size)])


def distances(size):
    return [0] + list(range(size - 1, 0, -1))


def params(kibibytes):
    return pltpu.CompilerParams(vmem_limit_bytes=kibibytes << 10)


def head_rows(block, row, steps, heads):
    mine = block[row * steps : (row + 1) * steps]
    return jnp.concatenate([mine[:, h * HD : (h + 1) * HD] for h in range(heads)], axis=0)


def dequantize(codes_ref, scales_ref, out_ref):
    columns = scales_ref[...].astype(jnp.float32).T
    for n in range(columns.shape[1]):
        lanes = slice(n * BLK, (n + 1) * BLK)
        values = codes_ref[:, lanes].astype(jnp.float32) * columns[:, n : n + 1]
        out_ref[:, lanes] = values.astype(jnp.bfloat16)


def mate_weights(codes, scales):
    return pl.pallas_call(
        dequantize,
        out_shape=jax.ShapeDtypeStruct(codes.shape, jnp.bfloat16),
        in_specs=[VMEM, VMEM],
        out_specs=VMEM,
        compiler_params=params(WEIGHTS_KIB),
        cost_estimate=hint(1000),
        name="mate_weights",
    )(codes, scales.T)


def prepare_kernel(
    rows, steps, own, chunk,
    owner_hbm, lengths_hbm, scales_hbm, codes_hbm, query_hbm, cache_hbm, base_hbm,
    *refs,
):
    delta_ref, base_ref, own_query_ref, places_ref = refs[:4]
    parts = refs[4:-7]
    owner_ref, lengths_ref, scales_ref, codes_ref, query_ref, cache_ref, arrived = refs[-7:]
    order = distances(len(parts))
    place = lax.axis_index("tensor")
    block = codes_ref.shape[0]
    cache_len = cache_ref.shape[0] // rows
    used = []

    def load(source, target):
        copy = pltpu.make_async_copy(source, target, arrived.at[len(used)])
        copy.start()
        used.append(copy)
        return [copy]

    def load_rows(source, first, target, size):
        part = min(PART, size)
        copies = []
        for n in range(0, size, part):
            start = first + n if isinstance(first, int) else pl.multiple_of(first + n, part)
            copies += load(source.at[pl.ds(start, part)], target.at[pl.ds(n, part)])
        return copies

    def wait(copies):
        for copy in copies:
            copy.wait()

    owner_load = load(owner_hbm, owner_ref)
    first_loads = load(lengths_hbm, lengths_ref) + load(scales_hbm, scales_ref)
    first_loads += load_rows(codes_hbm, 0, codes_ref, block) + load(query_hbm, query_ref)
    cache_loads = []
    for r in range(rows):
        target = cache_ref.at[pl.ds(r * cache_len, cache_len)]
        cache_loads.append(load_rows(cache_hbm, r * cache_len, target, cache_len))
    wait(owner_load)
    base_loads = []
    for k in range(2):
        start = pl.multiple_of(owner_ref[lax.axis_index("group") ^ k] * block, block)
        base_loads += load_rows(base_hbm, start, base_ref.at[k], block)
    for n in range(places_ref.shape[0]):
        owner = owner_ref[lax.axis_index("group") ^ n]
        places_ref[n : n + 1] = jnp.full((1, LANES), owner, jnp.int32)
    wait(first_loads)
    dequantize(codes_ref, scales_ref, delta_ref)

    chunks = own // chunk
    height = chunk * steps
    width = chunks * HD
    position = lax.broadcasted_iota(jnp.int32, (cache_len, chunks * height), 0)

    def kv_lane(d):
        return pl.multiple_of(((place ^ d) * own // (H // KVH)) * HD, HD)

    def score(r, d):
        head = (place ^ d) * own
        queries = query_ref[:, pl.ds(pl.multiple_of(head * HD, HD), own * HD)]
        query = head_rows(queries.astype(jnp.float32), r, steps, own)
        if d == 0:
            at = r * chunks * height
            own_query_ref[at : at + chunks * height] = query.astype(jnp.bfloat16)
        spread = []
        for j in range(chunks):
            line = [jnp.zeros((height, HD), jnp.float32)] * chunks
            line[j] = query[j * height : (j + 1) * height]
            spread.append(jnp.concatenate(line, axis=1))
        spread = jnp.concatenate(spread, axis=0).astype(jnp.bfloat16)
        keys = cache_ref[pl.ds(r * cache_len, cache_len), pl.ds(kv_lane(d), width)]
        return dot(keys, spread, NT)

    units = [(r, n) for r in range(rows) for n in range(len(parts))]
    stats = [[] for _ in parts]
    ahead = []
    for at in range(len(units) + 1):
        if at < len(units):
            r, n = units[at]
            if n == 0:
                wait(cache_loads[r])
            ahead.append(score(r, order[n]))
        if at == 0:
            continue
        r, n = units[at - 1]
        usable = position < lengths_ref[r] - place * cache_len
        scores = jnp.where(usable, ahead.pop(0) * SCORE_SCALE, 2.0 * NEGATIVE)
        peak = jnp.maximum(jnp.max(scores, axis=0, keepdims=True), NEGATIVE)
        weights = jnp.exp(scores - peak)
        total = jnp.sum(weights, axis=0, keepdims=True)
        lane = pl.ds(kv_lane(order[n]) + KVH * HD, width)
        values = cache_ref[pl.ds(r * cache_len, cache_len), lane]
        sums = dot(weights.astype(jnp.bfloat16), values, TN)
        for j in range(chunks):
            here = slice(j * height, (j + 1) * height)
            first = (r * chunks + j) * height
            mine = sums[here, j * HD : (j + 1) * HD].astype(parts[n].dtype)
            parts[n][first : first + height] = mine
        stats[n] += [peak, total]
        if r == rows - 1:
            put_stats(parts[n], stats[n])
    wait(base_loads)


def part_shape(height, dtype):
    return jax.ShapeDtypeStruct((height + stats_rows(dtype), LANES), dtype)


def prepare(owner_map, lengths, scales, codes, queries, cache, base, rows, steps, own, ways):
    height = rows * own * steps
    loads = 4 + 3 * -(-codes.shape[0] // PART) + rows * -(-cache.shape[0] // rows // PART)
    operands = [
        pltpu.with_memory_space_constraint(x, pltpu.HBM)
        for x in (owner_map, lengths, scales.T, codes, queries, cache, base)
    ]
    out = pl.pallas_call(
        functools.partial(prepare_kernel, rows, steps, own, min(own, H // KVH)),
        out_shape=[
            jax.ShapeDtypeStruct(codes.shape, jnp.bfloat16),
            jax.ShapeDtypeStruct((2,) + codes.shape, jnp.bfloat16),
            jax.ShapeDtypeStruct((height, HD), jnp.bfloat16),
            jax.ShapeDtypeStruct((owner_map.shape[0], LANES), jnp.int32),
            part_shape(height, jnp.float32),
        ]
        + [part_shape(height, jnp.bfloat16)] * (ways - 1),
        in_specs=[HBM] * len(operands),
        out_specs=[VMEM] * (4 + ways),
        scratch_shapes=[
            pltpu.SMEM(owner_map.shape, owner_map.dtype),
            pltpu.SMEM(lengths.shape, lengths.dtype),
            pltpu.VMEM(scales.shape[::-1], scales.dtype),
            pltpu.VMEM(codes.shape, codes.dtype),
            pltpu.VMEM(queries.shape, queries.dtype),
            pltpu.VMEM(cache.shape, cache.dtype),
            pltpu.SemaphoreType.DMA((loads,)),
        ],
        compiler_params=params(CACHE_KIB),
        cost_estimate=hint(CACHE_HINT),
        name="prepare",
    )(*operands)
    return out[0], out[1], out[2], out[3], out[4:]


def merge_kernel(rows, span, *refs):
    parts, out_ref = refs[:-1], refs[-1]
    everything = [get_stats(part, rows) for part in parts]
    stats, factors = [], []
    for r in range(rows):
        peak = functools.reduce(jnp.maximum, [one[r][0] for one in everything])
        scales = [jnp.exp(one[r][0] - peak) for one in everything]
        stats += [peak, sum(one[r][1] * scale for one, scale in zip(everything, scales))]
        factors += scales
    lines = -(-len(factors) // SUBLANES) * SUBLANES
    if lines > len(factors):
        factors.append(jnp.zeros((lines - len(factors), LANES), jnp.float32))
    columns = jnp.concatenate(factors, axis=0).T[:span]
    for r in range(rows):
        here = slice(r * span, (r + 1) * span)
        terms = []
        for n, part in enumerate(parts):
            at = r * len(parts) + n
            terms.append(part[here].astype(jnp.float32) * columns[:, at : at + 1])
        out_ref[here] = sum(terms[1:], terms[0])
    put_stats(out_ref, stats)


def merge(parts, rows):
    height = parts[0].shape[0] - stats_rows(parts[0].dtype)
    return pl.pallas_call(
        functools.partial(merge_kernel, rows, height // rows),
        out_shape=part_shape(height, jnp.float32),
        in_specs=[VMEM] * len(parts),
        out_specs=VMEM,
        compiler_params=params(8192),
        cost_estimate=hint(1000),
        name="merge_partials",
    )(*parts)


def project_kernel(pairs, own_ref, mate_ref, base_ref, *refs):
    tokens, outs = refs[:pairs], refs[pairs:]
    block = own_ref.shape[0]
    stacked = jnp.concatenate([ref[...] for ref in tokens], axis=0)
    count = tokens[0].shape[0]
    for k, delta_ref in enumerate((own_ref, mate_ref)):
        whole = (dot(base_ref[k], stacked, NT) + dot(delta_ref[...], stacked, NT)).T
        for n in range(pairs):
            outs[n][:, k * block : (k + 1) * block] = whole[n * count : (n + 1) * count]


def project(own, mate, base, tokens):
    pairs = len(tokens)
    block = own.shape[0]
    count, width = tokens[0].shape
    return pl.pallas_call(
        functools.partial(project_kernel, pairs),
        out_shape=[jax.ShapeDtypeStruct((count, 2 * block), jnp.float32)] * pairs,
        in_specs=[VMEM] * (3 + pairs),
        out_specs=[VMEM] * pairs,
        compiler_params=params(PROJECT_KIB),
        cost_estimate=hint(PROJECT_HINT),
        name="project",
    )(own, mate, base, *tokens)


def pack_kernel(pairs, ways, near, wide, block, places_ref, *refs):
    arrived, outs = refs[:pairs], refs[pairs:]
    to_place = lax.axis_index("tensor")
    count = arrived[0].shape[0]
    blocks = []
    for piece, d in zip(arrived, distances(pairs)):
        for k in range(2):
            at = 2 * d + k
            place = jnp.broadcast_to(places_ref[at : at + 1], (count, LANES))
            lanes = [slice(n, n + LANES) for n in range(k * block, (k + 1) * block, LANES)]
            blocks.append((place, [piece[:, one] for one in lanes]))

    def pick(which):
        out = [jnp.zeros((count, LANES), jnp.float32)] * (block // LANES)
        for place, values in blocks:
            out = [jnp.where(place == which, new, old) for new, old in zip(values, out)]
        return jnp.concatenate(out, axis=1)

    for out, d in zip(outs, distances(ways)):
        to = to_place ^ d
        columns = []
        keys = [pick(to * near + n) for n in range(near)]
        columns += keys
        if d != 0:
            columns += [key - key.astype(out.dtype).astype(jnp.float32) for key in keys]
        columns += [pick(pairs + to * near + n) for n in range(near)]
        columns += [pick(to * wide + n) for n in range(wide)]
        for n, values in enumerate(columns):
            out[:, n * block : (n + 1) * block] = values.astype(out.dtype)


def pack_pieces(owner_map, places, arrived, block, ways, near_width, slice_width):
    pairs = len(arrived)
    count = arrived[0].shape[0]
    shards = 2 * pairs
    kv_width = KVH * HD
    if block % LANES == 0 and near_width % block == 0 and slice_width % block == 0:
        piece = jax.ShapeDtypeStruct((count, 2 * near_width + slice_width), jnp.float32)
        sent = jax.ShapeDtypeStruct((count, 3 * near_width + slice_width), jnp.bfloat16)
        kernel = functools.partial(
            pack_kernel, pairs, ways, near_width // block, slice_width // block, block
        )
        return pl.pallas_call(
            kernel,
            out_shape=[piece] + [sent] * (ways - 1),
            in_specs=[VMEM] * (1 + pairs),
            out_specs=[VMEM] * ways,
            compiler_params=params(8192),
            cost_estimate=hint(PACK_HINT),
            name="pack_pieces",
        )(places, *arrived)
    nearest = [arrived[distances(pairs).index(d)] for d in range(pairs)]
    blocks = jnp.stack(nearest, axis=0).reshape(pairs, count, 2, block).transpose(0, 2, 1, 3)
    shard_of = jnp.zeros((shards,), jnp.int32).at[owner_map].set(
        jnp.arange(shards, dtype=jnp.int32)
    )
    taken = jnp.take(
        blocks.reshape(shards, count, block), shard_of ^ lax.axis_index("group"), axis=0
    )
    ordered = taken.transpose(1, 0, 2).reshape(count, shards * block)
    per_device = H // ways
    pieces = []
    for d in distances(ways):
        to = lax.axis_index("tensor") ^ d
        near = (to * per_device // (H // KVH)) * HD
        parts = [(near, near_width), (kv_width + near, near_width), (to * slice_width, slice_width)]
        cuts = [lax.dynamic_slice_in_dim(ordered, start, width, 1) for start, width in parts]
        if d != 0:
            rounded = [cut.astype(jnp.bfloat16) for cut in cuts]
            rest = (cuts[0] - rounded[0].astype(jnp.float32)).astype(jnp.bfloat16)
            cuts = [rounded[0], rest] + rounded[1:]
        pieces.append(jnp.concatenate(cuts, axis=1))
    return pieces


def finish_kernel(rows, steps, own, chunk, near_width, ways, query_ref, *refs):
    pieces, part = refs[:ways], refs[ways]
    new_ref, attended_ref = refs[ways + 1 :]
    chunks = own // chunk
    height = chunk * steps
    span = chunks * height
    summed = pieces[0][...]
    for piece in pieces[1:]:
        came = piece[...].astype(jnp.float32)
        keys = came[:, :near_width] + came[:, near_width : 2 * near_width]
        summed = summed + jnp.concatenate([keys, came[:, 2 * near_width :]], axis=1)
    stored = summed.astype(jnp.bfloat16)
    new_ref[...] = stored[:, 2 * near_width :]
    near = stored[:, : 2 * near_width].astype(jnp.float32)
    key_step = lax.broadcasted_iota(jnp.int32, (steps, span), 0)
    query_step = lax.broadcasted_iota(jnp.int32, (steps, span), 1) % steps
    causal = key_step <= query_step
    scores = []
    for r in range(rows):
        spread = []
        for j in range(chunks):
            line = [jnp.zeros((height, HD), jnp.bfloat16)] * chunks
            line[j] = query_ref[r * span + j * height : r * span + (j + 1) * height]
            spread.append(jnp.concatenate(line, axis=1))
        keys = near[r * steps : (r + 1) * steps, :near_width].astype(jnp.bfloat16)
        scores.append(dot(keys, jnp.concatenate(spread, axis=0), NT) * SCORE_SCALE)
    factors, near_sums = [], []
    for r, (cache_peak, cache_total) in enumerate(get_stats(part, rows)):
        masked = jnp.where(causal, scores[r], NEGATIVE)
        peak = jnp.max(masked, axis=0, keepdims=True)
        weights = jnp.where(causal, jnp.exp(masked - peak), 0.0)
        total = jnp.sum(weights, axis=0, keepdims=True)
        values = near[r * steps : (r + 1) * steps, near_width:].astype(jnp.bfloat16)
        near_sums.append(dot(weights.astype(jnp.bfloat16), values, TN))
        cache_peak, cache_total = cache_peak[:, :span], cache_total[:, :span]
        top = jnp.maximum(peak, cache_peak)
        scales = [jnp.exp(cache_peak - top), jnp.exp(peak - top)]
        whole = cache_total * scales[0] + total * scales[1]
        factors += [scale / whole for scale in scales]
    factors.append(jnp.zeros((SUBLANES - len(factors), span), jnp.float32))
    columns = jnp.concatenate(factors, axis=0)
    if span < LANES:
        pad = jnp.zeros((SUBLANES, LANES - span), jnp.float32)
        columns = jnp.concatenate([columns, pad], axis=1)
    columns = columns.T
    for j in range(chunks):
        here = slice(j * height, (j + 1) * height)
        merged = []
        for r in range(rows):
            cached = part[r * span + j * height : r * span + (j + 1) * height]
            fresh = near_sums[r][here, j * HD : (j + 1) * HD]
            merged.append(
                cached * columns[here, 2 * r : 2 * r + 1]
                + fresh * columns[here, 2 * r + 1 : 2 * r + 2]
            )
        for h in range(chunk):
            both = [out[h * steps : (h + 1) * steps] for out in merged]
            lane = (j * chunk + h) * HD
            attended_ref[:, lane : lane + HD] = jnp.concatenate(both, axis=0).astype(jnp.bfloat16)


def finish(own_query, pieces, part, rows, steps, own, near_width):
    ways = len(pieces)
    count, width = pieces[0].shape
    return pl.pallas_call(
        functools.partial(
            finish_kernel, rows, steps, own, min(own, H // KVH), near_width, ways
        ),
        out_shape=[
            jax.ShapeDtypeStruct((count, width - 2 * near_width), jnp.bfloat16),
            jax.ShapeDtypeStruct((count, own * HD), jnp.bfloat16),
        ],
        in_specs=[VMEM] * (2 + ways),
        out_specs=[VMEM] * 2,
        compiler_params=params(8192),
        name="finish",
    )(own_query, *pieces, part)


def on_device(
    hidden_x, base_weight, delta_codes, delta_scales, owner_map, kv_cache, queries, lengths
):
    group_count = lax.axis_size("group")
    tensor_count = lax.axis_size("tensor")
    rows, steps, local_width = hidden_x.shape
    tokens = rows * steps
    owner_block = delta_codes.shape[0]
    heads_own = H // tensor_count
    slice_width = base_weight.shape[0] // tensor_count
    near_width = max(1, heads_own // (H // KVH)) * HD
    pairs = group_count // 2

    def exchange(arrays, axis, stride):
        places = distances(len(arrays))[1:]
        return [arrays[0]] + [swap(x, axis, stride * d) for x, d in zip(arrays[1:], places)]

    def near_first(arrays):
        return arrays[:1] + arrays[:0:-1]

    token_rows = exchange([hidden_x.reshape(tokens, local_width)] * pairs, "group", 2)
    mate_codes = swap(delta_codes, "group", 1)
    mate_scales = swap(delta_scales, "group", 1)

    own_delta, base_blocks, own_query, places, partials = prepare(
        owner_map,
        lengths,
        delta_scales,
        delta_codes,
        queries.reshape(tokens, H * HD),
        kv_cache.reshape(-1, 2 * KVH * HD),
        base_weight,
        rows,
        steps,
        heads_own,
        tensor_count,
    )
    mate_delta = mate_weights(mate_codes, mate_scales)
    behind = lax.optimization_barrier((*near_first(token_rows), mate_delta, own_query))
    token_rows, mate_delta, own_query = near_first(list(behind[:pairs])), behind[-2], behind[-1]
    projected = project(own_delta, mate_delta, base_blocks, near_first(token_rows))
    arrived = exchange(near_first(projected), "group", 2)
    partials = exchange(partials, "tensor", 1)
    pieces = pack_pieces(
        owner_map, places, arrived, owner_block, tensor_count, near_width, slice_width
    )
    pieces = exchange(pieces, "tensor", 1)
    partial = merge(near_first(partials), rows)
    new_out, attended = finish(own_query, pieces, partial, rows, steps, heads_own, near_width)
    return (new_out.reshape(rows, steps, -1), attended.reshape(rows, steps, -1))


def solution(mesh):
    in_specs = (
        P("group", None, "tensor"),
        P(None, "tensor"),
        P("group", "tensor"),
        P("group", "tensor"),
        P(),
        P("group", "tensor", None),
        P("group", None, None),
        P("group"),
    )
    out_specs = (P("group", None, "tensor"), P("group", None, "tensor"))
    return jax.shard_map(
        on_device, mesh=mesh, in_specs=in_specs, out_specs=out_specs, check_vma=False
    )
```

```python
import functools
import jax
import jax.numpy as jnp
from jax import lax
from jax.experimental import pallas as pl
from jax.experimental.pallas import tpu as pltpu
from jax.sharding import PartitionSpec as P

H = 64
KVH = 8
HD = 128
BLK = 128
LANES = 128
SUBLANES = 8


NEGATIVE = -1e30
SCORE_SCALE = HD ** (-0.5)
PART = 64
CACHE_HINT = 120_000_000
PROJECT_HINT = 60_000_000
PACK_HINT = 60_000_000
CACHE_KIB = 24 << 10
PROJECT_KIB = 16 << 10
NT = (((1,), (1,)), ((), ()))
TN = (((0,), (0,)), ((), ()))
VMEM = pl.BlockSpec(memory_space=pltpu.VMEM)
SMEM = pl.BlockSpec(memory_space=pltpu.SMEM)
HBM = pl.BlockSpec(memory_space=pltpu.HBM)


def split(x):
    high = x.astype(jnp.bfloat16).astype(jnp.float32)
    middle = (x - high).astype(jnp.bfloat16).astype(jnp.float32)
    return [high, middle, x - high - middle]


def stats_rows(dtype):
    return SUBLANES if dtype == jnp.float32 else 2 * SUBLANES


def put_stats(ref, stats):
    dtype = ref.dtype
    lines = [x for one in stats for x in ([one] if dtype == jnp.float32 else split(one))]
    lanes = lines[0].shape[1]
    count = stats_rows(dtype)
    lines.append(jnp.zeros((count - len(lines), lanes), jnp.float32))
    tile = jnp.concatenate(lines, axis=0)
    if lanes < LANES:
        tile = jnp.concatenate([tile, jnp.zeros((count, LANES - lanes), jnp.float32)], axis=1)
    ref[ref.shape[0] - count :] = tile.astype(dtype)


def get_stats(ref, rows):
    dtype = ref.dtype
    tile = ref[ref.shape[0] - stats_rows(dtype) :].astype(jnp.float32)
    lines = [tile[n : n + 1] for n in range(2 * rows * (1 if dtype == jnp.float32 else 3))]
    if dtype != jnp.float32:
        lines = [a + b + c for a, b, c in zip(lines[::3], lines[1::3], lines[2::3])]
    return [(lines[2 * r], lines[2 * r + 1]) for r in range(rows)]


def hint(size):
    return pl.CostEstimate(flops=0, bytes_accessed=size, transcendentals=0)


def dot(left, right, dims):
    return lax.dot_general(left, right, dims, preferred_element_type=jnp.float32)


def swap(x, axis, distance):
    size = lax.axis_size(axis)
    return lax.ppermute(x, axis, [(k, k ^ distance) for k in range(size)])


def distances(size):
    return [0] + list(range(size - 1, 0, -1))


def params(kibibytes):
    return pltpu.CompilerParams(vmem_limit_bytes=kibibytes << 10)


def head_rows(block, row, steps, heads):
    mine = block[row * steps : (row + 1) * steps]
    return jnp.concatenate([mine[:, h * HD : (h + 1) * HD] for h in range(heads)], axis=0)


def dequantize(codes_ref, scales_ref, out_ref):
    columns = scales_ref[...].astype(jnp.float32).T
    for n in range(columns.shape[1]):
        lanes = slice(n * BLK, (n + 1) * BLK)
        values = codes_ref[:, lanes].astype(jnp.float32) * columns[:, n : n + 1]
        out_ref[:, lanes] = values.astype(jnp.bfloat16)


def prepare_kernel(
    rows, steps, own, chunk,
    owner_hbm, lengths_hbm, scales_hbm, codes_hbm, query_hbm, cache_hbm, base_hbm,
    *refs,
):
    delta_ref, base_ref, own_query_ref, places_ref = refs[:4]
    parts = refs[4:-7]
    owner_ref, lengths_ref, scales_ref, codes_ref, query_ref, cache_ref, arrived = refs[-7:]
    order = distances(len(parts))
    place = lax.axis_index("tensor")
    block = codes_ref.shape[0]
    cache_len = cache_ref.shape[0] // rows
    used = []

    def load(source, target):
        copy = pltpu.make_async_copy(source, target, arrived.at[len(used)])
        copy.start()
        used.append(copy)
        return [copy]

    def load_rows(source, first, target, size):
        part = min(PART, size)
        copies = []
        for n in range(0, size, part):
            start = first + n if isinstance(first, int) else pl.multiple_of(first + n, part)
            copies += load(source.at[pl.ds(start, part)], target.at[pl.ds(n, part)])
        return copies

    def wait(copies):
        for copy in copies:
            copy.wait()

    owner_load = load(owner_hbm, owner_ref)
    first_loads = load(lengths_hbm, lengths_ref) + load(query_hbm, query_ref)
    cache_loads = []
    for r in range(rows):
        target = cache_ref.at[pl.ds(r * cache_len, cache_len)]
        cache_loads.append(load_rows(cache_hbm, r * cache_len, target, cache_len))
    code_loads = load(scales_hbm, scales_ref) + load_rows(codes_hbm, 0, codes_ref, block)
    wait(owner_load)
    base_loads = []
    for k in range(2):
        start = pl.multiple_of(owner_ref[lax.axis_index("group") ^ k] * block, block)
        base_loads += load_rows(base_hbm, start, base_ref.at[k], block)
    for n in range(places_ref.shape[0]):
        owner = owner_ref[lax.axis_index("group") ^ n]
        places_ref[n : n + 1] = jnp.full((1, LANES), owner, jnp.int32)
    wait(first_loads)

    chunks = own // chunk
    height = chunk * steps
    width = chunks * HD
    position = lax.broadcasted_iota(jnp.int32, (cache_len, chunks * height), 0)

    def kv_lane(d):
        return pl.multiple_of(((place ^ d) * own // (H // KVH)) * HD, HD)

    def score(r, d):
        head = (place ^ d) * own
        queries = query_ref[:, pl.ds(pl.multiple_of(head * HD, HD), own * HD)]
        query = head_rows(queries.astype(jnp.float32), r, steps, own)
        if d == 0:
            at = r * chunks * height
            own_query_ref[at : at + chunks * height] = query.astype(jnp.bfloat16)
        spread = []
        for j in range(chunks):
            line = [jnp.zeros((height, HD), jnp.float32)] * chunks
            line[j] = query[j * height : (j + 1) * height]
            spread.append(jnp.concatenate(line, axis=1))
        spread = jnp.concatenate(spread, axis=0).astype(jnp.bfloat16)
        keys = cache_ref[pl.ds(r * cache_len, cache_len), pl.ds(kv_lane(d), width)]
        return dot(keys, spread, NT)

    units = [(r, n) for r in range(rows) for n in range(len(parts))]
    stats = [[] for _ in parts]
    ahead = []
    for at in range(len(units) + 1):
        if at < len(units):
            r, n = units[at]
            if n == 0:
                wait(cache_loads[r])
            ahead.append(score(r, order[n]))
        if at == 0:
            continue
        r, n = units[at - 1]
        usable = position < lengths_ref[r] - place * cache_len
        scores = jnp.where(usable, ahead.pop(0) * SCORE_SCALE, 2.0 * NEGATIVE)
        peak = jnp.maximum(jnp.max(scores, axis=0, keepdims=True), NEGATIVE)
        weights = jnp.exp(scores - peak)
        total = jnp.sum(weights, axis=0, keepdims=True)
        lane = pl.ds(kv_lane(order[n]) + KVH * HD, width)
        values = cache_ref[pl.ds(r * cache_len, cache_len), lane]
        sums = dot(weights.astype(jnp.bfloat16), values, TN)
        for j in range(chunks):
            here = slice(j * height, (j + 1) * height)
            first = (r * chunks + j) * height
            mine = sums[here, j * HD : (j + 1) * HD].astype(parts[n].dtype)
            parts[n][first : first + height] = mine
        stats[n] += [peak, total]
        if r == rows - 1:
            put_stats(parts[n], stats[n])
    wait(code_loads)
    dequantize(codes_ref, scales_ref, delta_ref)
    wait(base_loads)


def part_shape(height, dtype):
    return jax.ShapeDtypeStruct((height + stats_rows(dtype), LANES), dtype)


def prepare(owner_map, lengths, scales, codes, queries, cache, base, rows, steps, own, ways):
    height = rows * own * steps
    loads = 4 + 3 * -(-codes.shape[0] // PART) + rows * -(-cache.shape[0] // rows // PART)
    operands = [
        pltpu.with_memory_space_constraint(x, pltpu.HBM)
        for x in (owner_map, lengths, scales.T, codes, queries, cache, base)
    ]
    out = pl.pallas_call(
        functools.partial(prepare_kernel, rows, steps, own, min(own, H // KVH)),
        out_shape=[
            jax.ShapeDtypeStruct(codes.shape, jnp.bfloat16),
            jax.ShapeDtypeStruct((2,) + codes.shape, jnp.bfloat16),
            jax.ShapeDtypeStruct((height, HD), jnp.bfloat16),
            jax.ShapeDtypeStruct((owner_map.shape[0], LANES), jnp.int32),
            part_shape(height, jnp.float32),
        ]
        + [part_shape(height, jnp.bfloat16)] * (ways - 1),
        in_specs=[HBM] * len(operands),
        out_specs=[VMEM] * (4 + ways),
        scratch_shapes=[
            pltpu.SMEM(owner_map.shape, owner_map.dtype),
            pltpu.SMEM(lengths.shape, lengths.dtype),
            pltpu.VMEM(scales.shape[::-1], scales.dtype),
            pltpu.VMEM(codes.shape, codes.dtype),
            pltpu.VMEM(queries.shape, queries.dtype),
            pltpu.VMEM(cache.shape, cache.dtype),
            pltpu.SemaphoreType.DMA((loads,)),
        ],
        compiler_params=params(CACHE_KIB),
        cost_estimate=hint(CACHE_HINT),
        name="prepare",
    )(*operands)
    return out[0], out[1], out[2], out[3], list(out[4:])


def merge_kernel(rows, span, *refs):
    parts, out_ref = refs[:-1], refs[-1]
    everything = [get_stats(part, rows) for part in parts]
    stats, factors = [], []
    for r in range(rows):
        peak = functools.reduce(jnp.maximum, [one[r][0] for one in everything])
        scales = [jnp.exp(one[r][0] - peak) for one in everything]
        stats += [peak, sum(one[r][1] * scale for one, scale in zip(everything, scales))]
        factors += scales
    lines = -(-len(factors) // SUBLANES) * SUBLANES
    if lines > len(factors):
        factors.append(jnp.zeros((lines - len(factors), LANES), jnp.float32))
    columns = jnp.concatenate(factors, axis=0).T[:span]
    for r in range(rows):
        here = slice(r * span, (r + 1) * span)
        terms = []
        for n, part in enumerate(parts):
            at = r * len(parts) + n
            terms.append(part[here].astype(jnp.float32) * columns[:, at : at + 1])
        out_ref[here] = sum(terms[1:], terms[0])
    put_stats(out_ref, stats)


def merge(parts, rows):
    height = parts[0].shape[0] - stats_rows(parts[0].dtype)
    return pl.pallas_call(
        functools.partial(merge_kernel, rows, height // rows),
        out_shape=part_shape(height, jnp.float32),
        in_specs=[VMEM] * len(parts),
        out_specs=VMEM,
        compiler_params=params(8192),
        cost_estimate=hint(1000),
        name="merge_partials",
    )(*parts)


def project_kernel(pairs, own_ref, base_ref, codes_ref, scales_ref, *refs):
    tokens, outs, mate_ref = refs[:pairs], refs[pairs:-1], refs[-1]
    block = own_ref.shape[0]
    stacked = jnp.concatenate([ref[...] for ref in tokens], axis=0)
    count = tokens[0].shape[0]

    def put(k, whole):
        whole = whole.T
        for n in range(pairs):
            outs[n][:, k * block : (k + 1) * block] = whole[n * count : (n + 1) * count]

    mine = dot(base_ref[0], stacked, NT) + dot(own_ref[...], stacked, NT)
    other = dot(base_ref[1], stacked, NT)
    dequantize(codes_ref, scales_ref, mate_ref)
    put(0, mine)
    put(1, other + dot(mate_ref[...], stacked, NT))


def project(own, base, mate_codes, mate_scales, tokens):
    pairs = len(tokens)
    block = own.shape[0]
    count = tokens[0].shape[0]
    return pl.pallas_call(
        functools.partial(project_kernel, pairs),
        out_shape=[jax.ShapeDtypeStruct((count, 2 * block), jnp.float32)] * pairs,
        in_specs=[VMEM] * (4 + pairs),
        out_specs=[VMEM] * pairs,
        scratch_shapes=[pltpu.VMEM(own.shape, own.dtype)],
        compiler_params=params(PROJECT_KIB),
        cost_estimate=hint(PROJECT_HINT),
        name="project",
    )(own, base, mate_codes, mate_scales.T, *tokens)


def pack_kernel(pairs, ways, near, wide, block, places_ref, *refs):
    arrived, outs = refs[:pairs], refs[pairs:]
    to_place = lax.axis_index("tensor")
    count = arrived[0].shape[0]
    blocks = []
    for piece, d in zip(arrived, distances(pairs)):
        for k in range(2):
            at = 2 * d + k
            place = jnp.broadcast_to(places_ref[at : at + 1], (count, LANES))
            lanes = [slice(n, n + LANES) for n in range(k * block, (k + 1) * block, LANES)]
            blocks.append((place, [piece[:, one] for one in lanes]))

    def pick(which):
        out = [jnp.zeros((count, LANES), jnp.float32)] * (block // LANES)
        for place, values in blocks:
            out = [jnp.where(place == which, new, old) for new, old in zip(values, out)]
        return jnp.concatenate(out, axis=1)

    for out, d in zip(outs, distances(ways)):
        to = to_place ^ d
        columns = []
        keys = [pick(to * near + n) for n in range(near)]
        columns += keys
        if d != 0:
            columns += [key - key.astype(out.dtype).astype(jnp.float32) for key in keys]
        columns += [pick(pairs + to * near + n) for n in range(near)]
        columns += [pick(to * wide + n) for n in range(wide)]
        for n, values in enumerate(columns):
            out[:, n * block : (n + 1) * block] = values.astype(out.dtype)


def pack_pieces(owner_map, places, arrived, block, ways, near_width, slice_width):
    pairs = len(arrived)
    count = arrived[0].shape[0]
    shards = 2 * pairs
    kv_width = KVH * HD
    if block % LANES == 0 and near_width % block == 0 and slice_width % block == 0:
        piece = jax.ShapeDtypeStruct((count, 2 * near_width + slice_width), jnp.float32)
        sent = jax.ShapeDtypeStruct((count, 3 * near_width + slice_width), jnp.bfloat16)
        kernel = functools.partial(
            pack_kernel, pairs, ways, near_width // block, slice_width // block, block
        )
        return pl.pallas_call(
            kernel,
            out_shape=[piece] + [sent] * (ways - 1),
            in_specs=[VMEM] * (1 + pairs),
            out_specs=[VMEM] * ways,
            compiler_params=params(8192),
            cost_estimate=hint(PACK_HINT),
            name="pack_pieces",
        )(places, *arrived)
    nearest = [arrived[distances(pairs).index(d)] for d in range(pairs)]
    blocks = jnp.stack(nearest, axis=0).reshape(pairs, count, 2, block).transpose(0, 2, 1, 3)
    shard_of = jnp.zeros((shards,), jnp.int32).at[owner_map].set(
        jnp.arange(shards, dtype=jnp.int32)
    )
    taken = jnp.take(
        blocks.reshape(shards, count, block), shard_of ^ lax.axis_index("group"), axis=0
    )
    ordered = taken.transpose(1, 0, 2).reshape(count, shards * block)
    per_device = H // ways
    pieces = []
    for d in distances(ways):
        to = lax.axis_index("tensor") ^ d
        near = (to * per_device // (H // KVH)) * HD
        parts = [(near, near_width), (kv_width + near, near_width), (to * slice_width, slice_width)]
        cuts = [lax.dynamic_slice_in_dim(ordered, start, width, 1) for start, width in parts]
        if d != 0:
            rounded = [cut.astype(jnp.bfloat16) for cut in cuts]
            rest = (cuts[0] - rounded[0].astype(jnp.float32)).astype(jnp.bfloat16)
            cuts = [rounded[0], rest] + rounded[1:]
        pieces.append(jnp.concatenate(cuts, axis=1))
    return pieces


def finish_kernel(rows, steps, own, chunk, near_width, ways, query_ref, *refs):
    pieces, part = refs[:ways], refs[ways]
    new_ref, attended_ref = refs[ways + 1 :]
    chunks = own // chunk
    height = chunk * steps
    span = chunks * height
    summed = pieces[0][...]
    for piece in pieces[1:]:
        came = piece[...].astype(jnp.float32)
        keys = came[:, :near_width] + came[:, near_width : 2 * near_width]
        summed = summed + jnp.concatenate([keys, came[:, 2 * near_width :]], axis=1)
    stored = summed.astype(jnp.bfloat16)
    new_ref[...] = stored[:, 2 * near_width :]
    near = stored[:, : 2 * near_width].astype(jnp.float32)
    key_step = lax.broadcasted_iota(jnp.int32, (steps, span), 0)
    query_step = lax.broadcasted_iota(jnp.int32, (steps, span), 1) % steps
    causal = key_step <= query_step
    scores = []
    for r in range(rows):
        spread = []
        for j in range(chunks):
            line = [jnp.zeros((height, HD), jnp.bfloat16)] * chunks
            line[j] = query_ref[r * span + j * height : r * span + (j + 1) * height]
            spread.append(jnp.concatenate(line, axis=1))
        keys = near[r * steps : (r + 1) * steps, :near_width].astype(jnp.bfloat16)
        scores.append(dot(keys, jnp.concatenate(spread, axis=0), NT) * SCORE_SCALE)
    factors, near_sums = [], []
    for r, (cache_peak, cache_total) in enumerate(get_stats(part, rows)):
        masked = jnp.where(causal, scores[r], NEGATIVE)
        peak = jnp.max(masked, axis=0, keepdims=True)
        weights = jnp.where(causal, jnp.exp(masked - peak), 0.0)
        total = jnp.sum(weights, axis=0, keepdims=True)
        values = near[r * steps : (r + 1) * steps, near_width:].astype(jnp.bfloat16)
        near_sums.append(dot(weights.astype(jnp.bfloat16), values, TN))
        cache_peak, cache_total = cache_peak[:, :span], cache_total[:, :span]
        top = jnp.maximum(peak, cache_peak)
        scales = [jnp.exp(cache_peak - top), jnp.exp(peak - top)]
        whole = cache_total * scales[0] + total * scales[1]
        factors += [scale / whole for scale in scales]
    factors.append(jnp.zeros((SUBLANES - len(factors), span), jnp.float32))
    columns = jnp.concatenate(factors, axis=0)
    if span < LANES:
        pad = jnp.zeros((SUBLANES, LANES - span), jnp.float32)
        columns = jnp.concatenate([columns, pad], axis=1)
    columns = columns.T
    for j in range(chunks):
        here = slice(j * height, (j + 1) * height)
        merged = []
        for r in range(rows):
            cached = part[r * span + j * height : r * span + (j + 1) * height]
            fresh = near_sums[r][here, j * HD : (j + 1) * HD]
            merged.append(
                cached * columns[here, 2 * r : 2 * r + 1]
                + fresh * columns[here, 2 * r + 1 : 2 * r + 2]
            )
        for h in range(chunk):
            both = [out[h * steps : (h + 1) * steps] for out in merged]
            lane = (j * chunk + h) * HD
            attended_ref[:, lane : lane + HD] = jnp.concatenate(both, axis=0).astype(jnp.bfloat16)


def finish(own_query, pieces, part, rows, steps, own, near_width):
    ways = len(pieces)
    count, width = pieces[0].shape
    return pl.pallas_call(
        functools.partial(
            finish_kernel, rows, steps, own, min(own, H // KVH), near_width, ways
        ),
        out_shape=[
            jax.ShapeDtypeStruct((count, width - 2 * near_width), jnp.bfloat16),
            jax.ShapeDtypeStruct((count, own * HD), jnp.bfloat16),
        ],
        in_specs=[VMEM] * (2 + ways),
        out_specs=[VMEM] * 2,
        compiler_params=params(8192),
        name="finish",
    )(own_query, *pieces, part)


def on_device(
    hidden_x, base_weight, delta_codes, delta_scales, owner_map, kv_cache, queries, lengths
):
    group_count = lax.axis_size("group")
    tensor_count = lax.axis_size("tensor")
    rows, steps, local_width = hidden_x.shape
    tokens = rows * steps
    owner_block = delta_codes.shape[0]
    heads_own = H // tensor_count
    slice_width = base_weight.shape[0] // tensor_count
    near_width = max(1, heads_own // (H // KVH)) * HD
    pairs = group_count // 2

    def exchange(arrays, axis, stride):
        places = distances(len(arrays))[1:]
        return [arrays[0]] + [swap(x, axis, stride * d) for x, d in zip(arrays[1:], places)]

    def near_first(arrays):
        return arrays[:1] + arrays[:0:-1]

    token_rows = exchange([hidden_x.reshape(tokens, local_width)] * pairs, "group", 2)
    mate_codes = swap(delta_codes, "group", 1)
    mate_scales = swap(delta_scales, "group", 1)

    own_delta, base_blocks, own_query, places, partials = prepare(
        owner_map,
        lengths,
        delta_scales,
        delta_codes,
        queries.reshape(tokens, H * HD),
        kv_cache.reshape(-1, 2 * KVH * HD),
        base_weight,
        rows,
        steps,
        heads_own,
        tensor_count,
    )
    mate_scales, partials[-1] = lax.optimization_barrier((mate_scales, partials[-1]))
    behind = lax.optimization_barrier((*near_first(token_rows), own_query))
    token_rows, own_query = near_first(list(behind[:pairs])), behind[-1]
    projected = project(
        own_delta, base_blocks, mate_codes, mate_scales, near_first(token_rows)
    )
    arrived = exchange(near_first(projected), "group", 2)
    partials = exchange(partials, "tensor", 1)
    pieces = pack_pieces(
        owner_map, places, arrived, owner_block, tensor_count, near_width, slice_width
    )
    pieces = exchange(pieces, "tensor", 1)
    partial = merge(near_first(partials), rows)
    new_out, attended = finish(own_query, pieces, partial, rows, steps, heads_own, near_width)
    return (new_out.reshape(rows, steps, -1), attended.reshape(rows, steps, -1))


def solution(mesh):
    in_specs = (
        P("group", None, "tensor"),
        P(None, "tensor"),
        P("group", "tensor"),
        P("group", "tensor"),
        P(),
        P("group", "tensor", None),
        P("group", None, None),
        P("group"),
    )
    out_specs = (P("group", None, "tensor"), P("group", None, "tensor"))
    return jax.shard_map(
        on_device, mesh=mesh, in_specs=in_specs, out_specs=out_specs, check_vma=False
    )
```

```python
import functools
import jax
import jax.numpy as jnp
from jax import lax
from jax.experimental import pallas as pl
from jax.experimental.pallas import tpu as pltpu
from jax.sharding import PartitionSpec as P

H = 64
KVH = 8
HD = 128
BLK = 128
LANES = 128
SUBLANES = 8


NEGATIVE = -1e30
SCORE_SCALE = HD ** (-0.5)
PART = 256
PREPARE_FLOPS = 1_000_000_000_000
CACHE_HINT = 120_000_000
PROJECT_HINT = 60_000_000
PACK_HINT = 60_000_000
CACHE_KIB = 24 << 10
WEIGHTS_KIB = 16 << 10
PROJECT_KIB = 16 << 10
NT = (((1,), (1,)), ((), ()))
TN = (((0,), (0,)), ((), ()))
VMEM = pl.BlockSpec(memory_space=pltpu.VMEM)
SMEM = pl.BlockSpec(memory_space=pltpu.SMEM)
HBM = pl.BlockSpec(memory_space=pltpu.HBM)


def split(x):
    high = x.astype(jnp.bfloat16).astype(jnp.float32)
    middle = (x - high).astype(jnp.bfloat16).astype(jnp.float32)
    return [high, middle, x - high - middle]


def stats_rows(dtype):
    return SUBLANES if dtype == jnp.float32 else 2 * SUBLANES


def put_stats(ref, stats):
    dtype = ref.dtype
    lines = [x for one in stats for x in ([one] if dtype == jnp.float32 else split(one))]
    lanes = lines[0].shape[1]
    count = stats_rows(dtype)
    lines.append(jnp.zeros((count - len(lines), lanes), jnp.float32))
    tile = jnp.concatenate(lines, axis=0)
    if lanes < LANES:
        tile = jnp.concatenate([tile, jnp.zeros((count, LANES - lanes), jnp.float32)], axis=1)
    ref[ref.shape[0] - count :] = tile.astype(dtype)


def get_stats(ref, rows):
    dtype = ref.dtype
    tile = ref[ref.shape[0] - stats_rows(dtype) :].astype(jnp.float32)
    lines = [tile[n : n + 1] for n in range(2 * rows * (1 if dtype == jnp.float32 else 3))]
    if dtype != jnp.float32:
        lines = [a + b + c for a, b, c in zip(lines[::3], lines[1::3], lines[2::3])]
    return [(lines[2 * r], lines[2 * r + 1]) for r in range(rows)]


def hint(size, flops=0):
    return pl.CostEstimate(flops=flops, bytes_accessed=size, transcendentals=0)


def dot(left, right, dims):
    return lax.dot_general(left, right, dims, preferred_element_type=jnp.float32)


def swap(x, axis, distance):
    size = lax.axis_size(axis)
    return lax.ppermute(x, axis, [(k, k ^ distance) for k in range(size)])


def distances(size):
    return [0] + list(range(size - 1, 0, -1))


def params(kibibytes):
    return pltpu.CompilerParams(vmem_limit_bytes=kibibytes << 10)


def head_rows(block, row, steps, heads):
    mine = block[row * steps : (row + 1) * steps]
    return jnp.concatenate([mine[:, h * HD : (h + 1) * HD] for h in range(heads)], axis=0)


def dequantize(codes_ref, scales_ref, out_ref):
    columns = scales_ref[...].astype(jnp.float32).T
    for n in range(columns.shape[1]):
        lanes = slice(n * BLK, (n + 1) * BLK)
        values = codes_ref[:, lanes].astype(jnp.float32) * columns[:, n : n + 1]
        out_ref[:, lanes] = values.astype(jnp.bfloat16)


def mate_weights(codes, scales):
    return pl.pallas_call(
        dequantize,
        out_shape=jax.ShapeDtypeStruct(codes.shape, jnp.bfloat16),
        in_specs=[VMEM, VMEM],
        out_specs=VMEM,
        compiler_params=params(WEIGHTS_KIB),
        cost_estimate=hint(1000),
        name="mate_weights",
    )(codes, scales.T)


def prepare_kernel(
    rows, steps, own, chunk,
    owner_hbm, lengths_hbm, scales_hbm, codes_hbm, query_hbm, cache_hbm, base_hbm,
    *refs,
):
    delta_ref, base_ref, own_query_ref, places_ref = refs[:4]
    parts = refs[4:-7]
    owner_ref, lengths_ref, scales_ref, codes_ref, query_ref, cache_ref, arrived = refs[-7:]
    order = distances(len(parts))
    place = lax.axis_index("tensor")
    block = codes_ref.shape[0]
    cache_len = cache_ref.shape[0] // rows
    used = []

    def load(source, target):
        copy = pltpu.make_async_copy(source, target, arrived.at[len(used)])
        copy.start()
        used.append(copy)
        return [copy]

    def load_rows(source, first, target, size):
        part = min(PART, size)
        copies = []
        for n in range(0, size, part):
            start = first + n if isinstance(first, int) else pl.multiple_of(first + n, part)
            copies += load(source.at[pl.ds(start, part)], target.at[pl.ds(n, part)])
        return copies

    def wait(copies):
        for copy in copies:
            copy.wait()

    owner_load = load(owner_hbm, owner_ref)
    first_loads = load(lengths_hbm, lengths_ref) + load(scales_hbm, scales_ref)
    first_loads += load_rows(codes_hbm, 0, codes_ref, block) + load(query_hbm, query_ref)
    cache_loads = []
    for r in range(rows):
        target = cache_ref.at[pl.ds(r * cache_len, cache_len)]
        cache_loads.append(load_rows(cache_hbm, r * cache_len, target, cache_len))
    wait(owner_load)
    base_loads = []
    for k in range(2):
        start = pl.multiple_of(owner_ref[lax.axis_index("group") ^ k] * block, block)
        base_loads += load_rows(base_hbm, start, base_ref.at[k], block)
    for n in range(places_ref.shape[0]):
        owner = owner_ref[lax.axis_index("group") ^ n]
        places_ref[n : n + 1] = jnp.full((1, LANES), owner, jnp.int32)
    wait(first_loads)
    dequantize(codes_ref, scales_ref, delta_ref)

    chunks = own // chunk
    height = chunk * steps
    width = chunks * HD
    position = lax.broadcasted_iota(jnp.int32, (cache_len, chunks * height), 0)

    def kv_lane(d):
        return pl.multiple_of(((place ^ d) * own // (H // KVH)) * HD, HD)

    def score(r, d):
        head = (place ^ d) * own
        queries = query_ref[:, pl.ds(pl.multiple_of(head * HD, HD), own * HD)]
        query = head_rows(queries.astype(jnp.float32), r, steps, own)
        if d == 0:
            at = r * chunks * height
            own_query_ref[at : at + chunks * height] = query.astype(jnp.bfloat16)
        spread = []
        for j in range(chunks):
            line = [jnp.zeros((height, HD), jnp.float32)] * chunks
            line[j] = query[j * height : (j + 1) * height]
            spread.append(jnp.concatenate(line, axis=1))
        spread = jnp.concatenate(spread, axis=0).astype(jnp.bfloat16)
        keys = cache_ref[pl.ds(r * cache_len, cache_len), pl.ds(kv_lane(d), width)]
        return dot(keys, spread, NT)

    units = [(r, n) for r in range(rows) for n in range(len(parts))]
    stats = [[] for _ in parts]
    ahead = []
    for at in range(len(units) + 1):
        if at < len(units):
            r, n = units[at]
            if n == 0:
                wait(cache_loads[r])
            ahead.append(score(r, order[n]))
        if at == 0:
            continue
        r, n = units[at - 1]
        usable = position < lengths_ref[r] - place * cache_len
        scores = jnp.where(usable, ahead.pop(0) * SCORE_SCALE, 2.0 * NEGATIVE)
        peak = jnp.maximum(jnp.max(scores, axis=0, keepdims=True), NEGATIVE)
        weights = jnp.exp(scores - peak)
        total = jnp.sum(weights, axis=0, keepdims=True)
        lane = pl.ds(kv_lane(order[n]) + KVH * HD, width)
        values = cache_ref[pl.ds(r * cache_len, cache_len), lane]
        sums = dot(weights.astype(jnp.bfloat16), values, TN)
        for j in range(chunks):
            here = slice(j * height, (j + 1) * height)
            first = (r * chunks + j) * height
            mine = sums[here, j * HD : (j + 1) * HD].astype(parts[n].dtype)
            parts[n][first : first + height] = mine
        stats[n] += [peak, total]
        if r == rows - 1:
            put_stats(parts[n], stats[n])
    wait(base_loads)


def part_shape(height, dtype):
    return jax.ShapeDtypeStruct((height + stats_rows(dtype), LANES), dtype)


def prepare(owner_map, lengths, scales, codes, queries, cache, base, rows, steps, own, ways):
    height = rows * own * steps
    loads = 4 + 3 * -(-codes.shape[0] // PART) + rows * -(-cache.shape[0] // rows // PART)
    operands = [
        pltpu.with_memory_space_constraint(x, pltpu.HBM)
        for x in (owner_map, lengths, scales.T, codes, queries, cache, base)
    ]
    out = pl.pallas_call(
        functools.partial(prepare_kernel, rows, steps, own, min(own, H // KVH)),
        out_shape=[
            jax.ShapeDtypeStruct(codes.shape, jnp.bfloat16),
            jax.ShapeDtypeStruct((2,) + codes.shape, jnp.bfloat16),
            jax.ShapeDtypeStruct((height, HD), jnp.bfloat16),
            jax.ShapeDtypeStruct((owner_map.shape[0], LANES), jnp.int32),
            part_shape(height, jnp.float32),
        ]
        + [part_shape(height, jnp.bfloat16)] * (ways - 1),
        in_specs=[HBM] * len(operands),
        out_specs=[VMEM] * (4 + ways),
        scratch_shapes=[
            pltpu.SMEM(owner_map.shape, owner_map.dtype),
            pltpu.SMEM(lengths.shape, lengths.dtype),
            pltpu.VMEM(scales.shape[::-1], scales.dtype),
            pltpu.VMEM(codes.shape, codes.dtype),
            pltpu.VMEM(queries.shape, queries.dtype),
            pltpu.VMEM(cache.shape, cache.dtype),
            pltpu.SemaphoreType.DMA((loads,)),
        ],
        compiler_params=params(CACHE_KIB),
        cost_estimate=hint(CACHE_HINT, PREPARE_FLOPS),
        name="prepare",
    )(*operands)
    return out[0], out[1], out[2], out[3], out[4:]


def merge_kernel(rows, span, *refs):
    parts, out_ref = refs[:-1], refs[-1]
    everything = [get_stats(part, rows) for part in parts]
    stats, factors = [], []
    for r in range(rows):
        peak = functools.reduce(jnp.maximum, [one[r][0] for one in everything])
        scales = [jnp.exp(one[r][0] - peak) for one in everything]
        stats += [peak, sum(one[r][1] * scale for one, scale in zip(everything, scales))]
        factors += scales
    lines = -(-len(factors) // SUBLANES) * SUBLANES
    if lines > len(factors):
        factors.append(jnp.zeros((lines - len(factors), LANES), jnp.float32))
    columns = jnp.concatenate(factors, axis=0).T[:span]
    for r in range(rows):
        here = slice(r * span, (r + 1) * span)
        terms = []
        for n, part in enumerate(parts):
            at = r * len(parts) + n
            terms.append(part[here].astype(jnp.float32) * columns[:, at : at + 1])
        out_ref[here] = sum(terms[1:], terms[0])
    put_stats(out_ref, stats)


def merge(parts, rows):
    height = parts[0].shape[0] - stats_rows(parts[0].dtype)
    return pl.pallas_call(
        functools.partial(merge_kernel, rows, height // rows),
        out_shape=part_shape(height, jnp.float32),
        in_specs=[VMEM] * len(parts),
        out_specs=VMEM,
        compiler_params=params(8192),
        cost_estimate=hint(1000),
        name="merge_partials",
    )(*parts)


def project_kernel(pairs, own_ref, mate_ref, base_ref, *refs):
    tokens, outs = refs[:pairs], refs[pairs:]
    block = own_ref.shape[0]
    stacked = jnp.concatenate([ref[...] for ref in tokens], axis=0)
    count = tokens[0].shape[0]
    for k, delta_ref in enumerate((own_ref, mate_ref)):
        whole = (dot(base_ref[k], stacked, NT) + dot(delta_ref[...], stacked, NT)).T
        for n in range(pairs):
            outs[n][:, k * block : (k + 1) * block] = whole[n * count : (n + 1) * count]


def project(own, mate, base, tokens):
    pairs = len(tokens)
    block = own.shape[0]
    count, width = tokens[0].shape
    return pl.pallas_call(
        functools.partial(project_kernel, pairs),
        out_shape=[jax.ShapeDtypeStruct((count, 2 * block), jnp.float32)] * pairs,
        in_specs=[VMEM] * (3 + pairs),
        out_specs=[VMEM] * pairs,
        compiler_params=params(PROJECT_KIB),
        cost_estimate=hint(PROJECT_HINT),
        name="project",
    )(own, mate, base, *tokens)


def pack_kernel(pairs, ways, near, wide, block, places_ref, *refs):
    arrived, outs = refs[:pairs], refs[pairs:]
    to_place = lax.axis_index("tensor")
    count = arrived[0].shape[0]
    blocks = []
    for piece, d in zip(arrived, distances(pairs)):
        for k in range(2):
            at = 2 * d + k
            place = jnp.broadcast_to(places_ref[at : at + 1], (count, LANES))
            lanes = [slice(n, n + LANES) for n in range(k * block, (k + 1) * block, LANES)]
            blocks.append((place, [piece[:, one] for one in lanes]))

    def pick(which):
        out = [jnp.zeros((count, LANES), jnp.float32)] * (block // LANES)
        for place, values in blocks:
            out = [jnp.where(place == which, new, old) for new, old in zip(values, out)]
        return jnp.concatenate(out, axis=1)

    for out, d in zip(outs, distances(ways)):
        to = to_place ^ d
        columns = []
        keys = [pick(to * near + n) for n in range(near)]
        columns += keys
        if d != 0:
            columns += [key - key.astype(out.dtype).astype(jnp.float32) for key in keys]
        columns += [pick(pairs + to * near + n) for n in range(near)]
        columns += [pick(to * wide + n) for n in range(wide)]
        for n, values in enumerate(columns):
            out[:, n * block : (n + 1) * block] = values.astype(out.dtype)


def pack_pieces(owner_map, places, arrived, block, ways, near_width, slice_width):
    pairs = len(arrived)
    count = arrived[0].shape[0]
    shards = 2 * pairs
    kv_width = KVH * HD
    if block % LANES == 0 and near_width % block == 0 and slice_width % block == 0:
        piece = jax.ShapeDtypeStruct((count, 2 * near_width + slice_width), jnp.float32)
        sent = jax.ShapeDtypeStruct((count, 3 * near_width + slice_width), jnp.bfloat16)
        kernel = functools.partial(
            pack_kernel, pairs, ways, near_width // block, slice_width // block, block
        )
        return pl.pallas_call(
            kernel,
            out_shape=[piece] + [sent] * (ways - 1),
            in_specs=[VMEM] * (1 + pairs),
            out_specs=[VMEM] * ways,
            compiler_params=params(8192),
            cost_estimate=hint(PACK_HINT),
            name="pack_pieces",
        )(places, *arrived)
    nearest = [arrived[distances(pairs).index(d)] for d in range(pairs)]
    blocks = jnp.stack(nearest, axis=0).reshape(pairs, count, 2, block).transpose(0, 2, 1, 3)
    shard_of = jnp.zeros((shards,), jnp.int32).at[owner_map].set(
        jnp.arange(shards, dtype=jnp.int32)
    )
    taken = jnp.take(
        blocks.reshape(shards, count, block), shard_of ^ lax.axis_index("group"), axis=0
    )
    ordered = taken.transpose(1, 0, 2).reshape(count, shards * block)
    per_device = H // ways
    pieces = []
    for d in distances(ways):
        to = lax.axis_index("tensor") ^ d
        near = (to * per_device // (H // KVH)) * HD
        parts = [(near, near_width), (kv_width + near, near_width), (to * slice_width, slice_width)]
        cuts = [lax.dynamic_slice_in_dim(ordered, start, width, 1) for start, width in parts]
        if d != 0:
            rounded = [cut.astype(jnp.bfloat16) for cut in cuts]
            rest = (cuts[0] - rounded[0].astype(jnp.float32)).astype(jnp.bfloat16)
            cuts = [rounded[0], rest] + rounded[1:]
        pieces.append(jnp.concatenate(cuts, axis=1))
    return pieces


def finish_kernel(rows, steps, own, chunk, near_width, ways, query_ref, *refs):
    pieces, part = refs[:ways], refs[ways]
    new_ref, attended_ref = refs[ways + 1 :]
    chunks = own // chunk
    height = chunk * steps
    span = chunks * height
    summed = pieces[0][...]
    for piece in pieces[1:]:
        came = piece[...].astype(jnp.float32)
        keys = came[:, :near_width] + came[:, near_width : 2 * near_width]
        summed = summed + jnp.concatenate([keys, came[:, 2 * near_width :]], axis=1)
    stored = summed.astype(jnp.bfloat16)
    new_ref[...] = stored[:, 2 * near_width :]
    near = stored[:, : 2 * near_width].astype(jnp.float32)
    key_step = lax.broadcasted_iota(jnp.int32, (steps, span), 0)
    query_step = lax.broadcasted_iota(jnp.int32, (steps, span), 1) % steps
    causal = key_step <= query_step
    scores = []
    for r in range(rows):
        spread = []
        for j in range(chunks):
            line = [jnp.zeros((height, HD), jnp.bfloat16)] * chunks
            line[j] = query_ref[r * span + j * height : r * span + (j + 1) * height]
            spread.append(jnp.concatenate(line, axis=1))
        keys = near[r * steps : (r + 1) * steps, :near_width].astype(jnp.bfloat16)
        scores.append(dot(keys, jnp.concatenate(spread, axis=0), NT) * SCORE_SCALE)
    factors, near_sums = [], []
    for r, (cache_peak, cache_total) in enumerate(get_stats(part, rows)):
        masked = jnp.where(causal, scores[r], NEGATIVE)
        peak = jnp.max(masked, axis=0, keepdims=True)
        weights = jnp.where(causal, jnp.exp(masked - peak), 0.0)
        total = jnp.sum(weights, axis=0, keepdims=True)
        values = near[r * steps : (r + 1) * steps, near_width:].astype(jnp.bfloat16)
        near_sums.append(dot(weights.astype(jnp.bfloat16), values, TN))
        cache_peak, cache_total = cache_peak[:, :span], cache_total[:, :span]
        top = jnp.maximum(peak, cache_peak)
        scales = [jnp.exp(cache_peak - top), jnp.exp(peak - top)]
        whole = cache_total * scales[0] + total * scales[1]
        factors += [scale / whole for scale in scales]
    factors.append(jnp.zeros((SUBLANES - len(factors), span), jnp.float32))
    columns = jnp.concatenate(factors, axis=0)
    if span < LANES:
        pad = jnp.zeros((SUBLANES, LANES - span), jnp.float32)
        columns = jnp.concatenate([columns, pad], axis=1)
    columns = columns.T
    for j in range(chunks):
        here = slice(j * height, (j + 1) * height)
        merged = []
        for r in range(rows):
            cached = part[r * span + j * height : r * span + (j + 1) * height]
            fresh = near_sums[r][here, j * HD : (j + 1) * HD]
            merged.append(
                cached * columns[here, 2 * r : 2 * r + 1]
                + fresh * columns[here, 2 * r + 1 : 2 * r + 2]
            )
        for h in range(chunk):
            both = [out[h * steps : (h + 1) * steps] for out in merged]
            lane = (j * chunk + h) * HD
            attended_ref[:, lane : lane + HD] = jnp.concatenate(both, axis=0).astype(jnp.bfloat16)


def finish(own_query, pieces, part, rows, steps, own, near_width):
    ways = len(pieces)
    count, width = pieces[0].shape
    return pl.pallas_call(
        functools.partial(
            finish_kernel, rows, steps, own, min(own, H // KVH), near_width, ways
        ),
        out_shape=[
            jax.ShapeDtypeStruct((count, width - 2 * near_width), jnp.bfloat16),
            jax.ShapeDtypeStruct((count, own * HD), jnp.bfloat16),
        ],
        in_specs=[VMEM] * (2 + ways),
        out_specs=[VMEM] * 2,
        compiler_params=params(8192),
        name="finish",
    )(own_query, *pieces, part)


def on_device(
    hidden_x, base_weight, delta_codes, delta_scales, owner_map, kv_cache, queries, lengths
):
    group_count = lax.axis_size("group")
    tensor_count = lax.axis_size("tensor")
    rows, steps, local_width = hidden_x.shape
    tokens = rows * steps
    owner_block = delta_codes.shape[0]
    heads_own = H // tensor_count
    slice_width = base_weight.shape[0] // tensor_count
    near_width = max(1, heads_own // (H // KVH)) * HD
    pairs = group_count // 2

    def exchange(arrays, axis, stride):
        places = distances(len(arrays))[1:]
        return [arrays[0]] + [swap(x, axis, stride * d) for x, d in zip(arrays[1:], places)]

    def near_first(arrays):
        return arrays[:1] + arrays[:0:-1]

    token_rows = exchange([hidden_x.reshape(tokens, local_width)] * pairs, "group", 2)
    mate_codes = swap(delta_codes, "group", 1)
    mate_scales = swap(delta_scales, "group", 1)

    own_delta, base_blocks, own_query, places, partials = prepare(
        owner_map,
        lengths,
        delta_scales,
        delta_codes,
        queries.reshape(tokens, H * HD),
        kv_cache.reshape(-1, 2 * KVH * HD),
        base_weight,
        rows,
        steps,
        heads_own,
        tensor_count,
    )
    mate_delta = mate_weights(mate_codes, mate_scales)
    behind = lax.optimization_barrier((*near_first(token_rows), mate_delta, own_query))
    token_rows, mate_delta, own_query = near_first(list(behind[:pairs])), behind[-2], behind[-1]
    projected = project(own_delta, mate_delta, base_blocks, near_first(token_rows))
    arrived = exchange(near_first(projected), "group", 2)
    partials = exchange(partials, "tensor", 1)
    pieces = pack_pieces(
        owner_map, places, arrived, owner_block, tensor_count, near_width, slice_width
    )
    pieces = exchange(pieces, "tensor", 1)
    partial = merge(near_first(partials), rows)
    new_out, attended = finish(own_query, pieces, partial, rows, steps, heads_own, near_width)
    return (new_out.reshape(rows, steps, -1), attended.reshape(rows, steps, -1))


def solution(mesh):
    in_specs = (
        P("group", None, "tensor"),
        P(None, "tensor"),
        P("group", "tensor"),
        P("group", "tensor"),
        P(),
        P("group", "tensor", None),
        P("group", None, None),
        P("group"),
    )
    out_specs = (P("group", None, "tensor"), P("group", None, "tensor"))
    return jax.shard_map(
        on_device, mesh=mesh, in_specs=in_specs, out_specs=out_specs, check_vma=False
    )
```

```python
import functools
import jax
import jax.numpy as jnp
from jax import lax
from jax.experimental import pallas as pl
from jax.experimental.pallas import tpu as pltpu
from jax.sharding import PartitionSpec as P

H = 64
KVH = 8
HD = 128
BLK = 128
LANES = 128
SUBLANES = 8


NEGATIVE = -1e30
SCORE_SCALE = HD ** (-0.5)
PART = 256
PREPARE_FLOPS = 15_000_000_000
CACHE_HINT = 120_000_000
PROJECT_HINT = 60_000_000
PACK_HINT = 60_000_000
CACHE_KIB = 24 << 10
WEIGHTS_KIB = 16 << 10
PROJECT_KIB = 16 << 10
NT = (((1,), (1,)), ((), ()))
TN = (((0,), (0,)), ((), ()))
VMEM = pl.BlockSpec(memory_space=pltpu.VMEM)
SMEM = pl.BlockSpec(memory_space=pltpu.SMEM)
HBM = pl.BlockSpec(memory_space=pltpu.HBM)


def split(x):
    high = x.astype(jnp.bfloat16).astype(jnp.float32)
    middle = (x - high).astype(jnp.bfloat16).astype(jnp.float32)
    return [high, middle, x - high - middle]


def stats_rows(dtype):
    return SUBLANES if dtype == jnp.float32 else 2 * SUBLANES


def put_stats(ref, stats):
    dtype = ref.dtype
    lines = [x for one in stats for x in ([one] if dtype == jnp.float32 else split(one))]
    lanes = lines[0].shape[1]
    count = stats_rows(dtype)
    lines.append(jnp.zeros((count - len(lines), lanes), jnp.float32))
    tile = jnp.concatenate(lines, axis=0)
    if lanes < LANES:
        tile = jnp.concatenate([tile, jnp.zeros((count, LANES - lanes), jnp.float32)], axis=1)
    ref[ref.shape[0] - count :] = tile.astype(dtype)


def get_stats(ref, rows):
    dtype = ref.dtype
    tile = ref[ref.shape[0] - stats_rows(dtype) :].astype(jnp.float32)
    lines = [tile[n : n + 1] for n in range(2 * rows * (1 if dtype == jnp.float32 else 3))]
    if dtype != jnp.float32:
        lines = [a + b + c for a, b, c in zip(lines[::3], lines[1::3], lines[2::3])]
    return [(lines[2 * r], lines[2 * r + 1]) for r in range(rows)]


def hint(size, flops=0):
    return pl.CostEstimate(flops=flops, bytes_accessed=size, transcendentals=0)


def dot(left, right, dims):
    return lax.dot_general(left, right, dims, preferred_element_type=jnp.float32)


def swap(x, axis, distance):
    size = lax.axis_size(axis)
    return lax.ppermute(x, axis, [(k, k ^ distance) for k in range(size)])


def distances(size):
    return [0] + list(range(size - 1, 0, -1))


def params(kibibytes):
    return pltpu.CompilerParams(vmem_limit_bytes=kibibytes << 10)


def head_rows(block, row, steps, heads):
    mine = block[row * steps : (row + 1) * steps]
    return jnp.concatenate([mine[:, h * HD : (h + 1) * HD] for h in range(heads)], axis=0)


def dequantize(codes_ref, scales_ref, out_ref):
    columns = scales_ref[...].astype(jnp.float32).T
    for n in range(columns.shape[1]):
        lanes = slice(n * BLK, (n + 1) * BLK)
        values = codes_ref[:, lanes].astype(jnp.float32) * columns[:, n : n + 1]
        out_ref[:, lanes] = values.astype(jnp.bfloat16)


def mate_weights(codes, scales):
    return pl.pallas_call(
        dequantize,
        out_shape=jax.ShapeDtypeStruct(codes.shape, jnp.bfloat16),
        in_specs=[VMEM, VMEM],
        out_specs=VMEM,
        compiler_params=params(WEIGHTS_KIB),
        cost_estimate=hint(1000),
        name="mate_weights",
    )(codes, scales.T)


def prepare_kernel(
    rows, steps, own, chunk,
    owner_hbm, lengths_hbm, scales_hbm, codes_hbm, query_hbm, cache_hbm, base_hbm,
    *refs,
):
    delta_ref, base_ref, own_query_ref, places_ref = refs[:4]
    parts = refs[4:-7]
    owner_ref, lengths_ref, scales_ref, codes_ref, query_ref, cache_ref, arrived = refs[-7:]
    order = distances(len(parts))
    place = lax.axis_index("tensor")
    block = codes_ref.shape[0]
    cache_len = cache_ref.shape[0] // rows
    used = []

    def load(source, target):
        copy = pltpu.make_async_copy(source, target, arrived.at[len(used)])
        copy.start()
        used.append(copy)
        return [copy]

    def load_rows(source, first, target, size):
        part = min(PART, size)
        copies = []
        for n in range(0, size, part):
            start = first + n if isinstance(first, int) else pl.multiple_of(first + n, part)
            copies += load(source.at[pl.ds(start, part)], target.at[pl.ds(n, part)])
        return copies

    def wait(copies):
        for copy in copies:
            copy.wait()

    owner_load = load(owner_hbm, owner_ref)
    first_loads = load(lengths_hbm, lengths_ref) + load(scales_hbm, scales_ref)
    first_loads += load_rows(codes_hbm, 0, codes_ref, block) + load(query_hbm, query_ref)
    cache_loads = []
    for r in range(rows):
        target = cache_ref.at[pl.ds(r * cache_len, cache_len)]
        cache_loads.append(load_rows(cache_hbm, r * cache_len, target, cache_len))
    wait(owner_load)
    base_loads = []
    for k in range(2):
        start = pl.multiple_of(owner_ref[lax.axis_index("group") ^ k] * block, block)
        base_loads += load_rows(base_hbm, start, base_ref.at[k], block)
    for n in range(places_ref.shape[0]):
        owner = owner_ref[lax.axis_index("group") ^ n]
        places_ref[n : n + 1] = jnp.full((1, LANES), owner, jnp.int32)
    wait(first_loads)
    dequantize(codes_ref, scales_ref, delta_ref)

    chunks = own // chunk
    height = chunk * steps
    width = chunks * HD
    position = lax.broadcasted_iota(jnp.int32, (cache_len, chunks * height), 0)

    def kv_lane(d):
        return pl.multiple_of(((place ^ d) * own // (H // KVH)) * HD, HD)

    def score(r, d):
        head = (place ^ d) * own
        queries = query_ref[:, pl.ds(pl.multiple_of(head * HD, HD), own * HD)]
        query = head_rows(queries.astype(jnp.float32), r, steps, own)
        if d == 0:
            at = r * chunks * height
            own_query_ref[at : at + chunks * height] = query.astype(jnp.bfloat16)
        spread = []
        for j in range(chunks):
            line = [jnp.zeros((height, HD), jnp.float32)] * chunks
            line[j] = query[j * height : (j + 1) * height]
            spread.append(jnp.concatenate(line, axis=1))
        spread = jnp.concatenate(spread, axis=0).astype(jnp.bfloat16)
        keys = cache_ref[pl.ds(r * cache_len, cache_len), pl.ds(kv_lane(d), width)]
        return dot(keys, spread, NT)

    units = [(r, n) for r in range(rows) for n in range(len(parts))]
    stats = [[] for _ in parts]
    ahead = []
    for at in range(len(units) + 1):
        if at < len(units):
            r, n = units[at]
            if n == 0:
                wait(cache_loads[r])
            ahead.append(score(r, order[n]))
        if at == 0:
            continue
        r, n = units[at - 1]
        usable = position < lengths_ref[r] - place * cache_len
        scores = jnp.where(usable, ahead.pop(0) * SCORE_SCALE, 2.0 * NEGATIVE)
        peak = jnp.maximum(jnp.max(scores, axis=0, keepdims=True), NEGATIVE)
        weights = jnp.exp(scores - peak)
        total = jnp.sum(weights, axis=0, keepdims=True)
        lane = pl.ds(kv_lane(order[n]) + KVH * HD, width)
        values = cache_ref[pl.ds(r * cache_len, cache_len), lane]
        sums = dot(weights.astype(jnp.bfloat16), values, TN)
        for j in range(chunks):
            here = slice(j * height, (j + 1) * height)
            first = (r * chunks + j) * height
            mine = sums[here, j * HD : (j + 1) * HD].astype(parts[n].dtype)
            parts[n][first : first + height] = mine
        stats[n] += [peak, total]
        if r == rows - 1:
            put_stats(parts[n], stats[n])
    wait(base_loads)


def part_shape(height, dtype):
    return jax.ShapeDtypeStruct((height + stats_rows(dtype), LANES), dtype)


def prepare(owner_map, lengths, scales, codes, queries, cache, base, rows, steps, own, ways):
    height = rows * own * steps
    loads = 4 + 3 * -(-codes.shape[0] // PART) + rows * -(-cache.shape[0] // rows // PART)
    operands = [
        pltpu.with_memory_space_constraint(x, pltpu.HBM)
        for x in (owner_map, lengths, scales.T, codes, queries, cache, base)
    ]
    out = pl.pallas_call(
        functools.partial(prepare_kernel, rows, steps, own, min(own, H // KVH)),
        out_shape=[
            jax.ShapeDtypeStruct(codes.shape, jnp.bfloat16),
            jax.ShapeDtypeStruct((2,) + codes.shape, jnp.bfloat16),
            jax.ShapeDtypeStruct((height, HD), jnp.bfloat16),
            jax.ShapeDtypeStruct((owner_map.shape[0], LANES), jnp.int32),
            part_shape(height, jnp.float32),
        ]
        + [part_shape(height, jnp.bfloat16)] * (ways - 1),
        in_specs=[HBM] * len(operands),
        out_specs=[VMEM] * (4 + ways),
        scratch_shapes=[
            pltpu.SMEM(owner_map.shape, owner_map.dtype),
            pltpu.SMEM(lengths.shape, lengths.dtype),
            pltpu.VMEM(scales.shape[::-1], scales.dtype),
            pltpu.VMEM(codes.shape, codes.dtype),
            pltpu.VMEM(queries.shape, queries.dtype),
            pltpu.VMEM(cache.shape, cache.dtype),
            pltpu.SemaphoreType.DMA((loads,)),
        ],
        compiler_params=params(CACHE_KIB),
        cost_estimate=hint(CACHE_HINT, PREPARE_FLOPS),
        name="prepare",
    )(*operands)
    return out[0], out[1], out[2], out[3], out[4:]


def merge_kernel(rows, span, *refs):
    parts, out_ref = refs[:-1], refs[-1]
    everything = [get_stats(part, rows) for part in parts]
    stats, factors = [], []
    for r in range(rows):
        peak = functools.reduce(jnp.maximum, [one[r][0] for one in everything])
        scales = [jnp.exp(one[r][0] - peak) for one in everything]
        stats += [peak, sum(one[r][1] * scale for one, scale in zip(everything, scales))]
        factors += scales
    lines = -(-len(factors) // SUBLANES) * SUBLANES
    if lines > len(factors):
        factors.append(jnp.zeros((lines - len(factors), LANES), jnp.float32))
    columns = jnp.concatenate(factors, axis=0).T[:span]
    for r in range(rows):
        here = slice(r * span, (r + 1) * span)
        terms = []
        for n, part in enumerate(parts):
            at = r * len(parts) + n
            terms.append(part[here].astype(jnp.float32) * columns[:, at : at + 1])
        out_ref[here] = sum(terms[1:], terms[0])
    put_stats(out_ref, stats)


def merge(parts, rows):
    height = parts[0].shape[0] - stats_rows(parts[0].dtype)
    return pl.pallas_call(
        functools.partial(merge_kernel, rows, height // rows),
        out_shape=part_shape(height, jnp.float32),
        in_specs=[VMEM] * len(parts),
        out_specs=VMEM,
        compiler_params=params(8192),
        cost_estimate=hint(1000),
        name="merge_partials",
    )(*parts)


def project_kernel(pairs, own_ref, mate_ref, base_ref, *refs):
    tokens, outs = refs[:pairs], refs[pairs:]
    block = own_ref.shape[0]
    stacked = jnp.concatenate([ref[...] for ref in tokens], axis=0)
    count = tokens[0].shape[0]
    for k, delta_ref in enumerate((own_ref, mate_ref)):
        whole = (dot(base_ref[k], stacked, NT) + dot(delta_ref[...], stacked, NT)).T
        for n in range(pairs):
            outs[n][:, k * block : (k + 1) * block] = whole[n * count : (n + 1) * count]


def project(own, mate, base, tokens):
    pairs = len(tokens)
    block = own.shape[0]
    count, width = tokens[0].shape
    return pl.pallas_call(
        functools.partial(project_kernel, pairs),
        out_shape=[jax.ShapeDtypeStruct((count, 2 * block), jnp.float32)] * pairs,
        in_specs=[VMEM] * (3 + pairs),
        out_specs=[VMEM] * pairs,
        compiler_params=params(PROJECT_KIB),
        cost_estimate=hint(PROJECT_HINT),
        name="project",
    )(own, mate, base, *tokens)


def pack_kernel(pairs, ways, near, wide, block, places_ref, *refs):
    arrived, outs = refs[:pairs], refs[pairs:]
    to_place = lax.axis_index("tensor")
    count = arrived[0].shape[0]
    blocks = []
    for piece, d in zip(arrived, distances(pairs)):
        for k in range(2):
            at = 2 * d + k
            place = jnp.broadcast_to(places_ref[at : at + 1], (count, LANES))
            lanes = [slice(n, n + LANES) for n in range(k * block, (k + 1) * block, LANES)]
            blocks.append((place, [piece[:, one] for one in lanes]))

    def pick(which):
        out = [jnp.zeros((count, LANES), jnp.float32)] * (block // LANES)
        for place, values in blocks:
            out = [jnp.where(place == which, new, old) for new, old in zip(values, out)]
        return jnp.concatenate(out, axis=1)

    for out, d in zip(outs, distances(ways)):
        to = to_place ^ d
        columns = []
        keys = [pick(to * near + n) for n in range(near)]
        columns += keys
        if d != 0:
            columns += [key - key.astype(out.dtype).astype(jnp.float32) for key in keys]
        columns += [pick(pairs + to * near + n) for n in range(near)]
        columns += [pick(to * wide + n) for n in range(wide)]
        for n, values in enumerate(columns):
            out[:, n * block : (n + 1) * block] = values.astype(out.dtype)


def pack_pieces(owner_map, places, arrived, block, ways, near_width, slice_width):
    pairs = len(arrived)
    count = arrived[0].shape[0]
    shards = 2 * pairs
    kv_width = KVH * HD
    if block % LANES == 0 and near_width % block == 0 and slice_width % block == 0:
        piece = jax.ShapeDtypeStruct((count, 2 * near_width + slice_width), jnp.float32)
        sent = jax.ShapeDtypeStruct((count, 3 * near_width + slice_width), jnp.bfloat16)
        kernel = functools.partial(
            pack_kernel, pairs, ways, near_width // block, slice_width // block, block
        )
        return pl.pallas_call(
            kernel,
            out_shape=[piece] + [sent] * (ways - 1),
            in_specs=[VMEM] * (1 + pairs),
            out_specs=[VMEM] * ways,
            compiler_params=params(8192),
            cost_estimate=hint(PACK_HINT),
            name="pack_pieces",
        )(places, *arrived)
    nearest = [arrived[distances(pairs).index(d)] for d in range(pairs)]
    blocks = jnp.stack(nearest, axis=0).reshape(pairs, count, 2, block).transpose(0, 2, 1, 3)
    shard_of = jnp.zeros((shards,), jnp.int32).at[owner_map].set(
        jnp.arange(shards, dtype=jnp.int32)
    )
    taken = jnp.take(
        blocks.reshape(shards, count, block), shard_of ^ lax.axis_index("group"), axis=0
    )
    ordered = taken.transpose(1, 0, 2).reshape(count, shards * block)
    per_device = H // ways
    pieces = []
    for d in distances(ways):
        to = lax.axis_index("tensor") ^ d
        near = (to * per_device // (H // KVH)) * HD
        parts = [(near, near_width), (kv_width + near, near_width), (to * slice_width, slice_width)]
        cuts = [lax.dynamic_slice_in_dim(ordered, start, width, 1) for start, width in parts]
        if d != 0:
            rounded = [cut.astype(jnp.bfloat16) for cut in cuts]
            rest = (cuts[0] - rounded[0].astype(jnp.float32)).astype(jnp.bfloat16)
            cuts = [rounded[0], rest] + rounded[1:]
        pieces.append(jnp.concatenate(cuts, axis=1))
    return pieces


def finish_kernel(rows, steps, own, chunk, near_width, ways, query_ref, *refs):
    pieces, part = refs[:ways], refs[ways]
    new_ref, attended_ref = refs[ways + 1 :]
    chunks = own // chunk
    height = chunk * steps
    span = chunks * height
    summed = pieces[0][...]
    for piece in pieces[1:]:
        came = piece[...].astype(jnp.float32)
        keys = came[:, :near_width] + came[:, near_width : 2 * near_width]
        summed = summed + jnp.concatenate([keys, came[:, 2 * near_width :]], axis=1)
    stored = summed.astype(jnp.bfloat16)
    new_ref[...] = stored[:, 2 * near_width :]
    near = stored[:, : 2 * near_width].astype(jnp.float32)
    key_step = lax.broadcasted_iota(jnp.int32, (steps, span), 0)
    query_step = lax.broadcasted_iota(jnp.int32, (steps, span), 1) % steps
    causal = key_step <= query_step
    scores = []
    for r in range(rows):
        spread = []
        for j in range(chunks):
            line = [jnp.zeros((height, HD), jnp.bfloat16)] * chunks
            line[j] = query_ref[r * span + j * height : r * span + (j + 1) * height]
            spread.append(jnp.concatenate(line, axis=1))
        keys = near[r * steps : (r + 1) * steps, :near_width].astype(jnp.bfloat16)
        scores.append(dot(keys, jnp.concatenate(spread, axis=0), NT) * SCORE_SCALE)
    factors, near_sums = [], []
    for r, (cache_peak, cache_total) in enumerate(get_stats(part, rows)):
        masked = jnp.where(causal, scores[r], NEGATIVE)
        peak = jnp.max(masked, axis=0, keepdims=True)
        weights = jnp.where(causal, jnp.exp(masked - peak), 0.0)
        total = jnp.sum(weights, axis=0, keepdims=True)
        values = near[r * steps : (r + 1) * steps, near_width:].astype(jnp.bfloat16)
        near_sums.append(dot(weights.astype(jnp.bfloat16), values, TN))
        cache_peak, cache_total = cache_peak[:, :span], cache_total[:, :span]
        top = jnp.maximum(peak, cache_peak)
        scales = [jnp.exp(cache_peak - top), jnp.exp(peak - top)]
        whole = cache_total * scales[0] + total * scales[1]
        factors += [scale / whole for scale in scales]
    factors.append(jnp.zeros((SUBLANES - len(factors), span), jnp.float32))
    columns = jnp.concatenate(factors, axis=0)
    if span < LANES:
        pad = jnp.zeros((SUBLANES, LANES - span), jnp.float32)
        columns = jnp.concatenate([columns, pad], axis=1)
    columns = columns.T
    for j in range(chunks):
        here = slice(j * height, (j + 1) * height)
        merged = []
        for r in range(rows):
            cached = part[r * span + j * height : r * span + (j + 1) * height]
            fresh = near_sums[r][here, j * HD : (j + 1) * HD]
            merged.append(
                cached * columns[here, 2 * r : 2 * r + 1]
                + fresh * columns[here, 2 * r + 1 : 2 * r + 2]
            )
        for h in range(chunk):
            both = [out[h * steps : (h + 1) * steps] for out in merged]
            lane = (j * chunk + h) * HD
            attended_ref[:, lane : lane + HD] = jnp.concatenate(both, axis=0).astype(jnp.bfloat16)


def finish(own_query, pieces, part, rows, steps, own, near_width):
    ways = len(pieces)
    count, width = pieces[0].shape
    return pl.pallas_call(
        functools.partial(
            finish_kernel, rows, steps, own, min(own, H // KVH), near_width, ways
        ),
        out_shape=[
            jax.ShapeDtypeStruct((count, width - 2 * near_width), jnp.bfloat16),
            jax.ShapeDtypeStruct((count, own * HD), jnp.bfloat16),
        ],
        in_specs=[VMEM] * (2 + ways),
        out_specs=[VMEM] * 2,
        compiler_params=params(8192),
        name="finish",
    )(own_query, *pieces, part)


def on_device(
    hidden_x, base_weight, delta_codes, delta_scales, owner_map, kv_cache, queries, lengths
):
    group_count = lax.axis_size("group")
    tensor_count = lax.axis_size("tensor")
    rows, steps, local_width = hidden_x.shape
    tokens = rows * steps
    owner_block = delta_codes.shape[0]
    heads_own = H // tensor_count
    slice_width = base_weight.shape[0] // tensor_count
    near_width = max(1, heads_own // (H // KVH)) * HD
    pairs = group_count // 2

    def exchange(arrays, axis, stride):
        places = distances(len(arrays))[1:]
        return [arrays[0]] + [swap(x, axis, stride * d) for x, d in zip(arrays[1:], places)]

    def near_first(arrays):
        return arrays[:1] + arrays[:0:-1]

    token_rows = exchange([hidden_x.reshape(tokens, local_width)] * pairs, "group", 2)
    mate_codes = swap(delta_codes, "group", 1)
    mate_scales = swap(delta_scales, "group", 1)

    own_delta, base_blocks, own_query, places, partials = prepare(
        owner_map,
        lengths,
        delta_scales,
        delta_codes,
        queries.reshape(tokens, H * HD),
        kv_cache.reshape(-1, 2 * KVH * HD),
        base_weight,
        rows,
        steps,
        heads_own,
        tensor_count,
    )
    mate_delta = mate_weights(mate_codes, mate_scales)
    behind = lax.optimization_barrier((*near_first(token_rows), mate_delta, own_query))
    token_rows, mate_delta, own_query = near_first(list(behind[:pairs])), behind[-2], behind[-1]
    projected = project(own_delta, mate_delta, base_blocks, near_first(token_rows))
    arrived = exchange(near_first(projected), "group", 2)
    partials = exchange(partials, "tensor", 1)
    pieces = pack_pieces(
        owner_map, places, arrived, owner_block, tensor_count, near_width, slice_width
    )
    pieces = exchange(pieces, "tensor", 1)
    partial = merge(near_first(partials), rows)
    new_out, attended = finish(own_query, pieces, partial, rows, steps, heads_own, near_width)
    return (new_out.reshape(rows, steps, -1), attended.reshape(rows, steps, -1))


def solution(mesh):
    in_specs = (
        P("group", None, "tensor"),
        P(None, "tensor"),
        P("group", "tensor"),
        P("group", "tensor"),
        P(),
        P("group", "tensor", None),
        P("group", None, None),
        P("group"),
    )
    out_specs = (P("group", None, "tensor"), P("group", None, "tensor"))
    return jax.shard_map(
        on_device, mesh=mesh, in_specs=in_specs, out_specs=out_specs, check_vma=False
    )
```

```python
import functools
import jax
import jax.numpy as jnp
from jax import lax
from jax.experimental import pallas as pl
from jax.experimental.pallas import tpu as pltpu
from jax.sharding import PartitionSpec as P

H = 64
KVH = 8
HD = 128
BLK = 128
LANES = 128
SUBLANES = 8


NEGATIVE = -1e30
SCORE_SCALE = HD ** (-0.5)
PART = 256
PREPARE_FLOPS = 15_000_000_000
CACHE_HINT = 120_000_000
PROJECT_HINT = 60_000_000
PACK_HINT = 60_000_000
CACHE_KIB = 24 << 10
PROJECT_KIB = 16 << 10
NT = (((1,), (1,)), ((), ()))
TN = (((0,), (0,)), ((), ()))
VMEM = pl.BlockSpec(memory_space=pltpu.VMEM)
SMEM = pl.BlockSpec(memory_space=pltpu.SMEM)
HBM = pl.BlockSpec(memory_space=pltpu.HBM)


def split(x):
    high = x.astype(jnp.bfloat16).astype(jnp.float32)
    middle = (x - high).astype(jnp.bfloat16).astype(jnp.float32)
    return [high, middle, x - high - middle]


def stats_rows(dtype):
    return SUBLANES if dtype == jnp.float32 else 2 * SUBLANES


def put_stats(ref, stats):
    dtype = ref.dtype
    lines = [x for one in stats for x in ([one] if dtype == jnp.float32 else split(one))]
    lanes = lines[0].shape[1]
    count = stats_rows(dtype)
    lines.append(jnp.zeros((count - len(lines), lanes), jnp.float32))
    tile = jnp.concatenate(lines, axis=0)
    if lanes < LANES:
        tile = jnp.concatenate([tile, jnp.zeros((count, LANES - lanes), jnp.float32)], axis=1)
    ref[ref.shape[0] - count :] = tile.astype(dtype)


def get_stats(ref, rows):
    dtype = ref.dtype
    tile = ref[ref.shape[0] - stats_rows(dtype) :].astype(jnp.float32)
    lines = [tile[n : n + 1] for n in range(2 * rows * (1 if dtype == jnp.float32 else 3))]
    if dtype != jnp.float32:
        lines = [a + b + c for a, b, c in zip(lines[::3], lines[1::3], lines[2::3])]
    return [(lines[2 * r], lines[2 * r + 1]) for r in range(rows)]


def hint(size, flops=0):
    return pl.CostEstimate(flops=flops, bytes_accessed=size, transcendentals=0)


def dot(left, right, dims):
    return lax.dot_general(left, right, dims, preferred_element_type=jnp.float32)


def swap(x, axis, distance):
    size = lax.axis_size(axis)
    return lax.ppermute(x, axis, [(k, k ^ distance) for k in range(size)])


def distances(size):
    return [0] + list(range(size - 1, 0, -1))


def params(kibibytes):
    return pltpu.CompilerParams(vmem_limit_bytes=kibibytes << 10)


def head_rows(block, row, steps, heads):
    mine = block[row * steps : (row + 1) * steps]
    return jnp.concatenate([mine[:, h * HD : (h + 1) * HD] for h in range(heads)], axis=0)


def dequantize(codes_ref, scales_ref, out_ref):
    columns = scales_ref[...].astype(jnp.float32).T
    for n in range(columns.shape[1]):
        lanes = slice(n * BLK, (n + 1) * BLK)
        values = codes_ref[:, lanes].astype(jnp.float32) * columns[:, n : n + 1]
        out_ref[:, lanes] = values.astype(jnp.bfloat16)


def prepare_kernel(
    rows, steps, own, chunk,
    owner_hbm, lengths_hbm, scales_hbm, codes_hbm, query_hbm, cache_hbm, base_hbm,
    *refs,
):
    delta_ref, base_ref, own_query_ref, places_ref = refs[:4]
    parts = refs[4:-7]
    owner_ref, lengths_ref, scales_ref, codes_ref, query_ref, cache_ref, arrived = refs[-7:]
    order = distances(len(parts))
    place = lax.axis_index("tensor")
    block = codes_ref.shape[0]
    cache_len = cache_ref.shape[0] // rows
    used = []

    def load(source, target):
        copy = pltpu.make_async_copy(source, target, arrived.at[len(used)])
        copy.start()
        used.append(copy)
        return [copy]

    def load_rows(source, first, target, size):
        part = min(PART, size)
        copies = []
        for n in range(0, size, part):
            start = first + n if isinstance(first, int) else pl.multiple_of(first + n, part)
            copies += load(source.at[pl.ds(start, part)], target.at[pl.ds(n, part)])
        return copies

    def wait(copies):
        for copy in copies:
            copy.wait()

    owner_load = load(owner_hbm, owner_ref)
    first_loads = load(lengths_hbm, lengths_ref) + load(scales_hbm, scales_ref)
    first_loads += load_rows(codes_hbm, 0, codes_ref, block) + load(query_hbm, query_ref)
    cache_loads = []
    for r in range(rows):
        target = cache_ref.at[pl.ds(r * cache_len, cache_len)]
        cache_loads.append(load_rows(cache_hbm, r * cache_len, target, cache_len))
    wait(owner_load)
    base_loads = []
    for k in range(2):
        start = pl.multiple_of(owner_ref[lax.axis_index("group") ^ k] * block, block)
        base_loads += load_rows(base_hbm, start, base_ref.at[k], block)
    for n in range(places_ref.shape[0]):
        owner = owner_ref[lax.axis_index("group") ^ n]
        places_ref[n : n + 1] = jnp.full((1, LANES), owner, jnp.int32)
    wait(first_loads)
    dequantize(codes_ref, scales_ref, delta_ref)

    chunks = own // chunk
    height = chunk * steps
    width = chunks * HD
    position = lax.broadcasted_iota(jnp.int32, (cache_len, chunks * height), 0)

    def kv_lane(d):
        return pl.multiple_of(((place ^ d) * own // (H // KVH)) * HD, HD)

    def score(r, d):
        head = (place ^ d) * own
        queries = query_ref[:, pl.ds(pl.multiple_of(head * HD, HD), own * HD)]
        query = head_rows(queries.astype(jnp.float32), r, steps, own)
        if d == 0:
            at = r * chunks * height
            own_query_ref[at : at + chunks * height] = query.astype(jnp.bfloat16)
        spread = []
        for j in range(chunks):
            line = [jnp.zeros((height, HD), jnp.float32)] * chunks
            line[j] = query[j * height : (j + 1) * height]
            spread.append(jnp.concatenate(line, axis=1))
        spread = jnp.concatenate(spread, axis=0).astype(jnp.bfloat16)
        keys = cache_ref[pl.ds(r * cache_len, cache_len), pl.ds(kv_lane(d), width)]
        return dot(keys, spread, NT)

    units = [(r, n) for r in range(rows) for n in range(len(parts))]
    stats = [[] for _ in parts]
    ahead = []
    for at in range(len(units) + 1):
        if at < len(units):
            r, n = units[at]
            if n == 0:
                wait(cache_loads[r])
            ahead.append(score(r, order[n]))
        if at == 0:
            continue
        r, n = units[at - 1]
        usable = position < lengths_ref[r] - place * cache_len
        scores = jnp.where(usable, ahead.pop(0) * SCORE_SCALE, 2.0 * NEGATIVE)
        peak = jnp.maximum(jnp.max(scores, axis=0, keepdims=True), NEGATIVE)
        weights = jnp.exp(scores - peak)
        total = jnp.sum(weights, axis=0, keepdims=True)
        lane = pl.ds(kv_lane(order[n]) + KVH * HD, width)
        values = cache_ref[pl.ds(r * cache_len, cache_len), lane]
        sums = dot(weights.astype(jnp.bfloat16), values, TN)
        for j in range(chunks):
            here = slice(j * height, (j + 1) * height)
            first = (r * chunks + j) * height
            mine = sums[here, j * HD : (j + 1) * HD].astype(parts[n].dtype)
            parts[n][first : first + height] = mine
        stats[n] += [peak, total]
        if r == rows - 1:
            put_stats(parts[n], stats[n])
    wait(base_loads)


def part_shape(height, dtype):
    return jax.ShapeDtypeStruct((height + stats_rows(dtype), LANES), dtype)


def prepare(owner_map, lengths, scales, codes, queries, cache, base, rows, steps, own, ways):
    height = rows * own * steps
    loads = 4 + 3 * -(-codes.shape[0] // PART) + rows * -(-cache.shape[0] // rows // PART)
    operands = [
        pltpu.with_memory_space_constraint(x, pltpu.HBM)
        for x in (owner_map, lengths, scales.T, codes, queries, cache, base)
    ]
    out = pl.pallas_call(
        functools.partial(prepare_kernel, rows, steps, own, min(own, H // KVH)),
        out_shape=[
            jax.ShapeDtypeStruct(codes.shape, jnp.bfloat16),
            jax.ShapeDtypeStruct((2,) + codes.shape, jnp.bfloat16),
            jax.ShapeDtypeStruct((height, HD), jnp.bfloat16),
            jax.ShapeDtypeStruct((owner_map.shape[0], LANES), jnp.int32),
            part_shape(height, jnp.float32),
        ]
        + [part_shape(height, jnp.bfloat16)] * (ways - 1),
        in_specs=[HBM] * len(operands),
        out_specs=[VMEM] * (4 + ways),
        scratch_shapes=[
            pltpu.SMEM(owner_map.shape, owner_map.dtype),
            pltpu.SMEM(lengths.shape, lengths.dtype),
            pltpu.VMEM(scales.shape[::-1], scales.dtype),
            pltpu.VMEM(codes.shape, codes.dtype),
            pltpu.VMEM(queries.shape, queries.dtype),
            pltpu.VMEM(cache.shape, cache.dtype),
            pltpu.SemaphoreType.DMA((loads,)),
        ],
        compiler_params=params(CACHE_KIB),
        cost_estimate=hint(CACHE_HINT, PREPARE_FLOPS),
        name="prepare",
    )(*operands)
    return out[0], out[1], out[2], out[3], list(out[4:])


def merge_kernel(rows, span, *refs):
    parts, out_ref = refs[:-1], refs[-1]
    everything = [get_stats(part, rows) for part in parts]
    stats, factors = [], []
    for r in range(rows):
        peak = functools.reduce(jnp.maximum, [one[r][0] for one in everything])
        scales = [jnp.exp(one[r][0] - peak) for one in everything]
        stats += [peak, sum(one[r][1] * scale for one, scale in zip(everything, scales))]
        factors += scales
    lines = -(-len(factors) // SUBLANES) * SUBLANES
    if lines > len(factors):
        factors.append(jnp.zeros((lines - len(factors), LANES), jnp.float32))
    columns = jnp.concatenate(factors, axis=0).T[:span]
    for r in range(rows):
        here = slice(r * span, (r + 1) * span)
        terms = []
        for n, part in enumerate(parts):
            at = r * len(parts) + n
            terms.append(part[here].astype(jnp.float32) * columns[:, at : at + 1])
        out_ref[here] = sum(terms[1:], terms[0])
    put_stats(out_ref, stats)


def merge(parts, rows):
    height = parts[0].shape[0] - stats_rows(parts[0].dtype)
    return pl.pallas_call(
        functools.partial(merge_kernel, rows, height // rows),
        out_shape=part_shape(height, jnp.float32),
        in_specs=[VMEM] * len(parts),
        out_specs=VMEM,
        compiler_params=params(8192),
        cost_estimate=hint(1000),
        name="merge_partials",
    )(*parts)


def project_kernel(pairs, own_ref, base_ref, codes_ref, scales_ref, *refs):
    tokens, outs, mate_ref = refs[:pairs], refs[pairs:-1], refs[-1]
    block = own_ref.shape[0]
    stacked = jnp.concatenate([ref[...] for ref in tokens], axis=0)
    count = tokens[0].shape[0]

    def put(k, whole):
        whole = whole.T
        for n in range(pairs):
            outs[n][:, k * block : (k + 1) * block] = whole[n * count : (n + 1) * count]

    mine = dot(base_ref[0], stacked, NT) + dot(own_ref[...], stacked, NT)
    other = dot(base_ref[1], stacked, NT)
    dequantize(codes_ref, scales_ref, mate_ref)
    put(0, mine)
    put(1, other + dot(mate_ref[...], stacked, NT))


def project(own, base, mate_codes, mate_scales, tokens):
    pairs = len(tokens)
    block = own.shape[0]
    count = tokens[0].shape[0]
    return pl.pallas_call(
        functools.partial(project_kernel, pairs),
        out_shape=[jax.ShapeDtypeStruct((count, 2 * block), jnp.float32)] * pairs,
        in_specs=[VMEM] * (4 + pairs),
        out_specs=[VMEM] * pairs,
        scratch_shapes=[pltpu.VMEM(own.shape, own.dtype)],
        compiler_params=params(PROJECT_KIB),
        cost_estimate=hint(PROJECT_HINT),
        name="project",
    )(own, base, mate_codes, mate_scales.T, *tokens)


def pack_kernel(pairs, ways, near, wide, block, places_ref, *refs):
    arrived, outs = refs[:pairs], refs[pairs:]
    to_place = lax.axis_index("tensor")
    count = arrived[0].shape[0]
    blocks = []
    for piece, d in zip(arrived, distances(pairs)):
        for k in range(2):
            at = 2 * d + k
            place = jnp.broadcast_to(places_ref[at : at + 1], (count, LANES))
            lanes = [slice(n, n + LANES) for n in range(k * block, (k + 1) * block, LANES)]
            blocks.append((place, [piece[:, one] for one in lanes]))

    def pick(which):
        out = [jnp.zeros((count, LANES), jnp.float32)] * (block // LANES)
        for place, values in blocks:
            out = [jnp.where(place == which, new, old) for new, old in zip(values, out)]
        return jnp.concatenate(out, axis=1)

    for out, d in zip(outs, distances(ways)):
        to = to_place ^ d
        columns = []
        keys = [pick(to * near + n) for n in range(near)]
        columns += keys
        if d != 0:
            columns += [key - key.astype(out.dtype).astype(jnp.float32) for key in keys]
        columns += [pick(pairs + to * near + n) for n in range(near)]
        columns += [pick(to * wide + n) for n in range(wide)]
        for n, values in enumerate(columns):
            out[:, n * block : (n + 1) * block] = values.astype(out.dtype)


def pack_pieces(owner_map, places, arrived, block, ways, near_width, slice_width):
    pairs = len(arrived)
    count = arrived[0].shape[0]
    shards = 2 * pairs
    kv_width = KVH * HD
    if block % LANES == 0 and near_width % block == 0 and slice_width % block == 0:
        piece = jax.ShapeDtypeStruct((count, 2 * near_width + slice_width), jnp.float32)
        sent = jax.ShapeDtypeStruct((count, 3 * near_width + slice_width), jnp.bfloat16)
        kernel = functools.partial(
            pack_kernel, pairs, ways, near_width // block, slice_width // block, block
        )
        return pl.pallas_call(
            kernel,
            out_shape=[piece] + [sent] * (ways - 1),
            in_specs=[VMEM] * (1 + pairs),
            out_specs=[VMEM] * ways,
            compiler_params=params(8192),
            cost_estimate=hint(PACK_HINT),
            name="pack_pieces",
        )(places, *arrived)
    nearest = [arrived[distances(pairs).index(d)] for d in range(pairs)]
    blocks = jnp.stack(nearest, axis=0).reshape(pairs, count, 2, block).transpose(0, 2, 1, 3)
    shard_of = jnp.zeros((shards,), jnp.int32).at[owner_map].set(
        jnp.arange(shards, dtype=jnp.int32)
    )
    taken = jnp.take(
        blocks.reshape(shards, count, block), shard_of ^ lax.axis_index("group"), axis=0
    )
    ordered = taken.transpose(1, 0, 2).reshape(count, shards * block)
    per_device = H // ways
    pieces = []
    for d in distances(ways):
        to = lax.axis_index("tensor") ^ d
        near = (to * per_device // (H // KVH)) * HD
        parts = [(near, near_width), (kv_width + near, near_width), (to * slice_width, slice_width)]
        cuts = [lax.dynamic_slice_in_dim(ordered, start, width, 1) for start, width in parts]
        if d != 0:
            rounded = [cut.astype(jnp.bfloat16) for cut in cuts]
            rest = (cuts[0] - rounded[0].astype(jnp.float32)).astype(jnp.bfloat16)
            cuts = [rounded[0], rest] + rounded[1:]
        pieces.append(jnp.concatenate(cuts, axis=1))
    return pieces


def finish_kernel(rows, steps, own, chunk, near_width, ways, query_ref, *refs):
    pieces, part = refs[:ways], refs[ways]
    new_ref, attended_ref = refs[ways + 1 :]
    chunks = own // chunk
    height = chunk * steps
    span = chunks * height
    summed = pieces[0][...]
    for piece in pieces[1:]:
        came = piece[...].astype(jnp.float32)
        keys = came[:, :near_width] + came[:, near_width : 2 * near_width]
        summed = summed + jnp.concatenate([keys, came[:, 2 * near_width :]], axis=1)
    stored = summed.astype(jnp.bfloat16)
    new_ref[...] = stored[:, 2 * near_width :]
    near = stored[:, : 2 * near_width].astype(jnp.float32)
    key_step = lax.broadcasted_iota(jnp.int32, (steps, span), 0)
    query_step = lax.broadcasted_iota(jnp.int32, (steps, span), 1) % steps
    causal = key_step <= query_step
    scores = []
    for r in range(rows):
        spread = []
        for j in range(chunks):
            line = [jnp.zeros((height, HD), jnp.bfloat16)] * chunks
            line[j] = query_ref[r * span + j * height : r * span + (j + 1) * height]
            spread.append(jnp.concatenate(line, axis=1))
        keys = near[r * steps : (r + 1) * steps, :near_width].astype(jnp.bfloat16)
        scores.append(dot(keys, jnp.concatenate(spread, axis=0), NT) * SCORE_SCALE)
    factors, near_sums = [], []
    for r, (cache_peak, cache_total) in enumerate(get_stats(part, rows)):
        masked = jnp.where(causal, scores[r], NEGATIVE)
        peak = jnp.max(masked, axis=0, keepdims=True)
        weights = jnp.where(causal, jnp.exp(masked - peak), 0.0)
        total = jnp.sum(weights, axis=0, keepdims=True)
        values = near[r * steps : (r + 1) * steps, near_width:].astype(jnp.bfloat16)
        near_sums.append(dot(weights.astype(jnp.bfloat16), values, TN))
        cache_peak, cache_total = cache_peak[:, :span], cache_total[:, :span]
        top = jnp.maximum(peak, cache_peak)
        scales = [jnp.exp(cache_peak - top), jnp.exp(peak - top)]
        whole = cache_total * scales[0] + total * scales[1]
        factors += [scale / whole for scale in scales]
    factors.append(jnp.zeros((SUBLANES - len(factors), span), jnp.float32))
    columns = jnp.concatenate(factors, axis=0)
    if span < LANES:
        pad = jnp.zeros((SUBLANES, LANES - span), jnp.float32)
        columns = jnp.concatenate([columns, pad], axis=1)
    columns = columns.T
    for j in range(chunks):
        here = slice(j * height, (j + 1) * height)
        merged = []
        for r in range(rows):
            cached = part[r * span + j * height : r * span + (j + 1) * height]
            fresh = near_sums[r][here, j * HD : (j + 1) * HD]
            merged.append(
                cached * columns[here, 2 * r : 2 * r + 1]
                + fresh * columns[here, 2 * r + 1 : 2 * r + 2]
            )
        for h in range(chunk):
            both = [out[h * steps : (h + 1) * steps] for out in merged]
            lane = (j * chunk + h) * HD
            attended_ref[:, lane : lane + HD] = jnp.concatenate(both, axis=0).astype(jnp.bfloat16)


def finish(own_query, pieces, part, rows, steps, own, near_width):
    ways = len(pieces)
    count, width = pieces[0].shape
    return pl.pallas_call(
        functools.partial(
            finish_kernel, rows, steps, own, min(own, H // KVH), near_width, ways
        ),
        out_shape=[
            jax.ShapeDtypeStruct((count, width - 2 * near_width), jnp.bfloat16),
            jax.ShapeDtypeStruct((count, own * HD), jnp.bfloat16),
        ],
        in_specs=[VMEM] * (2 + ways),
        out_specs=[VMEM] * 2,
        compiler_params=params(8192),
        name="finish",
    )(own_query, *pieces, part)


def on_device(
    hidden_x, base_weight, delta_codes, delta_scales, owner_map, kv_cache, queries, lengths
):
    group_count = lax.axis_size("group")
    tensor_count = lax.axis_size("tensor")
    rows, steps, local_width = hidden_x.shape
    tokens = rows * steps
    owner_block = delta_codes.shape[0]
    heads_own = H // tensor_count
    slice_width = base_weight.shape[0] // tensor_count
    near_width = max(1, heads_own // (H // KVH)) * HD
    pairs = group_count // 2

    def exchange(arrays, axis, stride):
        places = distances(len(arrays))[1:]
        return [arrays[0]] + [swap(x, axis, stride * d) for x, d in zip(arrays[1:], places)]

    def near_first(arrays):
        return arrays[:1] + arrays[:0:-1]

    token_rows = exchange([hidden_x.reshape(tokens, local_width)] * pairs, "group", 2)
    mate_codes = swap(delta_codes, "group", 1)
    mate_scales = swap(delta_scales, "group", 1)

    own_delta, base_blocks, own_query, places, partials = prepare(
        owner_map,
        lengths,
        delta_scales,
        delta_codes,
        queries.reshape(tokens, H * HD),
        kv_cache.reshape(-1, 2 * KVH * HD),
        base_weight,
        rows,
        steps,
        heads_own,
        tensor_count,
    )
    mate_scales, partials[-1] = lax.optimization_barrier((mate_scales, partials[-1]))
    behind = lax.optimization_barrier((*near_first(token_rows), own_query))
    token_rows, own_query = near_first(list(behind[:pairs])), behind[-1]
    projected = project(
        own_delta, base_blocks, mate_codes, mate_scales, near_first(token_rows)
    )
    arrived = exchange(near_first(projected), "group", 2)
    partials = exchange(partials, "tensor", 1)
    pieces = pack_pieces(
        owner_map, places, arrived, owner_block, tensor_count, near_width, slice_width
    )
    pieces = exchange(pieces, "tensor", 1)
    partial = merge(near_first(partials), rows)
    new_out, attended = finish(own_query, pieces, partial, rows, steps, heads_own, near_width)
    return (new_out.reshape(rows, steps, -1), attended.reshape(rows, steps, -1))


def solution(mesh):
    in_specs = (
        P("group", None, "tensor"),
        P(None, "tensor"),
        P("group", "tensor"),
        P("group", "tensor"),
        P(),
        P("group", "tensor", None),
        P("group", None, None),
        P("group"),
    )
    out_specs = (P("group", None, "tensor"), P("group", None, "tensor"))
    return jax.shard_map(
        on_device, mesh=mesh, in_specs=in_specs, out_specs=out_specs, check_vma=False
    )
```

```python
import functools
import jax
import jax.numpy as jnp
from jax import lax
from jax.experimental import pallas as pl
from jax.experimental.pallas import tpu as pltpu
from jax.sharding import PartitionSpec as P

H = 64
KVH = 8
HD = 128
BLK = 128
LANES = 128
SUBLANES = 8


NEGATIVE = -1e30
SCORE_SCALE = HD ** (-0.5)
PART = 256
PREPARE_FLOPS = 15_000_000_000
CACHE_HINT = 120_000_000
PROJECT_HINT = 60_000_000
PACK_HINT = 60_000_000
CACHE_KIB = 24 << 10
PROJECT_KIB = 16 << 10
NT = (((1,), (1,)), ((), ()))
TN = (((0,), (0,)), ((), ()))
VMEM = pl.BlockSpec(memory_space=pltpu.VMEM)
SMEM = pl.BlockSpec(memory_space=pltpu.SMEM)
HBM = pl.BlockSpec(memory_space=pltpu.HBM)


def split(x):
    high = x.astype(jnp.bfloat16).astype(jnp.float32)
    middle = (x - high).astype(jnp.bfloat16).astype(jnp.float32)
    return [high, middle, x - high - middle]


def stats_rows(dtype):
    return SUBLANES if dtype == jnp.float32 else 2 * SUBLANES


def put_stats(ref, stats):
    dtype = ref.dtype
    lines = [x for one in stats for x in ([one] if dtype == jnp.float32 else split(one))]
    lanes = lines[0].shape[1]
    count = stats_rows(dtype)
    lines.append(jnp.zeros((count - len(lines), lanes), jnp.float32))
    tile = jnp.concatenate(lines, axis=0)
    if lanes < LANES:
        tile = jnp.concatenate([tile, jnp.zeros((count, LANES - lanes), jnp.float32)], axis=1)
    ref[ref.shape[0] - count :] = tile.astype(dtype)


def get_stats(ref, rows):
    dtype = ref.dtype
    tile = ref[ref.shape[0] - stats_rows(dtype) :].astype(jnp.float32)
    lines = [tile[n : n + 1] for n in range(2 * rows * (1 if dtype == jnp.float32 else 3))]
    if dtype != jnp.float32:
        lines = [a + b + c for a, b, c in zip(lines[::3], lines[1::3], lines[2::3])]
    return [(lines[2 * r], lines[2 * r + 1]) for r in range(rows)]


def hint(size, flops=0):
    return pl.CostEstimate(flops=flops, bytes_accessed=size, transcendentals=0)


def dot(left, right, dims):
    return lax.dot_general(left, right, dims, preferred_element_type=jnp.float32)


def swap(x, axis, distance):
    size = lax.axis_size(axis)
    return lax.ppermute(x, axis, [(k, k ^ distance) for k in range(size)])


def distances(size):
    return [0] + list(range(size - 1, 0, -1))


def params(kibibytes):
    return pltpu.CompilerParams(vmem_limit_bytes=kibibytes << 10)


def head_rows(block, row, steps, heads):
    mine = block[row * steps : (row + 1) * steps]
    return jnp.concatenate([mine[:, h * HD : (h + 1) * HD] for h in range(heads)], axis=0)


def dequantize(codes_ref, scales_ref, out_ref):
    columns = scales_ref[...].astype(jnp.float32).T
    for n in range(columns.shape[1]):
        lanes = slice(n * BLK, (n + 1) * BLK)
        values = codes_ref[:, lanes].astype(jnp.float32) * columns[:, n : n + 1]
        out_ref[:, lanes] = values.astype(jnp.bfloat16)


def prepare_kernel(
    rows, steps, own, chunk,
    owner_hbm, lengths_hbm, scales_hbm, codes_hbm, query_hbm, cache_hbm, base_hbm,
    *refs,
):
    delta_ref, base_ref, own_query_ref, places_ref = refs[:4]
    parts = refs[4:-7]
    owner_ref, lengths_ref, scales_ref, codes_ref, query_ref, cache_ref, arrived = refs[-7:]
    order = distances(len(parts))
    place = lax.axis_index("tensor")
    block = codes_ref.shape[0]
    cache_len = cache_ref.shape[0] // rows
    used = []

    def load(source, target):
        copy = pltpu.make_async_copy(source, target, arrived.at[len(used)])
        copy.start()
        used.append(copy)
        return [copy]

    def load_rows(source, first, target, size):
        part = min(PART, size)
        copies = []
        for n in range(0, size, part):
            start = first + n if isinstance(first, int) else pl.multiple_of(first + n, part)
            copies += load(source.at[pl.ds(start, part)], target.at[pl.ds(n, part)])
        return copies

    def wait(copies):
        for copy in copies:
            copy.wait()

    owner_load = load(owner_hbm, owner_ref)
    first_loads = load(lengths_hbm, lengths_ref) + load(scales_hbm, scales_ref)
    first_loads += load_rows(codes_hbm, 0, codes_ref, block) + load(query_hbm, query_ref)
    cache_loads = []
    for r in range(rows):
        target = cache_ref.at[pl.ds(r * cache_len, cache_len)]
        cache_loads.append(load_rows(cache_hbm, r * cache_len, target, cache_len))
    wait(owner_load)
    base_loads = []
    for k in range(2):
        start = pl.multiple_of(owner_ref[lax.axis_index("group") ^ k] * block, block)
        base_loads += load_rows(base_hbm, start, base_ref.at[k], block)
    for n in range(places_ref.shape[0]):
        owner = owner_ref[lax.axis_index("group") ^ n]
        places_ref[n : n + 1] = jnp.full((1, LANES), owner, jnp.int32)
    wait(first_loads)
    dequantize(codes_ref, scales_ref, delta_ref)

    chunks = own // chunk
    height = chunk * steps
    width = chunks * HD
    position = lax.broadcasted_iota(jnp.int32, (cache_len, chunks * height), 0)

    def kv_lane(d):
        return pl.multiple_of(((place ^ d) * own // (H // KVH)) * HD, HD)

    def score(r, d):
        head = (place ^ d) * own
        queries = query_ref[:, pl.ds(pl.multiple_of(head * HD, HD), own * HD)]
        query = head_rows(queries.astype(jnp.float32), r, steps, own)
        if d == 0:
            at = r * chunks * height
            own_query_ref[at : at + chunks * height] = query.astype(jnp.bfloat16)
        spread = []
        for j in range(chunks):
            line = [jnp.zeros((height, HD), jnp.float32)] * chunks
            line[j] = query[j * height : (j + 1) * height]
            spread.append(jnp.concatenate(line, axis=1))
        spread = jnp.concatenate(spread, axis=0).astype(jnp.bfloat16)
        keys = cache_ref[pl.ds(r * cache_len, cache_len), pl.ds(kv_lane(d), width)]
        return dot(keys, spread, NT)

    units = [(r, n) for r in range(rows) for n in range(len(parts))]
    stats = [[] for _ in parts]
    ahead = []
    for at in range(len(units) + 1):
        if at < len(units):
            r, n = units[at]
            if n == 0:
                wait(cache_loads[r])
            ahead.append(score(r, order[n]))
        if at == 0:
            continue
        r, n = units[at - 1]
        usable = position < lengths_ref[r] - place * cache_len
        scores = jnp.where(usable, ahead.pop(0) * SCORE_SCALE, 2.0 * NEGATIVE)
        peak = jnp.maximum(jnp.max(scores, axis=0, keepdims=True), NEGATIVE)
        weights = jnp.exp(scores - peak)
        total = jnp.sum(weights, axis=0, keepdims=True)
        lane = pl.ds(kv_lane(order[n]) + KVH * HD, width)
        values = cache_ref[pl.ds(r * cache_len, cache_len), lane]
        sums = dot(weights.astype(jnp.bfloat16), values, TN)
        for j in range(chunks):
            here = slice(j * height, (j + 1) * height)
            first = (r * chunks + j) * height
            mine = sums[here, j * HD : (j + 1) * HD].astype(parts[n].dtype)
            parts[n][first : first + height] = mine
        stats[n] += [peak, total]
        if r == rows - 1:
            put_stats(parts[n], stats[n])
    wait(base_loads)


def part_shape(height, dtype):
    return jax.ShapeDtypeStruct((height + stats_rows(dtype), LANES), dtype)


def prepare(owner_map, lengths, scales, codes, queries, cache, base, rows, steps, own, ways):
    height = rows * own * steps
    loads = 4 + 3 * -(-codes.shape[0] // PART) + rows * -(-cache.shape[0] // rows // PART)
    operands = [
        pltpu.with_memory_space_constraint(x, pltpu.HBM)
        for x in (owner_map, lengths, scales.T, codes, queries, cache, base)
    ]
    out = pl.pallas_call(
        functools.partial(prepare_kernel, rows, steps, own, min(own, H // KVH)),
        out_shape=[
            jax.ShapeDtypeStruct(codes.shape, jnp.bfloat16),
            jax.ShapeDtypeStruct((2,) + codes.shape, jnp.bfloat16),
            jax.ShapeDtypeStruct((height, HD), jnp.bfloat16),
            jax.ShapeDtypeStruct((owner_map.shape[0], LANES), jnp.int32),
            part_shape(height, jnp.float32),
        ]
        + [part_shape(height, jnp.bfloat16)] * (ways - 1),
        in_specs=[HBM] * len(operands),
        out_specs=[VMEM] * (4 + ways),
        scratch_shapes=[
            pltpu.SMEM(owner_map.shape, owner_map.dtype),
            pltpu.SMEM(lengths.shape, lengths.dtype),
            pltpu.VMEM(scales.shape[::-1], scales.dtype),
            pltpu.VMEM(codes.shape, codes.dtype),
            pltpu.VMEM(queries.shape, queries.dtype),
            pltpu.VMEM(cache.shape, cache.dtype),
            pltpu.SemaphoreType.DMA((loads,)),
        ],
        compiler_params=params(CACHE_KIB),
        cost_estimate=hint(CACHE_HINT, PREPARE_FLOPS),
        name="prepare",
    )(*operands)
    return out[0], out[1], out[2], out[3], list(out[4:])


def merge_kernel(rows, span, *refs):
    parts, out_ref = refs[:-1], refs[-1]
    everything = [get_stats(part, rows) for part in parts]
    stats, factors = [], []
    for r in range(rows):
        peak = functools.reduce(jnp.maximum, [one[r][0] for one in everything])
        scales = [jnp.exp(one[r][0] - peak) for one in everything]
        stats += [peak, sum(one[r][1] * scale for one, scale in zip(everything, scales))]
        factors += scales
    lines = -(-len(factors) // SUBLANES) * SUBLANES
    if lines > len(factors):
        factors.append(jnp.zeros((lines - len(factors), LANES), jnp.float32))
    columns = jnp.concatenate(factors, axis=0).T[:span]
    for r in range(rows):
        here = slice(r * span, (r + 1) * span)
        terms = []
        for n, part in enumerate(parts):
            at = r * len(parts) + n
            terms.append(part[here].astype(jnp.float32) * columns[:, at : at + 1])
        out_ref[here] = sum(terms[1:], terms[0])
    put_stats(out_ref, stats)


def merge(parts, rows):
    height = parts[0].shape[0] - stats_rows(parts[0].dtype)
    return pl.pallas_call(
        functools.partial(merge_kernel, rows, height // rows),
        out_shape=part_shape(height, jnp.float32),
        in_specs=[VMEM] * len(parts),
        out_specs=VMEM,
        compiler_params=params(8192),
        cost_estimate=hint(1000),
        name="merge_partials",
    )(*parts)


def project_kernel(pairs, own_ref, base_ref, codes_ref, scales_ref, *refs):
    tokens, outs, mate_ref = refs[:pairs], refs[pairs:-1], refs[-1]
    block = own_ref.shape[0]
    stacked = jnp.concatenate([ref[...] for ref in tokens], axis=0)
    count = tokens[0].shape[0]

    def put(k, whole):
        whole = whole.T
        for n in range(pairs):
            outs[n][:, k * block : (k + 1) * block] = whole[n * count : (n + 1) * count]

    mine = dot(base_ref[0], stacked, NT) + dot(own_ref[...], stacked, NT)
    other = dot(base_ref[1], stacked, NT)
    dequantize(codes_ref, scales_ref, mate_ref)
    put(0, mine)
    put(1, other + dot(mate_ref[...], stacked, NT))


def project(own, base, mate_codes, mate_scales, tokens):
    pairs = len(tokens)
    block = own.shape[0]
    count = tokens[0].shape[0]
    return pl.pallas_call(
        functools.partial(project_kernel, pairs),
        out_shape=[jax.ShapeDtypeStruct((count, 2 * block), jnp.float32)] * pairs,
        in_specs=[VMEM] * (4 + pairs),
        out_specs=[VMEM] * pairs,
        scratch_shapes=[pltpu.VMEM(own.shape, own.dtype)],
        compiler_params=params(PROJECT_KIB),
        cost_estimate=hint(PROJECT_HINT),
        name="project",
    )(own, base, mate_codes, mate_scales.T, *tokens)


def pack_kernel(pairs, ways, near, wide, block, places_ref, *refs):
    arrived, outs = refs[:pairs], refs[pairs:]
    to_place = lax.axis_index("tensor")
    count = arrived[0].shape[0]
    blocks = []
    for piece, d in zip(arrived, distances(pairs)):
        for k in range(2):
            at = 2 * d + k
            place = jnp.broadcast_to(places_ref[at : at + 1], (count, LANES))
            lanes = [slice(n, n + LANES) for n in range(k * block, (k + 1) * block, LANES)]
            blocks.append((place, [piece[:, one] for one in lanes]))

    def pick(which):
        out = [jnp.zeros((count, LANES), jnp.float32)] * (block // LANES)
        for place, values in blocks:
            out = [jnp.where(place == which, new, old) for new, old in zip(values, out)]
        return jnp.concatenate(out, axis=1)

    for out, d in zip(outs, distances(ways)):
        to = to_place ^ d
        columns = []
        keys = [pick(to * near + n) for n in range(near)]
        columns += keys
        if d != 0:
            columns += [key - key.astype(out.dtype).astype(jnp.float32) for key in keys]
        columns += [pick(pairs + to * near + n) for n in range(near)]
        columns += [pick(to * wide + n) for n in range(wide)]
        for n, values in enumerate(columns):
            out[:, n * block : (n + 1) * block] = values.astype(out.dtype)


def pack_pieces(owner_map, places, arrived, block, ways, near_width, slice_width):
    pairs = len(arrived)
    count = arrived[0].shape[0]
    shards = 2 * pairs
    kv_width = KVH * HD
    if block % LANES == 0 and near_width % block == 0 and slice_width % block == 0:
        piece = jax.ShapeDtypeStruct((count, 2 * near_width + slice_width), jnp.float32)
        sent = jax.ShapeDtypeStruct((count, 3 * near_width + slice_width), jnp.bfloat16)
        kernel = functools.partial(
            pack_kernel, pairs, ways, near_width // block, slice_width // block, block
        )
        return pl.pallas_call(
            kernel,
            out_shape=[piece] + [sent] * (ways - 1),
            in_specs=[VMEM] * (1 + pairs),
            out_specs=[VMEM] * ways,
            compiler_params=params(8192),
            cost_estimate=hint(PACK_HINT),
            name="pack_pieces",
        )(places, *arrived)
    nearest = [arrived[distances(pairs).index(d)] for d in range(pairs)]
    blocks = jnp.stack(nearest, axis=0).reshape(pairs, count, 2, block).transpose(0, 2, 1, 3)
    shard_of = jnp.zeros((shards,), jnp.int32).at[owner_map].set(
        jnp.arange(shards, dtype=jnp.int32)
    )
    taken = jnp.take(
        blocks.reshape(shards, count, block), shard_of ^ lax.axis_index("group"), axis=0
    )
    ordered = taken.transpose(1, 0, 2).reshape(count, shards * block)
    per_device = H // ways
    pieces = []
    for d in distances(ways):
        to = lax.axis_index("tensor") ^ d
        near = (to * per_device // (H // KVH)) * HD
        parts = [(near, near_width), (kv_width + near, near_width), (to * slice_width, slice_width)]
        cuts = [lax.dynamic_slice_in_dim(ordered, start, width, 1) for start, width in parts]
        if d != 0:
            rounded = [cut.astype(jnp.bfloat16) for cut in cuts]
            rest = (cuts[0] - rounded[0].astype(jnp.float32)).astype(jnp.bfloat16)
            cuts = [rounded[0], rest] + rounded[1:]
        pieces.append(jnp.concatenate(cuts, axis=1))
    return pieces


def finish_kernel(rows, steps, own, chunk, near_width, ways, query_ref, *refs):
    pieces, part = refs[:ways], refs[ways]
    new_ref, attended_ref = refs[ways + 1 :]
    chunks = own // chunk
    height = chunk * steps
    span = chunks * height
    summed = pieces[0][...]
    for piece in pieces[1:]:
        came = piece[...].astype(jnp.float32)
        keys = came[:, :near_width] + came[:, near_width : 2 * near_width]
        summed = summed + jnp.concatenate([keys, came[:, 2 * near_width :]], axis=1)
    stored = summed.astype(jnp.bfloat16)
    new_ref[...] = stored[:, 2 * near_width :]
    near = stored[:, : 2 * near_width].astype(jnp.float32)
    key_step = lax.broadcasted_iota(jnp.int32, (steps, span), 0)
    query_step = lax.broadcasted_iota(jnp.int32, (steps, span), 1) % steps
    causal = key_step <= query_step
    scores = []
    for r in range(rows):
        spread = []
        for j in range(chunks):
            line = [jnp.zeros((height, HD), jnp.bfloat16)] * chunks
            line[j] = query_ref[r * span + j * height : r * span + (j + 1) * height]
            spread.append(jnp.concatenate(line, axis=1))
        keys = near[r * steps : (r + 1) * steps, :near_width].astype(jnp.bfloat16)
        scores.append(dot(keys, jnp.concatenate(spread, axis=0), NT) * SCORE_SCALE)
    factors, near_sums = [], []
    for r, (cache_peak, cache_total) in enumerate(get_stats(part, rows)):
        masked = jnp.where(causal, scores[r], NEGATIVE)
        peak = jnp.max(masked, axis=0, keepdims=True)
        weights = jnp.where(causal, jnp.exp(masked - peak), 0.0)
        total = jnp.sum(weights, axis=0, keepdims=True)
        values = near[r * steps : (r + 1) * steps, near_width:].astype(jnp.bfloat16)
        near_sums.append(dot(weights.astype(jnp.bfloat16), values, TN))
        cache_peak, cache_total = cache_peak[:, :span], cache_total[:, :span]
        top = jnp.maximum(peak, cache_peak)
        scales = [jnp.exp(cache_peak - top), jnp.exp(peak - top)]
        whole = cache_total * scales[0] + total * scales[1]
        factors += [scale / whole for scale in scales]
    factors.append(jnp.zeros((SUBLANES - len(factors), span), jnp.float32))
    columns = jnp.concatenate(factors, axis=0)
    if span < LANES:
        pad = jnp.zeros((SUBLANES, LANES - span), jnp.float32)
        columns = jnp.concatenate([columns, pad], axis=1)
    columns = columns.T
    for j in range(chunks):
        here = slice(j * height, (j + 1) * height)
        merged = []
        for r in range(rows):
            cached = part[r * span + j * height : r * span + (j + 1) * height]
            fresh = near_sums[r][here, j * HD : (j + 1) * HD]
            merged.append(
                cached * columns[here, 2 * r : 2 * r + 1]
                + fresh * columns[here, 2 * r + 1 : 2 * r + 2]
            )
        for h in range(chunk):
            both = [out[h * steps : (h + 1) * steps] for out in merged]
            lane = (j * chunk + h) * HD
            attended_ref[:, lane : lane + HD] = jnp.concatenate(both, axis=0).astype(jnp.bfloat16)


def finish(own_query, pieces, part, rows, steps, own, near_width):
    ways = len(pieces)
    count, width = pieces[0].shape
    return pl.pallas_call(
        functools.partial(
            finish_kernel, rows, steps, own, min(own, H // KVH), near_width, ways
        ),
        out_shape=[
            jax.ShapeDtypeStruct((count, width - 2 * near_width), jnp.bfloat16),
            jax.ShapeDtypeStruct((count, own * HD), jnp.bfloat16),
        ],
        in_specs=[VMEM] * (2 + ways),
        out_specs=[VMEM] * 2,
        compiler_params=params(8192),
        name="finish",
    )(own_query, *pieces, part)


def on_device(
    hidden_x, base_weight, delta_codes, delta_scales, owner_map, kv_cache, queries, lengths
):
    group_count = lax.axis_size("group")
    tensor_count = lax.axis_size("tensor")
    rows, steps, local_width = hidden_x.shape
    tokens = rows * steps
    owner_block = delta_codes.shape[0]
    heads_own = H // tensor_count
    slice_width = base_weight.shape[0] // tensor_count
    near_width = max(1, heads_own // (H // KVH)) * HD
    pairs = group_count // 2

    def exchange(arrays, axis, stride):
        places = distances(len(arrays))[1:]
        return [arrays[0]] + [swap(x, axis, stride * d) for x, d in zip(arrays[1:], places)]

    def near_first(arrays):
        return arrays[:1] + arrays[:0:-1]

    token_rows = exchange([hidden_x.reshape(tokens, local_width)] * pairs, "group", 2)
    mate_codes = swap(delta_codes, "group", 1)
    mate_scales = swap(delta_scales, "group", 1)

    own_delta, base_blocks, own_query, places, partials = prepare(
        owner_map,
        lengths,
        delta_scales,
        delta_codes,
        queries.reshape(tokens, H * HD),
        kv_cache.reshape(-1, 2 * KVH * HD),
        base_weight,
        rows,
        steps,
        heads_own,
        tensor_count,
    )
    mate_scales, sent = lax.optimization_barrier((mate_scales, partials[1:]))
    partials = partials[:1] + list(sent)
    behind = lax.optimization_barrier((*near_first(token_rows), own_query))
    token_rows, own_query = near_first(list(behind[:pairs])), behind[-1]
    projected = project(
        own_delta, base_blocks, mate_codes, mate_scales, near_first(token_rows)
    )
    arrived = exchange(near_first(projected), "group", 2)
    partials = exchange(partials, "tensor", 1)
    pieces = pack_pieces(
        owner_map, places, arrived, owner_block, tensor_count, near_width, slice_width
    )
    pieces = exchange(pieces, "tensor", 1)
    partial = merge(near_first(partials), rows)
    new_out, attended = finish(own_query, pieces, partial, rows, steps, heads_own, near_width)
    return (new_out.reshape(rows, steps, -1), attended.reshape(rows, steps, -1))


def solution(mesh):
    in_specs = (
        P("group", None, "tensor"),
        P(None, "tensor"),
        P("group", "tensor"),
        P("group", "tensor"),
        P(),
        P("group", "tensor", None),
        P("group", None, None),
        P("group"),
    )
    out_specs = (P("group", None, "tensor"), P("group", None, "tensor"))
    return jax.shard_map(
        on_device, mesh=mesh, in_specs=in_specs, out_specs=out_specs, check_vma=False
    )
```

```python
import functools
import jax
import jax.numpy as jnp
from jax import lax
from jax.experimental import pallas as pl
from jax.experimental.pallas import tpu as pltpu
from jax.sharding import PartitionSpec as P

H = 64
KVH = 8
HD = 128
BLK = 128
LANES = 128
SUBLANES = 8


NEGATIVE = -1e30
SCORE_SCALE = HD ** (-0.5)
PART = 256
CACHE_HINT = 120_000_000
PROJECT_HINT = 60_000_000
PACK_HINT = 60_000_000
CACHE_KIB = 24 << 10
WEIGHTS_KIB = 16 << 10
PROJECT_KIB = 16 << 10
NT = (((1,), (1,)), ((), ()))
TN = (((0,), (0,)), ((), ()))
VMEM = pl.BlockSpec(memory_space=pltpu.VMEM)
SMEM = pl.BlockSpec(memory_space=pltpu.SMEM)
HBM = pl.BlockSpec(memory_space=pltpu.HBM)


def split(x):
    high = x.astype(jnp.bfloat16).astype(jnp.float32)
    middle = (x - high).astype(jnp.bfloat16).astype(jnp.float32)
    return [high, middle, x - high - middle]


def stats_rows(dtype):
    return SUBLANES if dtype == jnp.float32 else 2 * SUBLANES


def put_stats(ref, stats):
    dtype = ref.dtype
    lines = [x for one in stats for x in ([one] if dtype == jnp.float32 else split(one))]
    lanes = lines[0].shape[1]
    count = stats_rows(dtype)
    lines.append(jnp.zeros((count - len(lines), lanes), jnp.float32))
    tile = jnp.concatenate(lines, axis=0)
    if lanes < LANES:
        tile = jnp.concatenate([tile, jnp.zeros((count, LANES - lanes), jnp.float32)], axis=1)
    ref[ref.shape[0] - count :] = tile.astype(dtype)


def get_stats(ref, rows):
    dtype = ref.dtype
    tile = ref[ref.shape[0] - stats_rows(dtype) :].astype(jnp.float32)
    lines = [tile[n : n + 1] for n in range(2 * rows * (1 if dtype == jnp.float32 else 3))]
    if dtype != jnp.float32:
        lines = [a + b + c for a, b, c in zip(lines[::3], lines[1::3], lines[2::3])]
    return [(lines[2 * r], lines[2 * r + 1]) for r in range(rows)]


def hint(size):
    return pl.CostEstimate(flops=0, bytes_accessed=size, transcendentals=0)


def dot(left, right, dims):
    return lax.dot_general(left, right, dims, preferred_element_type=jnp.float32)


def swap(x, axis, distance):
    size = lax.axis_size(axis)
    return lax.ppermute(x, axis, [(k, k ^ distance) for k in range(size)])


def distances(size):
    return [0] + list(range(size - 1, 0, -1))


def params(kibibytes):
    return pltpu.CompilerParams(vmem_limit_bytes=kibibytes << 10)


def head_rows(block, row, steps, heads):
    mine = block[row * steps : (row + 1) * steps]
    return jnp.concatenate([mine[:, h * HD : (h + 1) * HD] for h in range(heads)], axis=0)


def dequantize(codes_ref, scales_ref, out_ref):
    columns = scales_ref[...].astype(jnp.float32).T
    for n in range(columns.shape[1]):
        lanes = slice(n * BLK, (n + 1) * BLK)
        values = codes_ref[:, lanes].astype(jnp.float32) * columns[:, n : n + 1]
        out_ref[:, lanes] = values.astype(jnp.bfloat16)


def mate_weights(codes, scales):
    return pl.pallas_call(
        dequantize,
        out_shape=jax.ShapeDtypeStruct(codes.shape, jnp.bfloat16),
        in_specs=[VMEM, VMEM],
        out_specs=VMEM,
        compiler_params=params(WEIGHTS_KIB),
        cost_estimate=hint(1000),
        name="mate_weights",
    )(codes, scales.T)


def prepare_kernel(
    rows, steps, own, chunk,
    owner_hbm, lengths_hbm, scales_hbm, codes_hbm, query_hbm, cache_hbm, base_hbm,
    *refs,
):
    delta_ref, base_ref, own_query_ref, places_ref = refs[:4]
    parts = refs[4:-7]
    owner_ref, lengths_ref, scales_ref, codes_ref, query_ref, cache_ref, arrived = refs[-7:]
    order = distances(len(parts))
    place = lax.axis_index("tensor")
    block = codes_ref.shape[0]
    cache_len = cache_ref.shape[0] // rows
    used = []

    def load(source, target):
        copy = pltpu.make_async_copy(source, target, arrived.at[len(used)])
        copy.start()
        used.append(copy)
        return [copy]

    def load_rows(source, first, target, size):
        part = min(PART, size)
        copies = []
        for n in range(0, size, part):
            start = first + n if isinstance(first, int) else pl.multiple_of(first + n, part)
            copies += load(source.at[pl.ds(start, part)], target.at[pl.ds(n, part)])
        return copies

    def wait(copies):
        for copy in copies:
            copy.wait()

    owner_load = load(owner_hbm, owner_ref)
    first_loads = load(lengths_hbm, lengths_ref) + load(scales_hbm, scales_ref)
    first_loads += load_rows(codes_hbm, 0, codes_ref, block) + load(query_hbm, query_ref)
    cache_loads = []
    for r in range(rows):
        target = cache_ref.at[pl.ds(r * cache_len, cache_len)]
        cache_loads.append(load_rows(cache_hbm, r * cache_len, target, cache_len))
    wait(owner_load)
    base_loads = []
    for k in range(2):
        start = pl.multiple_of(owner_ref[lax.axis_index("group") ^ k] * block, block)
        base_loads += load_rows(base_hbm, start, base_ref.at[k], block)
    for n in range(places_ref.shape[0]):
        owner = owner_ref[lax.axis_index("group") ^ n]
        places_ref[n : n + 1] = jnp.full((1, LANES), owner, jnp.int32)
    wait(first_loads)
    dequantize(codes_ref, scales_ref, delta_ref)

    chunks = own // chunk
    height = chunk * steps
    width = chunks * HD
    position = lax.broadcasted_iota(jnp.int32, (cache_len, chunks * height), 0)

    def kv_lane(d):
        return pl.multiple_of(((place ^ d) * own // (H // KVH)) * HD, HD)

    def score(r, d):
        head = (place ^ d) * own
        queries = query_ref[:, pl.ds(pl.multiple_of(head * HD, HD), own * HD)]
        query = head_rows(queries.astype(jnp.float32), r, steps, own)
        if d == 0:
            at = r * chunks * height
            own_query_ref[at : at + chunks * height] = query.astype(jnp.bfloat16)
        spread = []
        for j in range(chunks):
            line = [jnp.zeros((height, HD), jnp.float32)] * chunks
            line[j] = query[j * height : (j + 1) * height]
            spread.append(jnp.concatenate(line, axis=1))
        spread = jnp.concatenate(spread, axis=0).astype(jnp.bfloat16)
        keys = cache_ref[pl.ds(r * cache_len, cache_len), pl.ds(kv_lane(d), width)]
        return dot(keys, spread, NT)

    units = [(r, n) for r in range(rows) for n in range(len(parts))]
    stats = [[] for _ in parts]
    ahead = []
    for at in range(len(units) + 1):
        if at < len(units):
            r, n = units[at]
            if n == 0:
                wait(cache_loads[r])
            ahead.append(score(r, order[n]))
        if at == 0:
            continue
        r, n = units[at - 1]
        usable = position < lengths_ref[r] - place * cache_len
        scores = jnp.where(usable, ahead.pop(0) * SCORE_SCALE, 2.0 * NEGATIVE)
        peak = jnp.maximum(jnp.max(scores, axis=0, keepdims=True), NEGATIVE)
        weights = jnp.exp(scores - peak)
        total = jnp.sum(weights, axis=0, keepdims=True)
        lane = pl.ds(kv_lane(order[n]) + KVH * HD, width)
        values = cache_ref[pl.ds(r * cache_len, cache_len), lane]
        sums = dot(weights.astype(jnp.bfloat16), values, TN)
        for j in range(chunks):
            here = slice(j * height, (j + 1) * height)
            first = (r * chunks + j) * height
            mine = sums[here, j * HD : (j + 1) * HD].astype(parts[n].dtype)
            parts[n][first : first + height] = mine
        stats[n] += [peak, total]
        if r == rows - 1:
            put_stats(parts[n], stats[n])
    wait(base_loads)


def part_shape(height, dtype):
    return jax.ShapeDtypeStruct((height + stats_rows(dtype), LANES), dtype)


def prepare(owner_map, lengths, scales, codes, queries, cache, base, rows, steps, own, ways):
    height = rows * own * steps
    loads = 4 + 3 * -(-codes.shape[0] // PART) + rows * -(-cache.shape[0] // rows // PART)
    operands = [
        pltpu.with_memory_space_constraint(x, pltpu.HBM)
        for x in (owner_map, lengths, scales.T, codes, queries, cache, base)
    ]
    out = pl.pallas_call(
        functools.partial(prepare_kernel, rows, steps, own, min(own, H // KVH)),
        out_shape=[
            jax.ShapeDtypeStruct(codes.shape, jnp.bfloat16),
            jax.ShapeDtypeStruct((2,) + codes.shape, jnp.bfloat16),
            jax.ShapeDtypeStruct((height, HD), jnp.bfloat16),
            jax.ShapeDtypeStruct((owner_map.shape[0], LANES), jnp.int32),
            part_shape(height, jnp.float32),
        ]
        + [part_shape(height, jnp.bfloat16)] * (ways - 1),
        in_specs=[HBM] * len(operands),
        out_specs=[VMEM] * (4 + ways),
        scratch_shapes=[
            pltpu.SMEM(owner_map.shape, owner_map.dtype),
            pltpu.SMEM(lengths.shape, lengths.dtype),
            pltpu.VMEM(scales.shape[::-1], scales.dtype),
            pltpu.VMEM(codes.shape, codes.dtype),
            pltpu.VMEM(queries.shape, queries.dtype),
            pltpu.VMEM(cache.shape, cache.dtype),
            pltpu.SemaphoreType.DMA((loads,)),
        ],
        compiler_params=params(CACHE_KIB),
        cost_estimate=hint(CACHE_HINT),
        name="prepare",
    )(*operands)
    return out[0], out[1], out[2], out[3], out[4:]


def merge_kernel(rows, span, *refs):
    parts, out_ref = refs[:-1], refs[-1]
    everything = [get_stats(part, rows) for part in parts]
    stats, factors = [], []
    for r in range(rows):
        peak = functools.reduce(jnp.maximum, [one[r][0] for one in everything])
        scales = [jnp.exp(one[r][0] - peak) for one in everything]
        stats += [peak, sum(one[r][1] * scale for one, scale in zip(everything, scales))]
        factors += scales
    lines = -(-len(factors) // SUBLANES) * SUBLANES
    if lines > len(factors):
        factors.append(jnp.zeros((lines - len(factors), LANES), jnp.float32))
    columns = jnp.concatenate(factors, axis=0).T[:span]
    for r in range(rows):
        here = slice(r * span, (r + 1) * span)
        terms = []
        for n, part in enumerate(parts):
            at = r * len(parts) + n
            terms.append(part[here].astype(jnp.float32) * columns[:, at : at + 1])
        out_ref[here] = sum(terms[1:], terms[0])
    put_stats(out_ref, stats)


def merge(parts, rows):
    height = parts[0].shape[0] - stats_rows(parts[0].dtype)
    return pl.pallas_call(
        functools.partial(merge_kernel, rows, height // rows),
        out_shape=part_shape(height, jnp.float32),
        in_specs=[VMEM] * len(parts),
        out_specs=VMEM,
        compiler_params=params(8192),
        cost_estimate=hint(1000),
        name="merge_partials",
    )(*parts)


def project_kernel(pairs, own_ref, mate_ref, base_ref, *refs):
    tokens, outs = refs[:pairs], refs[pairs:]
    block = own_ref.shape[0]
    stacked = jnp.concatenate([ref[...] for ref in tokens], axis=0)
    count = tokens[0].shape[0]
    for k, delta_ref in enumerate((own_ref, mate_ref)):
        whole = (dot(base_ref[k], stacked, NT) + dot(delta_ref[...], stacked, NT)).T
        for n in range(pairs):
            outs[n][:, k * block : (k + 1) * block] = whole[n * count : (n + 1) * count]


def project(own, mate, base, tokens):
    pairs = len(tokens)
    block = own.shape[0]
    count, width = tokens[0].shape
    return pl.pallas_call(
        functools.partial(project_kernel, pairs),
        out_shape=[jax.ShapeDtypeStruct((count, 2 * block), jnp.float32)] * pairs,
        in_specs=[VMEM] * (3 + pairs),
        out_specs=[VMEM] * pairs,
        compiler_params=params(PROJECT_KIB),
        cost_estimate=hint(PROJECT_HINT),
        name="project",
    )(own, mate, base, *tokens)


def pack_kernel(pairs, ways, near, wide, block, places_ref, *refs):
    arrived, outs = refs[:pairs], refs[pairs:]
    to_place = lax.axis_index("tensor")
    count = arrived[0].shape[0]
    blocks = []
    for piece, d in zip(arrived, distances(pairs)):
        for k in range(2):
            at = 2 * d + k
            place = jnp.broadcast_to(places_ref[at : at + 1], (count, LANES))
            lanes = [slice(n, n + LANES) for n in range(k * block, (k + 1) * block, LANES)]
            blocks.append((place, [piece[:, one] for one in lanes]))

    def pick(which):
        out = [jnp.zeros((count, LANES), jnp.float32)] * (block // LANES)
        for place, values in blocks:
            out = [jnp.where(place == which, new, old) for new, old in zip(values, out)]
        return jnp.concatenate(out, axis=1)

    for out, d in zip(outs, distances(ways)):
        to = to_place ^ d
        columns = []
        keys = [pick(to * near + n) for n in range(near)]
        columns += keys
        if d != 0:
            columns += [key - key.astype(out.dtype).astype(jnp.float32) for key in keys]
        columns += [pick(pairs + to * near + n) for n in range(near)]
        columns += [pick(to * wide + n) for n in range(wide)]
        for n, values in enumerate(columns):
            out[:, n * block : (n + 1) * block] = values.astype(out.dtype)


def pack_pieces(owner_map, places, arrived, block, ways, near_width, slice_width):
    pairs = len(arrived)
    count = arrived[0].shape[0]
    shards = 2 * pairs
    kv_width = KVH * HD
    if block % LANES == 0 and near_width % block == 0 and slice_width % block == 0:
        piece = jax.ShapeDtypeStruct((count, 2 * near_width + slice_width), jnp.float32)
        sent = jax.ShapeDtypeStruct((count, 3 * near_width + slice_width), jnp.bfloat16)
        kernel = functools.partial(
            pack_kernel, pairs, ways, near_width // block, slice_width // block, block
        )
        return pl.pallas_call(
            kernel,
            out_shape=[piece] + [sent] * (ways - 1),
            in_specs=[VMEM] * (1 + pairs),
            out_specs=[VMEM] * ways,
            compiler_params=params(8192),
            cost_estimate=hint(PACK_HINT),
            name="pack_pieces",
        )(places, *arrived)
    nearest = [arrived[distances(pairs).index(d)] for d in range(pairs)]
    blocks = jnp.stack(nearest, axis=0).reshape(pairs, count, 2, block).transpose(0, 2, 1, 3)
    shard_of = jnp.zeros((shards,), jnp.int32).at[owner_map].set(
        jnp.arange(shards, dtype=jnp.int32)
    )
    taken = jnp.take(
        blocks.reshape(shards, count, block), shard_of ^ lax.axis_index("group"), axis=0
    )
    ordered = taken.transpose(1, 0, 2).reshape(count, shards * block)
    per_device = H // ways
    pieces = []
    for d in distances(ways):
        to = lax.axis_index("tensor") ^ d
        near = (to * per_device // (H // KVH)) * HD
        parts = [(near, near_width), (kv_width + near, near_width), (to * slice_width, slice_width)]
        cuts = [lax.dynamic_slice_in_dim(ordered, start, width, 1) for start, width in parts]
        if d != 0:
            rounded = [cut.astype(jnp.bfloat16) for cut in cuts]
            rest = (cuts[0] - rounded[0].astype(jnp.float32)).astype(jnp.bfloat16)
            cuts = [rounded[0], rest] + rounded[1:]
        pieces.append(jnp.concatenate(cuts, axis=1))
    return pieces


def finish_kernel(rows, steps, own, chunk, near_width, ways, query_ref, *refs):
    pieces, part = refs[:ways], refs[ways]
    new_ref, attended_ref = refs[ways + 1 :]
    chunks = own // chunk
    height = chunk * steps
    span = chunks * height
    summed = pieces[0][...]
    for piece in pieces[1:]:
        came = piece[...].astype(jnp.float32)
        keys = came[:, :near_width] + came[:, near_width : 2 * near_width]
        summed = summed + jnp.concatenate([keys, came[:, 2 * near_width :]], axis=1)
    stored = summed.astype(jnp.bfloat16)
    new_ref[...] = stored[:, 2 * near_width :]
    near = stored[:, : 2 * near_width].astype(jnp.float32)
    key_step = lax.broadcasted_iota(jnp.int32, (steps, span), 0)
    query_step = lax.broadcasted_iota(jnp.int32, (steps, span), 1) % steps
    causal = key_step <= query_step
    scores = []
    for r in range(rows):
        spread = []
        for j in range(chunks):
            line = [jnp.zeros((height, HD), jnp.bfloat16)] * chunks
            line[j] = query_ref[r * span + j * height : r * span + (j + 1) * height]
            spread.append(jnp.concatenate(line, axis=1))
        keys = near[r * steps : (r + 1) * steps, :near_width].astype(jnp.bfloat16)
        scores.append(dot(keys, jnp.concatenate(spread, axis=0), NT) * SCORE_SCALE)
    factors, near_sums = [], []
    for r, (cache_peak, cache_total) in enumerate(get_stats(part, rows)):
        masked = jnp.where(causal, scores[r], NEGATIVE)
        peak = jnp.max(masked, axis=0, keepdims=True)
        weights = jnp.where(causal, jnp.exp(masked - peak), 0.0)
        total = jnp.sum(weights, axis=0, keepdims=True)
        values = near[r * steps : (r + 1) * steps, near_width:].astype(jnp.bfloat16)
        near_sums.append(dot(weights.astype(jnp.bfloat16), values, TN))
        cache_peak, cache_total = cache_peak[:, :span], cache_total[:, :span]
        top = jnp.maximum(peak, cache_peak)
        scales = [jnp.exp(cache_peak - top), jnp.exp(peak - top)]
        whole = cache_total * scales[0] + total * scales[1]
        factors += [scale / whole for scale in scales]
    factors.append(jnp.zeros((SUBLANES - len(factors), span), jnp.float32))
    columns = jnp.concatenate(factors, axis=0)
    if span < LANES:
        pad = jnp.zeros((SUBLANES, LANES - span), jnp.float32)
        columns = jnp.concatenate([columns, pad], axis=1)
    columns = columns.T
    for j in range(chunks):
        here = slice(j * height, (j + 1) * height)
        merged = []
        for r in range(rows):
            cached = part[r * span + j * height : r * span + (j + 1) * height]
            fresh = near_sums[r][here, j * HD : (j + 1) * HD]
            merged.append(
                cached * columns[here, 2 * r : 2 * r + 1]
                + fresh * columns[here, 2 * r + 1 : 2 * r + 2]
            )
        for h in range(chunk):
            both = [out[h * steps : (h + 1) * steps] for out in merged]
            lane = (j * chunk + h) * HD
            attended_ref[:, lane : lane + HD] = jnp.concatenate(both, axis=0).astype(jnp.bfloat16)


def finish(own_query, pieces, part, rows, steps, own, near_width):
    ways = len(pieces)
    count, width = pieces[0].shape
    return pl.pallas_call(
        functools.partial(
            finish_kernel, rows, steps, own, min(own, H // KVH), near_width, ways
        ),
        out_shape=[
            jax.ShapeDtypeStruct((count, width - 2 * near_width), jnp.bfloat16),
            jax.ShapeDtypeStruct((count, own * HD), jnp.bfloat16),
        ],
        in_specs=[VMEM] * (2 + ways),
        out_specs=[VMEM] * 2,
        compiler_params=params(8192),
        name="finish",
    )(own_query, *pieces, part)


def on_device(
    hidden_x, base_weight, delta_codes, delta_scales, owner_map, kv_cache, queries, lengths
):
    group_count = lax.axis_size("group")
    tensor_count = lax.axis_size("tensor")
    rows, steps, local_width = hidden_x.shape
    tokens = rows * steps
    owner_block = delta_codes.shape[0]
    heads_own = H // tensor_count
    slice_width = base_weight.shape[0] // tensor_count
    near_width = max(1, heads_own // (H // KVH)) * HD
    pairs = group_count // 2

    def exchange(arrays, axis, stride):
        places = distances(len(arrays))[1:]
        return [arrays[0]] + [swap(x, axis, stride * d) for x, d in zip(arrays[1:], places)]

    def near_first(arrays):
        return arrays[:1] + arrays[:0:-1]

    token_rows = exchange([hidden_x.reshape(tokens, local_width)] * pairs, "group", 2)
    mate_codes = swap(delta_codes, "group", 1)
    mate_scales = swap(delta_scales, "group", 1)

    own_delta, base_blocks, own_query, places, partials = prepare(
        owner_map,
        lengths,
        delta_scales,
        delta_codes,
        queries.reshape(tokens, H * HD),
        kv_cache.reshape(-1, 2 * KVH * HD),
        base_weight,
        rows,
        steps,
        heads_own,
        tensor_count,
    )
    mate_delta = mate_weights(mate_codes, mate_scales)
    behind = lax.optimization_barrier((*near_first(token_rows), mate_delta, own_query))
    token_rows, mate_delta, own_query = near_first(list(behind[:pairs])), behind[-2], behind[-1]
    projected = project(own_delta, mate_delta, base_blocks, near_first(token_rows))
    arrived = exchange(near_first(projected), "group", 2)
    partials = exchange(partials, "tensor", 1)
    pieces = pack_pieces(
        owner_map, places, arrived, owner_block, tensor_count, near_width, slice_width
    )
    pieces = exchange(pieces, "tensor", 1)
    partial = merge(near_first(partials), rows)
    new_out, attended = finish(own_query, pieces, partial, rows, steps, heads_own, near_width)
    return (new_out.reshape(rows, steps, -1), attended.reshape(rows, steps, -1))


def solution(mesh):
    in_specs = (
        P("group", None, "tensor"),
        P(None, "tensor"),
        P("group", "tensor"),
        P("group", "tensor"),
        P(),
        P("group", "tensor", None),
        P("group", None, None),
        P("group"),
    )
    out_specs = (P("group", None, "tensor"), P("group", None, "tensor"))
    return jax.shard_map(
        on_device, mesh=mesh, in_specs=in_specs, out_specs=out_specs, check_vma=False
    )
```

```python
import functools
import jax
import jax.numpy as jnp
from jax import lax
from jax.experimental import pallas as pl
from jax.experimental.pallas import tpu as pltpu
from jax.sharding import PartitionSpec as P

H = 64
KVH = 8
HD = 128
BLK = 128
LANES = 128
SUBLANES = 8


NEGATIVE = -1e30
SCORE_SCALE = HD ** (-0.5)
PART = 256
PREPARE_FLOPS = 15_000_000_000
CACHE_HINT = 120_000_000
PROJECT_HINT = 60_000_000
PACK_HINT = 60_000_000
CACHE_KIB = 24 << 10
PROJECT_KIB = 16 << 10
NT = (((1,), (1,)), ((), ()))
TN = (((0,), (0,)), ((), ()))
VMEM = pl.BlockSpec(memory_space=pltpu.VMEM)
SMEM = pl.BlockSpec(memory_space=pltpu.SMEM)
HBM = pl.BlockSpec(memory_space=pltpu.HBM)


def split(x):
    high = x.astype(jnp.bfloat16).astype(jnp.float32)
    middle = (x - high).astype(jnp.bfloat16).astype(jnp.float32)
    return [high, middle, x - high - middle]


def stats_rows(dtype):
    return SUBLANES if dtype == jnp.float32 else 2 * SUBLANES


def put_stats(ref, stats):
    dtype = ref.dtype
    lines = [x for one in stats for x in ([one] if dtype == jnp.float32 else split(one))]
    lanes = lines[0].shape[1]
    count = stats_rows(dtype)
    lines.append(jnp.zeros((count - len(lines), lanes), jnp.float32))
    tile = jnp.concatenate(lines, axis=0)
    if lanes < LANES:
        tile = jnp.concatenate([tile, jnp.zeros((count, LANES - lanes), jnp.float32)], axis=1)
    ref[ref.shape[0] - count :] = tile.astype(dtype)


def get_stats(ref, rows):
    dtype = ref.dtype
    tile = ref[ref.shape[0] - stats_rows(dtype) :].astype(jnp.float32)
    lines = [tile[n : n + 1] for n in range(2 * rows * (1 if dtype == jnp.float32 else 3))]
    if dtype != jnp.float32:
        lines = [a + b + c for a, b, c in zip(lines[::3], lines[1::3], lines[2::3])]
    return [(lines[2 * r], lines[2 * r + 1]) for r in range(rows)]


def hint(size, flops=0):
    return pl.CostEstimate(flops=flops, bytes_accessed=size, transcendentals=0)


def dot(left, right, dims):
    return lax.dot_general(left, right, dims, preferred_element_type=jnp.float32)


def swap(x, axis, distance):
    size = lax.axis_size(axis)
    return lax.ppermute(x, axis, [(k, k ^ distance) for k in range(size)])


def distances(size):
    return [0] + list(range(size - 1, 0, -1))


def params(kibibytes):
    return pltpu.CompilerParams(vmem_limit_bytes=kibibytes << 10)


def head_rows(block, row, steps, heads):
    mine = block[row * steps : (row + 1) * steps]
    return jnp.concatenate([mine[:, h * HD : (h + 1) * HD] for h in range(heads)], axis=0)


def dequantize(codes_ref, scales_ref, out_ref):
    columns = scales_ref[...].astype(jnp.float32).T
    for n in range(columns.shape[1]):
        lanes = slice(n * BLK, (n + 1) * BLK)
        values = codes_ref[:, lanes].astype(jnp.float32) * columns[:, n : n + 1]
        out_ref[:, lanes] = values.astype(jnp.bfloat16)


def prepare_kernel(
    rows, steps, own, chunk,
    owner_hbm, lengths_hbm, scales_hbm, codes_hbm, query_hbm, cache_hbm, base_hbm,
    *refs,
):
    delta_ref, base_ref, own_query_ref, places_ref = refs[:4]
    parts = refs[4:-7]
    owner_ref, lengths_ref, scales_ref, codes_ref, query_ref, cache_ref, arrived = refs[-7:]
    order = distances(len(parts))
    place = lax.axis_index("tensor")
    block = codes_ref.shape[0]
    cache_len = cache_ref.shape[0] // rows
    used = []

    def load(source, target):
        copy = pltpu.make_async_copy(source, target, arrived.at[len(used)])
        copy.start()
        used.append(copy)
        return [copy]

    def load_rows(source, first, target, size):
        part = min(PART, size)
        copies = []
        for n in range(0, size, part):
            start = first + n if isinstance(first, int) else pl.multiple_of(first + n, part)
            copies += load(source.at[pl.ds(start, part)], target.at[pl.ds(n, part)])
        return copies

    def wait(copies):
        for copy in copies:
            copy.wait()

    owner_load = load(owner_hbm, owner_ref)
    first_loads = load(lengths_hbm, lengths_ref) + load(scales_hbm, scales_ref)
    first_loads += load_rows(codes_hbm, 0, codes_ref, block) + load(query_hbm, query_ref)
    cache_loads = []
    for r in range(rows):
        target = cache_ref.at[pl.ds(r * cache_len, cache_len)]
        cache_loads.append(load_rows(cache_hbm, r * cache_len, target, cache_len))
    wait(owner_load)
    base_loads = []
    for k in range(2):
        start = pl.multiple_of(owner_ref[lax.axis_index("group") ^ k] * block, block)
        base_loads += load_rows(base_hbm, start, base_ref.at[k], block)
    for n in range(places_ref.shape[0]):
        owner = owner_ref[lax.axis_index("group") ^ n]
        places_ref[n : n + 1] = jnp.full((1, LANES), owner, jnp.int32)
    wait(first_loads)
    dequantize(codes_ref, scales_ref, delta_ref)

    chunks = own // chunk
    height = chunk * steps
    width = chunks * HD
    position = lax.broadcasted_iota(jnp.int32, (cache_len, chunks * height), 0)

    def kv_lane(d):
        return pl.multiple_of(((place ^ d) * own // (H // KVH)) * HD, HD)

    def score(r, d):
        head = (place ^ d) * own
        queries = query_ref[:, pl.ds(pl.multiple_of(head * HD, HD), own * HD)]
        query = head_rows(queries.astype(jnp.float32), r, steps, own)
        if d == 0:
            at = r * chunks * height
            own_query_ref[at : at + chunks * height] = query.astype(jnp.bfloat16)
        spread = []
        for j in range(chunks):
            line = [jnp.zeros((height, HD), jnp.float32)] * chunks
            line[j] = query[j * height : (j + 1) * height]
            spread.append(jnp.concatenate(line, axis=1))
        spread = jnp.concatenate(spread, axis=0).astype(jnp.bfloat16)
        keys = cache_ref[pl.ds(r * cache_len, cache_len), pl.ds(kv_lane(d), width)]
        return dot(keys, spread, NT)

    units = [(r, n) for r in range(rows) for n in range(len(parts))]
    stats = [[] for _ in parts]
    ahead = []
    for at in range(len(units) + 1):
        if at < len(units):
            r, n = units[at]
            if n == 0:
                wait(cache_loads[r])
            ahead.append(score(r, order[n]))
        if at == 0:
            continue
        r, n = units[at - 1]
        usable = position < lengths_ref[r] - place * cache_len
        scores = jnp.where(usable, ahead.pop(0) * SCORE_SCALE, 2.0 * NEGATIVE)
        peak = jnp.maximum(jnp.max(scores, axis=0, keepdims=True), NEGATIVE)
        weights = jnp.exp(scores - peak)
        total = jnp.sum(weights, axis=0, keepdims=True)
        lane = pl.ds(kv_lane(order[n]) + KVH * HD, width)
        values = cache_ref[pl.ds(r * cache_len, cache_len), lane]
        sums = dot(weights.astype(jnp.bfloat16), values, TN)
        for j in range(chunks):
            here = slice(j * height, (j + 1) * height)
            first = (r * chunks + j) * height
            mine = sums[here, j * HD : (j + 1) * HD].astype(parts[n].dtype)
            parts[n][first : first + height] = mine
        stats[n] += [peak, total]
        if r == rows - 1:
            put_stats(parts[n], stats[n])
    wait(base_loads)


def part_shape(height, dtype):
    return jax.ShapeDtypeStruct((height + stats_rows(dtype), LANES), dtype)


def prepare(owner_map, lengths, scales, codes, queries, cache, base, rows, steps, own, ways):
    height = rows * own * steps
    loads = 4 + 3 * -(-codes.shape[0] // PART) + rows * -(-cache.shape[0] // rows // PART)
    operands = [
        pltpu.with_memory_space_constraint(x, pltpu.HBM)
        for x in (owner_map, lengths, scales.T, codes, queries, cache, base)
    ]
    out = pl.pallas_call(
        functools.partial(prepare_kernel, rows, steps, own, min(own, H // KVH)),
        out_shape=[
            jax.ShapeDtypeStruct(codes.shape, jnp.bfloat16),
            jax.ShapeDtypeStruct((2,) + codes.shape, jnp.bfloat16),
            jax.ShapeDtypeStruct((height, HD), jnp.bfloat16),
            jax.ShapeDtypeStruct((owner_map.shape[0], LANES), jnp.int32),
            part_shape(height, jnp.float32),
        ]
        + [part_shape(height, jnp.bfloat16)] * (ways - 1),
        in_specs=[HBM] * len(operands),
        out_specs=[VMEM] * (4 + ways),
        scratch_shapes=[
            pltpu.SMEM(owner_map.shape, owner_map.dtype),
            pltpu.SMEM(lengths.shape, lengths.dtype),
            pltpu.VMEM(scales.shape[::-1], scales.dtype),
            pltpu.VMEM(codes.shape, codes.dtype),
            pltpu.VMEM(queries.shape, queries.dtype),
            pltpu.VMEM(cache.shape, cache.dtype),
            pltpu.SemaphoreType.DMA((loads,)),
        ],
        compiler_params=params(CACHE_KIB),
        cost_estimate=hint(CACHE_HINT, PREPARE_FLOPS),
        name="prepare",
    )(*operands)
    return out[0], out[1], out[2], out[3], list(out[4:])


def merge_kernel(rows, span, *refs):
    parts, out_ref = refs[:-1], refs[-1]
    everything = [get_stats(part, rows) for part in parts]
    stats, factors = [], []
    for r in range(rows):
        peak = functools.reduce(jnp.maximum, [one[r][0] for one in everything])
        scales = [jnp.exp(one[r][0] - peak) for one in everything]
        stats += [peak, sum(one[r][1] * scale for one, scale in zip(everything, scales))]
        factors += scales
    lines = -(-len(factors) // SUBLANES) * SUBLANES
    if lines > len(factors):
        factors.append(jnp.zeros((lines - len(factors), LANES), jnp.float32))
    columns = jnp.concatenate(factors, axis=0).T[:span]
    for r in range(rows):
        here = slice(r * span, (r + 1) * span)
        terms = []
        for n, part in enumerate(parts):
            at = r * len(parts) + n
            terms.append(part[here].astype(jnp.float32) * columns[:, at : at + 1])
        out_ref[here] = sum(terms[1:], terms[0])
    put_stats(out_ref, stats)


def merge(parts, rows):
    height = parts[0].shape[0] - stats_rows(parts[0].dtype)
    return pl.pallas_call(
        functools.partial(merge_kernel, rows, height // rows),
        out_shape=part_shape(height, jnp.float32),
        in_specs=[VMEM] * len(parts),
        out_specs=VMEM,
        compiler_params=params(8192),
        cost_estimate=hint(1000),
        name="merge_partials",
    )(*parts)


def project_kernel(pairs, own_ref, base_ref, codes_ref, scales_ref, *refs):
    tokens, outs, mate_ref = refs[:pairs], refs[pairs:-1], refs[-1]
    block = own_ref.shape[0]
    stacked = jnp.concatenate([ref[...] for ref in tokens], axis=0)
    count = tokens[0].shape[0]

    def put(k, whole):
        whole = whole.T
        for n in range(pairs):
            outs[n][:, k * block : (k + 1) * block] = whole[n * count : (n + 1) * count]

    mine = dot(base_ref[0], stacked, NT) + dot(own_ref[...], stacked, NT)
    other = dot(base_ref[1], stacked, NT)
    dequantize(codes_ref, scales_ref, mate_ref)
    put(0, mine)
    put(1, other + dot(mate_ref[...], stacked, NT))


def project(own, base, mate_codes, mate_scales, tokens):
    pairs = len(tokens)
    block = own.shape[0]
    count = tokens[0].shape[0]
    return pl.pallas_call(
        functools.partial(project_kernel, pairs),
        out_shape=[jax.ShapeDtypeStruct((count, 2 * block), jnp.float32)] * pairs,
        in_specs=[VMEM] * (4 + pairs),
        out_specs=[VMEM] * pairs,
        scratch_shapes=[pltpu.VMEM(own.shape, own.dtype)],
        compiler_params=params(PROJECT_KIB),
        cost_estimate=hint(PROJECT_HINT),
        name="project",
    )(own, base, mate_codes, mate_scales.T, *tokens)


def pack_kernel(pairs, ways, near, wide, block, places_ref, *refs):
    arrived, outs = refs[:pairs], refs[pairs:]
    to_place = lax.axis_index("tensor")
    count = arrived[0].shape[0]
    blocks = []
    for piece, d in zip(arrived, distances(pairs)):
        for k in range(2):
            at = 2 * d + k
            place = jnp.broadcast_to(places_ref[at : at + 1], (count, LANES))
            lanes = [slice(n, n + LANES) for n in range(k * block, (k + 1) * block, LANES)]
            blocks.append((place, [piece[:, one] for one in lanes]))

    def pick(which):
        out = [jnp.zeros((count, LANES), jnp.float32)] * (block // LANES)
        for place, values in blocks:
            out = [jnp.where(place == which, new, old) for new, old in zip(values, out)]
        return jnp.concatenate(out, axis=1)

    for out, d in zip(outs, distances(ways)):
        to = to_place ^ d
        columns = []
        keys = [pick(to * near + n) for n in range(near)]
        columns += keys
        if d != 0:
            columns += [key - key.astype(out.dtype).astype(jnp.float32) for key in keys]
        columns += [pick(pairs + to * near + n) for n in range(near)]
        columns += [pick(to * wide + n) for n in range(wide)]
        for n, values in enumerate(columns):
            out[:, n * block : (n + 1) * block] = values.astype(out.dtype)


def pack_pieces(owner_map, places, arrived, block, ways, near_width, slice_width):
    pairs = len(arrived)
    count = arrived[0].shape[0]
    shards = 2 * pairs
    kv_width = KVH * HD
    if block % LANES == 0 and near_width % block == 0 and slice_width % block == 0:
        piece = jax.ShapeDtypeStruct((count, 2 * near_width + slice_width), jnp.float32)
        sent = jax.ShapeDtypeStruct((count, 3 * near_width + slice_width), jnp.bfloat16)
        kernel = functools.partial(
            pack_kernel, pairs, ways, near_width // block, slice_width // block, block
        )
        return pl.pallas_call(
            kernel,
            out_shape=[piece] + [sent] * (ways - 1),
            in_specs=[VMEM] * (1 + pairs),
            out_specs=[VMEM] * ways,
            compiler_params=params(8192),
            cost_estimate=hint(PACK_HINT),
            name="pack_pieces",
        )(places, *arrived)
    nearest = [arrived[distances(pairs).index(d)] for d in range(pairs)]
    blocks = jnp.stack(nearest, axis=0).reshape(pairs, count, 2, block).transpose(0, 2, 1, 3)
    shard_of = jnp.zeros((shards,), jnp.int32).at[owner_map].set(
        jnp.arange(shards, dtype=jnp.int32)
    )
    taken = jnp.take(
        blocks.reshape(shards, count, block), shard_of ^ lax.axis_index("group"), axis=0
    )
    ordered = taken.transpose(1, 0, 2).reshape(count, shards * block)
    per_device = H // ways
    pieces = []
    for d in distances(ways):
        to = lax.axis_index("tensor") ^ d
        near = (to * per_device // (H // KVH)) * HD
        parts = [(near, near_width), (kv_width + near, near_width), (to * slice_width, slice_width)]
        cuts = [lax.dynamic_slice_in_dim(ordered, start, width, 1) for start, width in parts]
        if d != 0:
            rounded = [cut.astype(jnp.bfloat16) for cut in cuts]
            rest = (cuts[0] - rounded[0].astype(jnp.float32)).astype(jnp.bfloat16)
            cuts = [rounded[0], rest] + rounded[1:]
        pieces.append(jnp.concatenate(cuts, axis=1))
    return pieces


def finish_kernel(rows, steps, own, chunk, near_width, ways, query_ref, *refs):
    pieces, part = refs[:ways], refs[ways]
    new_ref, attended_ref = refs[ways + 1 :]
    chunks = own // chunk
    height = chunk * steps
    span = chunks * height
    summed = pieces[0][...]
    for piece in pieces[1:]:
        came = piece[...].astype(jnp.float32)
        keys = came[:, :near_width] + came[:, near_width : 2 * near_width]
        summed = summed + jnp.concatenate([keys, came[:, 2 * near_width :]], axis=1)
    stored = summed.astype(jnp.bfloat16)
    new_ref[...] = stored[:, 2 * near_width :]
    near = stored[:, : 2 * near_width].astype(jnp.float32)
    key_step = lax.broadcasted_iota(jnp.int32, (steps, span), 0)
    query_step = lax.broadcasted_iota(jnp.int32, (steps, span), 1) % steps
    causal = key_step <= query_step
    scores = []
    for r in range(rows):
        spread = []
        for j in range(chunks):
            line = [jnp.zeros((height, HD), jnp.bfloat16)] * chunks
            line[j] = query_ref[r * span + j * height : r * span + (j + 1) * height]
            spread.append(jnp.concatenate(line, axis=1))
        keys = near[r * steps : (r + 1) * steps, :near_width].astype(jnp.bfloat16)
        scores.append(dot(keys, jnp.concatenate(spread, axis=0), NT) * SCORE_SCALE)
    factors, near_sums = [], []
    for r, (cache_peak, cache_total) in enumerate(get_stats(part, rows)):
        masked = jnp.where(causal, scores[r], NEGATIVE)
        peak = jnp.max(masked, axis=0, keepdims=True)
        weights = jnp.where(causal, jnp.exp(masked - peak), 0.0)
        total = jnp.sum(weights, axis=0, keepdims=True)
        values = near[r * steps : (r + 1) * steps, near_width:].astype(jnp.bfloat16)
        near_sums.append(dot(weights.astype(jnp.bfloat16), values, TN))
        cache_peak, cache_total = cache_peak[:, :span], cache_total[:, :span]
        top = jnp.maximum(peak, cache_peak)
        scales = [jnp.exp(cache_peak - top), jnp.exp(peak - top)]
        whole = cache_total * scales[0] + total * scales[1]
        factors += [scale / whole for scale in scales]
    factors.append(jnp.zeros((SUBLANES - len(factors), span), jnp.float32))
    columns = jnp.concatenate(factors, axis=0)
    if span < LANES:
        pad = jnp.zeros((SUBLANES, LANES - span), jnp.float32)
        columns = jnp.concatenate([columns, pad], axis=1)
    columns = columns.T
    for j in range(chunks):
        here = slice(j * height, (j + 1) * height)
        merged = []
        for r in range(rows):
            cached = part[r * span + j * height : r * span + (j + 1) * height]
            fresh = near_sums[r][here, j * HD : (j + 1) * HD]
            merged.append(
                cached * columns[here, 2 * r : 2 * r + 1]
                + fresh * columns[here, 2 * r + 1 : 2 * r + 2]
            )
        for h in range(chunk):
            both = [out[h * steps : (h + 1) * steps] for out in merged]
            lane = (j * chunk + h) * HD
            attended_ref[:, lane : lane + HD] = jnp.concatenate(both, axis=0).astype(jnp.bfloat16)


def finish(own_query, pieces, part, rows, steps, own, near_width):
    ways = len(pieces)
    count, width = pieces[0].shape
    return pl.pallas_call(
        functools.partial(
            finish_kernel, rows, steps, own, min(own, H // KVH), near_width, ways
        ),
        out_shape=[
            jax.ShapeDtypeStruct((count, width - 2 * near_width), jnp.bfloat16),
            jax.ShapeDtypeStruct((count, own * HD), jnp.bfloat16),
        ],
        in_specs=[VMEM] * (2 + ways),
        out_specs=[VMEM] * 2,
        compiler_params=params(8192),
        name="finish",
    )(own_query, *pieces, part)


def on_device(
    hidden_x, base_weight, delta_codes, delta_scales, owner_map, kv_cache, queries, lengths
):
    group_count = lax.axis_size("group")
    tensor_count = lax.axis_size("tensor")
    rows, steps, local_width = hidden_x.shape
    tokens = rows * steps
    owner_block = delta_codes.shape[0]
    heads_own = H // tensor_count
    slice_width = base_weight.shape[0] // tensor_count
    near_width = max(1, heads_own // (H // KVH)) * HD
    pairs = group_count // 2

    def exchange(arrays, axis, stride):
        places = distances(len(arrays))[1:]
        return [arrays[0]] + [swap(x, axis, stride * d) for x, d in zip(arrays[1:], places)]

    def near_first(arrays):
        return arrays[:1] + arrays[:0:-1]

    token_rows = exchange([hidden_x.reshape(tokens, local_width)] * pairs, "group", 2)
    mate_codes = swap(delta_codes, "group", 1)
    mate_scales = swap(delta_scales, "group", 1)

    own_delta, base_blocks, own_query, places, partials = prepare(
        owner_map,
        lengths,
        delta_scales,
        delta_codes,
        queries.reshape(tokens, H * HD),
        kv_cache.reshape(-1, 2 * KVH * HD),
        base_weight,
        rows,
        steps,
        heads_own,
        tensor_count,
    )
    mate_scales, partials[2] = lax.optimization_barrier((mate_scales, partials[2]))
    behind = lax.optimization_barrier((*near_first(token_rows), own_query))
    token_rows, own_query = near_first(list(behind[:pairs])), behind[-1]
    projected = project(
        own_delta, base_blocks, mate_codes, mate_scales, near_first(token_rows)
    )
    arrived = exchange(near_first(projected), "group", 2)
    partials = exchange(partials, "tensor", 1)
    pieces = pack_pieces(
        owner_map, places, arrived, owner_block, tensor_count, near_width, slice_width
    )
    pieces = exchange(pieces, "tensor", 1)
    partial = merge(near_first(partials), rows)
    new_out, attended = finish(own_query, pieces, partial, rows, steps, heads_own, near_width)
    return (new_out.reshape(rows, steps, -1), attended.reshape(rows, steps, -1))


def solution(mesh):
    in_specs = (
        P("group", None, "tensor"),
        P(None, "tensor"),
        P("group", "tensor"),
        P("group", "tensor"),
        P(),
        P("group", "tensor", None),
        P("group", None, None),
        P("group"),
    )
    out_specs = (P("group", None, "tensor"), P("group", None, "tensor"))
    return jax.shard_map(
        on_device, mesh=mesh, in_specs=in_specs, out_specs=out_specs, check_vma=False
    )
```
